32 devices in a mesh: row: 8 (over z, core), col: 4 (over y, x).
Axes of the slice: x: 2, y: 2, z: 4, core: 2. Of those that a mesh axis runs over, the one named last changes fastest.
Arguments:
- cells: float32 [1024, 1024], P(('row', 'col')), may hold values from 0 to 1
- instance_cell: int32 [32, 128], P('row', 'col'), may hold values from 0 to 1023, as said below
- target: float32 [1024, 4096], P('row', 'col'), may hold values from 0 to 1
- row_taps: float32 [8, 65], replicated, may hold values from -0.75 to 0.75
- col_taps: float32 [8, 65], replicated, may hold values from -0.75 to 0.75
- kernel_weight: float32 [8], replicated, may hold values from 0.05 to 0.5
Outputs:
- cells_out: float32 [1024, 1024], P(('row', 'col'))
The draws below stay inside these ranges and needn't reach their ends.
Inputs may be any that keep to these rules, and one draw needn't show every extreme that they name: `instance_cell`: each entry is the index of the device that holds the cell, along row+col with row slowest, times 32, plus the cell's place there. Tile (a, b) lies on device (a // 4, b // 32). Among one device's tiles at most 8 name cells held by any one device, and one holding device is named by exactly 8 tiles of every device.
All inputs are finite; a program needn't handle non-finite values.
Results may differ from the reference program's by a relative error of at most 0.00016.
Values sent between devices are 32-bit elements; how exact they have to be, the bound alone decides.
No kernel may reach another device: no remote copies, remote signals or barrier semaphores. Data moves between devices by JAX's collectives and lax.ppermute only.
A program may use at most 128 MiB of HBM per device.

```python
import math
import jax
import jax.numpy as jnp
from jax import lax

TILE = 32
TAPS = 65
HALF = 32
KERNELS = 8
ITERS = 1
CR = 128
CC = 1024
SLOTS = 32
OWNERS = 32
NR = 1024
NC = 4096
TPD = 128
CAP = 8
CELLS = 1024


def draw_instance_cell(key, part):
    owners = OWNERS
    tiles_here = TPD
    hottest = jax.random.randint(jax.random.fold_in(key, 7), (), 0, owners)

    def one_device(device):
        subkey = jax.random.fold_in(key, device + 11)
        others = (hottest + 1 + jax.random.permutation(jax.random.fold_in(subkey, 1), owners - 1)) % owners
        placing = jnp.arange(tiles_here)
        rest_index = jnp.maximum(placing - CAP, 0) % (owners - 1)
        owner_index = jnp.where(placing < CAP, hottest, others[rest_index])
        owner_index = jax.random.permutation(jax.random.fold_in(subkey, 2), owner_index)
        slot_index = jax.random.randint(jax.random.fold_in(subkey, 3), (tiles_here,), 0, SLOTS)
        return owner_index * SLOTS + slot_index
    table = jax.vmap(one_device)(jnp.arange(owners))
    row_count = NR // CR
    col_count = NC // CC
    table = table.reshape(row_count, col_count, CR // TILE, CC // TILE).transpose(0, 2, 1, 3)
    return table.reshape(row_count * (CR // TILE), col_count * (CC // TILE)).astype(jnp.int32)


def level_of(rng, shape, split, least, largest):
    factor_of = 1.0
    for dim, shards_of in split:
        steps = jax.random.uniform(jax.random.fold_in(jax.random.fold_in(rng, 6), dim), (shards_of,), jnp.float32, least / len(split), largest / len(split))
        factor_of = factor_of * jnp.repeat(jnp.exp(steps), shape[dim] // shards_of).reshape((-1,) + (1,) * (len(shape) - 1 - dim))
    return factor_of


def bell_draw(rng, extent, scale, bound, kind=jnp.bfloat16):
    array = scale * jax.random.normal(rng, extent, jnp.float32)
    return jnp.clip(array, min=-bound, max=bound).astype(kind)


def setup_inputs(seed: int = 0) -> dict:
    arg_keys = jax.random.split(jax.random.key(seed), 7)
    cells = jnp.clip(1.0 * jax.random.uniform(arg_keys[0], (CELLS, TILE * TILE), jnp.float32) ** level_of(arg_keys[0], (CELLS, TILE * TILE), ((0, 32),), -0.2, 0.2), 0.0, 1.0)
    instance_cell = draw_instance_cell(jax.random.fold_in(arg_keys[6], 71), 0)
    target = jnp.clip(1.0 * jax.random.uniform(arg_keys[2], (NR, NC), jnp.float32) ** level_of(arg_keys[2], (NR, NC), ((0, 8), (1, 4)), -0.2, 0.2), 0.0, 1.0)
    row_taps = bell_draw(arg_keys[3], (KERNELS, TAPS), TAPS ** -0.5, 0.75, jnp.float32)
    col_taps = bell_draw(arg_keys[4], (KERNELS, TAPS), TAPS ** -0.5, 0.75, jnp.float32)
    kernel_weight = jnp.clip(jnp.exp(jax.random.uniform(arg_keys[5], (KERNELS,), jnp.float32, math.log(0.05), math.log(0.5))), 0.05, 0.5)
    return {"cells": cells, "instance_cell": instance_cell, "target": target, "row_taps": row_taps, "col_taps": col_taps, "kernel_weight": kernel_weight}


STEEPNESS = 4.0
THRESHOLD = 0.3
STEP_RATE = 0.5
HIGHEST = lax.Precision.HIGHEST


def toeplitz_bands(taps):
    kernels = taps.shape[0]
    front = jnp.zeros((kernels, 127), jnp.float32)
    back = jnp.zeros((kernels, 256), jnp.float32)
    padded = jnp.concatenate([front, taps.astype(jnp.float32), back], axis=1)
    length = padded.shape[1]
    repeated = jnp.tile(padded, (1, 128))[:, : 128 * (length - 1)]
    shaped = repeated.reshape(kernels, 128, length - 1)[:, :, 127:383]
    return shaped.transpose(0, 2, 1)


def along_last(values, band):
    breadth = values.shape[-1] - (TAPS - 1)
    blocks = -(-breadth // 128)
    padding = blocks * 128 + 128 - values.shape[-1]
    lead_shape = values.shape[:-1]
    padded = jnp.pad(values, [(0, 0)] * len(lead_shape) + [(0, padding)])
    leading = padded[..., : blocks * 128].reshape(lead_shape + (blocks, 128))
    trailing = padded[..., 128:].reshape(lead_shape + (blocks, 128))
    result = jnp.einsum("...nb,bm->...nm", leading, band[:128], precision=HIGHEST)
    result = result + jnp.einsum("...nb,bm->...nm", trailing, band[128:], precision=HIGHEST)
    return result.reshape(lead_shape + (blocks * 128,))[..., :breadth]


def along_first(values, band):
    height = values.shape[0] - (TAPS - 1)
    blocks = -(-height // 128)
    padding = blocks * 128 + 128 - values.shape[0]
    columns = values.shape[1]
    padded = jnp.pad(values, [(0, padding), (0, 0)])
    leading = padded[: blocks * 128].reshape(blocks, 128, columns)
    trailing = padded[128:].reshape(blocks, 128, columns)
    result = jnp.einsum("nbc,bm->nmc", leading, band[:128], precision=HIGHEST)
    result = result + jnp.einsum("nbc,bm->nmc", trailing, band[128:], precision=HIGHEST)
    return result.reshape(blocks * 128, columns)[:height]


def image_field(widened, row_band, col_band):
    return along_first(along_last(widened, col_band), row_band)


def reference(cells, instance_cell, target, row_taps, col_taps, kernel_weight):
    row_bands = toeplitz_bands(row_taps)
    col_bands = toeplitz_bands(col_taps)
    row_flips = toeplitz_bands(row_taps[:, ::-1])
    col_flips = toeplitz_bands(col_taps[:, ::-1])
    tile_rows, tile_cols = instance_cell.shape
    flat_cells = instance_cell.reshape(-1).astype(jnp.int32)
    current = cells
    for iteration in range(ITERS):
        tiles = jnp.take(current, flat_cells, axis=0)
        mask = tiles.reshape(tile_rows, tile_cols, TILE, TILE).transpose(0, 2, 1, 3).reshape(tile_rows * TILE, tile_cols * TILE)
        widened = jnp.pad(mask, HALF)

        def forward_kernel(total, pieces):
            row_band, col_band, weight = pieces
            field = image_field(widened, row_band, col_band)
            return total + weight * field * field, None

        intensity, unused = lax.scan(forward_kernel, jnp.zeros_like(mask), (row_bands, col_bands, kernel_weight))
        resist = jax.nn.sigmoid(STEEPNESS * (intensity - THRESHOLD))
        sensitivity = 2.0 * (resist - target) * STEEPNESS * resist * (1.0 - resist)

        def adjoint_kernel(total, pieces):
            row_band, col_band, row_flip, col_flip, weight = pieces
            field = image_field(widened, row_band, col_band)
            spread = jnp.pad(2.0 * weight * sensitivity * field, HALF)
            return total + image_field(spread, row_flip, col_flip), None

        gradient, unused = lax.scan(adjoint_kernel, jnp.zeros_like(mask), (row_bands, col_bands, row_flips, col_flips, kernel_weight))
        tile_grads = gradient.reshape(tile_rows, TILE, tile_cols, TILE).transpose(0, 2, 1, 3).reshape(-1, TILE * TILE)
        summed = jax.ops.segment_sum(tile_grads, flat_cells, num_segments=current.shape[0])
        current = current - STEP_RATE * summed
    return current
```

```python
import functools

import jax
import jax.numpy as jnp
from jax import lax
from jax.experimental import pallas as pl
from jax.experimental.pallas import tpu as pltpu
from jax.sharding import PartitionSpec as P

TILE = 32
TAPS = 65
HALF = 32
KERNELS = 8
LANES = 128
WIDE = 256

STEEPNESS = 4.0
THRESHOLD = 0.3
STEP_RATE = 0.5

F32 = jnp.float32
BF16 = jnp.bfloat16


def split(x):
    high = x.astype(BF16)
    return high, (x - high.astype(F32)).astype(BF16)


def mm(a, b):
    return jnp.dot(a, b, preferred_element_type=F32)


def bands_kernel(wave_ref, fcol_ref, frow_ref, brow_ref, bcol_ref):
    rows = lax.broadcasted_iota(jnp.int32, (LANES, LANES), 0)
    lanes = lax.broadcasted_iota(jnp.int32, (LANES, LANES), 1)
    zero = jnp.zeros((LANES, LANES), F32)

    def circular(index, start):
        base = jnp.broadcast_to(wave_ref[pl.ds(index, 1), :], (LANES, LANES))
        return pltpu.roll(base, start, 1, stride=1, stride_axis=0)

    def put(ref, kernel, r0, c0, block, height=LANES, breadth=LANES):
        high, low = split(block)
        ref[kernel, 0, r0 : r0 + height, c0 : c0 + breadth] = high[:height, :breadth]
        ref[kernel, 1, r0 : r0 + height, c0 : c0 + breadth] = low[:height, :breadth]

    @pl.loop(0, KERNELS)
    def _(k):
        near = circular(k, 0)
        put(frow_ref, k, 0, 0, jnp.where(lanes >= rows, near, zero))
        put(frow_ref, k, 0, LANES, jnp.where(lanes < rows, near, zero))
        put(frow_ref, k, LANES, 0, zero, 64)
        put(frow_ref, k, LANES, LANES, jnp.where(lanes >= rows, near, zero), 64)
        near = circular(2 * KERNELS + k, 0)
        put(brow_ref, k, 0, 0, jnp.where(lanes >= rows, near, zero))
        put(brow_ref, k, 0, LANES, jnp.where(lanes < rows, near, zero))
        near = circular(3 * KERNELS + k, LANES // 2)
        put(fcol_ref, k, 0, 0, jnp.where(rows >= lanes, near, zero))
        put(fcol_ref, k, LANES, 0, jnp.where(rows < lanes, near, zero))
        near = circular(KERNELS + k, LANES // 2)
        low = jnp.where(rows >= lanes, near, zero)
        high = jnp.where(rows < lanes, near, zero)
        put(bcol_ref, k, 0, 0, low)
        put(bcol_ref, k, LANES, 0, high)
        put(bcol_ref, k, 2 * LANES, 0, zero)
        put(bcol_ref, k, 0, LANES, zero)
        put(bcol_ref, k, LANES, LANES, low)
        put(bcol_ref, k, 2 * LANES, LANES, high)


def make_bands(row_taps, col_taps):
    taps = jnp.concatenate([row_taps, col_taps], axis=0)
    taps = jnp.concatenate([taps, taps[:, ::-1]], axis=0)
    wave = jnp.pad(taps, [(0, 0), (0, LANES - TAPS)])
    shapes = [
        (KERNELS, 2, 256, LANES),
        (KERNELS, 2, 192, 256),
        (KERNELS, 2, LANES, 256),
        (KERNELS, 2, 384, 256),
    ]
    return pl.pallas_call(
        bands_kernel,
        out_shape=[jax.ShapeDtypeStruct(s, BF16) for s in shapes],
        in_specs=[pl.BlockSpec(memory_space=pltpu.VMEM)],
        out_specs=[pl.BlockSpec(memory_space=pltpu.VMEM)] * 4,
        compiler_params=pltpu.CompilerParams(vmem_limit_bytes=40 * 2**20),
        name="bands",
    )(wave)


def transpose_blocks(parts, block):
    turned = []
    for d in range(4):
        x = parts[d]
        for s in range(1, 4):
            x = jnp.where(block == s, parts[(s + d) % 4], x)
        turned.append(pltpu.roll(x, 32 * d, 1) if d else x)
    out = []
    for s in range(4):
        x = turned[(-s) % 4]
        for b in range(1, 4):
            x = jnp.where(block == b, turned[(b - s) % 4], x)
        out.append(x)
    return out


def image_kernel(
    tile_rows,
    tile_cols,
    index_ref,
    where_ref,
    weight_ref,
    cells_ref,
    target_ref,
    fcol_ref,
    frow_ref,
    brow_ref,
    bcol_ref,
    out_ref,
    mask_ref,
    mhigh_ref,
    mlow_ref,
    field_ref,
    ghigh_ref,
    glow_ref,
    grad_ref,
):
    high_rows = tile_rows * TILE + 4 * HALF
    field_rows = tile_rows * TILE + 2 * HALF
    rows_here = tile_rows * TILE
    groups = tile_cols // 4
    block = lax.broadcasted_iota(jnp.int32, (8, LANES), 1) // 32
    nothing = jnp.zeros((8, LANES), F32)

    @pl.loop(0, tile_rows + 4)
    def _(a):
        for g in range(groups + 1):
            parts = []
            for b in range(4):
                start = index_ref[a, 4 * g + b]
                tile = cells_ref[pl.ds(jnp.maximum(start, 0), 8, stride=8), :]
                parts.append(jnp.where(start >= 0, tile, nothing))
            for s, piece in enumerate(transpose_blocks(parts, block)):
                mask_ref[pl.ds(g * high_rows + a * TILE + s, 8, stride=4), :] = piece

    for g in range(groups + 1):
        lanes = slice(LANES * g, LANES * (g + 1))
        high, low = split(mask_ref[g * high_rows : (g + 1) * high_rows, :])
        mhigh_ref[:, lanes] = high
        mlow_ref[:, lanes] = low
    for g in range(groups + 1, mhigh_ref.shape[1] // LANES):
        lanes = slice(LANES * g, LANES * (g + 1))
        mhigh_ref[:, lanes] = jnp.zeros((high_rows, LANES), BF16)
        mlow_ref[:, lanes] = jnp.zeros((high_rows, LANES), BF16)

    def columns(offset, width):
        def window(ref, j):
            return ref[:, pl.ds(pl.multiple_of(offset + j * LANES, LANES), WIDE)]

        blocks = width // LANES
        stacked = jnp.concatenate(
            [
                jnp.concatenate(
                    [window(mhigh_ref, j), window(mlow_ref, j), window(mhigh_ref, j)], axis=1
                )
                for j in range(blocks)
            ],
            axis=0,
        )
        intensity = None
        for pair in range(KERNELS // 2):
            two = [
                jnp.concatenate([fcol_ref[2 * pair, v], fcol_ref[2 * pair + 1, v]], axis=1)
                for v in range(2)
            ]
            wide = mm(stacked, jnp.concatenate([two[0], two[0], two[1]], axis=0))
            for h in range(2):
                k = 2 * pair + h
                half = jnp.concatenate(
                    [
                        wide[j * high_rows : (j + 1) * high_rows, h * LANES : (h + 1) * LANES]
                        for j in range(blocks)
                    ],
                    axis=1,
                )
                high, low = split(half)
                field = mm(
                    jnp.concatenate([frow_ref[k, 0], frow_ref[k, 0], frow_ref[k, 1]], axis=1),
                    jnp.concatenate([high, low, high], axis=0),
                )
                field_ref[k, :, :width] = field
                term = weight_ref[k] * field * field
                intensity = term if intensity is None else intensity + term
        resist = 1.0 / (1.0 + jnp.exp(-STEEPNESS * (intensity - THRESHOLD)))
        target = target_ref[:, pl.ds(pl.multiple_of(offset, LANES), width)]
        sensitivity = 2.0 * (resist - target) * STEEPNESS * resist * (1.0 - resist)
        row = where_ref[0] + lax.broadcasted_iota(jnp.int32, (field_rows, width), 0)
        col = where_ref[1] + offset + lax.broadcasted_iota(jnp.int32, (field_rows, width), 1)
        inside = (row >= 0) & (row < where_ref[2]) & (col >= 0) & (col < where_ref[3])
        sensitivity = jnp.where(inside, sensitivity, 0.0)
        for k in range(KERNELS):
            product = (2.0 * weight_ref[k]) * sensitivity * field_ref[k, :, :width]
            high, low = split(product)
            near = brow_ref[k, 0, :, :192]
            part = mm(near, high) + (mm(near, low) + mm(brow_ref[k, 1, :, :192], high))
            high, low = split(part)
            place = pl.ds(pl.multiple_of(offset, LANES), width)
            ghigh_ref[k, :, place] = high
            glow_ref[k, :, place] = low

    supers = tile_cols * TILE // WIDE

    @pl.loop(0, supers)
    def _(jj):
        columns(jj * WIDE, WIDE)

    columns(supers * WIDE, LANES)

    def spread_back(k):
        def window(ref, jj):
            return ref[k, :, WIDE * jj : WIDE * jj + 384]

        stacked = jnp.concatenate(
            [
                jnp.concatenate(
                    [window(ghigh_ref, jj), window(glow_ref, jj), window(ghigh_ref, jj)], axis=1
                )
                for jj in range(supers)
            ],
            axis=0,
        )
        return mm(
            stacked, jnp.concatenate([bcol_ref[k, 0], bcol_ref[k, 0], bcol_ref[k, 1]], axis=0)
        )

    def add(part, fresh):
        for g in range(groups):
            rows = slice(g * rows_here, (g + 1) * rows_here)
            top = (g // 2) * rows_here
            piece = part[top : top + rows_here, LANES * (g % 2) : LANES * (g % 2 + 1)]
            grad_ref[rows, :] = piece if fresh else grad_ref[rows, :] + piece

    add(spread_back(0), True)

    @pl.loop(1, KERNELS)
    def _(k):
        add(spread_back(k), False)

    out_ref[...] = jnp.zeros_like(out_ref)

    @pl.loop(0, tile_rows)
    def _(a):
        for g in range(groups):
            base = g * rows_here + a * TILE
            parts = [grad_ref[pl.ds(base + s, 8, stride=4), :] for s in range(4)]
            for b, tile in enumerate(transpose_blocks(parts, block)):
                place = pl.ds(index_ref[a + 2, 4 * g + b + 2], 8, stride=8)
                out_ref[place, :] += tile


def to_rows(x):
    count = x.shape[0]
    return x.reshape(count // 8, 8, 8, LANES).transpose(0, 2, 1, 3).reshape(count * 8, LANES)


def from_rows(x):
    count = x.shape[0] // 8
    return x.reshape(count // 8, 8, 8, LANES).transpose(0, 2, 1, 3).reshape(count, 8 * LANES)


def widened_2(x, width):
    for axis, dim in (("row", 0), ("col", 1)):
        count, length = lax.axis_size(axis), x.shape[dim]
        up = [(i, i + 1) for i in range(count - 1)]
        down = [(j, i) for i, j in up]
        before = lax.ppermute(lax.slice_in_dim(x, length - width, length, axis=dim), axis, up)
        after = lax.ppermute(lax.slice_in_dim(x, 0, width, axis=dim), axis, down)
        x = jnp.concatenate([before, x, after], axis=dim)
    return x


def shards(cells, instance_cell, target, row_taps, col_taps, kernel_weight):
    row_count = lax.axis_size("row")
    col_count = lax.axis_size("col")
    tile_rows, tile_cols = instance_cell.shape
    height, breadth = target.shape
    flat = to_rows(cells)
    everything = lax.all_gather(flat, ("row", "col"), axis=0, tiled=True)
    table = lax.all_gather(instance_cell, ("row", "col"), axis=0)
    table = table.reshape(row_count, col_count, tile_rows, tile_cols).transpose(0, 2, 1, 3)
    table = table.reshape(row_count * tile_rows, col_count * tile_cols)
    table = (table // 8) * 64 + table % 8
    table = jnp.pad(table, 2, constant_values=-1)
    my_row, my_col = lax.axis_index("row"), lax.axis_index("col")
    index = lax.dynamic_slice(
        table, (my_row * tile_rows, my_col * tile_cols), (tile_rows + 4, tile_cols + 4)
    )
    where = jnp.stack(
        [
            my_row * height - HALF,
            my_col * breadth - HALF,
            jnp.int32(row_count * height),
            jnp.int32(col_count * breadth),
        ]
    ).astype(jnp.int32)
    wide_target = jnp.pad(widened_2(target, HALF), [(0, 0), (0, 64)])
    bands = make_bands(row_taps, col_taps)
    field_rows = height + 2 * HALF
    summed = pl.pallas_call(
        functools.partial(image_kernel, tile_rows, tile_cols),
        out_shape=jax.ShapeDtypeStruct(everything.shape, F32),
        in_specs=[pl.BlockSpec(memory_space=pltpu.SMEM)] * 3
        + [pl.BlockSpec(memory_space=pltpu.VMEM)] * 6,
        out_specs=pl.BlockSpec(memory_space=pltpu.VMEM),
        scratch_shapes=[
            pltpu.VMEM(((height + 4 * HALF) * (breadth // LANES + 1), LANES), F32),
            pltpu.VMEM((height + 4 * HALF, breadth + 256), BF16),
            pltpu.VMEM((height + 4 * HALF, breadth + 256), BF16),
            pltpu.VMEM((KERNELS, field_rows, WIDE), F32),
            pltpu.VMEM((KERNELS, height, breadth + 128), BF16),
            pltpu.VMEM((KERNELS, height, breadth + 128), BF16),
            pltpu.VMEM((height * (breadth // LANES), LANES), F32),
        ],
        compiler_params=pltpu.CompilerParams(vmem_limit_bytes=60 * 2**20),
        name="image",
    )(index, where, kernel_weight, everything, wide_target, *bands)
    mine = lax.psum_scatter(summed, ("row", "col"), scatter_dimension=0, tiled=True)
    return cells - STEP_RATE * from_rows(mine)


def solution(mesh):
    placed = (P(("row", "col"), None), P("row", "col"), P("row", "col"), P(), P(), P())
    return jax.shard_map(
        shards, mesh=mesh, in_specs=placed, out_specs=P(("row", "col"), None), check_vma=False
    )
```

```python
import jax
import jax.numpy as jnp
from jax import lax
from jax.experimental import pallas as pl
from jax.experimental.pallas import tpu as pltpu
from jax.sharding import Mesh
from jax.sharding import PartitionSpec as P

TILE = 32
TAPS = 65
HALF = 32
KERNELS = 8
LANES = 128
WIDE = 256

STEEPNESS = 4.0
THRESHOLD = 0.3
STEP_RATE = 0.5

F32 = jnp.float32
BF16 = jnp.bfloat16


def split(x):
    high = x.astype(BF16)
    return high, (x - high.astype(F32)).astype(BF16)


def mm(a, b):
    return jnp.dot(a, b, preferred_element_type=F32)


def bands_kernel(wave_ref, fcol_ref, frow_ref, brow_ref, bcol_ref):
    rows = lax.broadcasted_iota(jnp.int32, (LANES, LANES), 0)
    lanes = lax.broadcasted_iota(jnp.int32, (LANES, LANES), 1)
    zero = jnp.zeros((LANES, LANES), F32)

    def circular(index, start):
        base = jnp.broadcast_to(wave_ref[pl.ds(index, 1), :], (LANES, LANES))
        return pltpu.roll(base, start, 1, stride=1, stride_axis=0)

    def put(ref, kernel, r0, c0, block, height=LANES, breadth=LANES):
        high, low = split(block)
        ref[kernel, 0, r0 : r0 + height, c0 : c0 + breadth] = high[:height, :breadth]
        ref[kernel, 1, r0 : r0 + height, c0 : c0 + breadth] = low[:height, :breadth]

    @pl.loop(0, KERNELS)
    def _(k):
        near = circular(k, 0)
        put(frow_ref, k, 0, 0, jnp.where(lanes >= rows, near, zero))
        put(frow_ref, k, 0, LANES, jnp.where(lanes < rows, near, zero))
        put(frow_ref, k, LANES, 0, zero, 64)
        put(frow_ref, k, LANES, LANES, jnp.where(lanes >= rows, near, zero), 64)
        near = circular(2 * KERNELS + k, 0)
        put(brow_ref, k, 0, 0, jnp.where(lanes >= rows, near, zero))
        put(brow_ref, k, 0, LANES, jnp.where(lanes < rows, near, zero))
        near = circular(3 * KERNELS + k, LANES // 2)
        put(fcol_ref, k, 0, 0, jnp.where(rows >= lanes, near, zero))
        put(fcol_ref, k, LANES, 0, jnp.where(rows < lanes, near, zero))
        near = circular(KERNELS + k, LANES // 2)
        low = jnp.where(rows >= lanes, near, zero)
        high = jnp.where(rows < lanes, near, zero)
        put(bcol_ref, k, 0, 0, low)
        put(bcol_ref, k, LANES, 0, high)
        put(bcol_ref, k, 2 * LANES, 0, zero)
        put(bcol_ref, k, 0, LANES, zero)
        put(bcol_ref, k, LANES, LANES, low)
        put(bcol_ref, k, 2 * LANES, LANES, high)


def make_bands(row_taps, col_taps):
    taps = jnp.concatenate([row_taps, col_taps], axis=0)
    taps = jnp.concatenate([taps, taps[:, ::-1]], axis=0)
    wave = jnp.pad(taps, [(0, 0), (0, LANES - TAPS)])
    shapes = [
        (KERNELS, 2, 256, LANES),
        (KERNELS, 2, 192, 256),
        (KERNELS, 2, LANES, 256),
        (KERNELS, 2, 384, 256),
    ]
    return pl.pallas_call(
        bands_kernel,
        out_shape=[jax.ShapeDtypeStruct(s, BF16) for s in shapes],
        in_specs=[pl.BlockSpec(memory_space=pltpu.VMEM)],
        out_specs=[pl.BlockSpec(memory_space=pltpu.VMEM)] * 4,
        compiler_params=pltpu.CompilerParams(vmem_limit_bytes=40 * 2**20),
        name="bands",
    )(wave)


def transpose_blocks(parts, block):
    turned = []
    for d in range(4):
        x = parts[d]
        for s in range(1, 4):
            x = jnp.where(block == s, parts[(s + d) % 4], x)
        turned.append(pltpu.roll(x, 32 * d, 1) if d else x)
    out = []
    for s in range(4):
        x = turned[(-s) % 4]
        for b in range(1, 4):
            x = jnp.where(block == b, turned[(b - s) % 4], x)
        out.append(x)
    return out


def pack_kernel(asked_ref, cells_ref, out_ref):
    def place(n):
        asked = jnp.maximum(asked_ref[n], 0)
        tile = cells_ref[pl.ds((asked // 8) * 64 + asked % 8, 8, stride=8), :]
        out_ref[pl.ds(pl.multiple_of(n * 8, 8), 8), :] = tile

    @pl.loop(0, asked_ref.shape[0] // 8)
    def _(group):
        for n in range(8):
            place(group * 8 + n)


def merge_kernel(asked_ref, tiles_ref, out_ref):
    out_ref[...] = jnp.zeros_like(out_ref)
    nothing = jnp.zeros((8, LANES), F32)

    def place(n):
        asked = asked_ref[n]
        tile = tiles_ref[pl.ds(pl.multiple_of(n * 8, 8), 8), :]
        cell = jnp.maximum(asked, 0)
        there = pl.ds((cell // 8) * 64 + cell % 8, 8, stride=8)
        out_ref[there, :] += jnp.where(asked >= 0, tile, nothing)

    @pl.loop(0, asked_ref.shape[0] // 8)
    def _(group):
        for n in range(8):
            place(group * 8 + n)


def step_kernel(cells_ref, sums_ref, out_ref):
    own = cells_ref.shape[0]
    total = sums_ref[:own, :]
    for d in range(1, sums_ref.shape[0] // own):
        total = total + sums_ref[d * own : (d + 1) * own, :]
    out_ref[...] = cells_ref[...] - STEP_RATE * total


def assemble_kernel(index_ref, tiles_ref, target_ref, mask_ref, first_ref, last_ref, turned_ref):
    tile_rows, tile_cols = index_ref.shape
    height = tile_rows * TILE
    groups = tile_cols // 4
    block = lax.broadcasted_iota(jnp.int32, (8, LANES), 1) // 32

    @pl.loop(0, tile_rows)
    def _(a):
        for g in range(groups):
            parts = [
                tiles_ref[pl.ds(pl.multiple_of(index_ref[a, 4 * g + b] * 8, 8), 8), :]
                for b in range(4)
            ]
            for s, piece in enumerate(transpose_blocks(parts, block)):
                turned_ref[pl.ds(g * height + a * TILE + s, 8, stride=4), :] = piece

    for g in range(groups):
        lanes = slice(LANES * g, LANES * (g + 1))
        piece = turned_ref[g * height : (g + 1) * height, :]
        mask_ref[:, lanes] = piece
        first_ref[: 2 * HALF, lanes] = piece[: 2 * HALF]
        last_ref[: 2 * HALF, lanes] = piece[height - 2 * HALF :]
    first_ref[2 * HALF :, :] = target_ref[:HALF, :]
    last_ref[2 * HALF :, :] = target_ref[height - HALF :, :]


def edges_kernel(mask_ref, target_ref, top_ref, bottom_ref, first_ref, last_ref):
    height, breadth = mask_ref.shape
    wide = 2 * HALF
    for ref, lanes in ((first_ref, slice(0, LANES)), (last_ref, slice(breadth - LANES, breadth))):
        ref[:wide, :] = top_ref[:wide, lanes]
        ref[wide : wide + height, :] = mask_ref[:, lanes]
        ref[wide + height : 2 * wide + height, :] = bottom_ref[:wide, lanes]
        start = 2 * wide + height
        ref[start : start + HALF, :] = top_ref[wide:, lanes]
        ref[start + HALF : start + HALF + height, :] = target_ref[:, lanes]
        ref[start + HALF + height :, :] = bottom_ref[wide:, lanes]


def image_kernel(
    index_ref,
    where_ref,
    weight_ref,
    mask_ref,
    own_ref,
    top_ref,
    bottom_ref,
    before_ref,
    after_ref,
    fcol_ref,
    frow_ref,
    brow_ref,
    bcol_ref,
    out_ref,
    mhigh_ref,
    mlow_ref,
    target_ref,
    field_ref,
    ghigh_ref,
    glow_ref,
    grad_ref,
):
    tile_rows, tile_cols = index_ref.shape
    rows_here = tile_rows * TILE
    high_rows = rows_here + 4 * HALF
    field_rows = rows_here + 2 * HALF
    groups = tile_cols // 4
    wide = 2 * HALF
    block = lax.broadcasted_iota(jnp.int32, (8, LANES), 1) // 32

    def shifted(shift, parts, edge, emit):
        for rows, ref, start, count in parts:
            lane = lax.broadcasted_iota(jnp.int32, (count, LANES), 1)
            turned = None
            for g in range(groups + 2):
                if g == 0:
                    piece = before_ref[edge + rows : edge + rows + count, :]
                elif g == groups + 1:
                    piece = after_ref[edge + rows : edge + rows + count, :]
                else:
                    piece = ref[start : start + count, LANES * (g - 1) : LANES * g]
                fresh = pltpu.roll(piece, shift, 1)
                if g:
                    emit(rows, count, g - 1, jnp.where(lane < shift, turned, fresh))
                turned = fresh

    def put_mask(rows, count, g, piece):
        high, low = split(piece)
        mhigh_ref[rows : rows + count, LANES * g : LANES * (g + 1)] = high
        mlow_ref[rows : rows + count, LANES * g : LANES * (g + 1)] = low

    def put_target(rows, count, g, piece):
        target_ref[rows : rows + count, LANES * g : LANES * (g + 1)] = piece

    shifted(
        wide,
        (
            (0, top_ref, 0, wide),
            (wide, mask_ref, 0, rows_here),
            (wide + rows_here, bottom_ref, 0, wide),
        ),
        0,
        put_mask,
    )
    shifted(
        HALF,
        (
            (0, top_ref, wide, HALF),
            (HALF, own_ref, 0, rows_here),
            (HALF + rows_here, bottom_ref, wide, HALF),
        ),
        high_rows,
        put_target,
    )
    for g in range(groups + 1, mhigh_ref.shape[1] // LANES):
        lanes = slice(LANES * g, LANES * (g + 1))
        mhigh_ref[:, lanes] = jnp.zeros((high_rows, LANES), BF16)
        mlow_ref[:, lanes] = jnp.zeros((high_rows, LANES), BF16)

    def columns(offset, width):
        def window(ref, j):
            return ref[:, pl.ds(pl.multiple_of(offset + j * LANES, LANES), WIDE)]

        blocks = width // LANES
        stacked = jnp.concatenate(
            [
                jnp.concatenate(
                    [window(mhigh_ref, j), window(mlow_ref, j), window(mhigh_ref, j)], axis=1
                )
                for j in range(blocks)
            ],
            axis=0,
        )
        intensity = None
        for pair in range(KERNELS // 2):
            two = [
                jnp.concatenate([fcol_ref[2 * pair, v], fcol_ref[2 * pair + 1, v]], axis=1)
                for v in range(2)
            ]
            wide = mm(stacked, jnp.concatenate([two[0], two[0], two[1]], axis=0))
            for h in range(2):
                k = 2 * pair + h
                half = jnp.concatenate(
                    [
                        wide[j * high_rows : (j + 1) * high_rows, h * LANES : (h + 1) * LANES]
                        for j in range(blocks)
                    ],
                    axis=1,
                )
                high, low = split(half)
                field = mm(
                    jnp.concatenate([frow_ref[k, 0], frow_ref[k, 0], frow_ref[k, 1]], axis=1),
                    jnp.concatenate([high, low, high], axis=0),
                )
                field_ref[k, :, :width] = field
                term = weight_ref[k] * field * field
                intensity = term if intensity is None else intensity + term
        resist = 1.0 / (1.0 + jnp.exp(-STEEPNESS * (intensity - THRESHOLD)))
        target = target_ref[:, pl.ds(pl.multiple_of(offset, LANES), width)]
        sensitivity = 2.0 * (resist - target) * STEEPNESS * resist * (1.0 - resist)
        row = where_ref[0] + lax.broadcasted_iota(jnp.int32, (field_rows, width), 0)
        col = where_ref[1] + offset + lax.broadcasted_iota(jnp.int32, (field_rows, width), 1)
        inside = (row >= 0) & (row < where_ref[2]) & (col >= 0) & (col < where_ref[3])
        sensitivity = jnp.where(inside, sensitivity, 0.0)
        for k in range(KERNELS):
            product = (2.0 * weight_ref[k]) * sensitivity * field_ref[k, :, :width]
            high, low = split(product)
            near = brow_ref[k, 0, :, :192]
            part = mm(near, high) + (mm(near, low) + mm(brow_ref[k, 1, :, :192], high))
            high, low = split(part)
            place = pl.ds(pl.multiple_of(offset, LANES), width)
            ghigh_ref[k, :, place] = high
            glow_ref[k, :, place] = low

    supers = tile_cols * TILE // WIDE

    @pl.loop(0, supers)
    def _(jj):
        columns(jj * WIDE, WIDE)

    columns(supers * WIDE, LANES)

    def spread_back(k):
        def window(ref, jj):
            return ref[k, :, WIDE * jj : WIDE * jj + 384]

        stacked = jnp.concatenate(
            [
                jnp.concatenate(
                    [window(ghigh_ref, jj), window(glow_ref, jj), window(ghigh_ref, jj)], axis=1
                )
                for jj in range(supers)
            ],
            axis=0,
        )
        return mm(
            stacked, jnp.concatenate([bcol_ref[k, 0], bcol_ref[k, 0], bcol_ref[k, 1]], axis=0)
        )

    def add(part, fresh):
        for g in range(groups):
            rows = slice(g * rows_here, (g + 1) * rows_here)
            top = (g // 2) * rows_here
            piece = part[top : top + rows_here, LANES * (g % 2) : LANES * (g % 2 + 1)]
            grad_ref[rows, :] = piece if fresh else grad_ref[rows, :] + piece

    add(spread_back(0), True)

    @pl.loop(1, KERNELS)
    def _(k):
        add(spread_back(k), False)

    @pl.loop(0, tile_rows)
    def _(a):
        for g in range(groups):
            base = g * rows_here + a * TILE
            parts = [grad_ref[pl.ds(base + s, 8, stride=4), :] for s in range(4)]
            for b, tile in enumerate(transpose_blocks(parts, block)):
                place = pl.multiple_of(index_ref[a, 4 * g + b] * 8, 8)
                out_ref[pl.ds(place, 8), :] = tile


def to_rows(x):
    count = x.shape[0]
    return x.reshape(count // 8, 8, 8, LANES).transpose(0, 2, 1, 3).reshape(count * 8, LANES)


def from_rows(x):
    count = x.shape[0] // 8
    return x.reshape(count // 8, 8, 8, LANES).transpose(0, 2, 1, 3).reshape(count, 8 * LANES)


def kernel_call(body, name, shapes, scratch, scalars, inputs, megabytes=40):
    single = not isinstance(shapes, list)
    spec = pl.BlockSpec(memory_space=pltpu.VMEM)
    outs = [shapes] if single else shapes
    result = pl.pallas_call(
        body,
        out_shape=outs,
        in_specs=[pl.BlockSpec(memory_space=pltpu.SMEM)] * len(scalars) + [spec] * len(inputs),
        out_specs=[spec] * len(outs),
        scratch_shapes=scratch,
        compiler_params=pltpu.CompilerParams(vmem_limit_bytes=megabytes * 2**20),
        name=name,
    )(*scalars, *inputs)
    return result[0] if single else result


def neighbours(first, last, axis):
    count = lax.axis_size(axis)
    up = [(i, i + 1) for i in range(count - 1)]
    down = [(j, i) for i, j in up]
    return lax.ppermute(last, axis, up), lax.ppermute(first, axis, down)


def shards(cells, instance_cell, target, row_taps, col_taps, kernel_weight):
    deep, cores, cols = lax.axis_size("deep"), lax.axis_size("core"), lax.axis_size("col")
    plane = ("core", "col")
    peers = cores * cols
    slots = cells.shape[0]
    tile_rows, tile_cols = instance_cell.shape
    tiles_here = tile_rows * tile_cols
    height, breadth = target.shape
    owners = deep * peers
    capacity = min(tiles_here, deep * 2 * ((tiles_here + owners - 1) // owners))
    f32 = lambda *shape: jax.ShapeDtypeStruct(shape, F32)

    named = instance_cell.reshape(-1)
    owner = named // slots
    peer = owner % peers
    local = (owner // peers) * slots + named % slots
    same = (peer[:, None] == peer[None, :]) & jnp.tri(tiles_here, k=-1, dtype=bool)
    position = peer * capacity + jnp.sum(same.astype(jnp.int32), axis=1)
    request = jnp.max(
        jnp.where(position[None, :] == jnp.arange(peers * capacity)[:, None], local[None, :], -1),
        axis=1,
    )
    asked = lax.all_to_all(request, plane, split_axis=0, concat_axis=0, tiled=True)

    flat = to_rows(cells)
    copies = jnp.broadcast_to(flat[None], (deep,) + flat.shape).reshape(-1, LANES)
    stack = lax.all_to_all(copies, "deep", split_axis=0, concat_axis=0, tiled=True)
    packed = kernel_call(
        pack_kernel, "pack", f32(peers * capacity * 8, LANES), [], [asked], [stack]
    )
    arrived = lax.all_to_all(packed, plane, split_axis=0, concat_axis=0, tiled=True)
    index = position.reshape(tile_rows, tile_cols)
    mask, first, last = kernel_call(
        assemble_kernel,
        "assemble",
        [f32(height, breadth), f32(3 * HALF, breadth), f32(3 * HALF, breadth)],
        [pltpu.VMEM((height * (breadth // LANES), LANES), F32)],
        [index],
        [arrived, target],
    )
    top, bottom = neighbours(first, last, ("deep", "core"))
    edge_rows = 2 * height + 6 * HALF
    first, last = kernel_call(
        edges_kernel,
        "edges",
        [f32(edge_rows, LANES), f32(edge_rows, LANES)],
        [],
        [],
        [mask, target, top, bottom],
    )
    before, after = neighbours(first, last, "col")
    my_row = lax.axis_index(("deep", "core"))
    my_col = lax.axis_index("col")
    where = jnp.stack(
        [
            my_row * height - HALF,
            my_col * breadth - HALF,
            jnp.int32(deep * cores * height),
            jnp.int32(cols * breadth),
        ]
    ).astype(jnp.int32)
    bands = make_bands(row_taps, col_taps)
    field_rows = height + 2 * HALF
    returned = kernel_call(
        image_kernel,
        "image",
        f32(peers * capacity * 8, LANES),
        [
            pltpu.VMEM((height + 4 * HALF, breadth + 256), BF16),
            pltpu.VMEM((height + 4 * HALF, breadth + 256), BF16),
            pltpu.VMEM((field_rows, breadth + 128), F32),
            pltpu.VMEM((KERNELS, field_rows, WIDE), F32),
            pltpu.VMEM((KERNELS, height, breadth + 128), BF16),
            pltpu.VMEM((KERNELS, height, breadth + 128), BF16),
            pltpu.VMEM((height * (breadth // LANES), LANES), F32),
        ],
        [index, where, kernel_weight],
        [mask, target, top, bottom, before, after, *bands],
        56,
    )
    back = lax.all_to_all(returned, plane, split_axis=0, concat_axis=0, tiled=True)
    merged = kernel_call(merge_kernel, "merge", f32(deep * slots * 8, LANES), [], [asked], [back])
    parts = lax.all_to_all(merged, "deep", split_axis=0, concat_axis=0, tiled=True)
    return from_rows(kernel_call(step_kernel, "step", f32(slots * 8, LANES), [], [], [flat, parts]))


def solution(mesh):
    rows, cols = mesh.devices.shape
    finer = Mesh(mesh.devices.reshape(rows // 2, 2, cols), ("deep", "core", "col"))
    row = ("deep", "core")
    placed = (P((*row, "col"), None), P(row, "col"), P(row, "col"), P(), P(), P())
    return jax.shard_map(
        shards, mesh=finer, in_specs=placed, out_specs=P((*row, "col"), None), check_vma=False
    )
```

```python
import jax
import jax.numpy as jnp
from jax import lax
from jax.experimental import pallas as pl
from jax.experimental.pallas import tpu as pltpu
from jax.sharding import Mesh
from jax.sharding import PartitionSpec as P

TILE = 32
TAPS = 65
HALF = 32
KERNELS = 8
LANES = 128
WIDE = 256

STEEPNESS = 4.0
THRESHOLD = 0.3
STEP_RATE = 0.5

F32 = jnp.float32
BF16 = jnp.bfloat16


def split(x):
    high = x.astype(BF16)
    return high, (x - high.astype(F32)).astype(BF16)


def mm(a, b):
    return jnp.dot(a, b, preferred_element_type=F32)


def bands_kernel(wave_ref, fcol_ref, frow_ref, brow_ref, bcol_ref):
    rows = lax.broadcasted_iota(jnp.int32, (LANES, LANES), 0)
    lanes = lax.broadcasted_iota(jnp.int32, (LANES, LANES), 1)
    zero = jnp.zeros((LANES, LANES), F32)

    def circular(index, start):
        base = jnp.broadcast_to(wave_ref[pl.ds(index, 1), :], (LANES, LANES))
        return pltpu.roll(base, start, 1, stride=1, stride_axis=0)

    def put(ref, kernel, r0, c0, block, height=LANES, breadth=LANES):
        high, low = split(block)
        ref[kernel, 0, r0 : r0 + height, c0 : c0 + breadth] = high[:height, :breadth]
        ref[kernel, 1, r0 : r0 + height, c0 : c0 + breadth] = low[:height, :breadth]

    @pl.loop(0, KERNELS)
    def _(k):
        near = circular(k, 0)
        put(frow_ref, k, 0, 0, jnp.where(lanes >= rows, near, zero))
        put(frow_ref, k, 0, LANES, jnp.where(lanes < rows, near, zero))
        put(frow_ref, k, LANES, 0, zero, 64)
        put(frow_ref, k, LANES, LANES, jnp.where(lanes >= rows, near, zero), 64)
        near = circular(2 * KERNELS + k, 0)
        put(brow_ref, k, 0, 0, jnp.where(lanes >= rows, near, zero))
        put(brow_ref, k, 0, LANES, jnp.where(lanes < rows, near, zero))
        near = circular(3 * KERNELS + k, LANES // 2)
        put(fcol_ref, k, 0, 0, jnp.where(rows >= lanes, near, zero))
        put(fcol_ref, k, LANES, 0, jnp.where(rows < lanes, near, zero))
        near = circular(KERNELS + k, LANES // 2)
        low = jnp.where(rows >= lanes, near, zero)
        high = jnp.where(rows < lanes, near, zero)
        put(bcol_ref, k, 0, 0, low)
        put(bcol_ref, k, LANES, 0, high)
        put(bcol_ref, k, 2 * LANES, 0, zero)
        put(bcol_ref, k, 0, LANES, zero)
        put(bcol_ref, k, LANES, LANES, low)
        put(bcol_ref, k, 2 * LANES, LANES, high)


def make_bands(row_taps, col_taps):
    taps = jnp.concatenate([row_taps, col_taps], axis=0)
    taps = jnp.concatenate([taps, taps[:, ::-1]], axis=0)
    wave = jnp.pad(taps, [(0, 0), (0, LANES - TAPS)])
    shapes = [
        (KERNELS, 2, 256, LANES),
        (KERNELS, 2, 192, 256),
        (KERNELS, 2, LANES, 256),
        (KERNELS, 2, 384, 256),
    ]
    return pl.pallas_call(
        bands_kernel,
        out_shape=[jax.ShapeDtypeStruct(s, BF16) for s in shapes],
        in_specs=[pl.BlockSpec(memory_space=pltpu.VMEM)],
        out_specs=[pl.BlockSpec(memory_space=pltpu.VMEM)] * 4,
        compiler_params=pltpu.CompilerParams(vmem_limit_bytes=16 * 2**20),
        name="bands",
    )(wave)


def transpose_blocks(parts, block):
    turned = []
    for d in range(4):
        x = parts[d]
        for s in range(1, 4):
            x = jnp.where(block == s, parts[(s + d) % 4], x)
        turned.append(pltpu.roll(x, 32 * d, 1) if d else x)
    out = []
    for s in range(4):
        x = turned[(-s) % 4]
        for b in range(1, 4):
            x = jnp.where(block == b, turned[(b - s) % 4], x)
        out.append(x)
    return out


def spread_kernel(cells_ref, out_ref):
    own = cells_ref.shape[0]
    for c in range(own // 8):
        tile = cells_ref[pl.ds((c // 8) * 64 + c % 8, 8, stride=8), :]
        for d in range(out_ref.shape[0] // own):
            out_ref[d * own + c * 8 : d * own + c * 8 + 8, :] = tile


def pack_kernel(asked_ref, me_ref, cells_ref, early_ref, out_ref):
    peers, capacity = asked_ref.shape

    @pl.loop(0, peers)
    def _(i):
        base = (me_ref[0] ^ i) * capacity
        for j in range(capacity):
            asked = jnp.maximum(asked_ref[i, j], 0)
            tile = cells_ref[pl.ds(pl.multiple_of(asked * 8, 8), 8), :]
            out_ref[pl.ds(pl.multiple_of((base + j) * 8, 8), 8), :] = tile


def step_kernel(asked_ref, me_ref, cells_ref, tiles_ref, out_ref, *totals):
    owners, capacity = asked_ref.shape
    nothing = jnp.zeros((8, LANES), F32)
    for total in totals:
        total[...] = jnp.zeros_like(total)

    @pl.loop(0, owners)
    def _(i):
        base = (me_ref[1] ^ i) * capacity
        for j in range(capacity):
            asked = asked_ref[i, j]
            tile = tiles_ref[pl.ds(pl.multiple_of((base + j) * 8, 8), 8), :]
            there = pl.ds(pl.multiple_of(jnp.maximum(asked, 0) * 8, 8), 8)
            total = totals[j % len(totals)]
            total[there, :] += jnp.where(asked >= 0, tile, nothing)

    for c in range(out_ref.shape[0] // 8):
        rows = slice(c * 8, c * 8 + 8)
        total = totals[0][rows, :]
        for other in totals[1:]:
            total = total + other[rows, :]
        there = pl.ds((c // 8) * 64 + c % 8, 8, stride=8)
        out_ref[there, :] = cells_ref[there, :] - STEP_RATE * total


def assemble_kernel(index_ref, tiles_ref, target_ref, mask_ref, first_ref, last_ref, turned_ref):
    tile_rows, tile_cols = index_ref.shape
    height = tile_rows * TILE
    groups = tile_cols // 4
    block = lax.broadcasted_iota(jnp.int32, (8, LANES), 1) // 32

    @pl.loop(0, tile_rows)
    def _(a):
        for g in range(groups):
            parts = [
                tiles_ref[pl.ds(pl.multiple_of(index_ref[a, 4 * g + b] * 8, 8), 8), :]
                for b in range(4)
            ]
            for s, piece in enumerate(transpose_blocks(parts, block)):
                turned_ref[pl.ds(g * height + a * TILE + s, 8, stride=4), :] = piece

    for g in range(groups):
        lanes = slice(LANES * g, LANES * (g + 1))
        piece = turned_ref[g * height : (g + 1) * height, :]
        mask_ref[:, lanes] = piece
        first_ref[: 2 * HALF, lanes] = piece[: 2 * HALF]
        last_ref[: 2 * HALF, lanes] = piece[height - 2 * HALF :]
    first_ref[2 * HALF :, :] = target_ref[:HALF, :]
    last_ref[2 * HALF :, :] = target_ref[height - HALF :, :]


def edges_kernel(mask_ref, target_ref, top_ref, bottom_ref, first_ref, last_ref):
    height, breadth = mask_ref.shape
    wide = 2 * HALF
    for ref, lanes in ((first_ref, slice(0, LANES)), (last_ref, slice(breadth - LANES, breadth))):
        ref[:wide, :] = top_ref[:wide, lanes]
        ref[wide : wide + height, :] = mask_ref[:, lanes]
        ref[wide + height : 2 * wide + height, :] = bottom_ref[:wide, lanes]
        start = 2 * wide + height
        ref[start : start + HALF, :] = top_ref[wide:, lanes]
        ref[start + HALF : start + HALF + height, :] = target_ref[:, lanes]
        ref[start + HALF + height :, :] = bottom_ref[wide:, lanes]


def image_kernel(
    index_ref,
    where_ref,
    weight_ref,
    mask_ref,
    own_ref,
    top_ref,
    bottom_ref,
    before_ref,
    after_ref,
    fcol_ref,
    frow_ref,
    brow_ref,
    bcol_ref,
    out_ref,
    mhigh_ref,
    mlow_ref,
    target_ref,
    field_ref,
    ghigh_ref,
    glow_ref,
    grad_ref,
):
    tile_rows, tile_cols = index_ref.shape
    rows_here = tile_rows * TILE
    high_rows = rows_here + 4 * HALF
    field_rows = rows_here + 2 * HALF
    groups = tile_cols // 4
    wide = 2 * HALF
    block = lax.broadcasted_iota(jnp.int32, (8, LANES), 1) // 32

    def shifted(shift, parts, edge, emit):
        for rows, ref, start, count in parts:
            lane = lax.broadcasted_iota(jnp.int32, (count, LANES), 1)
            turned = None
            for g in range(groups + 2):
                if g == 0:
                    piece = before_ref[edge + rows : edge + rows + count, :]
                elif g == groups + 1:
                    piece = after_ref[edge + rows : edge + rows + count, :]
                else:
                    piece = ref[start : start + count, LANES * (g - 1) : LANES * g]
                fresh = pltpu.roll(piece, shift, 1)
                if g:
                    emit(rows, count, g - 1, jnp.where(lane < shift, turned, fresh))
                turned = fresh

    def put_mask(rows, count, g, piece):
        high, low = split(piece)
        mhigh_ref[rows : rows + count, LANES * g : LANES * (g + 1)] = high
        mlow_ref[rows : rows + count, LANES * g : LANES * (g + 1)] = low

    def put_target(rows, count, g, piece):
        target_ref[rows : rows + count, LANES * g : LANES * (g + 1)] = piece

    shifted(
        wide,
        (
            (0, top_ref, 0, wide),
            (wide, mask_ref, 0, rows_here),
            (wide + rows_here, bottom_ref, 0, wide),
        ),
        0,
        put_mask,
    )
    shifted(
        HALF,
        (
            (0, top_ref, wide, HALF),
            (HALF, own_ref, 0, rows_here),
            (HALF + rows_here, bottom_ref, wide, HALF),
        ),
        high_rows,
        put_target,
    )
    for g in range(groups + 1, mhigh_ref.shape[1] // LANES):
        lanes = slice(LANES * g, LANES * (g + 1))
        mhigh_ref[:, lanes] = jnp.zeros((high_rows, LANES), BF16)
        mlow_ref[:, lanes] = jnp.zeros((high_rows, LANES), BF16)

    def columns(offset, width):
        def window(ref, j):
            return ref[:, pl.ds(pl.multiple_of(offset + j * LANES, LANES), WIDE)]

        blocks = width // LANES
        stacked = jnp.concatenate(
            [
                jnp.concatenate(
                    [window(mhigh_ref, j), window(mlow_ref, j), window(mhigh_ref, j)], axis=1
                )
                for j in range(blocks)
            ],
            axis=0,
        )
        intensity = None
        for pair in range(KERNELS // 2):
            two = [
                jnp.concatenate([fcol_ref[2 * pair, v], fcol_ref[2 * pair + 1, v]], axis=1)
                for v in range(2)
            ]
            wide = mm(stacked, jnp.concatenate([two[0], two[0], two[1]], axis=0))
            for h in range(2):
                k = 2 * pair + h
                half = jnp.concatenate(
                    [
                        wide[j * high_rows : (j + 1) * high_rows, h * LANES : (h + 1) * LANES]
                        for j in range(blocks)
                    ],
                    axis=1,
                )
                high, low = split(half)
                both = mm(jnp.concatenate([frow_ref[k, 0], frow_ref[k, 1]], axis=0), high)
                field = both[:field_rows] + both[field_rows:] + mm(frow_ref[k, 0], low)
                field_ref[k, :, :width] = field
                term = weight_ref[k] * field * field
                intensity = term if intensity is None else intensity + term
        resist = 1.0 / (1.0 + jnp.exp(-STEEPNESS * (intensity - THRESHOLD)))
        target = target_ref[:, pl.ds(pl.multiple_of(offset, LANES), width)]
        sensitivity = 2.0 * (resist - target) * STEEPNESS * resist * (1.0 - resist)
        row = where_ref[0] + lax.broadcasted_iota(jnp.int32, (field_rows, width), 0)
        col = where_ref[1] + offset + lax.broadcasted_iota(jnp.int32, (field_rows, width), 1)
        inside = (row >= 0) & (row < where_ref[2]) & (col >= 0) & (col < where_ref[3])
        sensitivity = jnp.where(inside, sensitivity, 0.0)
        for k in range(KERNELS):
            product = (2.0 * weight_ref[k]) * sensitivity * field_ref[k, :, :width]
            high, low = split(product)
            near = brow_ref[k, 0, :, :field_rows]
            both = mm(jnp.concatenate([near, brow_ref[k, 1, :, :field_rows]], axis=0), high)
            part = both[:rows_here] + both[rows_here:] + mm(near, low)
            high, low = split(part)
            place = pl.ds(pl.multiple_of(offset, LANES), width)
            ghigh_ref[k, :, place] = high
            glow_ref[k, :, place] = low

    supers = tile_cols * TILE // WIDE

    @pl.loop(0, supers)
    def _(jj):
        columns(jj * WIDE, WIDE)

    columns(supers * WIDE, LANES)

    def spread_back(k):
        def window(ref, jj):
            return ref[k, :, WIDE * jj : WIDE * jj + 384]

        stacked = jnp.concatenate(
            [
                jnp.concatenate(
                    [window(ghigh_ref, jj), window(glow_ref, jj), window(ghigh_ref, jj)], axis=1
                )
                for jj in range(supers)
            ],
            axis=0,
        )
        return mm(
            stacked, jnp.concatenate([bcol_ref[k, 0], bcol_ref[k, 0], bcol_ref[k, 1]], axis=0)
        )

    def add(part, fresh):
        for g in range(groups):
            rows = slice(g * rows_here, (g + 1) * rows_here)
            top = (g // 2) * rows_here
            piece = part[top : top + rows_here, LANES * (g % 2) : LANES * (g % 2 + 1)]
            grad_ref[rows, :] = piece if fresh else grad_ref[rows, :] + piece

    add(spread_back(0), True)

    @pl.loop(1, KERNELS)
    def _(k):
        add(spread_back(k), False)

    @pl.loop(0, tile_rows)
    def _(a):
        for g in range(groups):
            base = g * rows_here + a * TILE
            parts = [grad_ref[pl.ds(base + s, 8, stride=4), :] for s in range(4)]
            for b, tile in enumerate(transpose_blocks(parts, block)):
                place = pl.multiple_of(index_ref[a, 4 * g + b] * 8, 8)
                out_ref[pl.ds(place, 8), :] = tile


def to_rows(x):
    count = x.shape[0]
    return x.reshape(count // 8, 8, 8, LANES).transpose(0, 2, 1, 3).reshape(count * 8, LANES)


def from_rows(x):
    count = x.shape[0] // 8
    return x.reshape(count // 8, 8, 8, LANES).transpose(0, 2, 1, 3).reshape(count, 8 * LANES)


def kernel_call(body, name, shapes, scratch, scalars, inputs, megabytes, unread=()):
    single = not isinstance(shapes, list)
    spec = pl.BlockSpec(memory_space=pltpu.VMEM)
    outs = [shapes] if single else shapes
    result = pl.pallas_call(
        body,
        out_shape=outs,
        in_specs=[pl.BlockSpec(memory_space=pltpu.SMEM)] * len(scalars)
        + [spec] * len(inputs)
        + [pl.BlockSpec(memory_space=pl.ANY)] * len(unread),
        out_specs=[spec] * len(outs),
        scratch_shapes=scratch,
        compiler_params=pltpu.CompilerParams(vmem_limit_bytes=megabytes * 2**20),
        name=name,
    )(*scalars, *inputs, *unread)
    return result[0] if single else result


def neighbours(first, last, axis):
    count = lax.axis_size(axis)
    up = [(i, i + 1) for i in range(count - 1)]
    down = [(j, i) for i, j in up]
    return lax.ppermute(last, axis, up), lax.ppermute(first, axis, down)


def doubled(table, axis):
    count = lax.axis_size(axis)
    bit = 1
    while bit < count:
        got = lax.ppermute(table, axis, [(i, i ^ bit) for i in range(count)])
        table = jnp.concatenate([table, got], axis=0)
        bit *= 2
    return table


def requests(match, value, capacity):
    rank = jnp.cumsum(match.astype(jnp.int32), axis=1) - 1
    hit = match[:, None, :] & (rank[:, None, :] == jnp.arange(capacity)[None, :, None])
    return jnp.max(jnp.where(hit, value[:, None, :], -1), axis=2)


def shards(cells, instance_cell, target, row_taps, col_taps, kernel_weight):
    deep, cores, cols = lax.axis_size("deep"), lax.axis_size("core"), lax.axis_size("col")
    everyone = ("deep", "core", "col")
    plane = ("core", "col")
    peers = cores * cols
    slots = cells.shape[0]
    tile_rows, tile_cols = instance_cell.shape
    tiles_here = tile_rows * tile_cols
    height, breadth = target.shape
    owners = deep * peers
    capacity = 2 * ((tiles_here + owners - 1) // owners)
    wide_capacity = min(tiles_here, deep * capacity)
    f32 = lambda *shape: jax.ShapeDtypeStruct(shape, F32)

    flat = to_rows(cells)
    copies = kernel_call(
        spread_kernel, "spread", f32(deep * slots * 8, LANES), [], [], [flat], 8
    )
    stack = lax.all_to_all(copies, "deep", split_axis=0, concat_axis=0, tiled=True)

    named = instance_cell.reshape(1, -1)
    near = doubled(doubled(named, "col"), "core")
    me = jnp.stack([lax.axis_index(plane), lax.axis_index(everyone)]).astype(jnp.int32)
    owner = near // slots
    asked = requests(
        owner % peers == me[0], (owner // peers) * slots + near % slots, wide_capacity
    )
    bands = make_bands(row_taps, col_taps)
    packed = kernel_call(
        pack_kernel,
        "pack",
        f32(peers * wide_capacity * 8, LANES),
        [],
        [asked, me],
        [stack],
        8,
        [bands[0]],
    )
    arrived = lax.all_to_all(packed, plane, split_axis=0, concat_axis=0, tiled=True)

    everything = doubled(near, "deep")
    wanted = requests(everything // slots == me[1], everything % slots, capacity)
    mine = named[0] // slots
    earlier = jnp.tri(tiles_here, k=-1, dtype=bool)

    def place(group, size):
        same = (group[:, None] == group[None, :]) & earlier
        where = group * size + jnp.sum(same.astype(jnp.int32), axis=1)
        return where.reshape(tile_rows, tile_cols)

    mask, first, last = kernel_call(
        assemble_kernel,
        "assemble",
        [f32(height, breadth), f32(3 * HALF, breadth), f32(3 * HALF, breadth)],
        [pltpu.VMEM((height * (breadth // LANES), LANES), F32)],
        [place(mine % peers, wide_capacity)],
        [arrived, target],
        8,
    )
    top, bottom = neighbours(first, last, ("deep", "core"))
    edge_rows = 2 * height + 6 * HALF
    first, last = kernel_call(
        edges_kernel,
        "edges",
        [f32(edge_rows, LANES), f32(edge_rows, LANES)],
        [],
        [],
        [mask, target, top, bottom],
        8,
    )
    before, after = neighbours(first, last, "col")
    my_row = lax.axis_index(("deep", "core"))
    my_col = lax.axis_index("col")
    where = jnp.stack(
        [
            my_row * height - HALF,
            my_col * breadth - HALF,
            jnp.int32(deep * cores * height),
            jnp.int32(cols * breadth),
        ]
    ).astype(jnp.int32)
    field_rows = height + 2 * HALF
    returned = kernel_call(
        image_kernel,
        "image",
        f32(owners * capacity * 8, LANES),
        [
            pltpu.VMEM((height + 4 * HALF, breadth + 256), BF16),
            pltpu.VMEM((height + 4 * HALF, breadth + 256), BF16),
            pltpu.VMEM((field_rows, breadth + 128), F32),
            pltpu.VMEM((KERNELS, field_rows, WIDE), F32),
            pltpu.VMEM((KERNELS, height, breadth + 128), BF16),
            pltpu.VMEM((KERNELS, height, breadth + 128), BF16),
            pltpu.VMEM((height * (breadth // LANES), LANES), F32),
        ],
        [place(mine, capacity), where, kernel_weight],
        [mask, target, top, bottom, before, after, *bands],
        32,
    )
    back = lax.all_to_all(returned, everyone, split_axis=0, concat_axis=0, tiled=True)
    stepped = kernel_call(
        step_kernel,
        "step",
        f32(slots * 8, LANES),
        [pltpu.VMEM((slots * 8, LANES), F32)] * 4,
        [wanted, me],
        [flat, back],
        8,
    )
    return from_rows(stepped)


def solution(mesh):
    rows, cols = mesh.devices.shape
    finer = Mesh(mesh.devices.reshape(rows // 2, 2, cols), ("deep", "core", "col"))
    row = ("deep", "core")
    placed = (P((*row, "col"), None), P(row, "col"), P(row, "col"), P(), P(), P())
    return jax.shard_map(
        shards, mesh=finer, in_specs=placed, out_specs=P((*row, "col"), None), check_vma=False
    )
```

```python
import jax
import jax.numpy as jnp
from jax import lax
from jax.experimental import pallas as pl
from jax.experimental.pallas import tpu as pltpu
from jax.sharding import Mesh
from jax.sharding import PartitionSpec as P

TILE = 32
TAPS = 65
HALF = 32
KERNELS = 8
LANES = 128
WIDE = 256

STEEPNESS = 4.0
THRESHOLD = 0.3
STEP_RATE = 0.5

F32 = jnp.float32
BF16 = jnp.bfloat16


def split(x):
    high = x.astype(BF16)
    return high, (x - high.astype(F32)).astype(BF16)


def mm(a, b):
    return jnp.dot(a, b, preferred_element_type=F32)


def bands_kernel(wave_ref, fcol_ref, frow_ref, brow_ref, bcol_ref):
    rows = lax.broadcasted_iota(jnp.int32, (LANES, LANES), 0)
    lanes = lax.broadcasted_iota(jnp.int32, (LANES, LANES), 1)
    zero = jnp.zeros((LANES, LANES), F32)

    def circular(index, start):
        base = jnp.broadcast_to(wave_ref[pl.ds(index, 1), :], (LANES, LANES))
        return pltpu.roll(base, start, 1, stride=1, stride_axis=0)

    def put(ref, kernel, r0, c0, block, height=LANES, breadth=LANES):
        high, low = split(block)
        ref[kernel, 0, r0 : r0 + height, c0 : c0 + breadth] = high[:height, :breadth]
        ref[kernel, 1, r0 : r0 + height, c0 : c0 + breadth] = low[:height, :breadth]

    @pl.loop(0, KERNELS)
    def _(k):
        near = circular(k, 0)
        put(frow_ref, k, 0, 0, jnp.where(lanes >= rows, near, zero))
        put(frow_ref, k, 0, LANES, jnp.where(lanes < rows, near, zero))
        put(frow_ref, k, LANES, 0, zero, 64)
        put(frow_ref, k, LANES, LANES, jnp.where(lanes >= rows, near, zero), 64)
        near = circular(2 * KERNELS + k, 0)
        put(brow_ref, k, 0, 0, jnp.where(lanes >= rows, near, zero))
        put(brow_ref, k, 0, LANES, jnp.where(lanes < rows, near, zero))
        near = circular(3 * KERNELS + k, LANES // 2)
        put(fcol_ref, k, 0, 0, jnp.where(rows >= lanes, near, zero))
        put(fcol_ref, k, LANES, 0, jnp.where(rows < lanes, near, zero))
        near = circular(KERNELS + k, LANES // 2)
        low = jnp.where(rows >= lanes, near, zero)
        high = jnp.where(rows < lanes, near, zero)
        put(bcol_ref, k, 0, 0, low)
        put(bcol_ref, k, LANES, 0, high)
        put(bcol_ref, k, 2 * LANES, 0, zero)
        put(bcol_ref, k, 0, LANES, zero)
        put(bcol_ref, k, LANES, LANES, low)
        put(bcol_ref, k, 2 * LANES, LANES, high)


def make_bands(row_taps, col_taps):
    taps = jnp.concatenate([row_taps, col_taps], axis=0)
    taps = jnp.concatenate([taps, taps[:, ::-1]], axis=0)
    wave = jnp.pad(taps, [(0, 0), (0, LANES - TAPS)])
    shapes = [
        (KERNELS, 2, 256, LANES),
        (KERNELS, 2, 192, 256),
        (KERNELS, 2, LANES, 256),
        (KERNELS, 2, 384, 256),
    ]
    return pl.pallas_call(
        bands_kernel,
        out_shape=[jax.ShapeDtypeStruct(s, BF16) for s in shapes],
        in_specs=[pl.BlockSpec(memory_space=pltpu.VMEM)],
        out_specs=[pl.BlockSpec(memory_space=pltpu.VMEM)] * 4,
        compiler_params=pltpu.CompilerParams(vmem_limit_bytes=56 * 2**20),
        name="bands",
    )(wave)


def transpose_blocks(parts, block):
    turned = []
    for d in range(4):
        x = parts[d]
        for s in range(1, 4):
            x = jnp.where(block == s, parts[(s + d) % 4], x)
        turned.append(pltpu.roll(x, 32 * d, 1) if d else x)
    out = []
    for s in range(4):
        x = turned[(-s) % 4]
        for b in range(1, 4):
            x = jnp.where(block == b, turned[(b - s) % 4], x)
        out.append(x)
    return out


def spread_kernel(cells_ref, instance_ref, out_ref, named_ref):
    own = cells_ref.shape[0]
    for c in range(own // 8):
        tile = cells_ref[pl.ds((c // 8) * 64 + c % 8, 8, stride=8), :]
        for d in range(out_ref.shape[0] // own):
            out_ref[d * own + c * 8 : d * own + c * 8 + 8, :] = tile
    rows = [instance_ref[a : a + 1, :] for a in range(instance_ref.shape[0])]
    named_ref[...] = jnp.concatenate(rows, axis=1)


def pack_kernel(asked_ref, me_ref, cells_ref, *rest):
    out_ref = rest[-1]
    peers, capacity = asked_ref.shape

    @pl.loop(0, peers)
    def _(i):
        base = (me_ref[0] ^ i) * capacity
        for j in range(capacity):
            asked = jnp.maximum(asked_ref[i, j], 0)
            tile = cells_ref[pl.ds(pl.multiple_of(asked * 8, 8), 8), :]
            out_ref[pl.ds(pl.multiple_of((base + j) * 8, 8), 8), :] = tile


def step_kernel(asked_ref, me_ref, cells_ref, tiles_ref, out_ref, *totals):
    owners, capacity = asked_ref.shape
    nothing = jnp.zeros((8, LANES), F32)
    for total in totals:
        total[...] = jnp.zeros_like(total)

    @pl.loop(0, owners)
    def _(i):
        base = (me_ref[1] ^ i) * capacity
        for j in range(capacity):
            asked = asked_ref[i, j]
            tile = tiles_ref[pl.ds(pl.multiple_of((base + j) * 8, 8), 8), :]
            there = pl.ds(pl.multiple_of(jnp.maximum(asked, 0) * 8, 8), 8)
            total = totals[j % len(totals)]
            total[there, :] += jnp.where(asked >= 0, tile, nothing)

    for c in range(out_ref.shape[0] // 8):
        rows = slice(c * 8, c * 8 + 8)
        total = totals[0][rows, :]
        for other in totals[1:]:
            total = total + other[rows, :]
        there = pl.ds((c // 8) * 64 + c % 8, 8, stride=8)
        out_ref[there, :] = cells_ref[there, :] - STEP_RATE * total


def assemble_kernel(index_ref, tiles_ref, *rest):
    mask_ref, first_ref, last_ref, turned_ref = rest[-4:]
    tile_rows, tile_cols = index_ref.shape
    height = tile_rows * TILE
    groups = tile_cols // 4
    block = lax.broadcasted_iota(jnp.int32, (8, LANES), 1) // 32

    @pl.loop(0, tile_rows)
    def _(a):
        for g in range(groups):
            parts = [
                tiles_ref[pl.ds(pl.multiple_of(index_ref[a, 4 * g + b] * 8, 8), 8), :]
                for b in range(4)
            ]
            for s, piece in enumerate(transpose_blocks(parts, block)):
                turned_ref[pl.ds(g * height + a * TILE + s, 8, stride=4), :] = piece

    for g in range(groups):
        lanes = slice(LANES * g, LANES * (g + 1))
        piece = turned_ref[g * height : (g + 1) * height, :]
        mask_ref[:, lanes] = piece
        first_ref[:, lanes] = piece[: 2 * HALF]
        last_ref[:, lanes] = piece[height - 2 * HALF :]


def edges_kernel(mask_ref, top_ref, bottom_ref, first_ref, last_ref):
    height, breadth = mask_ref.shape
    wide = 2 * HALF
    half = height // 2
    lane = lax.broadcasted_iota(jnp.int32, (half + wide, LANES), 1)

    def sides(lanes):
        upper = jnp.concatenate([top_ref[:, lanes], mask_ref[:half, lanes]], axis=0)
        lower = jnp.concatenate([mask_ref[half:, lanes], bottom_ref[:, lanes]], axis=0)
        return upper, lower

    upper, lower = sides(slice(0, LANES))
    first_ref[...] = jnp.where(lane < wide, upper, pltpu.roll(lower, wide, 1))
    upper, lower = sides(slice(breadth - LANES, breadth))
    last_ref[...] = jnp.where(lane < wide, pltpu.roll(upper, wide, 1), lower)


def image_kernel(
    index_ref,
    where_ref,
    weight_ref,
    mask_ref,
    top_ref,
    bottom_ref,
    before_ref,
    after_ref,
    target_ref,
    ttop_ref,
    tbottom_ref,
    fcol_hbm,
    frow_hbm,
    brow_hbm,
    bcol_hbm,
    out_ref,
    fcol_ref,
    frow_ref,
    brow_ref,
    bcol_ref,
    sems,
    mhigh_ref,
    mlow_ref,
    field_ref,
    ghigh_ref,
    glow_ref,
    grad_ref,
):
    tile_rows, tile_cols = index_ref.shape
    rows_here = tile_rows * TILE
    high_rows = rows_here + 4 * HALF
    field_rows = rows_here + 2 * HALF
    groups = tile_cols // 4
    wide = 2 * HALF
    block = lax.broadcasted_iota(jnp.int32, (8, LANES), 1) // 32
    fetches = [
        pltpu.make_async_copy(source, there, sems.at[n])
        for n, (source, there) in enumerate(
            (
                (fcol_hbm, fcol_ref),
                (frow_hbm, frow_ref),
                (brow_hbm, brow_ref),
                (bcol_hbm, bcol_ref),
            )
        )
    ]
    for fetch in fetches:
        fetch.start()

    lane = lax.broadcasted_iota(jnp.int32, (wide, LANES), 1)
    for rows in range(0, high_rows, wide):
        if rows == 0:
            ref, start = top_ref, 0
        elif rows == high_rows - wide:
            ref, start = bottom_ref, 0
        else:
            ref, start = mask_ref, rows - wide
        half = high_rows // 2
        edge = slice(rows % half, rows % half + wide)
        turned = before_ref[edge, :]
        final = after_ref[edge, :]
        if rows < half:
            final = pltpu.roll(final, wide, 1)
        else:
            turned = pltpu.roll(turned, wide, 1)
        for g in range(groups + 1):
            fresh = final
            if g < groups:
                fresh = pltpu.roll(ref[start : start + wide, LANES * g : LANES * (g + 1)], wide, 1)
            high, low = split(jnp.where(lane < wide, turned, fresh))
            mhigh_ref[rows : rows + wide, LANES * g : LANES * (g + 1)] = high
            mlow_ref[rows : rows + wide, LANES * g : LANES * (g + 1)] = low
            turned = fresh
    for g in range(groups + 1, mhigh_ref.shape[1] // LANES):
        lanes = slice(LANES * g, LANES * (g + 1))
        mhigh_ref[:, lanes] = jnp.zeros((high_rows, LANES), BF16)
        mlow_ref[:, lanes] = jnp.zeros((high_rows, LANES), BF16)
    for fetch in fetches[:3]:
        fetch.wait()

    def columns(offset, width):
        def window(ref, j):
            return ref[:, pl.ds(pl.multiple_of(offset + j * LANES, LANES), WIDE)]

        blocks = width // LANES
        stacked = jnp.concatenate(
            [
                jnp.concatenate(
                    [window(mhigh_ref, j), window(mlow_ref, j), window(mhigh_ref, j)], axis=1
                )
                for j in range(blocks)
            ],
            axis=0,
        )
        intensity = None
        for pair in range(KERNELS // 2):
            two = [
                jnp.concatenate([fcol_ref[2 * pair, v], fcol_ref[2 * pair + 1, v]], axis=1)
                for v in range(2)
            ]
            wide = mm(stacked, jnp.concatenate([two[0], two[0], two[1]], axis=0))
            for h in range(2):
                k = 2 * pair + h
                half = jnp.concatenate(
                    [
                        wide[j * high_rows : (j + 1) * high_rows, h * LANES : (h + 1) * LANES]
                        for j in range(blocks)
                    ],
                    axis=1,
                )
                high, low = split(half)
                both = mm(jnp.concatenate([frow_ref[k, 0], frow_ref[k, 1]], axis=0), high)
                field = both[:field_rows] + both[field_rows:] + mm(frow_ref[k, 0], low)
                field_ref[k, :, :width] = field
                term = weight_ref[k] * field * field
                intensity = term if intensity is None else intensity + term
        resist = 1.0 / (1.0 + jnp.exp(-STEEPNESS * (intensity - THRESHOLD)))
        place = pl.ds(pl.multiple_of(offset, LANES), width)
        target = jnp.concatenate(
            [ttop_ref[:, place], target_ref[:, place], tbottom_ref[:, place]], axis=0
        )
        sensitivity = 2.0 * (resist - target) * STEEPNESS * resist * (1.0 - resist)
        row = where_ref[0] + lax.broadcasted_iota(jnp.int32, (field_rows, width), 0)
        col = where_ref[1] + offset + lax.broadcasted_iota(jnp.int32, (field_rows, width), 1)
        inside = (row >= 0) & (row < where_ref[2]) & (col >= 0) & (col < where_ref[3])
        sensitivity = jnp.where(inside, sensitivity, 0.0)
        for k in range(KERNELS):
            product = (2.0 * weight_ref[k]) * sensitivity * field_ref[k, :, :width]
            high, low = split(product)
            near = brow_ref[k, 0, :, :field_rows]
            both = mm(jnp.concatenate([near, brow_ref[k, 1, :, :field_rows]], axis=0), high)
            part = both[:rows_here] + both[rows_here:] + mm(near, low)
            high, low = split(part)
            ghigh_ref[k, :, place] = high
            glow_ref[k, :, place] = low

    supers = tile_cols * TILE // WIDE

    @pl.loop(0, supers)
    def _(jj):
        columns(jj * WIDE, WIDE)

    columns(supers * WIDE, LANES)
    fetches[3].wait()

    def spread_back(k):
        def window(ref, jj):
            return ref[k, :, WIDE * jj : WIDE * jj + 384]

        stacked = jnp.concatenate(
            [
                jnp.concatenate(
                    [window(ghigh_ref, jj), window(glow_ref, jj), window(ghigh_ref, jj)], axis=1
                )
                for jj in range(supers)
            ],
            axis=0,
        )
        return mm(
            stacked, jnp.concatenate([bcol_ref[k, 0], bcol_ref[k, 0], bcol_ref[k, 1]], axis=0)
        )

    def add(part, fresh):
        for g in range(groups):
            rows = slice(g * rows_here, (g + 1) * rows_here)
            top = (g // 2) * rows_here
            piece = part[top : top + rows_here, LANES * (g % 2) : LANES * (g % 2 + 1)]
            grad_ref[rows, :] = piece if fresh else grad_ref[rows, :] + piece

    add(spread_back(0), True)

    @pl.loop(1, KERNELS)
    def _(k):
        add(spread_back(k), False)

    @pl.loop(0, tile_rows)
    def _(a):
        for g in range(groups):
            base = g * rows_here + a * TILE
            parts = [grad_ref[pl.ds(base + s, 8, stride=4), :] for s in range(4)]
            for b, tile in enumerate(transpose_blocks(parts, block)):
                place = pl.multiple_of(index_ref[a, 4 * g + b] * 8, 8)
                out_ref[pl.ds(place, 8), :] = tile


def to_rows(x):
    count = x.shape[0]
    return x.reshape(count // 8, 8, 8, LANES).transpose(0, 2, 1, 3).reshape(count * 8, LANES)


def from_rows(x):
    count = x.shape[0] // 8
    return x.reshape(count // 8, 8, 8, LANES).transpose(0, 2, 1, 3).reshape(count, 8 * LANES)


def kernel_call(body, name, shapes, scratch, scalars, inputs, unread=()):
    single = not isinstance(shapes, list)
    spec = pl.BlockSpec(memory_space=pltpu.VMEM)
    outs = [shapes] if single else shapes
    result = pl.pallas_call(
        body,
        out_shape=outs,
        in_specs=[pl.BlockSpec(memory_space=pltpu.SMEM)] * len(scalars)
        + [spec] * len(inputs)
        + [pl.BlockSpec(memory_space=pl.ANY)] * len(unread),
        out_specs=[spec] * len(outs),
        scratch_shapes=scratch,
        compiler_params=pltpu.CompilerParams(vmem_limit_bytes=56 * 2**20),
        name=name,
    )(*scalars, *inputs, *unread)
    return result[0] if single else result


def neighbours(first, last, axis):
    count = lax.axis_size(axis)
    up = [(i, i + 1) for i in range(count - 1)]
    down = [(j, i) for i, j in up]
    return lax.ppermute(last, axis, up), lax.ppermute(first, axis, down)


def doubled(table, axis):
    count = lax.axis_size(axis)
    bit = 1
    while bit < count:
        got = lax.ppermute(table, axis, [(i, i ^ bit) for i in range(count)])
        table = jnp.concatenate([table, got], axis=0)
        bit *= 2
    return table


def requests(match, value, capacity):
    rank = jnp.cumsum(match.astype(jnp.int32), axis=1) - 1
    hit = match[:, None, :] & (rank[:, None, :] == jnp.arange(capacity)[None, :, None])
    return jnp.max(jnp.where(hit, value[:, None, :], -1), axis=2)


def shards(cells, instance_cell, target, row_taps, col_taps, kernel_weight):
    deep, cores, cols = lax.axis_size("deep"), lax.axis_size("core"), lax.axis_size("col")
    everyone = ("deep", "core", "col")
    plane = ("core", "col")
    peers = cores * cols
    slots = cells.shape[0]
    tile_rows, tile_cols = instance_cell.shape
    tiles_here = tile_rows * tile_cols
    height, breadth = target.shape
    owners = deep * peers
    capacity = 2 * ((tiles_here + owners - 1) // owners)
    wide_capacity = min(tiles_here, deep * capacity)
    f32 = lambda *shape: jax.ShapeDtypeStruct(shape, F32)

    flat = to_rows(cells)
    copies, named = kernel_call(
        spread_kernel,
        "spread",
        [
            f32(deep * slots * 8, LANES),
            jax.ShapeDtypeStruct((1, tiles_here), jnp.int32),
        ],
        [],
        [],
        [flat, instance_cell],
    )
    stack = lax.all_to_all(copies, "deep", split_axis=0, concat_axis=0, tiled=True)

    near = doubled(doubled(named, "col"), "core")
    me = jnp.stack([lax.axis_index(plane), lax.axis_index(everyone)]).astype(jnp.int32)
    owner = near // slots
    asked = requests(
        owner % peers == me[0], (owner // peers) * slots + near % slots, wide_capacity
    )
    sides = lax.optimization_barrier((target, named))[0]
    left, right = neighbours(sides[:, :HALF], sides[:, breadth - HALF :], "col")
    blank = jnp.zeros((height, LANES - 2 * HALF), F32)
    wide_target = jnp.concatenate([left, target, right, blank], axis=1)
    bands = make_bands(row_taps, col_taps)
    packed = kernel_call(
        pack_kernel,
        "pack",
        f32(peers * wide_capacity * 8, LANES),
        [],
        [asked, me],
        [stack],
        [bands[0], wide_target],
    )
    packed, near, wide_target = lax.optimization_barrier((packed, near, wide_target))
    arrived = lax.all_to_all(packed, plane, split_axis=0, concat_axis=0, tiled=True)

    everything = doubled(near, "deep")
    wanted = requests(everything // slots == me[1], everything % slots, capacity)
    above, below = neighbours(wide_target[:HALF], wide_target[height - HALF :], ("deep", "core"))
    mine = named[0] // slots
    earlier = jnp.tri(tiles_here, k=-1, dtype=bool)

    def place(group, size):
        same = (group[:, None] == group[None, :]) & earlier
        where = group * size + jnp.sum(same.astype(jnp.int32), axis=1)
        return where.reshape(tile_rows, tile_cols)

    mask, first, last = kernel_call(
        assemble_kernel,
        "assemble",
        [f32(height, breadth), f32(2 * HALF, breadth), f32(2 * HALF, breadth)],
        [pltpu.VMEM((height * (breadth // LANES), LANES), F32)],
        [place(mine % peers, wide_capacity)],
        [arrived],
        [wanted, above, below],
    )
    top, bottom = neighbours(first, last, ("deep", "core"))
    edge = f32(height // 2 + 2 * HALF, LANES)
    first, last = kernel_call(edges_kernel, "edges", [edge, edge], [], [], [mask, top, bottom])
    before, after = neighbours(first, last, "col")
    my_row = lax.axis_index(("deep", "core"))
    my_col = lax.axis_index("col")
    where = jnp.stack(
        [
            my_row * height - HALF,
            my_col * breadth - HALF,
            jnp.int32(deep * cores * height),
            jnp.int32(cols * breadth),
        ]
    ).astype(jnp.int32)
    field_rows = height + 2 * HALF
    returned = kernel_call(
        image_kernel,
        "image",
        f32(owners * capacity * 8, LANES),
        [pltpu.VMEM(band.shape, BF16) for band in bands]
        + [
            pltpu.SemaphoreType.DMA((4,)),
            pltpu.VMEM((height + 4 * HALF, breadth + 256), BF16),
            pltpu.VMEM((height + 4 * HALF, breadth + 256), BF16),
            pltpu.VMEM((KERNELS, field_rows, WIDE), F32),
            pltpu.VMEM((KERNELS, height, breadth + 128), BF16),
            pltpu.VMEM((KERNELS, height, breadth + 128), BF16),
            pltpu.VMEM((height * (breadth // LANES), LANES), F32),
        ],
        [place(mine, capacity), where, kernel_weight],
        [mask, top, bottom, before, after, wide_target, above, below],
        bands,
    )
    back = lax.all_to_all(returned, everyone, split_axis=0, concat_axis=0, tiled=True)
    stepped = kernel_call(
        step_kernel,
        "step",
        f32(slots * 8, LANES),
        [pltpu.VMEM((slots * 8, LANES), F32)] * 4,
        [wanted, me],
        [flat, back],
    )
    return from_rows(stepped)


def solution(mesh):
    rows, cols = mesh.devices.shape
    finer = Mesh(mesh.devices.reshape(rows // 2, 2, cols), ("deep", "core", "col"))
    row = ("deep", "core")
    placed = (P((*row, "col"), None), P(row, "col"), P(row, "col"), P(), P(), P())
    return jax.shard_map(
        shards, mesh=finer, in_specs=placed, out_specs=P((*row, "col"), None), check_vma=False
    )
```

```python
import jax
import jax.numpy as jnp
from jax import lax
from jax.experimental import pallas as pl
from jax.experimental.pallas import tpu as pltpu
from jax.sharding import Mesh
from jax.sharding import PartitionSpec as P

TILE = 32
TAPS = 65
HALF = 32
KERNELS = 8
LANES = 128
WIDE = 256

STEEPNESS = 4.0
THRESHOLD = 0.3
STEP_RATE = 0.5

F32 = jnp.float32
BF16 = jnp.bfloat16


def split(x):
    high = x.astype(BF16)
    return high, (x - high.astype(F32)).astype(BF16)


def mm(a, b):
    return jnp.dot(a, b, preferred_element_type=F32)


def build_bands(wave_ref, fcol_ref, frow_ref, brow_ref, bcol_ref):
    rows = lax.broadcasted_iota(jnp.int32, (LANES, LANES), 0)
    lanes = lax.broadcasted_iota(jnp.int32, (LANES, LANES), 1)
    zero = jnp.zeros((LANES, LANES), F32)

    def circular(index, start):
        base = jnp.broadcast_to(wave_ref[pl.ds(index, 1), :], (LANES, LANES))
        return pltpu.roll(base, start, 1, stride=1, stride_axis=0)

    def put(ref, kernel, r0, c0, block, height=LANES, breadth=LANES):
        high, low = split(block)
        ref[kernel, 0, r0 : r0 + height, c0 : c0 + breadth] = high[:height, :breadth]
        ref[kernel, 1, r0 : r0 + height, c0 : c0 + breadth] = low[:height, :breadth]

    @pl.loop(0, KERNELS)
    def _(k):
        near = circular(k, 0)
        put(frow_ref, k, 0, 0, jnp.where(lanes >= rows, near, zero))
        put(frow_ref, k, 0, LANES, jnp.where(lanes < rows, near, zero))
        put(frow_ref, k, LANES, 0, zero, 64)
        put(frow_ref, k, LANES, LANES, jnp.where(lanes >= rows, near, zero), 64)
        near = circular(2 * KERNELS + k, 0)
        put(brow_ref, k, 0, 0, jnp.where(lanes >= rows, near, zero))
        put(brow_ref, k, 0, LANES, jnp.where(lanes < rows, near, zero))
        near = circular(3 * KERNELS + k, LANES // 2)
        put(fcol_ref, k, 0, 0, jnp.where(rows >= lanes, near, zero))
        put(fcol_ref, k, LANES, 0, jnp.where(rows < lanes, near, zero))
        near = circular(KERNELS + k, LANES // 2)
        low = jnp.where(rows >= lanes, near, zero)
        high = jnp.where(rows < lanes, near, zero)
        put(bcol_ref, k, 0, 0, low)
        put(bcol_ref, k, LANES, 0, high)
        put(bcol_ref, k, 2 * LANES, 0, zero)
        put(bcol_ref, k, 0, LANES, zero)
        put(bcol_ref, k, LANES, LANES, low)
        put(bcol_ref, k, 2 * LANES, LANES, high)


def make_waves(row_taps, col_taps):
    taps = jnp.concatenate([row_taps, col_taps], axis=0)
    taps = jnp.concatenate([taps, taps[:, ::-1]], axis=0)
    return jnp.pad(taps, [(0, 0), (0, LANES - TAPS)])


def transpose_blocks(parts, block):
    turned = []
    for d in range(4):
        x = parts[d]
        for s in range(1, 4):
            x = jnp.where(block == s, parts[(s + d) % 4], x)
        turned.append(pltpu.roll(x, 32 * d, 1) if d else x)
    out = []
    for s in range(4):
        x = turned[(-s) % 4]
        for b in range(1, 4):
            x = jnp.where(block == b, turned[(b - s) % 4], x)
        out.append(x)
    return out


def spread_kernel(cells_ref, instance_ref, out_ref, named_ref):
    own = cells_ref.shape[0]
    for c in range(own // 8):
        tile = cells_ref[pl.ds((c // 8) * 64 + c % 8, 8, stride=8), :]
        for d in range(out_ref.shape[0] // own):
            out_ref[d * own + c * 8 : d * own + c * 8 + 8, :] = tile
    rows = [instance_ref[a : a + 1, :] for a in range(instance_ref.shape[0])]
    named_ref[...] = jnp.concatenate(rows, axis=1)


def pack_kernel(asked_ref, me_ref, cells_ref, *rest):
    out_ref = rest[-1]
    peers, capacity = asked_ref.shape

    @pl.loop(0, peers)
    def _(i):
        base = (me_ref[0] ^ i) * capacity
        for j in range(capacity):
            asked = jnp.maximum(asked_ref[i, j], 0)
            tile = cells_ref[pl.ds(pl.multiple_of(asked * 8, 8), 8), :]
            out_ref[pl.ds(pl.multiple_of((base + j) * 8, 8), 8), :] = tile


def step_kernel(asked_ref, me_ref, cells_ref, tiles_ref, out_ref, *totals):
    owners, capacity = asked_ref.shape
    nothing = jnp.zeros((8, LANES), F32)
    for total in totals:
        total[...] = jnp.zeros_like(total)

    @pl.loop(0, owners)
    def _(i):
        base = (me_ref[1] ^ i) * capacity
        for j in range(capacity):
            asked = asked_ref[i, j]
            tile = tiles_ref[pl.ds(pl.multiple_of((base + j) * 8, 8), 8), :]
            there = pl.ds(pl.multiple_of(jnp.maximum(asked, 0) * 8, 8), 8)
            total = totals[j % len(totals)]
            total[there, :] += jnp.where(asked >= 0, tile, nothing)

    for c in range(out_ref.shape[0] // 8):
        rows = slice(c * 8, c * 8 + 8)
        total = totals[0][rows, :]
        for other in totals[1:]:
            total = total + other[rows, :]
        there = pl.ds((c // 8) * 64 + c % 8, 8, stride=8)
        out_ref[there, :] = cells_ref[there, :] - STEP_RATE * total


def assemble_kernel(index_ref, tiles_ref, target_ref, *rest):
    mask_ref, first_ref, last_ref, turned_ref = rest[-4:]
    tile_rows, tile_cols = index_ref.shape
    height = tile_rows * TILE
    groups = tile_cols // 4
    block = lax.broadcasted_iota(jnp.int32, (8, LANES), 1) // 32

    @pl.loop(0, tile_rows)
    def _(a):
        for g in range(groups):
            parts = [
                tiles_ref[pl.ds(pl.multiple_of(index_ref[a, 4 * g + b] * 8, 8), 8), :]
                for b in range(4)
            ]
            for s, piece in enumerate(transpose_blocks(parts, block)):
                turned_ref[pl.ds(g * height + a * TILE + s, 8, stride=4), :] = piece

    for g in range(groups):
        lanes = slice(LANES * g, LANES * (g + 1))
        piece = turned_ref[g * height : (g + 1) * height, :]
        mask_ref[:, lanes] = piece
        first_ref[: 2 * HALF, lanes] = piece[: 2 * HALF]
        last_ref[: 2 * HALF, lanes] = piece[height - 2 * HALF :]
    first_ref[2 * HALF :, :] = target_ref[:HALF, :]
    last_ref[2 * HALF :, :] = target_ref[height - HALF :, :]


def target_strips(target_ref, top_ref, bottom_ref, strip):
    height = target_ref.shape[0]
    quarter = (height + 2 * HALF) // 4
    for row in range(0, height + 2 * HALF, 16):
        if row < HALF:
            ref, start = top_ref, 2 * HALF + row
        elif row < HALF + height:
            ref, start = target_ref, row - HALF
        else:
            ref, start = bottom_ref, 2 * HALF + row - HALF - height
        strip(row, ref, slice(start, start + 16), row // quarter, row % quarter)


def edges_kernel(mask_ref, target_ref, top_ref, bottom_ref, first_ref, last_ref, pack_ref):
    height, breadth = mask_ref.shape
    wide = 2 * HALF
    half = height // 2
    packed = half + wide
    lane = lax.broadcasted_iota(jnp.int32, (packed, LANES), 1)
    head, tail = slice(0, LANES), slice(breadth - LANES, breadth)

    def sides(lanes):
        upper = jnp.concatenate([top_ref[:wide, lanes], mask_ref[:half, lanes]], axis=0)
        lower = jnp.concatenate([mask_ref[half:, lanes], bottom_ref[:wide, lanes]], axis=0)
        return upper, lower

    upper, lower = sides(head)
    first_ref[:packed, :] = jnp.where(lane < wide, upper, pltpu.roll(lower, wide, 1))
    upper, lower = sides(tail)
    last_ref[:packed, :] = jnp.where(lane < wide, pltpu.roll(upper, wide, 1), lower)

    quarter = (height + 2 * HALF) // 4

    def strip(row, ref, rows, part, inner):
        for side, lanes in enumerate((head, tail)):
            shift = (HALF * (part + side)) % LANES
            piece = ref[rows, lanes]
            pack_ref[side, part, inner : inner + 16, :] = (
                pltpu.roll(piece, shift, 1) if shift else piece
            )

    target_strips(target_ref, top_ref, bottom_ref, strip)
    part_of = lax.broadcasted_iota(jnp.int32, (quarter, LANES), 1) // HALF
    for side, ref in enumerate((first_ref, last_ref)):
        piece = pack_ref[side, 0]
        for part in range(1, 4):
            piece = jnp.where(part_of == part, pack_ref[side, part], piece)
        ref[packed:, :] = piece


def image_kernel(
    index_ref,
    where_ref,
    weight_ref,
    mask_ref,
    top_ref,
    bottom_ref,
    before_ref,
    after_ref,
    own_ref,
    wave_ref,
    out_ref,
    fcol_ref,
    frow_ref,
    brow_ref,
    bcol_ref,
    target_ref,
    mhigh_ref,
    mlow_ref,
    field_ref,
    ghigh_ref,
    glow_ref,
    grad_ref,
):
    tile_rows, tile_cols = index_ref.shape
    rows_here = tile_rows * TILE
    high_rows = rows_here + 4 * HALF
    field_rows = rows_here + 2 * HALF
    groups = tile_cols // 4
    wide = 2 * HALF
    block = lax.broadcasted_iota(jnp.int32, (8, LANES), 1) // 32
    build_bands(wave_ref, fcol_ref, frow_ref, brow_ref, bcol_ref)

    lane = lax.broadcasted_iota(jnp.int32, (wide, LANES), 1)
    for rows in range(0, high_rows, wide):
        if rows == 0:
            ref, start = top_ref, 0
        elif rows == high_rows - wide:
            ref, start = bottom_ref, 0
        else:
            ref, start = mask_ref, rows - wide
        half = high_rows // 2
        edge = slice(rows % half, rows % half + wide)
        turned = before_ref[edge, :]
        final = after_ref[edge, :]
        if rows < half:
            final = pltpu.roll(final, wide, 1)
        else:
            turned = pltpu.roll(turned, wide, 1)
        for g in range(groups + 1):
            fresh = final
            if g < groups:
                fresh = pltpu.roll(ref[start : start + wide, LANES * g : LANES * (g + 1)], wide, 1)
            high, low = split(jnp.where(lane < wide, turned, fresh))
            mhigh_ref[rows : rows + wide, LANES * g : LANES * (g + 1)] = high
            mlow_ref[rows : rows + wide, LANES * g : LANES * (g + 1)] = low
            turned = fresh
    for g in range(groups + 1, mhigh_ref.shape[1] // LANES):
        lanes = slice(LANES * g, LANES * (g + 1))
        mhigh_ref[:, lanes] = jnp.zeros((high_rows, LANES), BF16)
        mlow_ref[:, lanes] = jnp.zeros((high_rows, LANES), BF16)
    packed = high_rows // 2
    near_lane = lax.broadcasted_iota(jnp.int32, (16, LANES), 1)

    def strip(row, ref, rows, part, inner):
        edge = slice(packed + inner, packed + inner + 16)
        back, ahead = (-HALF * part) % LANES, (HALF - HALF * part) % LANES
        turned = pltpu.roll(before_ref[edge, :], back, 1) if back else before_ref[edge, :]
        final = pltpu.roll(after_ref[edge, :], ahead, 1) if ahead else after_ref[edge, :]
        for g in range(groups + 1):
            fresh = final
            if g < groups:
                fresh = pltpu.roll(ref[rows, LANES * g : LANES * (g + 1)], HALF, 1)
            target_ref[row : row + 16, LANES * g : LANES * (g + 1)] = jnp.where(
                near_lane < HALF, turned, fresh
            )
            turned = fresh

    target_strips(own_ref, top_ref, bottom_ref, strip)

    def columns(offset, width):
        def window(ref, j):
            return ref[:, pl.ds(pl.multiple_of(offset + j * LANES, LANES), WIDE)]

        blocks = width // LANES
        stacked = jnp.concatenate(
            [
                jnp.concatenate(
                    [window(mhigh_ref, j), window(mlow_ref, j), window(mhigh_ref, j)], axis=1
                )
                for j in range(blocks)
            ],
            axis=0,
        )
        intensity = None
        for pair in range(KERNELS // 2):
            two = [
                jnp.concatenate([fcol_ref[2 * pair, v], fcol_ref[2 * pair + 1, v]], axis=1)
                for v in range(2)
            ]
            wide = mm(stacked, jnp.concatenate([two[0], two[0], two[1]], axis=0))
            for h in range(2):
                k = 2 * pair + h
                half = jnp.concatenate(
                    [
                        wide[j * high_rows : (j + 1) * high_rows, h * LANES : (h + 1) * LANES]
                        for j in range(blocks)
                    ],
                    axis=1,
                )
                high, low = split(half)
                both = mm(jnp.concatenate([frow_ref[k, 0], frow_ref[k, 1]], axis=0), high)
                field = both[:field_rows] + both[field_rows:] + mm(frow_ref[k, 0], low)
                field_ref[k, :, :width] = field
                term = weight_ref[k] * field * field
                intensity = term if intensity is None else intensity + term
        resist = 1.0 / (1.0 + jnp.exp(-STEEPNESS * (intensity - THRESHOLD)))
        place = pl.ds(pl.multiple_of(offset, LANES), width)
        target = target_ref[:, place]
        sensitivity = 2.0 * (resist - target) * STEEPNESS * resist * (1.0 - resist)
        row = where_ref[0] + lax.broadcasted_iota(jnp.int32, (field_rows, width), 0)
        col = where_ref[1] + offset + lax.broadcasted_iota(jnp.int32, (field_rows, width), 1)
        inside = (row >= 0) & (row < where_ref[2]) & (col >= 0) & (col < where_ref[3])
        sensitivity = jnp.where(inside, sensitivity, 0.0)
        for k in range(KERNELS):
            product = (2.0 * weight_ref[k]) * sensitivity * field_ref[k, :, :width]
            high, low = split(product)
            near = brow_ref[k, 0, :, :field_rows]
            both = mm(jnp.concatenate([near, brow_ref[k, 1, :, :field_rows]], axis=0), high)
            part = both[:rows_here] + both[rows_here:] + mm(near, low)
            high, low = split(part)
            ghigh_ref[k, :, place] = high
            glow_ref[k, :, place] = low

    supers = tile_cols * TILE // WIDE

    @pl.loop(0, supers)
    def _(jj):
        columns(jj * WIDE, WIDE)

    columns(supers * WIDE, LANES)

    def spread_back(k):
        def window(ref, jj):
            return ref[k, :, WIDE * jj : WIDE * jj + 384]

        stacked = jnp.concatenate(
            [
                jnp.concatenate(
                    [window(ghigh_ref, jj), window(glow_ref, jj), window(ghigh_ref, jj)], axis=1
                )
                for jj in range(supers)
            ],
            axis=0,
        )
        return mm(
            stacked, jnp.concatenate([bcol_ref[k, 0], bcol_ref[k, 0], bcol_ref[k, 1]], axis=0)
        )

    def add(part, fresh):
        for g in range(groups):
            rows = slice(g * rows_here, (g + 1) * rows_here)
            top = (g // 2) * rows_here
            piece = part[top : top + rows_here, LANES * (g % 2) : LANES * (g % 2 + 1)]
            grad_ref[rows, :] = piece if fresh else grad_ref[rows, :] + piece

    add(spread_back(0), True)

    @pl.loop(1, KERNELS)
    def _(k):
        add(spread_back(k), False)

    @pl.loop(0, tile_rows)
    def _(a):
        for g in range(groups):
            base = g * rows_here + a * TILE
            parts = [grad_ref[pl.ds(base + s, 8, stride=4), :] for s in range(4)]
            for b, tile in enumerate(transpose_blocks(parts, block)):
                place = pl.multiple_of(index_ref[a, 4 * g + b] * 8, 8)
                out_ref[pl.ds(place, 8), :] = tile


def to_rows(x):
    count = x.shape[0]
    return x.reshape(count // 8, 8, 8, LANES).transpose(0, 2, 1, 3).reshape(count * 8, LANES)


def from_rows(x):
    count = x.shape[0] // 8
    return x.reshape(count // 8, 8, 8, LANES).transpose(0, 2, 1, 3).reshape(count, 8 * LANES)


def kernel_call(body, name, shapes, scratch, scalars, inputs, unread=(), megabytes=8):
    single = not isinstance(shapes, list)
    spec = pl.BlockSpec(memory_space=pltpu.VMEM)
    outs = [shapes] if single else shapes
    result = pl.pallas_call(
        body,
        out_shape=outs,
        in_specs=[pl.BlockSpec(memory_space=pltpu.SMEM)] * len(scalars)
        + [spec] * len(inputs)
        + [pl.BlockSpec(memory_space=pl.ANY)] * len(unread),
        out_specs=[spec] * len(outs),
        scratch_shapes=scratch,
        compiler_params=pltpu.CompilerParams(vmem_limit_bytes=megabytes * 2**20),
        name=name,
    )(*scalars, *inputs, *unread)
    return result[0] if single else result


def neighbours(first, last, axis):
    count = lax.axis_size(axis)
    up = [(i, i + 1) for i in range(count - 1)]
    down = [(j, i) for i, j in up]
    return lax.ppermute(last, axis, up), lax.ppermute(first, axis, down)


def doubled(table, axis):
    count = lax.axis_size(axis)
    bit = 1
    while bit < count:
        got = lax.ppermute(table, axis, [(i, i ^ bit) for i in range(count)])
        table = jnp.concatenate([table, got], axis=0)
        bit *= 2
    return table


def requests(match, value, capacity):
    rank = jnp.cumsum(match.astype(jnp.int32), axis=1) - 1
    hit = match[:, None, :] & (rank[:, None, :] == jnp.arange(capacity)[None, :, None])
    return jnp.max(jnp.where(hit, value[:, None, :], -1), axis=2)


def shards(cells, instance_cell, target, row_taps, col_taps, kernel_weight):
    deep, cores, cols = lax.axis_size("deep"), lax.axis_size("core"), lax.axis_size("col")
    everyone = ("deep", "core", "col")
    plane = ("core", "col")
    peers = cores * cols
    slots = cells.shape[0]
    tile_rows, tile_cols = instance_cell.shape
    tiles_here = tile_rows * tile_cols
    height, breadth = target.shape
    owners = deep * peers
    capacity = 2 * ((tiles_here + owners - 1) // owners)
    wide_capacity = min(tiles_here, deep * capacity)
    f32 = lambda *shape: jax.ShapeDtypeStruct(shape, F32)

    flat = to_rows(cells)
    copies, named = kernel_call(
        spread_kernel,
        "spread",
        [
            f32(deep * slots * 8, LANES),
            jax.ShapeDtypeStruct((1, tiles_here), jnp.int32),
        ],
        [],
        [],
        [flat, instance_cell],
    )
    stack = lax.all_to_all(copies, "deep", split_axis=0, concat_axis=0, tiled=True)

    near = doubled(doubled(named, "col"), "core")
    me = jnp.stack([lax.axis_index(plane), lax.axis_index(everyone)]).astype(jnp.int32)
    owner = near // slots
    asked = requests(
        owner % peers == me[0], (owner // peers) * slots + near % slots, wide_capacity
    )
    waves = make_waves(row_taps, col_taps)
    packed = kernel_call(
        pack_kernel,
        "pack",
        f32(peers * wide_capacity * 8, LANES),
        [],
        [asked, me],
        [stack],
        [waves],
    )
    packed, near = lax.optimization_barrier((packed, near))
    arrived = lax.all_to_all(packed, plane, split_axis=0, concat_axis=0, tiled=True)

    everything = doubled(near, "deep")
    wanted = requests(everything // slots == me[1], everything % slots, capacity)
    mine = named[0] // slots
    earlier = jnp.tri(tiles_here, k=-1, dtype=bool)

    def place(group, size):
        same = (group[:, None] == group[None, :]) & earlier
        where = group * size + jnp.sum(same.astype(jnp.int32), axis=1)
        return where.reshape(tile_rows, tile_cols)

    mask, first, last = kernel_call(
        assemble_kernel,
        "assemble",
        [f32(height, breadth), f32(3 * HALF, breadth), f32(3 * HALF, breadth)],
        [pltpu.VMEM((height * (breadth // LANES), LANES), F32)],
        [place(mine % peers, wide_capacity)],
        [arrived, target],
        [wanted],
    )
    top, bottom = neighbours(first, last, ("deep", "core"))
    quarter = (height + 2 * HALF) // 4
    edge = f32(height // 2 + 2 * HALF + quarter, LANES)
    first, last = kernel_call(
        edges_kernel,
        "edges",
        [edge, edge],
        [pltpu.VMEM((2, 4, quarter, LANES), F32)],
        [],
        [mask, target, top, bottom],
    )
    before, after = neighbours(first, last, "col")
    my_row = lax.axis_index(("deep", "core"))
    my_col = lax.axis_index("col")
    where = jnp.stack(
        [
            my_row * height - HALF,
            my_col * breadth - HALF,
            jnp.int32(deep * cores * height),
            jnp.int32(cols * breadth),
        ]
    ).astype(jnp.int32)
    field_rows = height + 2 * HALF
    returned = kernel_call(
        image_kernel,
        "image",
        f32(owners * capacity * 8, LANES),
        [
            pltpu.VMEM((KERNELS, 2, 256, LANES), BF16),
            pltpu.VMEM((KERNELS, 2, field_rows, 256), BF16),
            pltpu.VMEM((KERNELS, 2, LANES, 256), BF16),
            pltpu.VMEM((KERNELS, 2, 384, 256), BF16),
            pltpu.VMEM((field_rows, breadth + 128), F32),
            pltpu.VMEM((height + 4 * HALF, breadth + 256), BF16),
            pltpu.VMEM((height + 4 * HALF, breadth + 256), BF16),
            pltpu.VMEM((KERNELS, field_rows, WIDE), F32),
            pltpu.VMEM((KERNELS, height, breadth + 128), BF16),
            pltpu.VMEM((KERNELS, height, breadth + 128), BF16),
            pltpu.VMEM((height * (breadth // LANES), LANES), F32),
        ],
        [place(mine, capacity), where, kernel_weight],
        [mask, top, bottom, before, after, target, waves],
        megabytes=36,
    )
    back = lax.all_to_all(returned, everyone, split_axis=0, concat_axis=0, tiled=True)
    stepped = kernel_call(
        step_kernel,
        "step",
        f32(slots * 8, LANES),
        [pltpu.VMEM((slots * 8, LANES), F32)] * 4,
        [wanted, me],
        [flat, back],
    )
    return from_rows(stepped)


def solution(mesh):
    rows, cols = mesh.devices.shape
    finer = Mesh(mesh.devices.reshape(rows // 2, 2, cols), ("deep", "core", "col"))
    row = ("deep", "core")
    placed = (P((*row, "col"), None), P(row, "col"), P(row, "col"), P(), P(), P())
    return jax.shard_map(
        shards, mesh=finer, in_specs=placed, out_specs=P((*row, "col"), None), check_vma=False
    )
```

```python
import jax
import jax.numpy as jnp
from jax import lax
from jax.experimental import pallas as pl
from jax.experimental.pallas import tpu as pltpu
from jax.sharding import Mesh
from jax.sharding import PartitionSpec as P

TILE = 32
TAPS = 65
HALF = 32
KERNELS = 8
LANES = 128
WIDE = 256

STEEPNESS = 4.0
THRESHOLD = 0.3
STEP_RATE = 0.5

F32 = jnp.float32
BF16 = jnp.bfloat16


def split(x):
    high = x.astype(BF16)
    return high, (x - high.astype(F32)).astype(BF16)


def mm(a, b):
    return jnp.dot(a, b, preferred_element_type=F32)


def build_bands(wave_ref, fcol_ref, frow_ref, brow_ref, bcol_ref):
    rows = lax.broadcasted_iota(jnp.int32, (LANES, LANES), 0)
    lanes = lax.broadcasted_iota(jnp.int32, (LANES, LANES), 1)
    zero = jnp.zeros((LANES, LANES), F32)

    def circular(index, start):
        base = jnp.broadcast_to(wave_ref[pl.ds(index, 1), :], (LANES, LANES))
        return pltpu.roll(base, start, 1, stride=1, stride_axis=0)

    def put(ref, kernel, r0, c0, block, height=LANES, breadth=LANES):
        high, low = split(block)
        ref[kernel, 0, r0 : r0 + height, c0 : c0 + breadth] = high[:height, :breadth]
        ref[kernel, 1, r0 : r0 + height, c0 : c0 + breadth] = low[:height, :breadth]

    half = lanes < LANES // 2

    @pl.loop(0, KERNELS)
    def _(k):
        near = circular(k, 0)
        put(frow_ref, k, 0, 0, jnp.where(lanes >= rows, near, zero))
        put(frow_ref, k, 0, LANES, jnp.where(lanes < rows, near, zero))
        put(frow_ref, k, LANES, 0, zero, 64)
        put(frow_ref, k, LANES, LANES, jnp.where(lanes >= rows, near, zero), 64)
        near = circular(2 * KERNELS + k, 0)
        put(brow_ref, k, 0, 0, jnp.where(lanes >= rows, near, zero))
        put(brow_ref, k, 0, LANES, jnp.where(lanes < rows, near, zero))
        near = circular(KERNELS + k, LANES // 2)
        diagonal = jnp.where(rows >= lanes, near, zero)
        beyond = jnp.where(rows < lanes, near, zero)
        for c0, blocks in ((0, (diagonal, beyond, zero)), (LANES, (zero, diagonal, beyond))):
            for n, block in enumerate(blocks):
                height = LANES if n < 2 else LANES // 2
                high, low = split(block)
                for start, piece in ((0, high), (320, high), (640, low)):
                    r0 = start + n * LANES
                    bcol_ref[k, r0 : r0 + height, c0 : c0 + LANES] = piece[:height]
        bcol_ref[k, 960:, :] = jnp.zeros((64, WIDE), BF16)

    @pl.loop(0, KERNELS // 2)
    def _(pair):
        first, second = 3 * KERNELS + 2 * pair, 3 * KERNELS + 2 * pair + 1
        for order, (one, other) in enumerate(((first, second), (second, first))):
            block = jnp.where(half, circular(one, LANES // 2), circular(other, 0))
            high, low = split(block)
            fcol_ref[pair, order, 0] = high
            fcol_ref[pair, order, 1] = low


def make_waves(row_taps, col_taps):
    taps = jnp.concatenate([row_taps, col_taps], axis=0)
    taps = jnp.concatenate([taps, taps[:, ::-1]], axis=0)
    return jnp.pad(taps, [(0, 0), (0, LANES - TAPS)])


def transpose_blocks(parts, block):
    turned = []
    for d in range(4):
        x = parts[d]
        for s in range(1, 4):
            x = jnp.where(block == s, parts[(s + d) % 4], x)
        turned.append(pltpu.roll(x, 32 * d, 1) if d else x)
    out = []
    for s in range(4):
        x = turned[(-s) % 4]
        for b in range(1, 4):
            x = jnp.where(block == b, turned[(b - s) % 4], x)
        out.append(x)
    return out


def spread_kernel(cells_ref, instance_ref, out_ref, named_ref):
    own = cells_ref.shape[0]
    for c in range(own // 8):
        tile = cells_ref[pl.ds((c // 8) * 64 + c % 8, 8, stride=8), :]
        for d in range(out_ref.shape[0] // own):
            out_ref[d * own + c * 8 : d * own + c * 8 + 8, :] = tile
    rows = [instance_ref[a : a + 1, :] for a in range(instance_ref.shape[0])]
    named_ref[...] = jnp.concatenate(rows, axis=1)


def pack_kernel(asked_ref, me_ref, cells_ref, *rest):
    out_ref = rest[-1]
    peers, capacity = asked_ref.shape

    @pl.loop(0, peers)
    def _(i):
        base = (me_ref[0] ^ i) * capacity
        for j in range(capacity):
            asked = jnp.maximum(asked_ref[i, j], 0)
            tile = cells_ref[pl.ds(pl.multiple_of(asked * 8, 8), 8), :]
            out_ref[pl.ds(pl.multiple_of((base + j) * 8, 8), 8), :] = tile


def step_kernel(asked_ref, me_ref, cells_ref, tiles_ref, out_ref, *totals):
    owners, capacity = asked_ref.shape
    nothing = jnp.zeros((8, LANES), F32)
    for total in totals:
        total[...] = jnp.zeros_like(total)

    @pl.loop(0, owners)
    def _(i):
        base = (me_ref[1] ^ i) * capacity
        for j in range(capacity):
            asked = asked_ref[i, j]
            tile = tiles_ref[pl.ds(pl.multiple_of((base + j) * 8, 8), 8), :]
            there = pl.ds(pl.multiple_of(jnp.maximum(asked, 0) * 8, 8), 8)
            total = totals[j % len(totals)]
            total[there, :] += jnp.where(asked >= 0, tile, nothing)

    for c in range(out_ref.shape[0] // 8):
        rows = slice(c * 8, c * 8 + 8)
        total = totals[0][rows, :]
        for other in totals[1:]:
            total = total + other[rows, :]
        there = pl.ds((c // 8) * 64 + c % 8, 8, stride=8)
        out_ref[there, :] = cells_ref[there, :] - STEP_RATE * total


def assemble_kernel(index_ref, tiles_ref, target_ref, *rest):
    mask_ref, first_ref, last_ref, turned_ref = rest[-4:]
    tile_rows, tile_cols = index_ref.shape
    height = tile_rows * TILE
    groups = tile_cols // 4
    block = lax.broadcasted_iota(jnp.int32, (8, LANES), 1) // 32

    @pl.loop(0, tile_rows)
    def _(a):
        for g in range(groups):
            parts = [
                tiles_ref[pl.ds(pl.multiple_of(index_ref[a, 4 * g + b] * 8, 8), 8), :]
                for b in range(4)
            ]
            for s, piece in enumerate(transpose_blocks(parts, block)):
                turned_ref[pl.ds(g * height + a * TILE + s, 8, stride=4), :] = piece

    for g in range(groups):
        lanes = slice(LANES * g, LANES * (g + 1))
        piece = turned_ref[g * height : (g + 1) * height, :]
        mask_ref[:, lanes] = piece
        first_ref[: 2 * HALF, lanes] = piece[: 2 * HALF]
        last_ref[: 2 * HALF, lanes] = piece[height - 2 * HALF :]
    first_ref[2 * HALF :, :] = target_ref[:HALF, :]
    last_ref[2 * HALF :, :] = target_ref[height - HALF :, :]


def target_strips(target_ref, top_ref, bottom_ref, strip):
    height = target_ref.shape[0]
    quarter = (height + 2 * HALF) // 4
    for row in range(0, height + 2 * HALF, 16):
        if row < HALF:
            ref, start = top_ref, 2 * HALF + row
        elif row < HALF + height:
            ref, start = target_ref, row - HALF
        else:
            ref, start = bottom_ref, 2 * HALF + row - HALF - height
        strip(row, ref, slice(start, start + 16), row // quarter, row % quarter)


def edges_kernel(mask_ref, target_ref, top_ref, bottom_ref, first_ref, last_ref, pack_ref):
    height, breadth = mask_ref.shape
    wide = 2 * HALF
    half = height // 2
    packed = half + wide
    lane = lax.broadcasted_iota(jnp.int32, (packed, LANES), 1)
    head, tail = slice(0, LANES), slice(breadth - LANES, breadth)

    def sides(lanes):
        upper = jnp.concatenate([top_ref[:wide, lanes], mask_ref[:half, lanes]], axis=0)
        lower = jnp.concatenate([mask_ref[half:, lanes], bottom_ref[:wide, lanes]], axis=0)
        return upper, lower

    upper, lower = sides(head)
    first_ref[:packed, :] = jnp.where(lane < wide, upper, pltpu.roll(lower, wide, 1))
    upper, lower = sides(tail)
    last_ref[:packed, :] = jnp.where(lane < wide, pltpu.roll(upper, wide, 1), lower)

    quarter = (height + 2 * HALF) // 4

    def strip(row, ref, rows, part, inner):
        for side, lanes in enumerate((head, tail)):
            shift = (HALF * (part + side)) % LANES
            piece = ref[rows, lanes]
            pack_ref[side, part, inner : inner + 16, :] = (
                pltpu.roll(piece, shift, 1) if shift else piece
            )

    target_strips(target_ref, top_ref, bottom_ref, strip)
    part_of = lax.broadcasted_iota(jnp.int32, (quarter, LANES), 1) // HALF
    for side, ref in enumerate((first_ref, last_ref)):
        piece = pack_ref[side, 0]
        for part in range(1, 4):
            piece = jnp.where(part_of == part, pack_ref[side, part], piece)
        ref[packed:, :] = piece


def image_kernel(
    index_ref,
    where_ref,
    weight_ref,
    mask_ref,
    top_ref,
    bottom_ref,
    before_ref,
    after_ref,
    own_ref,
    wave_ref,
    out_ref,
    fcol_ref,
    frow_ref,
    brow_ref,
    bcol_ref,
    target_ref,
    mhigh_ref,
    mlow_ref,
    nhigh_ref,
    nlow_ref,
    field_ref,
    ghigh_ref,
    gturn_ref,
    grad_ref,
):
    tile_rows, tile_cols = index_ref.shape
    rows_here = tile_rows * TILE
    high_rows = rows_here + 4 * HALF
    field_rows = rows_here + 2 * HALF
    groups = tile_cols // 4
    wide = 2 * HALF
    block = lax.broadcasted_iota(jnp.int32, (8, LANES), 1) // 32
    build_bands(wave_ref, fcol_ref, frow_ref, brow_ref, bcol_ref)

    lane = lax.broadcasted_iota(jnp.int32, (wide, LANES), 1)
    for rows in range(0, high_rows, wide):
        if rows == 0:
            ref, start = top_ref, 0
        elif rows == high_rows - wide:
            ref, start = bottom_ref, 0
        else:
            ref, start = mask_ref, rows - wide
        half = high_rows // 2
        edge = slice(rows % half, rows % half + wide)
        turned = before_ref[edge, :]
        final = after_ref[edge, :]
        if rows < half:
            final = pltpu.roll(final, wide, 1)
        else:
            turned = pltpu.roll(turned, wide, 1)
        for g in range(groups + 1):
            fresh = final
            if g < groups:
                piece = ref[start : start + wide, LANES * g : LANES * (g + 1)]
                high, low = split(piece)
                nhigh_ref[rows : rows + wide, LANES * g : LANES * (g + 1)] = high
                nlow_ref[rows : rows + wide, LANES * g : LANES * (g + 1)] = low
                fresh = pltpu.roll(piece, wide, 1)
            high, low = split(jnp.where(lane < wide, turned, fresh))
            mhigh_ref[rows : rows + wide, LANES * g : LANES * (g + 1)] = high
            mlow_ref[rows : rows + wide, LANES * g : LANES * (g + 1)] = low
            turned = fresh
    packed = high_rows // 2
    near_lane = lax.broadcasted_iota(jnp.int32, (16, LANES), 1)

    def strip(row, ref, rows, part, inner):
        edge = slice(packed + inner, packed + inner + 16)
        back, ahead = (-HALF * part) % LANES, (HALF - HALF * part) % LANES
        turned = pltpu.roll(before_ref[edge, :], back, 1) if back else before_ref[edge, :]
        final = pltpu.roll(after_ref[edge, :], ahead, 1) if ahead else after_ref[edge, :]
        for g in range(groups + 1):
            fresh = final
            if g < groups:
                fresh = pltpu.roll(ref[rows, LANES * g : LANES * (g + 1)], HALF, 1)
            target_ref[row : row + 16, LANES * g : LANES * (g + 1)] = jnp.where(
                near_lane < HALF, turned, fresh
            )
            turned = fresh

    target_strips(own_ref, top_ref, bottom_ref, strip)

    def swapped(x):
        pieces = [
            pltpu.roll(x[:, c : c + LANES], LANES // 2, 1) for c in range(0, x.shape[1], LANES)
        ]
        return pieces[0] if len(pieces) == 1 else jnp.concatenate(pieces, axis=1)

    def columns(offset, width):
        blocks = width // LANES
        last = blocks == 1

        def windows(high_ref, low_ref):
            rows = []
            for j in range(blocks):
                place = pl.ds(pl.multiple_of(offset + j * LANES, LANES), LANES)
                high, low = high_ref[:, place], low_ref[:, place]
                rows.append(jnp.concatenate([high, low, high], axis=1))
            return rows[0] if last else jnp.concatenate(rows, axis=0)

        even_rows = windows(mhigh_ref, mlow_ref)
        odd_rows = None if last else windows(nhigh_ref, nlow_ref)
        left = lax.broadcasted_iota(jnp.int32, (high_rows, LANES), 1) < LANES // 2

        def band(quad, order):
            both = [
                jnp.concatenate(
                    [fcol_ref[2 * quad, order, v], fcol_ref[2 * quad + 1, order, v]], axis=1
                )
                for v in range(2)
            ]
            return jnp.concatenate([both[0], both[0], both[1]], axis=0)

        sums = [None, None]
        for quad in range(KERNELS // 4):
            even = mm(even_rows, band(quad, 0))
            odd = even if last else mm(odd_rows, band(quad, 1))
            for h in range(4):
                k = 4 * quad + h
                pieces = []
                for j in range(blocks):
                    rows = slice(j * high_rows, (j + 1) * high_rows)
                    lanes = slice((h // 2) * LANES, (h // 2 + 1) * LANES)
                    if last:
                        pieces.append(even[rows, lanes])
                    elif h % 2 == 0:
                        pieces.append(jnp.where(left, even[rows, lanes], odd[rows, lanes]))
                    else:
                        pieces.append(jnp.where(left, odd[rows, lanes], even[rows, lanes]))
                high, low = split(pieces[0] if last else jnp.concatenate(pieces, axis=1))
                both = mm(jnp.concatenate([frow_ref[k, 0], frow_ref[k, 1]], axis=0), high)
                field = both[:field_rows] + both[field_rows:] + mm(frow_ref[k, 0], low)
                field_ref[k, :, :width] = field
                term = weight_ref[k] * field * field
                sums[h % 2] = term if sums[h % 2] is None else sums[h % 2] + term
        intensity = sums[0] + swapped(sums[1])
        resist = 1.0 / (1.0 + jnp.exp(-STEEPNESS * (intensity - THRESHOLD)))
        place = pl.ds(pl.multiple_of(offset, LANES), width)
        target = target_ref[:, place]
        sensitivity = 2.0 * (resist - target) * STEEPNESS * resist * (1.0 - resist)
        row = where_ref[0] + lax.broadcasted_iota(jnp.int32, (field_rows, width), 0)
        col = where_ref[1] + offset + lax.broadcasted_iota(jnp.int32, (field_rows, width), 1)
        inside = (row >= 0) & (row < where_ref[2]) & (col >= 0) & (col < where_ref[3])
        sensitivity = jnp.where(inside, sensitivity, 0.0)
        ordered = (sensitivity, swapped(sensitivity))
        for k in range(KERNELS):
            product = (2.0 * weight_ref[k]) * ordered[k % 2] * field_ref[k, :, :width]
            high, low = split(product)
            near = brow_ref[k, 0, :, :field_rows]
            both = mm(jnp.concatenate([near, brow_ref[k, 1, :, :field_rows]], axis=0), high)
            part = both[:rows_here] + both[rows_here:] + mm(near, low)
            straight, turned = (part, swapped(part))[:: 1 - 2 * (k % 2)]
            ghigh_ref[k, :, place] = straight.astype(BF16)
            gturn_ref[k, :, place] = split(turned)[1]

    supers = tile_cols * TILE // WIDE

    @pl.loop(0, supers)
    def _(jj):
        columns(jj * WIDE, WIDE)

    columns(supers * WIDE, LANES)

    lower = lax.broadcasted_iota(jnp.int32, (rows_here, LANES), 1) < LANES // 2

    def spread_back(k):
        stacked = []
        for jj in range(supers):
            c0 = WIDE * jj
            high = [ghigh_ref[k, :, c0 + LANES * n : c0 + LANES * (n + 1)] for n in range(3)]
            turn = [gturn_ref[k, :, c0 + LANES * n : c0 + LANES * (n + 1)] for n in range(3)]
            row = [
                high[0],
                high[1],
                jnp.where(lower, high[2], turn[0]),
                jnp.where(lower, turn[0], turn[1]),
                jnp.where(lower, turn[1], turn[2]),
                *high,
            ]
            stacked.append(jnp.concatenate(row, axis=1))
        return mm(jnp.concatenate(stacked, axis=0), bcol_ref[k])

    def add(part, fresh):
        for g in range(groups):
            rows = slice(g * rows_here, (g + 1) * rows_here)
            top = (g // 2) * rows_here
            piece = part[top : top + rows_here, LANES * (g % 2) : LANES * (g % 2 + 1)]
            grad_ref[rows, :] = piece if fresh else grad_ref[rows, :] + piece

    add(spread_back(0), True)

    @pl.loop(1, KERNELS)
    def _(k):
        add(spread_back(k), False)

    @pl.loop(0, tile_rows)
    def _(a):
        for g in range(groups):
            base = g * rows_here + a * TILE
            parts = [grad_ref[pl.ds(base + s, 8, stride=4), :] for s in range(4)]
            for b, tile in enumerate(transpose_blocks(parts, block)):
                place = pl.multiple_of(index_ref[a, 4 * g + b] * 8, 8)
                out_ref[pl.ds(place, 8), :] = tile


def to_rows(x):
    count = x.shape[0]
    return x.reshape(count // 8, 8, 8, LANES).transpose(0, 2, 1, 3).reshape(count * 8, LANES)


def from_rows(x):
    count = x.shape[0] // 8
    return x.reshape(count // 8, 8, 8, LANES).transpose(0, 2, 1, 3).reshape(count, 8 * LANES)


def kernel_call(body, name, shapes, scratch, scalars, inputs, unread=(), megabytes=8):
    single = not isinstance(shapes, list)
    spec = pl.BlockSpec(memory_space=pltpu.VMEM)
    outs = [shapes] if single else shapes
    result = pl.pallas_call(
        body,
        out_shape=outs,
        in_specs=[pl.BlockSpec(memory_space=pltpu.SMEM)] * len(scalars)
        + [spec] * len(inputs)
        + [pl.BlockSpec(memory_space=pl.ANY)] * len(unread),
        out_specs=[spec] * len(outs),
        scratch_shapes=scratch,
        compiler_params=pltpu.CompilerParams(vmem_limit_bytes=megabytes * 2**20),
        name=name,
    )(*scalars, *inputs, *unread)
    return result[0] if single else result


def neighbours(first, last, axis):
    count = lax.axis_size(axis)
    up = [(i, i + 1) for i in range(count - 1)]
    down = [(j, i) for i, j in up]
    return lax.ppermute(last, axis, up), lax.ppermute(first, axis, down)


def doubled(table, axis):
    count = lax.axis_size(axis)
    bit = 1
    while bit < count:
        got = lax.ppermute(table, axis, [(i, i ^ bit) for i in range(count)])
        table = jnp.concatenate([table, got], axis=0)
        bit *= 2
    return table


def requests(match, value, capacity):
    rank = jnp.cumsum(match.astype(jnp.int32), axis=1) - 1
    hit = match[:, None, :] & (rank[:, None, :] == jnp.arange(capacity)[None, :, None])
    return jnp.max(jnp.where(hit, value[:, None, :], -1), axis=2)


def shards(cells, instance_cell, target, row_taps, col_taps, kernel_weight):
    deep, cores, cols = lax.axis_size("deep"), lax.axis_size("core"), lax.axis_size("col")
    everyone = ("deep", "core", "col")
    plane = ("core", "col")
    peers = cores * cols
    slots = cells.shape[0]
    tile_rows, tile_cols = instance_cell.shape
    tiles_here = tile_rows * tile_cols
    height, breadth = target.shape
    owners = deep * peers
    capacity = 2 * ((tiles_here + owners - 1) // owners)
    wide_capacity = min(tiles_here, deep * capacity)
    f32 = lambda *shape: jax.ShapeDtypeStruct(shape, F32)

    flat = to_rows(cells)
    copies, named = kernel_call(
        spread_kernel,
        "spread",
        [
            f32(deep * slots * 8, LANES),
            jax.ShapeDtypeStruct((1, tiles_here), jnp.int32),
        ],
        [],
        [],
        [flat, instance_cell],
    )
    stack = lax.all_to_all(copies, "deep", split_axis=0, concat_axis=0, tiled=True)

    near = doubled(doubled(named, "col"), "core")
    me = jnp.stack([lax.axis_index(plane), lax.axis_index(everyone)]).astype(jnp.int32)
    owner = near // slots
    asked = requests(
        owner % peers == me[0], (owner // peers) * slots + near % slots, wide_capacity
    )
    waves = make_waves(row_taps, col_taps)
    packed = kernel_call(
        pack_kernel,
        "pack",
        f32(peers * wide_capacity * 8, LANES),
        [],
        [asked, me],
        [stack],
        [waves],
    )
    packed, near = lax.optimization_barrier((packed, near))
    arrived = lax.all_to_all(packed, plane, split_axis=0, concat_axis=0, tiled=True)

    everything = doubled(near, "deep")
    wanted = requests(everything // slots == me[1], everything % slots, capacity)
    mine = named[0] // slots
    earlier = jnp.tri(tiles_here, k=-1, dtype=bool)

    def place(group, size):
        same = (group[:, None] == group[None, :]) & earlier
        where = group * size + jnp.sum(same.astype(jnp.int32), axis=1)
        return where.reshape(tile_rows, tile_cols)

    mask, first, last = kernel_call(
        assemble_kernel,
        "assemble",
        [f32(height, breadth), f32(3 * HALF, breadth), f32(3 * HALF, breadth)],
        [pltpu.VMEM((height * (breadth // LANES), LANES), F32)],
        [place(mine % peers, wide_capacity)],
        [arrived, target],
        [wanted],
    )
    top, bottom = neighbours(first, last, ("deep", "core"))
    quarter = (height + 2 * HALF) // 4
    edge = f32(height // 2 + 2 * HALF + quarter, LANES)
    first, last = kernel_call(
        edges_kernel,
        "edges",
        [edge, edge],
        [pltpu.VMEM((2, 4, quarter, LANES), F32)],
        [],
        [mask, target, top, bottom],
    )
    before, after = neighbours(first, last, "col")
    my_row = lax.axis_index(("deep", "core"))
    my_col = lax.axis_index("col")
    where = jnp.stack(
        [
            my_row * height - HALF,
            my_col * breadth - HALF,
            jnp.int32(deep * cores * height),
            jnp.int32(cols * breadth),
        ]
    ).astype(jnp.int32)
    field_rows = height + 2 * HALF
    returned = kernel_call(
        image_kernel,
        "image",
        f32(owners * capacity * 8, LANES),
        [
            pltpu.VMEM((KERNELS // 2, 2, 2, LANES, LANES), BF16),
            pltpu.VMEM((KERNELS, 2, field_rows, 256), BF16),
            pltpu.VMEM((KERNELS, 2, LANES, 256), BF16),
            pltpu.VMEM((KERNELS, 1024, WIDE), BF16),
            pltpu.VMEM((field_rows, breadth + 128), F32),
            pltpu.VMEM((height + 4 * HALF, breadth + 128), BF16),
            pltpu.VMEM((height + 4 * HALF, breadth + 128), BF16),
            pltpu.VMEM((height + 4 * HALF, breadth), BF16),
            pltpu.VMEM((height + 4 * HALF, breadth), BF16),
            pltpu.VMEM((KERNELS, field_rows, WIDE), F32),
            pltpu.VMEM((KERNELS, height, breadth + 128), BF16),
            pltpu.VMEM((KERNELS, height, breadth + 128), BF16),
            pltpu.VMEM((height * (breadth // LANES), LANES), F32),
        ],
        [place(mine, capacity), where, kernel_weight],
        [mask, top, bottom, before, after, target, waves],
        megabytes=36,
    )
    back = lax.all_to_all(returned, everyone, split_axis=0, concat_axis=0, tiled=True)
    stepped = kernel_call(
        step_kernel,
        "step",
        f32(slots * 8, LANES),
        [pltpu.VMEM((slots * 8, LANES), F32)] * 4,
        [wanted, me],
        [flat, back],
    )
    return from_rows(stepped)


def solution(mesh):
    rows, cols = mesh.devices.shape
    finer = Mesh(mesh.devices.reshape(rows // 2, 2, cols), ("deep", "core", "col"))
    row = ("deep", "core")
    placed = (P((*row, "col"), None), P(row, "col"), P(row, "col"), P(), P(), P())
    return jax.shard_map(
        shards, mesh=finer, in_specs=placed, out_specs=P((*row, "col"), None), check_vma=False
    )
```

```python
import jax
import jax.numpy as jnp
from jax import lax
from jax.experimental import pallas as pl
from jax.experimental.pallas import tpu as pltpu
from jax.sharding import Mesh
from jax.sharding import PartitionSpec as P

TILE = 32
TAPS = 65
HALF = 32
KERNELS = 8
LANES = 128
WIDE = 256

STEEPNESS = 4.0
THRESHOLD = 0.3
STEP_RATE = 0.5

F32 = jnp.float32
BF16 = jnp.bfloat16


def split(x):
    high = x.astype(BF16)
    return high, (x - high.astype(F32)).astype(BF16)


def mm(a, b):
    return jnp.dot(a, b, preferred_element_type=F32)


def build_bands(wave_ref, fcol_ref, frow_ref, brow_ref, bcol_ref):
    rows = lax.broadcasted_iota(jnp.int32, (LANES, LANES), 0)
    lanes = lax.broadcasted_iota(jnp.int32, (LANES, LANES), 1)
    zero = jnp.zeros((LANES, LANES), F32)

    def circular(index, start):
        base = jnp.broadcast_to(wave_ref[pl.ds(index, 1), :], (LANES, LANES))
        return pltpu.roll(base, start, 1, stride=1, stride_axis=0)

    def put(ref, kernel, r0, c0, block, height=LANES, breadth=LANES):
        high, low = split(block)
        ref[kernel, 0, r0 : r0 + height, c0 : c0 + breadth] = high[:height, :breadth]
        ref[kernel, 1, r0 : r0 + height, c0 : c0 + breadth] = low[:height, :breadth]

    half = lanes < LANES // 2

    @pl.loop(0, KERNELS)
    def _(k):
        near = circular(k, 0)
        put(frow_ref, k, 0, 0, jnp.where(lanes >= rows, near, zero))
        put(frow_ref, k, 0, LANES, jnp.where(lanes < rows, near, zero))
        put(frow_ref, k, LANES, 0, zero, 64)
        put(frow_ref, k, LANES, LANES, jnp.where(lanes >= rows, near, zero), 64)
        near = circular(2 * KERNELS + k, 0)
        put(brow_ref, k, 0, 0, jnp.where(lanes >= rows, near, zero))
        put(brow_ref, k, 0, LANES, jnp.where(lanes < rows, near, zero))
        near = circular(KERNELS + k, LANES // 2)
        diagonal = jnp.where(rows >= lanes, near, zero)
        beyond = jnp.where(rows < lanes, near, zero)
        for c0, blocks in ((0, (diagonal, beyond, zero)), (LANES, (zero, diagonal, beyond))):
            for n, block in enumerate(blocks):
                height = LANES if n < 2 else LANES // 2
                high, low = split(block)
                for start, piece in ((0, high), (320, high), (640, low)):
                    r0 = start + n * LANES
                    bcol_ref[k, r0 : r0 + height, c0 : c0 + LANES] = piece[:height]
        bcol_ref[k, 960:, :] = jnp.zeros((64, WIDE), BF16)

    @pl.loop(0, KERNELS // 2)
    def _(pair):
        first, second = 3 * KERNELS + 2 * pair, 3 * KERNELS + 2 * pair + 1
        for order, (one, other) in enumerate(((first, second), (second, first))):
            block = jnp.where(half, circular(one, LANES // 2), circular(other, 0))
            high, low = split(block)
            fcol_ref[pair, order, 0] = high
            fcol_ref[pair, order, 1] = low


def make_waves(row_taps, col_taps):
    taps = jnp.concatenate([row_taps, col_taps], axis=0)
    taps = jnp.concatenate([taps, taps[:, ::-1]], axis=0)
    return jnp.pad(taps, [(0, 0), (0, LANES - TAPS)])


def transpose_blocks(parts, block):
    turned = []
    for d in range(4):
        x = parts[d]
        for s in range(1, 4):
            x = jnp.where(block == s, parts[(s + d) % 4], x)
        turned.append(pltpu.roll(x, 32 * d, 1) if d else x)
    out = []
    for s in range(4):
        x = turned[(-s) % 4]
        for b in range(1, 4):
            x = jnp.where(block == b, turned[(b - s) % 4], x)
        out.append(x)
    return out


def spread_kernel(cells_ref, instance_ref, out_ref, named_ref):
    own = cells_ref.shape[0]
    for c in range(own // 8):
        tile = cells_ref[pl.ds((c // 8) * 64 + c % 8, 8, stride=8), :]
        for d in range(out_ref.shape[0] // own):
            out_ref[d * own + c * 8 : d * own + c * 8 + 8, :] = tile
    rows = [instance_ref[a : a + 1, :] for a in range(instance_ref.shape[0])]
    named_ref[...] = jnp.concatenate(rows, axis=1)


def pack_kernel(asked_ref, me_ref, cells_ref, *rest):
    out_ref, stage_ref, sems = rest[-3:]
    peers, capacity = asked_ref.shape
    chunk = capacity * 8

    def send(i):
        rows = pl.ds(pl.multiple_of((me_ref[0] ^ i) * chunk, chunk), chunk)
        return pltpu.make_async_copy(stage_ref.at[rows, :], out_ref.at[rows, :], sems.at[i])

    @pl.loop(0, peers)
    def _(i):
        base = (me_ref[0] ^ i) * capacity
        for j in range(capacity):
            asked = jnp.maximum(asked_ref[i, j], 0)
            tile = cells_ref[pl.ds(pl.multiple_of(asked * 8, 8), 8), :]
            stage_ref[pl.ds(pl.multiple_of((base + j) * 8, 8), 8), :] = tile
        send(i).start()

    @pl.loop(0, peers)
    def _(i):
        send(i).wait()


def step_kernel(asked_ref, me_ref, cells_ref, tiles_ref, out_ref, *totals):
    owners, capacity = asked_ref.shape
    nothing = jnp.zeros((8, LANES), F32)
    for total in totals:
        total[...] = jnp.zeros_like(total)

    @pl.loop(0, owners)
    def _(i):
        base = (me_ref[1] ^ i) * capacity
        for j in range(capacity):
            asked = asked_ref[i, j]
            tile = tiles_ref[pl.ds(pl.multiple_of((base + j) * 8, 8), 8), :]
            there = pl.ds(pl.multiple_of(jnp.maximum(asked, 0) * 8, 8), 8)
            total = totals[j % len(totals)]
            total[there, :] += jnp.where(asked >= 0, tile, nothing)

    for c in range(out_ref.shape[0] // 8):
        rows = slice(c * 8, c * 8 + 8)
        total = totals[0][rows, :]
        for other in totals[1:]:
            total = total + other[rows, :]
        there = pl.ds((c // 8) * 64 + c % 8, 8, stride=8)
        out_ref[there, :] = cells_ref[there, :] - STEP_RATE * total


def target_strips(target_ref, top_ref, bottom_ref, strip):
    height = target_ref.shape[0]
    quarter = (height + 2 * HALF) // 4
    for row in range(0, height + 2 * HALF, 16):
        if row < HALF:
            ref, start = top_ref, row
        elif row < HALF + height:
            ref, start = target_ref, row - HALF
        else:
            ref, start = bottom_ref, row - HALF - height
        strip(row, ref, slice(start, start + 16), row // quarter, row % quarter)


def assemble_kernel(index_ref, tiles_ref, target_ref, ttop_ref, tbottom_ref, *rest):
    mask_ref, first_ref, last_ref, left_ref, right_ref, turned_ref, pack_ref = rest[-7:]
    tile_rows, tile_cols = index_ref.shape
    height, breadth = target_ref.shape
    wide = 2 * HALF
    half = height // 2
    groups = tile_cols // 4
    block = lax.broadcasted_iota(jnp.int32, (8, LANES), 1) // 32

    @pl.loop(0, tile_rows)
    def _(a):
        for g in range(groups):
            parts = [
                tiles_ref[pl.ds(pl.multiple_of(index_ref[a, 4 * g + b] * 8, 8), 8), :]
                for b in range(4)
            ]
            for s, piece in enumerate(transpose_blocks(parts, block)):
                turned_ref[pl.ds(g * height + a * TILE + s, 8, stride=4), :] = piece

    lane = lax.broadcasted_iota(jnp.int32, (half, LANES), 1)
    for g in range(groups):
        lanes = slice(LANES * g, LANES * (g + 1))
        piece = turned_ref[g * height : (g + 1) * height, :]
        mask_ref[:, lanes] = piece
        first_ref[:, lanes] = piece[:wide]
        last_ref[:, lanes] = piece[height - wide :]
        upper, lower = piece[:half], piece[half:]
        if g == 0:
            left_ref[:half, :] = jnp.where(lane < wide, upper, pltpu.roll(lower, wide, 1))
        if g == groups - 1:
            right_ref[:half, :] = jnp.where(lane < wide, pltpu.roll(upper, wide, 1), lower)

    quarter = (height + 2 * HALF) // 4

    def strip(row, ref, rows, part, inner):
        for side, lanes in enumerate((slice(0, LANES), slice(breadth - LANES, breadth))):
            shift = (HALF * (part + side)) % LANES
            piece = ref[rows, lanes]
            pack_ref[side, part, inner : inner + 16, :] = (
                pltpu.roll(piece, shift, 1) if shift else piece
            )

    target_strips(target_ref, ttop_ref, tbottom_ref, strip)
    part_of = lax.broadcasted_iota(jnp.int32, (quarter, LANES), 1) // HALF
    for side, ref in enumerate((left_ref, right_ref)):
        piece = pack_ref[side, 0]
        for part in range(1, 4):
            piece = jnp.where(part_of == part, pack_ref[side, part], piece)
        ref[half:, :] = piece


def corners_kernel(before_ref, after_ref, first_ref, last_ref):
    wide = 2 * HALF
    lane = lax.broadcasted_iota(jnp.int32, (wide, LANES), 1)
    before, after = before_ref[:wide, :], after_ref[:wide, :]
    first_ref[...] = jnp.where(lane < wide, before, pltpu.roll(after, wide, 1))
    last_ref[...] = jnp.where(lane < wide, pltpu.roll(before, wide, 1), after)


def image_kernel(
    index_ref,
    where_ref,
    weight_ref,
    mask_ref,
    top_ref,
    bottom_ref,
    before_ref,
    after_ref,
    ctop_ref,
    cbottom_ref,
    own_ref,
    ttop_ref,
    tbottom_ref,
    wave_ref,
    out_ref,
    fcol_ref,
    frow_ref,
    brow_ref,
    bcol_ref,
    target_ref,
    mhigh_ref,
    mlow_ref,
    nhigh_ref,
    nlow_ref,
    field_ref,
    ghigh_ref,
    gturn_ref,
    grad_ref,
):
    tile_rows, tile_cols = index_ref.shape
    rows_here = tile_rows * TILE
    high_rows = rows_here + 4 * HALF
    field_rows = rows_here + 2 * HALF
    groups = tile_cols // 4
    wide = 2 * HALF
    block = lax.broadcasted_iota(jnp.int32, (8, LANES), 1) // 32
    build_bands(wave_ref, fcol_ref, frow_ref, brow_ref, bcol_ref)

    lane = lax.broadcasted_iota(jnp.int32, (wide, LANES), 1)
    for rows in range(0, high_rows, wide):
        if rows == 0:
            ref, start = top_ref, 0
        elif rows == high_rows - wide:
            ref, start = bottom_ref, 0
        else:
            ref, start = mask_ref, rows - wide
        if rows == 0 or rows == high_rows - wide:
            corner = ctop_ref if rows == 0 else cbottom_ref
            turned = final = corner[...]
        else:
            turned, final = before_ref[:wide, :], after_ref[:wide, :]
            if rows == wide:
                final = pltpu.roll(final, wide, 1)
            else:
                turned = pltpu.roll(turned, wide, 1)
        for g in range(groups + 1):
            fresh = final
            if g < groups:
                piece = ref[start : start + wide, LANES * g : LANES * (g + 1)]
                high, low = split(piece)
                nhigh_ref[rows : rows + wide, LANES * g : LANES * (g + 1)] = high
                nlow_ref[rows : rows + wide, LANES * g : LANES * (g + 1)] = low
                fresh = pltpu.roll(piece, wide, 1)
            high, low = split(jnp.where(lane < wide, turned, fresh))
            mhigh_ref[rows : rows + wide, LANES * g : LANES * (g + 1)] = high
            mlow_ref[rows : rows + wide, LANES * g : LANES * (g + 1)] = low
            turned = fresh
    packed = rows_here // 2
    near_lane = lax.broadcasted_iota(jnp.int32, (16, LANES), 1)

    def strip(row, ref, rows, part, inner):
        edge = slice(packed + inner, packed + inner + 16)
        back, ahead = (-HALF * part) % LANES, (HALF - HALF * part) % LANES
        turned = pltpu.roll(before_ref[edge, :], back, 1) if back else before_ref[edge, :]
        final = pltpu.roll(after_ref[edge, :], ahead, 1) if ahead else after_ref[edge, :]
        for g in range(groups + 1):
            fresh = final
            if g < groups:
                fresh = pltpu.roll(ref[rows, LANES * g : LANES * (g + 1)], HALF, 1)
            target_ref[row : row + 16, LANES * g : LANES * (g + 1)] = jnp.where(
                near_lane < HALF, turned, fresh
            )
            turned = fresh

    target_strips(own_ref, ttop_ref, tbottom_ref, strip)

    def swapped(x):
        pieces = [
            pltpu.roll(x[:, c : c + LANES], LANES // 2, 1) for c in range(0, x.shape[1], LANES)
        ]
        return pieces[0] if len(pieces) == 1 else jnp.concatenate(pieces, axis=1)

    def columns(offset, width):
        blocks = width // LANES
        last = blocks == 1

        def windows(high_ref, low_ref):
            rows = []
            for j in range(blocks):
                place = pl.ds(pl.multiple_of(offset + j * LANES, LANES), LANES)
                high, low = high_ref[:, place], low_ref[:, place]
                rows.append(jnp.concatenate([high, low, high], axis=1))
            return rows[0] if last else jnp.concatenate(rows, axis=0)

        even_rows = windows(mhigh_ref, mlow_ref)
        odd_rows = None if last else windows(nhigh_ref, nlow_ref)
        left = lax.broadcasted_iota(jnp.int32, (high_rows, LANES), 1) < LANES // 2

        def band(quad, order):
            both = [
                jnp.concatenate(
                    [fcol_ref[2 * quad, order, v], fcol_ref[2 * quad + 1, order, v]], axis=1
                )
                for v in range(2)
            ]
            return jnp.concatenate([both[0], both[0], both[1]], axis=0)

        sums = [None, None]
        for quad in range(KERNELS // 4):
            even = mm(even_rows, band(quad, 0))
            odd = even if last else mm(odd_rows, band(quad, 1))
            for h in range(4):
                k = 4 * quad + h
                pieces = []
                for j in range(blocks):
                    rows = slice(j * high_rows, (j + 1) * high_rows)
                    lanes = slice((h // 2) * LANES, (h // 2 + 1) * LANES)
                    if last:
                        pieces.append(even[rows, lanes])
                    elif h % 2 == 0:
                        pieces.append(jnp.where(left, even[rows, lanes], odd[rows, lanes]))
                    else:
                        pieces.append(jnp.where(left, odd[rows, lanes], even[rows, lanes]))
                high, low = split(pieces[0] if last else jnp.concatenate(pieces, axis=1))
                both = mm(jnp.concatenate([frow_ref[k, 0], frow_ref[k, 1]], axis=0), high)
                field = both[:field_rows] + both[field_rows:] + mm(frow_ref[k, 0], low)
                field_ref[k, :, :width] = field
                term = weight_ref[k] * field * field
                sums[h % 2] = term if sums[h % 2] is None else sums[h % 2] + term
        intensity = sums[0] + swapped(sums[1])
        resist = 1.0 / (1.0 + jnp.exp(-STEEPNESS * (intensity - THRESHOLD)))
        place = pl.ds(pl.multiple_of(offset, LANES), width)
        target = target_ref[:, place]
        sensitivity = 2.0 * (resist - target) * STEEPNESS * resist * (1.0 - resist)
        row = where_ref[0] + lax.broadcasted_iota(jnp.int32, (field_rows, width), 0)
        col = where_ref[1] + offset + lax.broadcasted_iota(jnp.int32, (field_rows, width), 1)
        inside = (row >= 0) & (row < where_ref[2]) & (col >= 0) & (col < where_ref[3])
        sensitivity = jnp.where(inside, sensitivity, 0.0)
        ordered = (sensitivity, swapped(sensitivity))
        for k in range(KERNELS):
            product = (2.0 * weight_ref[k]) * ordered[k % 2] * field_ref[k, :, :width]
            high, low = split(product)
            near = brow_ref[k, 0, :, :field_rows]
            both = mm(jnp.concatenate([near, brow_ref[k, 1, :, :field_rows]], axis=0), high)
            part = both[:rows_here] + both[rows_here:] + mm(near, low)
            straight, turned = (part, swapped(part))[:: 1 - 2 * (k % 2)]
            ghigh_ref[k, :, place] = straight.astype(BF16)
            gturn_ref[k, :, place] = split(turned)[1]

    supers = tile_cols * TILE // WIDE

    @pl.loop(0, supers)
    def _(jj):
        columns(jj * WIDE, WIDE)

    columns(supers * WIDE, LANES)

    lower = lax.broadcasted_iota(jnp.int32, (rows_here, LANES), 1) < LANES // 2

    def spread_back(k):
        stacked = []
        for jj in range(supers):
            c0 = WIDE * jj
            high = [ghigh_ref[k, :, c0 + LANES * n : c0 + LANES * (n + 1)] for n in range(3)]
            turn = [gturn_ref[k, :, c0 + LANES * n : c0 + LANES * (n + 1)] for n in range(3)]
            row = [
                high[0],
                high[1],
                jnp.where(lower, high[2], turn[0]),
                jnp.where(lower, turn[0], turn[1]),
                jnp.where(lower, turn[1], turn[2]),
                *high,
            ]
            stacked.append(jnp.concatenate(row, axis=1))
        return mm(jnp.concatenate(stacked, axis=0), bcol_ref[k])

    def add(part, fresh):
        for g in range(groups):
            rows = slice(g * rows_here, (g + 1) * rows_here)
            top = (g // 2) * rows_here
            piece = part[top : top + rows_here, LANES * (g % 2) : LANES * (g % 2 + 1)]
            grad_ref[rows, :] = piece if fresh else grad_ref[rows, :] + piece

    add(spread_back(0), True)

    @pl.loop(1, KERNELS)
    def _(k):
        add(spread_back(k), False)

    @pl.loop(0, tile_rows)
    def _(a):
        for g in range(groups):
            base = g * rows_here + a * TILE
            parts = [grad_ref[pl.ds(base + s, 8, stride=4), :] for s in range(4)]
            for b, tile in enumerate(transpose_blocks(parts, block)):
                place = pl.multiple_of(index_ref[a, 4 * g + b] * 8, 8)
                out_ref[pl.ds(place, 8), :] = tile


def to_rows(x):
    count = x.shape[0]
    return x.reshape(count // 8, 8, 8, LANES).transpose(0, 2, 1, 3).reshape(count * 8, LANES)


def from_rows(x):
    count = x.shape[0] // 8
    return x.reshape(count // 8, 8, 8, LANES).transpose(0, 2, 1, 3).reshape(count, 8 * LANES)


def kernel_call(body, name, shapes, scratch, scalars, inputs, unread=(), megabytes=8, out_space=pltpu.VMEM):
    single = not isinstance(shapes, list)
    spec = pl.BlockSpec(memory_space=pltpu.VMEM)
    outs = [shapes] if single else shapes
    result = pl.pallas_call(
        body,
        out_shape=outs,
        in_specs=[pl.BlockSpec(memory_space=pltpu.SMEM)] * len(scalars)
        + [spec] * len(inputs)
        + [pl.BlockSpec(memory_space=pl.ANY)] * len(unread),
        out_specs=[pl.BlockSpec(memory_space=out_space)] * len(outs),
        scratch_shapes=scratch,
        compiler_params=pltpu.CompilerParams(vmem_limit_bytes=megabytes * 2**20),
        name=name,
    )(*scalars, *inputs, *unread)
    return result[0] if single else result


def neighbours(first, last, axis):
    count = lax.axis_size(axis)
    up = [(i, i + 1) for i in range(count - 1)]
    down = [(j, i) for i, j in up]
    return lax.ppermute(last, axis, up), lax.ppermute(first, axis, down)


def doubled(table, axis):
    count = lax.axis_size(axis)
    bit = 1
    while bit < count:
        got = lax.ppermute(table, axis, [(i, i ^ bit) for i in range(count)])
        table = jnp.concatenate([table, got], axis=0)
        bit *= 2
    return table


def requests(match, value, capacity):
    rank = jnp.cumsum(match.astype(jnp.int32), axis=1) - 1
    hit = match[:, None, :] & (rank[:, None, :] == jnp.arange(capacity)[None, :, None])
    return jnp.max(jnp.where(hit, value[:, None, :], -1), axis=2)


def shards(cells, instance_cell, target, row_taps, col_taps, kernel_weight):
    deep, cores, cols = lax.axis_size("deep"), lax.axis_size("core"), lax.axis_size("col")
    everyone = ("deep", "core", "col")
    plane = ("core", "col")
    peers = cores * cols
    slots = cells.shape[0]
    tile_rows, tile_cols = instance_cell.shape
    tiles_here = tile_rows * tile_cols
    height, breadth = target.shape
    owners = deep * peers
    capacity = 2 * ((tiles_here + owners - 1) // owners)
    wide_capacity = min(tiles_here, deep * capacity)
    f32 = lambda *shape: jax.ShapeDtypeStruct(shape, F32)

    flat = to_rows(cells)
    copies, named = kernel_call(
        spread_kernel,
        "spread",
        [
            f32(deep * slots * 8, LANES),
            jax.ShapeDtypeStruct((1, tiles_here), jnp.int32),
        ],
        [],
        [],
        [flat, instance_cell],
    )
    stack = lax.all_to_all(copies, "deep", split_axis=0, concat_axis=0, tiled=True)

    near = doubled(doubled(named, "col"), "core")
    me = jnp.stack([lax.axis_index(plane), lax.axis_index(everyone)]).astype(jnp.int32)
    owner = near // slots
    asked = requests(
        owner % peers == me[0], (owner // peers) * slots + near % slots, wide_capacity
    )
    waves = make_waves(row_taps, col_taps)
    packed = kernel_call(
        pack_kernel,
        "pack",
        f32(peers * wide_capacity * 8, LANES),
        [
            pltpu.VMEM((peers * wide_capacity * 8, LANES), F32),
            pltpu.SemaphoreType.DMA((peers,)),
        ],
        [asked, me],
        [stack],
        [waves],
        out_space=pl.ANY,
    )
    packed, near, above, below = lax.optimization_barrier(
        (packed, near, target[:HALF], target[height - HALF :])
    )
    row_axes = ("deep", "core")
    above, below = neighbours(above, below, row_axes)
    arrived = lax.all_to_all(packed, plane, split_axis=0, concat_axis=0, tiled=True)

    everything = doubled(near, "deep")
    wanted = requests(everything // slots == me[1], everything % slots, capacity)
    mine = named[0] // slots
    earlier = jnp.tri(tiles_here, k=-1, dtype=bool)

    def place(group, size):
        same = (group[:, None] == group[None, :]) & earlier
        where = group * size + jnp.sum(same.astype(jnp.int32), axis=1)
        return where.reshape(tile_rows, tile_cols)

    wide = 2 * HALF
    quarter = (height + wide) // 4
    edge = f32(height // 2 + quarter, LANES)
    mask, first, last, left, right = kernel_call(
        assemble_kernel,
        "assemble",
        [f32(height, breadth), f32(wide, breadth), f32(wide, breadth), edge, edge],
        [
            pltpu.VMEM((height * (breadth // LANES), LANES), F32),
            pltpu.VMEM((2, 4, quarter, LANES), F32),
        ],
        [place(mine % peers, wide_capacity)],
        [arrived, target, above, below],
        [wanted],
    )
    before, after = neighbours(left, right, "col")
    top, bottom = neighbours(first, last, row_axes)
    corner = f32(wide, LANES)
    first, last = kernel_call(corners_kernel, "corners", [corner, corner], [], [], [before, after])
    corner_top, corner_bottom = neighbours(first, last, row_axes)
    my_row = lax.axis_index(("deep", "core"))
    my_col = lax.axis_index("col")
    where = jnp.stack(
        [
            my_row * height - HALF,
            my_col * breadth - HALF,
            jnp.int32(deep * cores * height),
            jnp.int32(cols * breadth),
        ]
    ).astype(jnp.int32)
    field_rows = height + 2 * HALF
    returned = kernel_call(
        image_kernel,
        "image",
        f32(owners * capacity * 8, LANES),
        [
            pltpu.VMEM((KERNELS // 2, 2, 2, LANES, LANES), BF16),
            pltpu.VMEM((KERNELS, 2, field_rows, 256), BF16),
            pltpu.VMEM((KERNELS, 2, LANES, 256), BF16),
            pltpu.VMEM((KERNELS, 1024, WIDE), BF16),
            pltpu.VMEM((field_rows, breadth + 128), F32),
            pltpu.VMEM((height + 4 * HALF, breadth + 128), BF16),
            pltpu.VMEM((height + 4 * HALF, breadth + 128), BF16),
            pltpu.VMEM((height + 4 * HALF, breadth), BF16),
            pltpu.VMEM((height + 4 * HALF, breadth), BF16),
            pltpu.VMEM((KERNELS, field_rows, WIDE), F32),
            pltpu.VMEM((KERNELS, height, breadth + 128), BF16),
            pltpu.VMEM((KERNELS, height, breadth + 128), BF16),
            pltpu.VMEM((height * (breadth // LANES), LANES), F32),
        ],
        [place(mine, capacity), where, kernel_weight],
        [mask, top, bottom, before, after, corner_top, corner_bottom]
        + [target, above, below, waves],
        megabytes=36,
    )
    back = lax.all_to_all(returned, everyone, split_axis=0, concat_axis=0, tiled=True)
    stepped = kernel_call(
        step_kernel,
        "step",
        f32(slots * 8, LANES),
        [pltpu.VMEM((slots * 8, LANES), F32)] * 4,
        [wanted, me],
        [flat, back],
    )
    return from_rows(stepped)


def solution(mesh):
    rows, cols = mesh.devices.shape
    finer = Mesh(mesh.devices.reshape(rows // 2, 2, cols), ("deep", "core", "col"))
    row = ("deep", "core")
    placed = (P((*row, "col"), None), P(row, "col"), P(row, "col"), P(), P(), P())
    return jax.shard_map(
        shards, mesh=finer, in_specs=placed, out_specs=P((*row, "col"), None), check_vma=False
    )
```

```python
import jax
import jax.numpy as jnp
from jax import lax
from jax.experimental import pallas as pl
from jax.experimental.pallas import tpu as pltpu
from jax.sharding import Mesh
from jax.sharding import PartitionSpec as P

TILE = 32
TAPS = 65
HALF = 32
KERNELS = 8
LANES = 128
WIDE = 256

STEEPNESS = 4.0
THRESHOLD = 0.3
STEP_RATE = 0.5

F32 = jnp.float32
BF16 = jnp.bfloat16


def split(x):
    high = x.astype(BF16)
    return high, (x - high.astype(F32)).astype(BF16)


def mm(a, b):
    return jnp.dot(a, b, preferred_element_type=F32)


def build_bands(wave_ref, fcol_ref, frow_ref, brow_ref, bcol_ref):
    rows = lax.broadcasted_iota(jnp.int32, (LANES, LANES), 0)
    lanes = lax.broadcasted_iota(jnp.int32, (LANES, LANES), 1)
    zero = jnp.zeros((LANES, LANES), F32)

    def circular(index, start):
        base = jnp.broadcast_to(wave_ref[pl.ds(index, 1), :], (LANES, LANES))
        return pltpu.roll(base, start, 1, stride=1, stride_axis=0)

    def put(ref, kernel, r0, c0, block, height=LANES, breadth=LANES):
        high, low = split(block)
        ref[kernel, 0, r0 : r0 + height, c0 : c0 + breadth] = high[:height, :breadth]
        ref[kernel, 1, r0 : r0 + height, c0 : c0 + breadth] = low[:height, :breadth]

    half = lanes < LANES // 2

    @pl.loop(0, KERNELS)
    def _(k):
        near = circular(k, 0)
        put(frow_ref, k, 0, 0, jnp.where(lanes >= rows, near, zero))
        put(frow_ref, k, 0, LANES, jnp.where(lanes < rows, near, zero))
        put(frow_ref, k, LANES, 0, zero, 64)
        put(frow_ref, k, LANES, LANES, jnp.where(lanes >= rows, near, zero), 64)
        near = circular(2 * KERNELS + k, 0)
        put(brow_ref, k, 0, 0, jnp.where(lanes >= rows, near, zero))
        put(brow_ref, k, 0, LANES, jnp.where(lanes < rows, near, zero))
        near = circular(KERNELS + k, LANES // 2)
        diagonal = jnp.where(rows >= lanes, near, zero)
        beyond = jnp.where(rows < lanes, near, zero)
        for c0, blocks in ((0, (diagonal, beyond, zero)), (LANES, (zero, diagonal, beyond))):
            for n, block in enumerate(blocks):
                height = LANES if n < 2 else LANES // 2
                high, low = split(block)
                for start, piece in ((0, high), (320, high), (640, low)):
                    r0 = start + n * LANES
                    bcol_ref[k, r0 : r0 + height, c0 : c0 + LANES] = piece[:height]
        bcol_ref[k, 960:, :] = jnp.zeros((64, WIDE), BF16)

    @pl.loop(0, KERNELS // 2)
    def _(pair):
        first, second = 3 * KERNELS + 2 * pair, 3 * KERNELS + 2 * pair + 1
        for order, (one, other) in enumerate(((first, second), (second, first))):
            block = jnp.where(half, circular(one, LANES // 2), circular(other, 0))
            high, low = split(block)
            fcol_ref[pair, order, 0] = high
            fcol_ref[pair, order, 1] = low


def make_waves(row_taps, col_taps):
    taps = jnp.concatenate([row_taps, col_taps], axis=0)
    taps = jnp.concatenate([taps, taps[:, ::-1]], axis=0)
    return jnp.pad(taps, [(0, 0), (0, LANES - TAPS)])


def transpose_blocks(parts, block):
    turned = []
    for d in range(4):
        x = parts[d]
        for s in range(1, 4):
            x = jnp.where(block == s, parts[(s + d) % 4], x)
        turned.append(pltpu.roll(x, 32 * d, 1) if d else x)
    out = []
    for s in range(4):
        x = turned[(-s) % 4]
        for b in range(1, 4):
            x = jnp.where(block == b, turned[(b - s) % 4], x)
        out.append(x)
    return out


def spread_kernel(cells_ref, instance_ref, out_ref, named_ref):
    own = cells_ref.shape[0]
    for c in range(own // 8):
        tile = cells_ref[pl.ds((c // 8) * 64 + c % 8, 8, stride=8), :]
        for d in range(out_ref.shape[0] // own):
            out_ref[d * own + c * 8 : d * own + c * 8 + 8, :] = tile
    rows = [instance_ref[a : a + 1, :] for a in range(instance_ref.shape[0])]
    named_ref[...] = jnp.concatenate(rows, axis=1)


def pack_kernel(asked_ref, me_ref, cells_ref, *rest):
    out_ref, stage_ref, sems = rest[-3:]
    peers, capacity = asked_ref.shape
    chunk = capacity * 8

    def send(i):
        rows = pl.ds(pl.multiple_of((me_ref[0] ^ i) * chunk, chunk), chunk)
        return pltpu.make_async_copy(stage_ref.at[rows, :], out_ref.at[rows, :], sems.at[i])

    @pl.loop(0, peers)
    def _(i):
        base = (me_ref[0] ^ i) * capacity
        for j in range(capacity):
            asked = jnp.maximum(asked_ref[i, j], 0)
            tile = cells_ref[pl.ds(pl.multiple_of(asked * 8, 8), 8), :]
            stage_ref[pl.ds(pl.multiple_of((base + j) * 8, 8), 8), :] = tile
        send(i).start()

    @pl.loop(0, peers)
    def _(i):
        send(i).wait()


def step_kernel(asked_ref, me_ref, cells_ref, tiles_ref, out_ref, *totals):
    owners, capacity = asked_ref.shape
    nothing = jnp.zeros((8, LANES), F32)
    for total in totals:
        total[...] = jnp.zeros_like(total)

    @pl.loop(0, owners)
    def _(i):
        base = (me_ref[1] ^ i) * capacity
        for j in range(capacity):
            asked = asked_ref[i, j]
            tile = tiles_ref[pl.ds(pl.multiple_of((base + j) * 8, 8), 8), :]
            there = pl.ds(pl.multiple_of(jnp.maximum(asked, 0) * 8, 8), 8)
            total = totals[j % len(totals)]
            total[there, :] += jnp.where(asked >= 0, tile, nothing)

    for c in range(out_ref.shape[0] // 8):
        rows = slice(c * 8, c * 8 + 8)
        total = totals[0][rows, :]
        for other in totals[1:]:
            total = total + other[rows, :]
        there = pl.ds((c // 8) * 64 + c % 8, 8, stride=8)
        out_ref[there, :] = cells_ref[there, :] - STEP_RATE * total


def target_strips(target_ref, top_ref, bottom_ref, strip):
    height = target_ref.shape[0]
    quarter = (height + 2 * HALF) // 4
    for row in range(0, height + 2 * HALF, 16):
        if row < HALF:
            ref, start = top_ref, row
        elif row < HALF + height:
            ref, start = target_ref, row - HALF
        else:
            ref, start = bottom_ref, row - HALF - height
        strip(row, ref, slice(start, start + 16), row // quarter, row % quarter)


def assemble_kernel(index_ref, spot_ref, tiles_ref, target_ref, ttop_ref, tbottom_ref, *rest):
    mask_ref, rowa_ref, rowb_ref, cola_ref, colb_ref, turned_ref, pack_ref = rest[-7:]
    odd_row, odd_col = spot_ref[6] > 0, spot_ref[7] > 0
    tile_rows, tile_cols = index_ref.shape
    height, breadth = target_ref.shape
    wide = 2 * HALF
    half = height // 2
    groups = tile_cols // 4
    block = lax.broadcasted_iota(jnp.int32, (8, LANES), 1) // 32

    @pl.loop(0, tile_rows)
    def _(a):
        for g in range(groups):
            parts = [
                tiles_ref[pl.ds(pl.multiple_of(index_ref[a, 4 * g + b] * 8, 8), 8), :]
                for b in range(4)
            ]
            for s, piece in enumerate(transpose_blocks(parts, block)):
                turned_ref[pl.ds(g * height + a * TILE + s, 8, stride=4), :] = piece

    lane = lax.broadcasted_iota(jnp.int32, (half, LANES), 1)
    for g in range(groups):
        lanes = slice(LANES * g, LANES * (g + 1))
        piece = turned_ref[g * height : (g + 1) * height, :]
        mask_ref[:, lanes] = piece
        rowa_ref[:, lanes] = jnp.where(odd_row, piece[:wide], piece[height - wide :])
        rowb_ref[:, lanes] = jnp.where(odd_row, piece[height - wide :], piece[:wide])
        upper, lower = piece[:half], piece[half:]
        if g == 0:
            left = jnp.where(lane < wide, upper, pltpu.roll(lower, wide, 1))
        if g == groups - 1:
            right = jnp.where(lane < wide, pltpu.roll(upper, wide, 1), lower)
    cola_ref[:half, :] = jnp.where(odd_col, left, right)
    colb_ref[:half, :] = jnp.where(odd_col, right, left)

    quarter = (height + 2 * HALF) // 4

    def strip(row, ref, rows, part, inner):
        for side, lanes in enumerate((slice(0, LANES), slice(breadth - LANES, breadth))):
            shift = (HALF * (part + side)) % LANES
            piece = ref[rows, lanes]
            pack_ref[side, part, inner : inner + 16, :] = (
                pltpu.roll(piece, shift, 1) if shift else piece
            )

    target_strips(target_ref, ttop_ref, tbottom_ref, strip)
    part_of = lax.broadcasted_iota(jnp.int32, (quarter, LANES), 1) // HALF
    sides = []
    for side in range(2):
        piece = pack_ref[side, 0]
        for part in range(1, 4):
            piece = jnp.where(part_of == part, pack_ref[side, part], piece)
        sides.append(piece)
    cola_ref[half:, :] = jnp.where(odd_col, sides[0], sides[1])
    colb_ref[half:, :] = jnp.where(odd_col, sides[1], sides[0])


def corners_kernel(spot_ref, cola_ref, colb_ref, rowa_ref, rowb_ref):
    odd_row, odd_col = spot_ref[6] > 0, spot_ref[7] > 0
    wide = 2 * HALF
    lane = lax.broadcasted_iota(jnp.int32, (wide, LANES), 1)
    one, other = cola_ref[:wide, :], colb_ref[:wide, :]
    before, after = jnp.where(odd_col, one, other), jnp.where(odd_col, other, one)
    first = jnp.where(lane < wide, before, pltpu.roll(after, wide, 1))
    last = jnp.where(lane < wide, pltpu.roll(before, wide, 1), after)
    rowa_ref[...] = jnp.where(odd_row, first, last)
    rowb_ref[...] = jnp.where(odd_row, last, first)


def image_kernel(
    index_ref,
    spot_ref,
    weight_ref,
    mask_ref,
    rowa_ref,
    rowb_ref,
    cola_ref,
    colb_ref,
    cornera_ref,
    cornerb_ref,
    own_ref,
    ttop_ref,
    tbottom_ref,
    wave_ref,
    out_ref,
    fcol_ref,
    frow_ref,
    brow_ref,
    bcol_ref,
    target_ref,
    mhigh_ref,
    mlow_ref,
    nhigh_ref,
    nlow_ref,
    field_ref,
    ghigh_ref,
    gturn_ref,
    grad_ref,
):
    tile_rows, tile_cols = index_ref.shape
    rows_here = tile_rows * TILE
    high_rows = rows_here + 4 * HALF
    field_rows = rows_here + 2 * HALF
    groups = tile_cols // 4
    wide = 2 * HALF
    block = lax.broadcasted_iota(jnp.int32, (8, LANES), 1) // 32
    odd_row, odd_col = spot_ref[6] > 0, spot_ref[7] > 0
    build_bands(wave_ref, fcol_ref, frow_ref, brow_ref, bcol_ref)

    lane = lax.broadcasted_iota(jnp.int32, (wide, LANES), 1)
    for rows in range(0, high_rows, wide):
        outer = rows == 0 or rows == high_rows - wide
        from_a = odd_row if rows == 0 else jnp.logical_not(odd_row)
        if outer:
            turned = final = jnp.where(from_a, cornera_ref[...], cornerb_ref[...])
        else:
            one, other = cola_ref[:wide, :], colb_ref[:wide, :]
            turned, final = jnp.where(odd_col, one, other), jnp.where(odd_col, other, one)
            if rows == wide:
                final = pltpu.roll(final, wide, 1)
            else:
                turned = pltpu.roll(turned, wide, 1)
        for g in range(groups + 1):
            fresh = final
            if g < groups:
                lanes = slice(LANES * g, LANES * (g + 1))
                if outer:
                    piece = jnp.where(from_a, rowa_ref[:, lanes], rowb_ref[:, lanes])
                else:
                    piece = mask_ref[rows - wide : rows, lanes]
                high, low = split(piece)
                nhigh_ref[rows : rows + wide, LANES * g : LANES * (g + 1)] = high
                nlow_ref[rows : rows + wide, LANES * g : LANES * (g + 1)] = low
                fresh = pltpu.roll(piece, wide, 1)
            high, low = split(jnp.where(lane < wide, turned, fresh))
            mhigh_ref[rows : rows + wide, LANES * g : LANES * (g + 1)] = high
            mlow_ref[rows : rows + wide, LANES * g : LANES * (g + 1)] = low
            turned = fresh
    packed = rows_here // 2
    near_lane = lax.broadcasted_iota(jnp.int32, (16, LANES), 1)

    def strip(row, ref, rows, part, inner):
        edge = slice(packed + inner, packed + inner + 16)
        back, ahead = (-HALF * part) % LANES, (HALF - HALF * part) % LANES
        one, other = cola_ref[edge, :], colb_ref[edge, :]
        turned, final = jnp.where(odd_col, one, other), jnp.where(odd_col, other, one)
        turned = pltpu.roll(turned, back, 1) if back else turned
        final = pltpu.roll(final, ahead, 1) if ahead else final
        for g in range(groups + 1):
            fresh = final
            if g < groups:
                fresh = pltpu.roll(ref[rows, LANES * g : LANES * (g + 1)], HALF, 1)
            target_ref[row : row + 16, LANES * g : LANES * (g + 1)] = jnp.where(
                near_lane < HALF, turned, fresh
            )
            turned = fresh

    target_strips(own_ref, ttop_ref, tbottom_ref, strip)

    def swapped(x):
        pieces = [
            pltpu.roll(x[:, c : c + LANES], LANES // 2, 1) for c in range(0, x.shape[1], LANES)
        ]
        return pieces[0] if len(pieces) == 1 else jnp.concatenate(pieces, axis=1)

    def columns(offset, width):
        blocks = width // LANES
        last = blocks == 1

        def windows(high_ref, low_ref):
            rows = []
            for j in range(blocks):
                place = pl.ds(pl.multiple_of(offset + j * LANES, LANES), LANES)
                high, low = high_ref[:, place], low_ref[:, place]
                rows.append(jnp.concatenate([high, low, high], axis=1))
            return rows[0] if last else jnp.concatenate(rows, axis=0)

        even_rows = windows(mhigh_ref, mlow_ref)
        odd_rows = None if last else windows(nhigh_ref, nlow_ref)
        left = lax.broadcasted_iota(jnp.int32, (high_rows, LANES), 1) < LANES // 2

        def band(quad, order):
            both = [
                jnp.concatenate(
                    [fcol_ref[2 * quad, order, v], fcol_ref[2 * quad + 1, order, v]], axis=1
                )
                for v in range(2)
            ]
            return jnp.concatenate([both[0], both[0], both[1]], axis=0)

        sums = [None, None]
        for quad in range(KERNELS // 4):
            even = mm(even_rows, band(quad, 0))
            odd = even if last else mm(odd_rows, band(quad, 1))
            for h in range(4):
                k = 4 * quad + h
                pieces = []
                for j in range(blocks):
                    rows = slice(j * high_rows, (j + 1) * high_rows)
                    lanes = slice((h // 2) * LANES, (h // 2 + 1) * LANES)
                    if last:
                        pieces.append(even[rows, lanes])
                    elif h % 2 == 0:
                        pieces.append(jnp.where(left, even[rows, lanes], odd[rows, lanes]))
                    else:
                        pieces.append(jnp.where(left, odd[rows, lanes], even[rows, lanes]))
                high, low = split(pieces[0] if last else jnp.concatenate(pieces, axis=1))
                both = mm(jnp.concatenate([frow_ref[k, 0], frow_ref[k, 1]], axis=0), high)
                field = both[:field_rows] + both[field_rows:] + mm(frow_ref[k, 0], low)
                field_ref[k, :, :width] = field
                term = weight_ref[k] * field * field
                sums[h % 2] = term if sums[h % 2] is None else sums[h % 2] + term
        intensity = sums[0] + swapped(sums[1])
        resist = 1.0 / (1.0 + jnp.exp(-STEEPNESS * (intensity - THRESHOLD)))
        place = pl.ds(pl.multiple_of(offset, LANES), width)
        target = target_ref[:, place]
        sensitivity = 2.0 * (resist - target) * STEEPNESS * resist * (1.0 - resist)
        row = spot_ref[2] + lax.broadcasted_iota(jnp.int32, (field_rows, width), 0)
        col = spot_ref[3] + offset + lax.broadcasted_iota(jnp.int32, (field_rows, width), 1)
        inside = (row >= 0) & (row < spot_ref[4]) & (col >= 0) & (col < spot_ref[5])
        sensitivity = jnp.where(inside, sensitivity, 0.0)
        ordered = (sensitivity, swapped(sensitivity))
        for k in range(KERNELS):
            product = (2.0 * weight_ref[k]) * ordered[k % 2] * field_ref[k, :, :width]
            high, low = split(product)
            near = brow_ref[k, 0, :, :field_rows]
            both = mm(jnp.concatenate([near, brow_ref[k, 1, :, :field_rows]], axis=0), high)
            part = both[:rows_here] + both[rows_here:] + mm(near, low)
            straight, turned = (part, swapped(part))[:: 1 - 2 * (k % 2)]
            ghigh_ref[k, :, place] = straight.astype(BF16)
            gturn_ref[k, :, place] = split(turned)[1]

    supers = tile_cols * TILE // WIDE

    @pl.loop(0, supers)
    def _(jj):
        columns(jj * WIDE, WIDE)

    columns(supers * WIDE, LANES)

    lower = lax.broadcasted_iota(jnp.int32, (rows_here, LANES), 1) < LANES // 2

    def spread_back(k):
        stacked = []
        for jj in range(supers):
            c0 = WIDE * jj
            high = [ghigh_ref[k, :, c0 + LANES * n : c0 + LANES * (n + 1)] for n in range(3)]
            turn = [gturn_ref[k, :, c0 + LANES * n : c0 + LANES * (n + 1)] for n in range(3)]
            row = [
                high[0],
                high[1],
                jnp.where(lower, high[2], turn[0]),
                jnp.where(lower, turn[0], turn[1]),
                jnp.where(lower, turn[1], turn[2]),
                *high,
            ]
            stacked.append(jnp.concatenate(row, axis=1))
        return mm(jnp.concatenate(stacked, axis=0), bcol_ref[k])

    def add(part, fresh):
        for g in range(groups):
            rows = slice(g * rows_here, (g + 1) * rows_here)
            top = (g // 2) * rows_here
            piece = part[top : top + rows_here, LANES * (g % 2) : LANES * (g % 2 + 1)]
            grad_ref[rows, :] = piece if fresh else grad_ref[rows, :] + piece

    add(spread_back(0), True)

    @pl.loop(1, KERNELS)
    def _(k):
        add(spread_back(k), False)

    @pl.loop(0, tile_rows)
    def _(a):
        for g in range(groups):
            base = g * rows_here + a * TILE
            parts = [grad_ref[pl.ds(base + s, 8, stride=4), :] for s in range(4)]
            for b, tile in enumerate(transpose_blocks(parts, block)):
                place = pl.multiple_of(index_ref[a, 4 * g + b] * 8, 8)
                out_ref[pl.ds(place, 8), :] = tile


def to_rows(x):
    count = x.shape[0]
    return x.reshape(count // 8, 8, 8, LANES).transpose(0, 2, 1, 3).reshape(count * 8, LANES)


def from_rows(x):
    count = x.shape[0] // 8
    return x.reshape(count // 8, 8, 8, LANES).transpose(0, 2, 1, 3).reshape(count, 8 * LANES)


def kernel_call(body, name, shapes, scratch, scalars, inputs, unread=(), megabytes=8, out_space=pltpu.VMEM):
    single = not isinstance(shapes, list)
    spec = pl.BlockSpec(memory_space=pltpu.VMEM)
    outs = [shapes] if single else shapes
    result = pl.pallas_call(
        body,
        out_shape=outs,
        in_specs=[pl.BlockSpec(memory_space=pltpu.SMEM)] * len(scalars)
        + [spec] * len(inputs)
        + [pl.BlockSpec(memory_space=pl.ANY)] * len(unread),
        out_specs=[pl.BlockSpec(memory_space=out_space)] * len(outs),
        scratch_shapes=scratch,
        compiler_params=pltpu.CompilerParams(vmem_limit_bytes=megabytes * 2**20),
        name=name,
    )(*scalars, *inputs, *unread)
    return result[0] if single else result


def pairs(one, other, axis):
    count = lax.axis_size(axis)
    out = []
    for x, start in ((one, 0), (other, 1)):
        swap = [(i, i + 1) for i in range(start, count - 1, 2)]
        out.append(lax.ppermute(x, axis, swap + [(j, i) for i, j in swap]))
    return out


def doubled(table, axis):
    count = lax.axis_size(axis)
    bit = 1
    while bit < count:
        got = lax.ppermute(table, axis, [(i, i ^ bit) for i in range(count)])
        table = jnp.concatenate([table, got], axis=0)
        bit *= 2
    return table


def requests(match, value, capacity):
    rank = jnp.cumsum(match.astype(jnp.int32), axis=1) - 1
    hit = match[:, None, :] & (rank[:, None, :] == jnp.arange(capacity)[None, :, None])
    return jnp.max(jnp.where(hit, value[:, None, :], -1), axis=2)


def shards(cells, instance_cell, target, row_taps, col_taps, kernel_weight):
    deep, cores, cols = lax.axis_size("deep"), lax.axis_size("core"), lax.axis_size("col")
    everyone = ("deep", "core", "col")
    plane = ("core", "col")
    peers = cores * cols
    slots = cells.shape[0]
    tile_rows, tile_cols = instance_cell.shape
    tiles_here = tile_rows * tile_cols
    height, breadth = target.shape
    owners = deep * peers
    capacity = 2 * ((tiles_here + owners - 1) // owners)
    wide_capacity = min(tiles_here, deep * capacity)
    f32 = lambda *shape: jax.ShapeDtypeStruct(shape, F32)

    flat = to_rows(cells)
    copies, named = kernel_call(
        spread_kernel,
        "spread",
        [
            f32(deep * slots * 8, LANES),
            jax.ShapeDtypeStruct((1, tiles_here), jnp.int32),
        ],
        [],
        [],
        [flat, instance_cell],
    )
    stack = lax.all_to_all(copies, "deep", split_axis=0, concat_axis=0, tiled=True)

    near = doubled(doubled(named, "col"), "core")
    row_axes = ("deep", "core")
    my_row, my_col = lax.axis_index(row_axes), lax.axis_index("col")
    me = jnp.stack(
        [
            lax.axis_index(plane),
            lax.axis_index(everyone),
            my_row * height - HALF,
            my_col * breadth - HALF,
            jnp.int32(deep * cores * height),
            jnp.int32(cols * breadth),
            my_row % 2,
            my_col % 2,
        ]
    ).astype(jnp.int32)
    owner = near // slots
    asked = requests(
        owner % peers == me[0], (owner // peers) * slots + near % slots, wide_capacity
    )
    waves = make_waves(row_taps, col_taps)
    packed = kernel_call(
        pack_kernel,
        "pack",
        f32(peers * wide_capacity * 8, LANES),
        [
            pltpu.VMEM((peers * wide_capacity * 8, LANES), F32),
            pltpu.SemaphoreType.DMA((peers,)),
        ],
        [asked, me],
        [stack],
        [waves],
        out_space=pl.ANY,
    )
    odd = me[6] > 0
    head, foot = target[:HALF], target[height - HALF :]
    packed, near, one, other = lax.optimization_barrier(
        (packed, near, jnp.where(odd, head, foot), jnp.where(odd, foot, head))
    )
    one, other = pairs(one, other, row_axes)
    above, below = jnp.where(odd, one, other), jnp.where(odd, other, one)
    arrived = lax.all_to_all(packed, plane, split_axis=0, concat_axis=0, tiled=True)

    everything = doubled(near, "deep")
    wanted = requests(everything // slots == me[1], everything % slots, capacity)
    mine = named[0] // slots
    earlier = jnp.tri(tiles_here, k=-1, dtype=bool)

    def place(group, size):
        same = (group[:, None] == group[None, :]) & earlier
        where = group * size + jnp.sum(same.astype(jnp.int32), axis=1)
        return where.reshape(tile_rows, tile_cols)

    wide = 2 * HALF
    quarter = (height + wide) // 4
    edge = f32(height // 2 + quarter, LANES)
    mask, rowa, rowb, cola, colb = kernel_call(
        assemble_kernel,
        "assemble",
        [f32(height, breadth), f32(wide, breadth), f32(wide, breadth), edge, edge],
        [
            pltpu.VMEM((height * (breadth // LANES), LANES), F32),
            pltpu.VMEM((2, 4, quarter, LANES), F32),
        ],
        [place(mine % peers, wide_capacity), me],
        [arrived, target, above, below],
        [wanted],
    )
    cola, colb = pairs(cola, colb, "col")
    rowa, rowb = pairs(rowa, rowb, row_axes)
    corner = f32(wide, LANES)
    corners = kernel_call(corners_kernel, "corners", [corner, corner], [], [me], [cola, colb])
    corners = pairs(*corners, row_axes)
    field_rows = height + 2 * HALF
    returned = kernel_call(
        image_kernel,
        "image",
        f32(owners * capacity * 8, LANES),
        [
            pltpu.VMEM((KERNELS // 2, 2, 2, LANES, LANES), BF16),
            pltpu.VMEM((KERNELS, 2, field_rows, 256), BF16),
            pltpu.VMEM((KERNELS, 2, LANES, 256), BF16),
            pltpu.VMEM((KERNELS, 1024, WIDE), BF16),
            pltpu.VMEM((field_rows, breadth + 128), F32),
            pltpu.VMEM((height + 4 * HALF, breadth + 128), BF16),
            pltpu.VMEM((height + 4 * HALF, breadth + 128), BF16),
            pltpu.VMEM((height + 4 * HALF, breadth), BF16),
            pltpu.VMEM((height + 4 * HALF, breadth), BF16),
            pltpu.VMEM((KERNELS, field_rows, WIDE), F32),
            pltpu.VMEM((KERNELS, height, breadth + 128), BF16),
            pltpu.VMEM((KERNELS, height, breadth + 128), BF16),
            pltpu.VMEM((height * (breadth // LANES), LANES), F32),
        ],
        [place(mine, capacity), me, kernel_weight],
        [mask, rowa, rowb, cola, colb, *corners, target, above, below, waves],
        megabytes=36,
    )
    back = lax.all_to_all(returned, everyone, split_axis=0, concat_axis=0, tiled=True)
    stepped = kernel_call(
        step_kernel,
        "step",
        f32(slots * 8, LANES),
        [pltpu.VMEM((slots * 8, LANES), F32)] * 4,
        [wanted, me],
        [flat, back],
    )
    return from_rows(stepped)


def solution(mesh):
    rows, cols = mesh.devices.shape
    finer = Mesh(mesh.devices.reshape(rows // 2, 2, cols), ("deep", "core", "col"))
    row = ("deep", "core")
    placed = (P((*row, "col"), None), P(row, "col"), P(row, "col"), P(), P(), P())
    return jax.shard_map(
        shards, mesh=finer, in_specs=placed, out_specs=P((*row, "col"), None), check_vma=False
    )
```

```python
import jax
import jax.numpy as jnp
from jax import lax
from jax.experimental import pallas as pl
from jax.experimental.pallas import tpu as pltpu
from jax.sharding import Mesh
from jax.sharding import PartitionSpec as P

TILE = 32
TAPS = 65
HALF = 32
KERNELS = 8
LANES = 128
WIDE = 256

STEEPNESS = 4.0
THRESHOLD = 0.3
STEP_RATE = 0.5

F32 = jnp.float32
BF16 = jnp.bfloat16


def split(x):
    high = x.astype(BF16)
    return high, (x - high.astype(F32)).astype(BF16)


def mm(a, b):
    return jnp.dot(a, b, preferred_element_type=F32)


def build_bands(wave_ref, fcol_ref, frow_ref, brow_ref, bcol_ref):
    rows = lax.broadcasted_iota(jnp.int32, (LANES, LANES), 0)
    lanes = lax.broadcasted_iota(jnp.int32, (LANES, LANES), 1)
    zero = jnp.zeros((LANES, LANES), F32)

    def circular(index, start):
        base = jnp.broadcast_to(wave_ref[pl.ds(index, 1), :], (LANES, LANES))
        return pltpu.roll(base, start, 1, stride=1, stride_axis=0)

    def put(ref, kernel, r0, c0, block, height=LANES, breadth=LANES):
        high, low = split(block)
        ref[kernel, 0, r0 : r0 + height, c0 : c0 + breadth] = high[:height, :breadth]
        ref[kernel, 1, r0 : r0 + height, c0 : c0 + breadth] = low[:height, :breadth]

    half = lanes < LANES // 2

    @pl.loop(0, KERNELS)
    def _(k):
        near = circular(k, 0)
        put(frow_ref, k, 0, 0, jnp.where(lanes >= rows, near, zero))
        put(frow_ref, k, 0, LANES, jnp.where(lanes < rows, near, zero))
        put(frow_ref, k, LANES, 0, zero, 64)
        put(frow_ref, k, LANES, LANES, jnp.where(lanes >= rows, near, zero), 64)
        near = circular(2 * KERNELS + k, 0)
        put(brow_ref, k, 0, 0, jnp.where(lanes >= rows, near, zero))
        put(brow_ref, k, 0, LANES, jnp.where(lanes < rows, near, zero))
        near = circular(KERNELS + k, LANES // 2)
        diagonal = jnp.where(rows >= lanes, near, zero)
        beyond = jnp.where(rows < lanes, near, zero)
        for c0, blocks in ((0, (diagonal, beyond, zero)), (LANES, (zero, diagonal, beyond))):
            for n, block in enumerate(blocks):
                height = LANES if n < 2 else LANES // 2
                high, low = split(block)
                for start, piece in ((0, high), (320, high), (640, low)):
                    r0 = start + n * LANES
                    bcol_ref[k, r0 : r0 + height, c0 : c0 + LANES] = piece[:height]
        bcol_ref[k, 960:, :] = jnp.zeros((64, WIDE), BF16)

    @pl.loop(0, KERNELS // 2)
    def _(pair):
        first, second = 3 * KERNELS + 2 * pair, 3 * KERNELS + 2 * pair + 1
        for order, (one, other) in enumerate(((first, second), (second, first))):
            block = jnp.where(half, circular(one, LANES // 2), circular(other, 0))
            high, low = split(block)
            fcol_ref[pair, order, 0] = high
            fcol_ref[pair, order, 1] = low


def make_waves(row_taps, col_taps):
    taps = jnp.concatenate([row_taps, col_taps], axis=0)
    taps = jnp.concatenate([taps, taps[:, ::-1]], axis=0)
    return jnp.pad(taps, [(0, 0), (0, LANES - TAPS)])


def transpose_blocks(parts, block):
    turned = []
    for d in range(4):
        x = parts[d]
        for s in range(1, 4):
            x = jnp.where(block == s, parts[(s + d) % 4], x)
        turned.append(pltpu.roll(x, 32 * d, 1) if d else x)
    out = []
    for s in range(4):
        x = turned[(-s) % 4]
        for b in range(1, 4):
            x = jnp.where(block == b, turned[(b - s) % 4], x)
        out.append(x)
    return out


def spread_kernel(cells_ref, instance_ref, out_ref, named_ref):
    own = cells_ref.shape[0]
    for c in range(own // 8):
        tile = cells_ref[pl.ds((c // 8) * 64 + c % 8, 8, stride=8), :]
        for d in range(out_ref.shape[0] // own):
            out_ref[d * own + c * 8 : d * own + c * 8 + 8, :] = tile
    rows = [instance_ref[a : a + 1, :] for a in range(instance_ref.shape[0])]
    named_ref[...] = jnp.concatenate(rows, axis=1)


def pack_kernel(asked_ref, me_ref, cells_ref, *rest):
    out_ref, stage_ref, sems = rest[-3:]
    peers, capacity = asked_ref.shape
    chunk = capacity * 8

    def send(i):
        rows = pl.ds(pl.multiple_of((me_ref[0] ^ i) * chunk, chunk), chunk)
        return pltpu.make_async_copy(stage_ref.at[rows, :], out_ref.at[rows, :], sems.at[i])

    @pl.loop(0, peers)
    def _(i):
        base = (me_ref[0] ^ i) * capacity
        for j in range(capacity):
            asked = jnp.maximum(asked_ref[i, j], 0)
            tile = cells_ref[pl.ds(pl.multiple_of(asked * 8, 8), 8), :]
            stage_ref[pl.ds(pl.multiple_of((base + j) * 8, 8), 8), :] = tile
        send(i).start()

    @pl.loop(0, peers)
    def _(i):
        send(i).wait()


def step_kernel(asked_ref, me_ref, cells_ref, tiles_ref, out_ref, *totals):
    owners, capacity = asked_ref.shape
    nothing = jnp.zeros((8, LANES), F32)
    for total in totals:
        total[...] = jnp.zeros_like(total)

    @pl.loop(0, owners)
    def _(i):
        base = (me_ref[1] ^ i) * capacity
        for j in range(capacity):
            asked = asked_ref[i, j]
            tile = tiles_ref[pl.ds(pl.multiple_of((base + j) * 8, 8), 8), :]
            there = pl.ds(pl.multiple_of(jnp.maximum(asked, 0) * 8, 8), 8)
            total = totals[j % len(totals)]
            total[there, :] += jnp.where(asked >= 0, tile, nothing)

    for c in range(out_ref.shape[0] // 8):
        rows = slice(c * 8, c * 8 + 8)
        total = totals[0][rows, :]
        for other in totals[1:]:
            total = total + other[rows, :]
        there = pl.ds((c // 8) * 64 + c % 8, 8, stride=8)
        out_ref[there, :] = cells_ref[there, :] - STEP_RATE * total


def target_strips(target_ref, top_ref, bottom_ref, strip):
    height = target_ref.shape[0]
    quarter = (height + 2 * HALF) // 4
    for row in range(0, height + 2 * HALF, 16):
        if row < HALF:
            ref, start = top_ref, row
        elif row < HALF + height:
            ref, start = target_ref, row - HALF
        else:
            ref, start = bottom_ref, row - HALF - height
        strip(row, ref, slice(start, start + 16), row // quarter, row % quarter)


def assemble_kernel(index_ref, spot_ref, tiles_ref, mask_ref, rowa_ref, rowb_ref, turned_ref):
    odd_row = spot_ref[6] > 0
    tile_rows, tile_cols = index_ref.shape
    height = tile_rows * TILE
    wide = 2 * HALF
    groups = tile_cols // 4
    block = lax.broadcasted_iota(jnp.int32, (8, LANES), 1) // 32

    @pl.loop(0, tile_rows)
    def _(a):
        for g in range(groups):
            parts = [
                tiles_ref[pl.ds(pl.multiple_of(index_ref[a, 4 * g + b] * 8, 8), 8), :]
                for b in range(4)
            ]
            for s, piece in enumerate(transpose_blocks(parts, block)):
                turned_ref[pl.ds(g * height + a * TILE + s, 8, stride=4), :] = piece

    for g in range(groups):
        lanes = slice(LANES * g, LANES * (g + 1))
        piece = turned_ref[g * height : (g + 1) * height, :]
        mask_ref[:, lanes] = piece
        rowa_ref[:, lanes] = jnp.where(odd_row, piece[:wide], piece[height - wide :])
        rowb_ref[:, lanes] = jnp.where(odd_row, piece[height - wide :], piece[:wide])


def edges_kernel(spot_ref, mask_ref, rowa_ref, rowb_ref, target_ref, ttop_ref, tbottom_ref, *rest):
    cola_ref, colb_ref, pack_ref = rest[-3:]
    odd_row, odd_col = spot_ref[6] > 0, spot_ref[7] > 0
    height, breadth = mask_ref.shape
    wide = 2 * HALF
    half = height // 2
    packed = half + wide
    lane = lax.broadcasted_iota(jnp.int32, (packed, LANES), 1)
    head, tail = slice(0, LANES), slice(breadth - LANES, breadth)

    def halves(lanes):
        one, other = rowa_ref[:, lanes], rowb_ref[:, lanes]
        top, bottom = jnp.where(odd_row, one, other), jnp.where(odd_row, other, one)
        upper = jnp.concatenate([top, mask_ref[:half, lanes]], axis=0)
        return upper, jnp.concatenate([mask_ref[half:, lanes], bottom], axis=0)

    upper, lower = halves(head)
    left = jnp.where(lane < wide, upper, pltpu.roll(lower, wide, 1))
    upper, lower = halves(tail)
    right = jnp.where(lane < wide, pltpu.roll(upper, wide, 1), lower)
    cola_ref[:packed, :] = jnp.where(odd_col, left, right)
    colb_ref[:packed, :] = jnp.where(odd_col, right, left)

    quarter = (height + 2 * HALF) // 4

    def strip(row, ref, rows, part, inner):
        for side, lanes in enumerate((head, tail)):
            shift = (HALF * (part + side)) % LANES
            piece = ref[rows, lanes]
            pack_ref[side, part, inner : inner + 16, :] = (
                pltpu.roll(piece, shift, 1) if shift else piece
            )

    target_strips(target_ref, ttop_ref, tbottom_ref, strip)
    part_of = lax.broadcasted_iota(jnp.int32, (quarter, LANES), 1) // HALF
    sides = []
    for side in range(2):
        piece = pack_ref[side, 0]
        for part in range(1, 4):
            piece = jnp.where(part_of == part, pack_ref[side, part], piece)
        sides.append(piece)
    cola_ref[packed:, :] = jnp.where(odd_col, sides[0], sides[1])
    colb_ref[packed:, :] = jnp.where(odd_col, sides[1], sides[0])


def image_kernel(
    index_ref,
    spot_ref,
    weight_ref,
    mask_ref,
    rowa_ref,
    rowb_ref,
    cola_ref,
    colb_ref,
    own_ref,
    ttop_ref,
    tbottom_ref,
    wave_ref,
    out_ref,
    fcol_ref,
    frow_ref,
    brow_ref,
    bcol_ref,
    target_ref,
    mhigh_ref,
    mlow_ref,
    nhigh_ref,
    nlow_ref,
    field_ref,
    ghigh_ref,
    gturn_ref,
    grad_ref,
):
    tile_rows, tile_cols = index_ref.shape
    rows_here = tile_rows * TILE
    high_rows = rows_here + 4 * HALF
    field_rows = rows_here + 2 * HALF
    groups = tile_cols // 4
    wide = 2 * HALF
    block = lax.broadcasted_iota(jnp.int32, (8, LANES), 1) // 32
    odd_row, odd_col = spot_ref[6] > 0, spot_ref[7] > 0
    build_bands(wave_ref, fcol_ref, frow_ref, brow_ref, bcol_ref)

    lane = lax.broadcasted_iota(jnp.int32, (wide, LANES), 1)
    for rows in range(0, high_rows, wide):
        outer = rows == 0 or rows == high_rows - wide
        from_a = odd_row if rows == 0 else jnp.logical_not(odd_row)
        half = high_rows // 2
        edge = slice(rows % half, rows % half + wide)
        one, other = cola_ref[edge, :], colb_ref[edge, :]
        turned, final = jnp.where(odd_col, one, other), jnp.where(odd_col, other, one)
        if rows < half:
            final = pltpu.roll(final, wide, 1)
        else:
            turned = pltpu.roll(turned, wide, 1)
        for g in range(groups + 1):
            fresh = final
            if g < groups:
                lanes = slice(LANES * g, LANES * (g + 1))
                if outer:
                    piece = jnp.where(from_a, rowa_ref[:, lanes], rowb_ref[:, lanes])
                else:
                    piece = mask_ref[rows - wide : rows, lanes]
                high, low = split(piece)
                nhigh_ref[rows : rows + wide, LANES * g : LANES * (g + 1)] = high
                nlow_ref[rows : rows + wide, LANES * g : LANES * (g + 1)] = low
                fresh = pltpu.roll(piece, wide, 1)
            high, low = split(jnp.where(lane < wide, turned, fresh))
            mhigh_ref[rows : rows + wide, LANES * g : LANES * (g + 1)] = high
            mlow_ref[rows : rows + wide, LANES * g : LANES * (g + 1)] = low
            turned = fresh
    packed = high_rows // 2
    near_lane = lax.broadcasted_iota(jnp.int32, (16, LANES), 1)

    def strip(row, ref, rows, part, inner):
        edge = slice(packed + inner, packed + inner + 16)
        back, ahead = (-HALF * part) % LANES, (HALF - HALF * part) % LANES
        one, other = cola_ref[edge, :], colb_ref[edge, :]
        turned, final = jnp.where(odd_col, one, other), jnp.where(odd_col, other, one)
        turned = pltpu.roll(turned, back, 1) if back else turned
        final = pltpu.roll(final, ahead, 1) if ahead else final
        for g in range(groups + 1):
            fresh = final
            if g < groups:
                fresh = pltpu.roll(ref[rows, LANES * g : LANES * (g + 1)], HALF, 1)
            target_ref[row : row + 16, LANES * g : LANES * (g + 1)] = jnp.where(
                near_lane < HALF, turned, fresh
            )
            turned = fresh

    target_strips(own_ref, ttop_ref, tbottom_ref, strip)

    def swapped(x):
        pieces = [
            pltpu.roll(x[:, c : c + LANES], LANES // 2, 1) for c in range(0, x.shape[1], LANES)
        ]
        return pieces[0] if len(pieces) == 1 else jnp.concatenate(pieces, axis=1)

    def columns(offset, width):
        blocks = width // LANES
        last = blocks == 1

        def windows(high_ref, low_ref):
            rows = []
            for j in range(blocks):
                place = pl.ds(pl.multiple_of(offset + j * LANES, LANES), LANES)
                high, low = high_ref[:, place], low_ref[:, place]
                rows.append(jnp.concatenate([high, low, high], axis=1))
            return rows[0] if last else jnp.concatenate(rows, axis=0)

        even_rows = windows(mhigh_ref, mlow_ref)
        odd_rows = None if last else windows(nhigh_ref, nlow_ref)
        left = lax.broadcasted_iota(jnp.int32, (high_rows, LANES), 1) < LANES // 2

        def band(quad, order):
            both = [
                jnp.concatenate(
                    [fcol_ref[2 * quad, order, v], fcol_ref[2 * quad + 1, order, v]], axis=1
                )
                for v in range(2)
            ]
            return jnp.concatenate([both[0], both[0], both[1]], axis=0)

        sums = [None, None]
        for quad in range(KERNELS // 4):
            even = mm(even_rows, band(quad, 0))
            odd = even if last else mm(odd_rows, band(quad, 1))
            four = range(4 * quad, 4 * quad + 4)
            if last:
                high, low = split(even)
                both = mm(jnp.concatenate([frow_ref[k, v] for k in four for v in range(2)], 0), high)
                more = mm(jnp.concatenate([frow_ref[k, 0] for k in four], axis=0), low)
            for h, k in enumerate(four):
                lanes = slice((h // 2) * LANES, (h // 2 + 1) * LANES)
                if last:
                    start = 2 * h * field_rows
                    field = both[start : start + field_rows, lanes]
                    field = field + both[start + field_rows : start + 2 * field_rows, lanes]
                    field = field + more[h * field_rows : (h + 1) * field_rows, lanes]
                else:
                    pieces = []
                    for j in range(blocks):
                        rows = slice(j * high_rows, (j + 1) * high_rows)
                        one, other = even[rows, lanes], odd[rows, lanes]
                        one, other = (other, one) if h % 2 else (one, other)
                        pieces.append(jnp.where(left, one, other))
                    high, low = split(jnp.concatenate(pieces, axis=1))
                    both = mm(jnp.concatenate([frow_ref[k, 0], frow_ref[k, 1]], axis=0), high)
                    field = both[:field_rows] + both[field_rows:] + mm(frow_ref[k, 0], low)
                field_ref[k, :, :width] = field
                term = weight_ref[k] * field * field
                sums[h % 2] = term if sums[h % 2] is None else sums[h % 2] + term
        intensity = sums[0] + swapped(sums[1])
        resist = 1.0 / (1.0 + jnp.exp(-STEEPNESS * (intensity - THRESHOLD)))
        place = pl.ds(pl.multiple_of(offset, LANES), width)
        target = target_ref[:, place]
        sensitivity = 2.0 * (resist - target) * STEEPNESS * resist * (1.0 - resist)
        row = spot_ref[2] + lax.broadcasted_iota(jnp.int32, (field_rows, width), 0)
        col = spot_ref[3] + offset + lax.broadcasted_iota(jnp.int32, (field_rows, width), 1)
        inside = (row >= 0) & (row < spot_ref[4]) & (col >= 0) & (col < spot_ref[5])
        sensitivity = jnp.where(inside, sensitivity, 0.0)
        ordered = (sensitivity, swapped(sensitivity))

        def product(k):
            return (2.0 * weight_ref[k]) * ordered[k % 2] * field_ref[k, :, :width]

        def keep(k, part):
            straight, turned = (part, swapped(part))[:: 1 - 2 * (k % 2)]
            ghigh_ref[k, :, place] = straight.astype(BF16)
            gturn_ref[k, :, place] = split(turned)[1]

        if last:
            half = left[:field_rows]
            for quad in range(KERNELS // 4):
                four = range(4 * quad, 4 * quad + 4)
                each = [product(k) for k in four]
                high, low = split(
                    jnp.concatenate(
                        [jnp.where(half, each[0], each[1]), jnp.where(half, each[2], each[3])],
                        axis=1,
                    )
                )
                near = [brow_ref[k, v, :, :field_rows] for k in four for v in range(2)]
                both = mm(jnp.concatenate(near, axis=0), high)
                more = mm(jnp.concatenate(near[::2], axis=0), low)
                for h, k in enumerate(four):
                    lanes = slice((h // 2) * LANES, (h // 2 + 1) * LANES)
                    start = 2 * h * rows_here
                    part = both[start : start + rows_here, lanes]
                    part = part + both[start + rows_here : start + 2 * rows_here, lanes]
                    keep(k, part + more[h * rows_here : (h + 1) * rows_here, lanes])
            return
        for k in range(KERNELS):
            high, low = split(product(k))
            near = brow_ref[k, 0, :, :field_rows]
            both = mm(jnp.concatenate([near, brow_ref[k, 1, :, :field_rows]], axis=0), high)
            keep(k, both[:rows_here] + both[rows_here:] + mm(near, low))

    supers = tile_cols * TILE // WIDE

    @pl.loop(0, supers)
    def _(jj):
        columns(jj * WIDE, WIDE)

    columns(supers * WIDE, LANES)

    lower = lax.broadcasted_iota(jnp.int32, (rows_here, LANES), 1) < LANES // 2

    def spread_back(k):
        stacked = []
        for jj in range(supers):
            c0 = WIDE * jj
            high = [ghigh_ref[k, :, c0 + LANES * n : c0 + LANES * (n + 1)] for n in range(3)]
            turn = [gturn_ref[k, :, c0 + LANES * n : c0 + LANES * (n + 1)] for n in range(3)]
            row = [
                high[0],
                high[1],
                jnp.where(lower, high[2], turn[0]),
                jnp.where(lower, turn[0], turn[1]),
                jnp.where(lower, turn[1], turn[2]),
                *high,
            ]
            stacked.append(jnp.concatenate(row, axis=1))
        return mm(jnp.concatenate(stacked, axis=0), bcol_ref[k])

    def add(part, fresh):
        for g in range(groups):
            rows = slice(g * rows_here, (g + 1) * rows_here)
            top = (g // 2) * rows_here
            piece = part[top : top + rows_here, LANES * (g % 2) : LANES * (g % 2 + 1)]
            grad_ref[rows, :] = piece if fresh else grad_ref[rows, :] + piece

    add(spread_back(0), True)

    @pl.loop(1, KERNELS)
    def _(k):
        add(spread_back(k), False)

    @pl.loop(0, tile_rows)
    def _(a):
        for g in range(groups):
            base = g * rows_here + a * TILE
            parts = [grad_ref[pl.ds(base + s, 8, stride=4), :] for s in range(4)]
            for b, tile in enumerate(transpose_blocks(parts, block)):
                place = pl.multiple_of(index_ref[a, 4 * g + b] * 8, 8)
                out_ref[pl.ds(place, 8), :] = tile


def to_rows(x):
    count = x.shape[0]
    return x.reshape(count // 8, 8, 8, LANES).transpose(0, 2, 1, 3).reshape(count * 8, LANES)


def from_rows(x):
    count = x.shape[0] // 8
    return x.reshape(count // 8, 8, 8, LANES).transpose(0, 2, 1, 3).reshape(count, 8 * LANES)


def kernel_call(body, name, shapes, scratch, scalars, inputs, unread=(), megabytes=8, out_space=pltpu.VMEM):
    single = not isinstance(shapes, list)
    spec = pl.BlockSpec(memory_space=pltpu.VMEM)
    outs = [shapes] if single else shapes
    result = pl.pallas_call(
        body,
        out_shape=outs,
        in_specs=[pl.BlockSpec(memory_space=pltpu.SMEM)] * len(scalars)
        + [spec] * len(inputs)
        + [pl.BlockSpec(memory_space=pl.ANY)] * len(unread),
        out_specs=[pl.BlockSpec(memory_space=out_space)] * len(outs),
        scratch_shapes=scratch,
        compiler_params=pltpu.CompilerParams(vmem_limit_bytes=megabytes * 2**20),
        name=name,
    )(*scalars, *inputs, *unread)
    return result[0] if single else result


def pairs(one, other, axis):
    count = lax.axis_size(axis)
    out = []
    for x, start in ((one, 0), (other, 1)):
        swap = [(i, i + 1) for i in range(start, count - 1, 2)]
        out.append(lax.ppermute(x, axis, swap + [(j, i) for i, j in swap]))
    return out


def doubled(table, axis):
    count = lax.axis_size(axis)
    bit = 1
    while bit < count:
        got = lax.ppermute(table, axis, [(i, i ^ bit) for i in range(count)])
        table = jnp.concatenate([table, got], axis=0)
        bit *= 2
    return table


def requests(match, value, capacity):
    rank = jnp.cumsum(match.astype(jnp.int32), axis=1) - 1
    hit = match[:, None, :] & (rank[:, None, :] == jnp.arange(capacity)[None, :, None])
    return jnp.max(jnp.where(hit, value[:, None, :], -1), axis=2)


def shards(cells, instance_cell, target, row_taps, col_taps, kernel_weight):
    deep, cores, cols = lax.axis_size("deep"), lax.axis_size("core"), lax.axis_size("col")
    everyone = ("deep", "core", "col")
    plane = ("core", "col")
    peers = cores * cols
    slots = cells.shape[0]
    tile_rows, tile_cols = instance_cell.shape
    tiles_here = tile_rows * tile_cols
    height, breadth = target.shape
    owners = deep * peers
    capacity = 2 * ((tiles_here + owners - 1) // owners)
    wide_capacity = min(tiles_here, deep * capacity)
    f32 = lambda *shape: jax.ShapeDtypeStruct(shape, F32)

    flat = to_rows(cells)
    copies, named = kernel_call(
        spread_kernel,
        "spread",
        [
            f32(deep * slots * 8, LANES),
            jax.ShapeDtypeStruct((1, tiles_here), jnp.int32),
        ],
        [],
        [],
        [flat, instance_cell],
    )
    stack = lax.all_to_all(copies, "deep", split_axis=0, concat_axis=0, tiled=True)

    near = doubled(doubled(named, "col"), "core")
    row_axes = ("deep", "core")
    my_row, my_col = lax.axis_index(row_axes), lax.axis_index("col")
    me = jnp.stack(
        [
            lax.axis_index(plane),
            lax.axis_index(everyone),
            my_row * height - HALF,
            my_col * breadth - HALF,
            jnp.int32(deep * cores * height),
            jnp.int32(cols * breadth),
            my_row % 2,
            my_col % 2,
        ]
    ).astype(jnp.int32)
    owner = near // slots
    asked = requests(
        owner % peers == me[0], (owner // peers) * slots + near % slots, wide_capacity
    )
    waves = make_waves(row_taps, col_taps)
    packed = kernel_call(
        pack_kernel,
        "pack",
        f32(peers * wide_capacity * 8, LANES),
        [
            pltpu.VMEM((peers * wide_capacity * 8, LANES), F32),
            pltpu.SemaphoreType.DMA((peers,)),
        ],
        [asked, me],
        [stack],
        [waves],
        out_space=pl.ANY,
    )
    odd = me[6] > 0
    head, foot = target[:HALF], target[height - HALF :]
    packed, near, one, other = lax.optimization_barrier(
        (packed, near, jnp.where(odd, head, foot), jnp.where(odd, foot, head))
    )
    one, other = pairs(one, other, row_axes)
    above, below = jnp.where(odd, one, other), jnp.where(odd, other, one)
    arrived = lax.all_to_all(packed, plane, split_axis=0, concat_axis=0, tiled=True)

    everything = doubled(near, "deep")
    wanted = requests(everything // slots == me[1], everything % slots, capacity)
    mine = named[0] // slots
    earlier = jnp.tri(tiles_here, k=-1, dtype=bool)

    def place(group, size):
        same = (group[:, None] == group[None, :]) & earlier
        where = group * size + jnp.sum(same.astype(jnp.int32), axis=1)
        return where.reshape(tile_rows, tile_cols)

    wide = 2 * HALF
    quarter = (height + wide) // 4
    edge = f32(height // 2 + wide + quarter, LANES)
    mask, rowa, rowb = kernel_call(
        assemble_kernel,
        "assemble",
        [f32(height, breadth), f32(wide, breadth), f32(wide, breadth)],
        [pltpu.VMEM((height * (breadth // LANES), LANES), F32)],
        [place(mine % peers, wide_capacity), me],
        [arrived],
    )
    rowa, rowb = pairs(rowa, rowb, row_axes)
    cola, colb = kernel_call(
        edges_kernel,
        "edges",
        [edge, edge],
        [pltpu.VMEM((2, 4, quarter, LANES), F32)],
        [me],
        [mask, rowa, rowb, target, above, below],
        [wanted],
    )
    cola, colb = pairs(cola, colb, "col")
    field_rows = height + 2 * HALF
    returned = kernel_call(
        image_kernel,
        "image",
        f32(owners * capacity * 8, LANES),
        [
            pltpu.VMEM((KERNELS // 2, 2, 2, LANES, LANES), BF16),
            pltpu.VMEM((KERNELS, 2, field_rows, 256), BF16),
            pltpu.VMEM((KERNELS, 2, LANES, 256), BF16),
            pltpu.VMEM((KERNELS, 1024, WIDE), BF16),
            pltpu.VMEM((field_rows, breadth + 128), F32),
            pltpu.VMEM((height + 4 * HALF, breadth + 128), BF16),
            pltpu.VMEM((height + 4 * HALF, breadth + 128), BF16),
            pltpu.VMEM((height + 4 * HALF, breadth), BF16),
            pltpu.VMEM((height + 4 * HALF, breadth), BF16),
            pltpu.VMEM((KERNELS, field_rows, WIDE), F32),
            pltpu.VMEM((KERNELS, height, breadth + 128), BF16),
            pltpu.VMEM((KERNELS, height, breadth + 128), BF16),
            pltpu.VMEM((height * (breadth // LANES), LANES), F32),
        ],
        [place(mine, capacity), me, kernel_weight],
        [mask, rowa, rowb, cola, colb, target, above, below, waves],
        megabytes=36,
    )
    back = lax.all_to_all(returned, everyone, split_axis=0, concat_axis=0, tiled=True)
    stepped = kernel_call(
        step_kernel,
        "step",
        f32(slots * 8, LANES),
        [pltpu.VMEM((slots * 8, LANES), F32)] * 4,
        [wanted, me],
        [flat, back],
    )
    return from_rows(stepped)


def solution(mesh):
    rows, cols = mesh.devices.shape
    finer = Mesh(mesh.devices.reshape(rows // 2, 2, cols), ("deep", "core", "col"))
    row = ("deep", "core")
    placed = (P((*row, "col"), None), P(row, "col"), P(row, "col"), P(), P(), P())
    return jax.shard_map(
        shards, mesh=finer, in_specs=placed, out_specs=P((*row, "col"), None), check_vma=False
    )
```

```python
import jax
import jax.numpy as jnp
from jax import lax
from jax.experimental import pallas as pl
from jax.experimental.pallas import tpu as pltpu
from jax.sharding import Mesh
from jax.sharding import PartitionSpec as P

TILE = 32
TAPS = 65
HALF = 32
KERNELS = 8
LANES = 128
WIDE = 256

STEEPNESS = 4.0
THRESHOLD = 0.3
STEP_RATE = 0.5

F32 = jnp.float32
BF16 = jnp.bfloat16


def split(x):
    high = x.astype(BF16)
    return high, (x - high.astype(F32)).astype(BF16)


def mm(a, b):
    return jnp.dot(a, b, preferred_element_type=F32)


def build_bands(wave_ref, fcol_ref, frow_ref, brow_ref, bcol_ref):
    rows = lax.broadcasted_iota(jnp.int32, (LANES, LANES), 0)
    lanes = lax.broadcasted_iota(jnp.int32, (LANES, LANES), 1)
    zero = jnp.zeros((LANES, LANES), F32)

    def circular(index, start):
        base = jnp.broadcast_to(wave_ref[pl.ds(index, 1), :], (LANES, LANES))
        return pltpu.roll(base, start, 1, stride=1, stride_axis=0)

    def put(ref, kernel, r0, c0, block, height=LANES, breadth=LANES):
        high, low = split(block)
        ref[kernel, 0, r0 : r0 + height, c0 : c0 + breadth] = high[:height, :breadth]
        ref[kernel, 1, r0 : r0 + height, c0 : c0 + breadth] = low[:height, :breadth]

    half = lanes < LANES // 2

    @pl.loop(0, KERNELS)
    def _(k):
        near = circular(k, 0)
        put(frow_ref, k, 0, 0, jnp.where(lanes >= rows, near, zero))
        put(frow_ref, k, 0, LANES, jnp.where(lanes < rows, near, zero))
        put(frow_ref, k, LANES, 0, zero, 64)
        put(frow_ref, k, LANES, LANES, jnp.where(lanes >= rows, near, zero), 64)
        near = circular(2 * KERNELS + k, 0)
        put(brow_ref, k, 0, 0, jnp.where(lanes >= rows, near, zero))
        put(brow_ref, k, 0, LANES, jnp.where(lanes < rows, near, zero))
        near = circular(KERNELS + k, LANES // 2)
        diagonal = jnp.where(rows >= lanes, near, zero)
        beyond = jnp.where(rows < lanes, near, zero)
        for c0, blocks in ((0, (diagonal, beyond, zero)), (LANES, (zero, diagonal, beyond))):
            for n, block in enumerate(blocks):
                height = LANES if n < 2 else LANES // 2
                high, low = split(block)
                for start, piece in ((0, high), (320, high), (640, low)):
                    r0 = start + n * LANES
                    bcol_ref[k, r0 : r0 + height, c0 : c0 + LANES] = piece[:height]
        bcol_ref[k, 960:, :] = jnp.zeros((64, WIDE), BF16)

    @pl.loop(0, KERNELS // 2)
    def _(pair):
        first, second = 3 * KERNELS + 2 * pair, 3 * KERNELS + 2 * pair + 1
        for order, (one, other) in enumerate(((first, second), (second, first))):
            block = jnp.where(half, circular(one, LANES // 2), circular(other, 0))
            high, low = split(block)
            fcol_ref[pair, order, 0] = high
            fcol_ref[pair, order, 1] = low


def make_waves(row_taps, col_taps):
    taps = jnp.concatenate([row_taps, col_taps], axis=0)
    taps = jnp.concatenate([taps, taps[:, ::-1]], axis=0)
    return jnp.pad(taps, [(0, 0), (0, LANES - TAPS)])


def transpose_blocks(parts, block):
    turned = []
    for d in range(4):
        x = parts[d]
        for s in range(1, 4):
            x = jnp.where(block == s, parts[(s + d) % 4], x)
        turned.append(pltpu.roll(x, 32 * d, 1) if d else x)
    out = []
    for s in range(4):
        x = turned[(-s) % 4]
        for b in range(1, 4):
            x = jnp.where(block == b, turned[(b - s) % 4], x)
        out.append(x)
    return out


def spread_kernel(cells_ref, instance_ref, out_ref, named_ref):
    own = cells_ref.shape[0]
    for c in range(own // 8):
        tile = cells_ref[pl.ds((c // 8) * 64 + c % 8, 8, stride=8), :]
        for d in range(out_ref.shape[0] // own):
            out_ref[d * own + c * 8 : d * own + c * 8 + 8, :] = tile
    rows = [instance_ref[a : a + 1, :] for a in range(instance_ref.shape[0])]
    named_ref[...] = jnp.concatenate(rows, axis=1)


def pack_kernel(asked_ref, me_ref, cells_ref, *rest):
    out_ref, stage_ref, sems = rest[-3:]
    peers, capacity = asked_ref.shape
    chunk = capacity * 8

    def send(i):
        rows = pl.ds(pl.multiple_of((me_ref[0] ^ i) * chunk, chunk), chunk)
        return pltpu.make_async_copy(stage_ref.at[rows, :], out_ref.at[rows, :], sems.at[i])

    @pl.loop(0, peers)
    def _(i):
        base = (me_ref[0] ^ i) * capacity
        for j in range(capacity):
            asked = jnp.maximum(asked_ref[i, j], 0)
            tile = cells_ref[pl.ds(pl.multiple_of(asked * 8, 8), 8), :]
            stage_ref[pl.ds(pl.multiple_of((base + j) * 8, 8), 8), :] = tile
        send(i).start()

    @pl.loop(0, peers)
    def _(i):
        send(i).wait()


def step_kernel(asked_ref, me_ref, cells_ref, tiles_ref, out_ref, *totals):
    owners, capacity = asked_ref.shape
    nothing = jnp.zeros((8, LANES), F32)
    for total in totals:
        total[...] = jnp.zeros_like(total)

    @pl.loop(0, owners)
    def _(i):
        base = (me_ref[1] ^ i) * capacity
        for j in range(capacity):
            asked = asked_ref[i, j]
            tile = tiles_ref[pl.ds(pl.multiple_of((base + j) * 8, 8), 8), :]
            there = pl.ds(pl.multiple_of(jnp.maximum(asked, 0) * 8, 8), 8)
            total = totals[j % len(totals)]
            total[there, :] += jnp.where(asked >= 0, tile, nothing)

    for c in range(out_ref.shape[0] // 8):
        rows = slice(c * 8, c * 8 + 8)
        total = totals[0][rows, :]
        for other in totals[1:]:
            total = total + other[rows, :]
        there = pl.ds((c // 8) * 64 + c % 8, 8, stride=8)
        out_ref[there, :] = cells_ref[there, :] - STEP_RATE * total


def target_strips(target_ref, top_ref, bottom_ref, strip):
    height = target_ref.shape[0]
    quarter = (height + 2 * HALF) // 4
    for row in range(0, height + 2 * HALF, 16):
        if row < HALF:
            ref, start = top_ref, row
        elif row < HALF + height:
            ref, start = target_ref, row - HALF
        else:
            ref, start = bottom_ref, row - HALF - height
        strip(row, ref, slice(start, start + 16), row // quarter, row % quarter)


def assemble_kernel(index_ref, spot_ref, tiles_ref, mask_ref, rowa_ref, rowb_ref, turned_ref):
    odd_row = spot_ref[6] > 0
    tile_rows, tile_cols = index_ref.shape
    height = tile_rows * TILE
    wide = 2 * HALF
    groups = tile_cols // 4
    block = lax.broadcasted_iota(jnp.int32, (8, LANES), 1) // 32

    @pl.loop(0, tile_rows)
    def _(a):
        for g in range(groups):
            parts = [
                tiles_ref[pl.ds(pl.multiple_of(index_ref[a, 4 * g + b] * 8, 8), 8), :]
                for b in range(4)
            ]
            for s, piece in enumerate(transpose_blocks(parts, block)):
                turned_ref[pl.ds(g * height + a * TILE + s, 8, stride=4), :] = piece

    for g in range(groups):
        lanes = slice(LANES * g, LANES * (g + 1))
        piece = turned_ref[g * height : (g + 1) * height, :]
        mask_ref[:, lanes] = piece
        rowa_ref[:, lanes] = jnp.where(odd_row, piece[:wide], piece[height - wide :])
        rowb_ref[:, lanes] = jnp.where(odd_row, piece[height - wide :], piece[:wide])


def edges_kernel(spot_ref, mask_ref, rowa_ref, rowb_ref, target_ref, ttop_ref, tbottom_ref, *rest):
    cola_ref, colb_ref, pack_ref = rest[-3:]
    odd_row, odd_col = spot_ref[6] > 0, spot_ref[7] > 0
    height, breadth = mask_ref.shape
    wide = 2 * HALF
    half = height // 2
    packed = half + wide
    lane = lax.broadcasted_iota(jnp.int32, (packed, LANES), 1)
    head, tail = slice(0, LANES), slice(breadth - LANES, breadth)

    def halves(lanes):
        one, other = rowa_ref[:, lanes], rowb_ref[:, lanes]
        top, bottom = jnp.where(odd_row, one, other), jnp.where(odd_row, other, one)
        upper = jnp.concatenate([top, mask_ref[:half, lanes]], axis=0)
        return upper, jnp.concatenate([mask_ref[half:, lanes], bottom], axis=0)

    upper, lower = halves(head)
    left = jnp.where(lane < wide, upper, pltpu.roll(lower, wide, 1))
    upper, lower = halves(tail)
    right = jnp.where(lane < wide, pltpu.roll(upper, wide, 1), lower)
    cola_ref[:packed, :] = jnp.where(odd_col, left, right)
    colb_ref[:packed, :] = jnp.where(odd_col, right, left)

    quarter = (height + 2 * HALF) // 4

    def strip(row, ref, rows, part, inner):
        for side, lanes in enumerate((head, tail)):
            shift = (HALF * (part + side)) % LANES
            piece = ref[rows, lanes]
            pack_ref[side, part, inner : inner + 16, :] = (
                pltpu.roll(piece, shift, 1) if shift else piece
            )

    target_strips(target_ref, ttop_ref, tbottom_ref, strip)
    part_of = lax.broadcasted_iota(jnp.int32, (quarter, LANES), 1) // HALF
    sides = []
    for side in range(2):
        piece = pack_ref[side, 0]
        for part in range(1, 4):
            piece = jnp.where(part_of == part, pack_ref[side, part], piece)
        sides.append(piece)
    cola_ref[packed:, :] = jnp.where(odd_col, sides[0], sides[1])
    colb_ref[packed:, :] = jnp.where(odd_col, sides[1], sides[0])


def image_kernel(
    index_ref,
    spot_ref,
    weight_ref,
    mask_ref,
    rowa_ref,
    rowb_ref,
    cola_ref,
    colb_ref,
    own_ref,
    ttop_ref,
    tbottom_ref,
    wave_ref,
    out_ref,
    fcol_ref,
    frow_ref,
    brow_ref,
    bcol_ref,
    target_ref,
    mhigh_ref,
    mlow_ref,
    nhigh_ref,
    nlow_ref,
    field_ref,
    ghigh_ref,
    gturn_ref,
    grad_ref,
):
    tile_rows, tile_cols = index_ref.shape
    rows_here = tile_rows * TILE
    high_rows = rows_here + 4 * HALF
    field_rows = rows_here + 2 * HALF
    groups = tile_cols // 4
    wide = 2 * HALF
    block = lax.broadcasted_iota(jnp.int32, (8, LANES), 1) // 32
    odd_row, odd_col = spot_ref[6] > 0, spot_ref[7] > 0
    build_bands(wave_ref, fcol_ref, frow_ref, brow_ref, bcol_ref)

    lane = lax.broadcasted_iota(jnp.int32, (wide, LANES), 1)
    for rows in range(0, high_rows, wide):
        outer = rows == 0 or rows == high_rows - wide
        from_a = odd_row if rows == 0 else jnp.logical_not(odd_row)
        half = high_rows // 2
        edge = slice(rows % half, rows % half + wide)
        one, other = cola_ref[edge, :], colb_ref[edge, :]
        turned, final = jnp.where(odd_col, one, other), jnp.where(odd_col, other, one)
        if rows < half:
            final = pltpu.roll(final, wide, 1)
        else:
            turned = pltpu.roll(turned, wide, 1)
        for g in range(groups + 1):
            fresh = final
            if g < groups:
                lanes = slice(LANES * g, LANES * (g + 1))
                if outer:
                    piece = jnp.where(from_a, rowa_ref[:, lanes], rowb_ref[:, lanes])
                else:
                    piece = mask_ref[rows - wide : rows, lanes]
                high, low = split(piece)
                nhigh_ref[rows : rows + wide, LANES * g : LANES * (g + 1)] = high
                nlow_ref[rows : rows + wide, LANES * g : LANES * (g + 1)] = low
                fresh = pltpu.roll(piece, wide, 1)
            high, low = split(jnp.where(lane < wide, turned, fresh))
            mhigh_ref[rows : rows + wide, LANES * g : LANES * (g + 1)] = high
            mlow_ref[rows : rows + wide, LANES * g : LANES * (g + 1)] = low
            turned = fresh
    packed = high_rows // 2
    near_lane = lax.broadcasted_iota(jnp.int32, (16, LANES), 1)

    def strip(row, ref, rows, part, inner):
        edge = slice(packed + inner, packed + inner + 16)
        back, ahead = (-HALF * part) % LANES, (HALF - HALF * part) % LANES
        one, other = cola_ref[edge, :], colb_ref[edge, :]
        turned, final = jnp.where(odd_col, one, other), jnp.where(odd_col, other, one)
        turned = pltpu.roll(turned, back, 1) if back else turned
        final = pltpu.roll(final, ahead, 1) if ahead else final
        for g in range(groups + 1):
            fresh = final
            if g < groups:
                fresh = pltpu.roll(ref[rows, LANES * g : LANES * (g + 1)], HALF, 1)
            target_ref[row : row + 16, LANES * g : LANES * (g + 1)] = jnp.where(
                near_lane < HALF, turned, fresh
            )
            turned = fresh

    target_strips(own_ref, ttop_ref, tbottom_ref, strip)

    def swapped(x):
        pieces = [
            pltpu.roll(x[:, c : c + LANES], LANES // 2, 1) for c in range(0, x.shape[1], LANES)
        ]
        return pieces[0] if len(pieces) == 1 else jnp.concatenate(pieces, axis=1)

    def columns(offset, width, turn):
        blocks = width // LANES
        last = blocks == 1

        def windows(high_ref, low_ref):
            rows = []
            for j in range(blocks):
                place = slice(offset + j * LANES, offset + (j + 1) * LANES)
                high, low = high_ref[:, place], low_ref[:, place]
                rows.append(jnp.concatenate([high, low, high], axis=1))
            return rows[0] if last else jnp.concatenate(rows, axis=0)

        even_rows = windows(mhigh_ref, mlow_ref)
        odd_rows = None if last else windows(nhigh_ref, nlow_ref)
        left = lax.broadcasted_iota(jnp.int32, (high_rows, LANES), 1) < LANES // 2

        def band(quad, order):
            both = [
                jnp.concatenate(
                    [fcol_ref[2 * quad, order, v], fcol_ref[2 * quad + 1, order, v]], axis=1
                )
                for v in range(2)
            ]
            return jnp.concatenate([both[0], both[0], both[1]], axis=0)

        sums = [None, None]
        for quad in range(KERNELS // 4):
            even = mm(even_rows, band(quad, 0))
            odd = even if last else mm(odd_rows, band(quad, 1))
            four = range(4 * quad, 4 * quad + 4)
            if last:
                high, low = split(even)
                both = mm(jnp.concatenate([frow_ref[k, v] for k in four for v in range(2)], 0), high)
                more = mm(jnp.concatenate([frow_ref[k, 0] for k in four], axis=0), low)
            for h, k in enumerate(four):
                lanes = slice((h // 2) * LANES, (h // 2 + 1) * LANES)
                if last:
                    start = 2 * h * field_rows
                    field = both[start : start + field_rows, lanes]
                    field = field + both[start + field_rows : start + 2 * field_rows, lanes]
                    field = field + more[h * field_rows : (h + 1) * field_rows, lanes]
                else:
                    pieces = []
                    for j in range(blocks):
                        rows = slice(j * high_rows, (j + 1) * high_rows)
                        one, other = even[rows, lanes], odd[rows, lanes]
                        one, other = (other, one) if h % 2 else (one, other)
                        pieces.append(jnp.where(left, one, other))
                    high, low = split(jnp.concatenate(pieces, axis=1))
                    both = mm(jnp.concatenate([frow_ref[k, 0], frow_ref[k, 1]], axis=0), high)
                    field = both[:field_rows] + both[field_rows:] + mm(frow_ref[k, 0], low)
                field_ref[turn, k, :, :width] = field
                term = weight_ref[k] * field * field
                sums[h % 2] = term if sums[h % 2] is None else sums[h % 2] + term
        intensity = sums[0] + swapped(sums[1])
        resist = 1.0 / (1.0 + jnp.exp(-STEEPNESS * (intensity - THRESHOLD)))
        place = slice(offset, offset + width)
        target = target_ref[:, place]
        sensitivity = 2.0 * (resist - target) * STEEPNESS * resist * (1.0 - resist)
        row = spot_ref[2] + lax.broadcasted_iota(jnp.int32, (field_rows, width), 0)
        col = spot_ref[3] + offset + lax.broadcasted_iota(jnp.int32, (field_rows, width), 1)
        inside = (row >= 0) & (row < spot_ref[4]) & (col >= 0) & (col < spot_ref[5])
        sensitivity = jnp.where(inside, sensitivity, 0.0)
        ordered = (sensitivity, swapped(sensitivity))

        def product(k):
            return (2.0 * weight_ref[k]) * ordered[k % 2] * field_ref[turn, k, :, :width]

        def keep(k, part):
            straight, turned = (part, swapped(part))[:: 1 - 2 * (k % 2)]
            ghigh_ref[k, :, place] = straight.astype(BF16)
            gturn_ref[k, :, place] = split(turned)[1]

        if last:
            half = left[:field_rows]
            for quad in range(KERNELS // 4):
                four = range(4 * quad, 4 * quad + 4)
                each = [product(k) for k in four]
                high, low = split(
                    jnp.concatenate(
                        [jnp.where(half, each[0], each[1]), jnp.where(half, each[2], each[3])],
                        axis=1,
                    )
                )
                near = [brow_ref[k, v, :, :field_rows] for k in four for v in range(2)]
                both = mm(jnp.concatenate(near, axis=0), high)
                more = mm(jnp.concatenate(near[::2], axis=0), low)
                for h, k in enumerate(four):
                    lanes = slice((h // 2) * LANES, (h // 2 + 1) * LANES)
                    start = 2 * h * rows_here
                    part = both[start : start + rows_here, lanes]
                    part = part + both[start + rows_here : start + 2 * rows_here, lanes]
                    keep(k, part + more[h * rows_here : (h + 1) * rows_here, lanes])
            return
        for k in range(KERNELS):
            high, low = split(product(k))
            near = brow_ref[k, 0, :, :field_rows]
            both = mm(jnp.concatenate([near, brow_ref[k, 1, :, :field_rows]], axis=0), high)
            keep(k, both[:rows_here] + both[rows_here:] + mm(near, low))

    supers = tile_cols * TILE // WIDE

    for jj in range(supers):
        columns(jj * WIDE, WIDE, jj % 2)
    columns(supers * WIDE, LANES, supers % 2)

    lower = lax.broadcasted_iota(jnp.int32, (rows_here, LANES), 1) < LANES // 2

    def windows_of(k, c0):
        high = [ghigh_ref[k, :, c0 + LANES * n : c0 + LANES * (n + 1)] for n in range(3)]
        turn = [gturn_ref[k, :, c0 + LANES * n : c0 + LANES * (n + 1)] for n in range(3)]
        return [
            high[0],
            high[1],
            jnp.where(lower, high[2], turn[0]),
            jnp.where(lower, turn[0], turn[1]),
            jnp.where(lower, turn[1], turn[2]),
            *high,
        ]

    together = KERNELS // 2
    for half in range(2):
        ks = range(half * together, (half + 1) * together)
        stacked = [
            jnp.concatenate([x for k in ks for x in windows_of(k, WIDE * jj)], axis=1)
            for jj in range(supers)
        ]
        band = jnp.concatenate([bcol_ref[k] for k in ks], axis=0)
        part = mm(jnp.concatenate(stacked, axis=0), band)
        for g in range(groups):
            rows = slice(g * rows_here, (g + 1) * rows_here)
            top = (g // 2) * rows_here
            piece = part[top : top + rows_here, LANES * (g % 2) : LANES * (g % 2 + 1)]
            grad_ref[rows, :] = piece if half == 0 else grad_ref[rows, :] + piece

    @pl.loop(0, tile_rows)
    def _(a):
        for g in range(groups):
            base = g * rows_here + a * TILE
            parts = [grad_ref[pl.ds(base + s, 8, stride=4), :] for s in range(4)]
            for b, tile in enumerate(transpose_blocks(parts, block)):
                place = pl.multiple_of(index_ref[a, 4 * g + b] * 8, 8)
                out_ref[pl.ds(place, 8), :] = tile


def to_rows(x):
    count = x.shape[0]
    return x.reshape(count // 8, 8, 8, LANES).transpose(0, 2, 1, 3).reshape(count * 8, LANES)


def from_rows(x):
    count = x.shape[0] // 8
    return x.reshape(count // 8, 8, 8, LANES).transpose(0, 2, 1, 3).reshape(count, 8 * LANES)


def kernel_call(body, name, shapes, scratch, scalars, inputs, unread=(), megabytes=8, out_space=pltpu.VMEM):
    single = not isinstance(shapes, list)
    spec = pl.BlockSpec(memory_space=pltpu.VMEM)
    outs = [shapes] if single else shapes
    result = pl.pallas_call(
        body,
        out_shape=outs,
        in_specs=[pl.BlockSpec(memory_space=pltpu.SMEM)] * len(scalars)
        + [spec] * len(inputs)
        + [pl.BlockSpec(memory_space=pl.ANY)] * len(unread),
        out_specs=[pl.BlockSpec(memory_space=out_space)] * len(outs),
        scratch_shapes=scratch,
        compiler_params=pltpu.CompilerParams(vmem_limit_bytes=megabytes * 2**20),
        name=name,
    )(*scalars, *inputs, *unread)
    return result[0] if single else result


def pairs(one, other, axis):
    count = lax.axis_size(axis)
    out = []
    for x, start in ((one, 0), (other, 1)):
        swap = [(i, i + 1) for i in range(start, count - 1, 2)]
        out.append(lax.ppermute(x, axis, swap + [(j, i) for i, j in swap]))
    return out


def doubled(table, axis):
    count = lax.axis_size(axis)
    bit = 1
    while bit < count:
        got = lax.ppermute(table, axis, [(i, i ^ bit) for i in range(count)])
        table = jnp.concatenate([table, got], axis=0)
        bit *= 2
    return table


def requests(match, value, capacity):
    rank = jnp.cumsum(match.astype(jnp.int32), axis=1) - 1
    hit = match[:, None, :] & (rank[:, None, :] == jnp.arange(capacity)[None, :, None])
    return jnp.max(jnp.where(hit, value[:, None, :], -1), axis=2)


def shards(cells, instance_cell, target, row_taps, col_taps, kernel_weight):
    deep, cores, cols = lax.axis_size("deep"), lax.axis_size("core"), lax.axis_size("col")
    everyone = ("deep", "core", "col")
    plane = ("core", "col")
    peers = cores * cols
    slots = cells.shape[0]
    tile_rows, tile_cols = instance_cell.shape
    tiles_here = tile_rows * tile_cols
    height, breadth = target.shape
    owners = deep * peers
    capacity = 2 * ((tiles_here + owners - 1) // owners)
    wide_capacity = min(tiles_here, deep * capacity)
    f32 = lambda *shape: jax.ShapeDtypeStruct(shape, F32)

    flat = to_rows(cells)
    copies, named = kernel_call(
        spread_kernel,
        "spread",
        [
            f32(deep * slots * 8, LANES),
            jax.ShapeDtypeStruct((1, tiles_here), jnp.int32),
        ],
        [],
        [],
        [flat, instance_cell],
    )
    stack = lax.all_to_all(copies, "deep", split_axis=0, concat_axis=0, tiled=True)

    near = doubled(doubled(named, "col"), "core")
    row_axes = ("deep", "core")
    my_row, my_col = lax.axis_index(row_axes), lax.axis_index("col")
    me = jnp.stack(
        [
            lax.axis_index(plane),
            lax.axis_index(everyone),
            my_row * height - HALF,
            my_col * breadth - HALF,
            jnp.int32(deep * cores * height),
            jnp.int32(cols * breadth),
            my_row % 2,
            my_col % 2,
        ]
    ).astype(jnp.int32)
    owner = near // slots
    asked = requests(
        owner % peers == me[0], (owner // peers) * slots + near % slots, wide_capacity
    )
    waves = make_waves(row_taps, col_taps)
    packed = kernel_call(
        pack_kernel,
        "pack",
        f32(peers * wide_capacity * 8, LANES),
        [
            pltpu.VMEM((peers * wide_capacity * 8, LANES), F32),
            pltpu.SemaphoreType.DMA((peers,)),
        ],
        [asked, me],
        [stack],
        [waves],
        out_space=pl.ANY,
    )
    odd = me[6] > 0
    head, foot = target[:HALF], target[height - HALF :]
    packed, near, one, other = lax.optimization_barrier(
        (packed, near, jnp.where(odd, head, foot), jnp.where(odd, foot, head))
    )
    one, other = pairs(one, other, row_axes)
    above, below = jnp.where(odd, one, other), jnp.where(odd, other, one)
    arrived = lax.all_to_all(packed, plane, split_axis=0, concat_axis=0, tiled=True)

    everything = doubled(near, "deep")
    wanted = requests(everything // slots == me[1], everything % slots, capacity)
    mine = named[0] // slots
    earlier = jnp.tri(tiles_here, k=-1, dtype=bool)

    def place(group, size):
        same = (group[:, None] == group[None, :]) & earlier
        where = group * size + jnp.sum(same.astype(jnp.int32), axis=1)
        return where.reshape(tile_rows, tile_cols)

    wide = 2 * HALF
    quarter = (height + wide) // 4
    edge = f32(height // 2 + wide + quarter, LANES)
    mask, rowa, rowb = kernel_call(
        assemble_kernel,
        "assemble",
        [f32(height, breadth), f32(wide, breadth), f32(wide, breadth)],
        [pltpu.VMEM((height * (breadth // LANES), LANES), F32)],
        [place(mine % peers, wide_capacity), me],
        [arrived],
    )
    rowa, rowb = pairs(rowa, rowb, row_axes)
    cola, colb = kernel_call(
        edges_kernel,
        "edges",
        [edge, edge],
        [pltpu.VMEM((2, 4, quarter, LANES), F32)],
        [me],
        [mask, rowa, rowb, target, above, below],
        [wanted],
    )
    cola, colb = pairs(cola, colb, "col")
    field_rows = height + 2 * HALF
    returned = kernel_call(
        image_kernel,
        "image",
        f32(owners * capacity * 8, LANES),
        [
            pltpu.VMEM((KERNELS // 2, 2, 2, LANES, LANES), BF16),
            pltpu.VMEM((KERNELS, 2, field_rows, 256), BF16),
            pltpu.VMEM((KERNELS, 2, LANES, 256), BF16),
            pltpu.VMEM((KERNELS, 1024, WIDE), BF16),
            pltpu.VMEM((field_rows, breadth + 128), F32),
            pltpu.VMEM((height + 4 * HALF, breadth + 128), BF16),
            pltpu.VMEM((height + 4 * HALF, breadth + 128), BF16),
            pltpu.VMEM((height + 4 * HALF, breadth), BF16),
            pltpu.VMEM((height + 4 * HALF, breadth), BF16),
            pltpu.VMEM((2, KERNELS, field_rows, WIDE), F32),
            pltpu.VMEM((KERNELS, height, breadth + 128), BF16),
            pltpu.VMEM((KERNELS, height, breadth + 128), BF16),
            pltpu.VMEM((height * (breadth // LANES), LANES), F32),
        ],
        [place(mine, capacity), me, kernel_weight],
        [mask, rowa, rowb, cola, colb, target, above, below, waves],
        megabytes=36,
    )
    back = lax.all_to_all(returned, everyone, split_axis=0, concat_axis=0, tiled=True)
    stepped = kernel_call(
        step_kernel,
        "step",
        f32(slots * 8, LANES),
        [pltpu.VMEM((slots * 8, LANES), F32)] * 4,
        [wanted, me],
        [flat, back],
    )
    return from_rows(stepped)


def solution(mesh):
    rows, cols = mesh.devices.shape
    finer = Mesh(mesh.devices.reshape(rows // 2, 2, cols), ("deep", "core", "col"))
    row = ("deep", "core")
    placed = (P((*row, "col"), None), P(row, "col"), P(row, "col"), P(), P(), P())
    return jax.shard_map(
        shards, mesh=finer, in_specs=placed, out_specs=P((*row, "col"), None), check_vma=False
    )
```

```python
import jax
import jax.numpy as jnp
from jax import lax
from jax.experimental import pallas as pl
from jax.experimental.pallas import tpu as pltpu
from jax.sharding import Mesh
from jax.sharding import PartitionSpec as P

TILE = 32
TAPS = 65
HALF = 32
KERNELS = 8
LANES = 128
WIDE = 256

STEEPNESS = 4.0
THRESHOLD = 0.3
STEP_RATE = 0.5

F32 = jnp.float32
BF16 = jnp.bfloat16


def split(x):
    high = x.astype(BF16)
    return high, (x - high.astype(F32)).astype(BF16)


def mm(a, b):
    return jnp.dot(a, b, preferred_element_type=F32)


def build_bands(wave_ref, fcol_ref, frow_ref, brow_ref, bcol_ref):
    rows = lax.broadcasted_iota(jnp.int32, (LANES, LANES), 0)
    lanes = lax.broadcasted_iota(jnp.int32, (LANES, LANES), 1)
    zero = jnp.zeros((LANES, LANES), F32)

    def circular(index, start):
        base = jnp.broadcast_to(wave_ref[pl.ds(index, 1), :], (LANES, LANES))
        return pltpu.roll(base, start, 1, stride=1, stride_axis=0)

    def put(ref, kernel, r0, c0, block, height=LANES, breadth=LANES):
        high, low = split(block)
        ref[kernel, 0, r0 : r0 + height, c0 : c0 + breadth] = high[:height, :breadth]
        ref[kernel, 1, r0 : r0 + height, c0 : c0 + breadth] = low[:height, :breadth]

    half = lanes < LANES // 2

    @pl.loop(0, KERNELS)
    def _(k):
        near = circular(k, 0)
        put(frow_ref, k, 0, 0, jnp.where(lanes >= rows, near, zero))
        put(frow_ref, k, 0, LANES, jnp.where(lanes < rows, near, zero))
        put(frow_ref, k, LANES, 0, zero, 64)
        put(frow_ref, k, LANES, LANES, jnp.where(lanes >= rows, near, zero), 64)
        near = circular(2 * KERNELS + k, 0)
        put(brow_ref, k, 0, 0, jnp.where(lanes >= rows, near, zero))
        put(brow_ref, k, 0, LANES, jnp.where(lanes < rows, near, zero))
        near = circular(KERNELS + k, LANES // 2)
        diagonal = jnp.where(rows >= lanes, near, zero)
        beyond = jnp.where(rows < lanes, near, zero)
        for c0, blocks in ((0, (diagonal, beyond, zero)), (LANES, (zero, diagonal, beyond))):
            for n, block in enumerate(blocks):
                height = LANES if n < 2 else LANES // 2
                high, low = split(block)
                for start, piece in ((0, high), (320, high), (640, low)):
                    r0 = start + n * LANES
                    bcol_ref[k, r0 : r0 + height, c0 : c0 + LANES] = piece[:height]
        bcol_ref[k, 960:, :] = jnp.zeros((64, WIDE), BF16)

    @pl.loop(0, KERNELS // 2)
    def _(pair):
        first, second = 3 * KERNELS + 2 * pair, 3 * KERNELS + 2 * pair + 1
        for order, (one, other) in enumerate(((first, second), (second, first))):
            block = jnp.where(half, circular(one, LANES // 2), circular(other, 0))
            high, low = split(block)
            fcol_ref[pair, order, 0] = high
            fcol_ref[pair, order, 1] = low


def make_waves(row_taps, col_taps):
    taps = jnp.concatenate([row_taps, col_taps], axis=0)
    taps = jnp.concatenate([taps, taps[:, ::-1]], axis=0)
    return jnp.pad(taps, [(0, 0), (0, LANES - TAPS)])


def transpose_blocks(parts, block):
    turned = []
    for d in range(4):
        x = parts[d]
        for s in range(1, 4):
            x = jnp.where(block == s, parts[(s + d) % 4], x)
        turned.append(pltpu.roll(x, 32 * d, 1) if d else x)
    out = []
    for s in range(4):
        x = turned[(-s) % 4]
        for b in range(1, 4):
            x = jnp.where(block == b, turned[(b - s) % 4], x)
        out.append(x)
    return out


def spread_kernel(cells_ref, instance_ref, out_ref, named_ref):
    for c in range(out_ref.shape[0] // 8):
        out_ref[c * 8 : c * 8 + 8, :] = cells_ref[pl.ds((c // 8) * 64 + c % 8, 8, stride=8), :]
    rows = [instance_ref[a : a + 1, :] for a in range(instance_ref.shape[0])]
    named_ref[...] = jnp.concatenate(rows, axis=1)


def pack_kernel(asked_ref, me_ref, *rest):
    out_ref, stage_ref, sems = rest[-3:]
    peers, planes, capacity = asked_ref.shape
    chunk = planes * capacity * 8

    def send(i):
        rows = pl.ds(pl.multiple_of((me_ref[0] ^ i) * chunk, chunk), chunk)
        return pltpu.make_async_copy(stage_ref.at[rows, :], out_ref.at[rows, :], sems.at[i])

    @pl.loop(0, peers)
    def _(i):
        base = (me_ref[0] ^ i) * planes * capacity
        for e in range(planes):
            for j in range(capacity):
                asked = jnp.maximum(asked_ref[i, e, j], 0)
                tile = rest[e][pl.ds(pl.multiple_of(asked * 8, 8), 8), :]
                there = (base + e * capacity + j) * 8
                stage_ref[pl.ds(pl.multiple_of(there, 8), 8), :] = tile
        send(i).start()

    @pl.loop(0, peers)
    def _(i):
        send(i).wait()


def step_kernel(asked_ref, me_ref, cells_ref, tiles_ref, out_ref, *totals):
    owners, capacity = asked_ref.shape
    nothing = jnp.zeros((8, LANES), F32)
    for total in totals:
        total[...] = jnp.zeros_like(total)

    @pl.loop(0, owners)
    def _(i):
        base = (me_ref[1] ^ i) * capacity
        for j in range(capacity):
            asked = asked_ref[i, j]
            tile = tiles_ref[pl.ds(pl.multiple_of((base + j) * 8, 8), 8), :]
            there = pl.ds(pl.multiple_of(jnp.maximum(asked, 0) * 8, 8), 8)
            total = totals[j % len(totals)]
            total[there, :] += jnp.where(asked >= 0, tile, nothing)

    for c in range(out_ref.shape[0] // 8):
        rows = slice(c * 8, c * 8 + 8)
        total = totals[0][rows, :]
        for other in totals[1:]:
            total = total + other[rows, :]
        there = pl.ds((c // 8) * 64 + c % 8, 8, stride=8)
        out_ref[there, :] = cells_ref[there, :] - STEP_RATE * total


def target_strips(target_ref, top_ref, bottom_ref, strip):
    height = target_ref.shape[0]
    quarter = (height + 2 * HALF) // 4
    for row in range(0, height + 2 * HALF, 16):
        if row < HALF:
            ref, start = top_ref, row
        elif row < HALF + height:
            ref, start = target_ref, row - HALF
        else:
            ref, start = bottom_ref, row - HALF - height
        strip(row, ref, slice(start, start + 16), row // quarter, row % quarter)


def assemble_kernel(index_ref, spot_ref, near_ref, far_ref, mask_ref, *rest):
    rowa_ref, rowb_ref, turned_ref = rest
    odd_row = spot_ref[6] > 0
    tiles = near_ref.shape[0] // 8
    tile_rows, tile_cols = index_ref.shape
    height = tile_rows * TILE
    wide = 2 * HALF
    groups = tile_cols // 4
    block = lax.broadcasted_iota(jnp.int32, (8, LANES), 1) // 32

    @pl.loop(0, tile_rows)
    def _(a):
        for g in range(groups):
            parts = []
            for b in range(4):
                index = index_ref[a, 4 * g + b]
                far = index >= tiles
                there = pl.ds(pl.multiple_of(jnp.where(far, index - tiles, index) * 8, 8), 8)
                parts.append(jnp.where(far, far_ref[there, :], near_ref[there, :]))
            for s, piece in enumerate(transpose_blocks(parts, block)):
                turned_ref[pl.ds(g * height + a * TILE + s, 8, stride=4), :] = piece

    for g in range(groups):
        lanes = slice(LANES * g, LANES * (g + 1))
        piece = turned_ref[g * height : (g + 1) * height, :]
        mask_ref[:, lanes] = piece
        rowa_ref[:, lanes] = jnp.where(odd_row, piece[:wide], piece[height - wide :])
        rowb_ref[:, lanes] = jnp.where(odd_row, piece[height - wide :], piece[:wide])


def edges_kernel(spot_ref, mask_ref, rowa_ref, rowb_ref, target_ref, ttop_ref, tbottom_ref, *rest):
    cola_ref, colb_ref, pack_ref = rest[-3:]
    odd_row, odd_col = spot_ref[6] > 0, spot_ref[7] > 0
    height, breadth = mask_ref.shape
    wide = 2 * HALF
    half = height // 2
    packed = half + wide
    lane = lax.broadcasted_iota(jnp.int32, (packed, LANES), 1)
    head, tail = slice(0, LANES), slice(breadth - LANES, breadth)

    def halves(lanes):
        one, other = rowa_ref[:, lanes], rowb_ref[:, lanes]
        top, bottom = jnp.where(odd_row, one, other), jnp.where(odd_row, other, one)
        upper = jnp.concatenate([top, mask_ref[:half, lanes]], axis=0)
        return upper, jnp.concatenate([mask_ref[half:, lanes], bottom], axis=0)

    upper, lower = halves(head)
    left = jnp.where(lane < wide, upper, pltpu.roll(lower, wide, 1))
    upper, lower = halves(tail)
    right = jnp.where(lane < wide, pltpu.roll(upper, wide, 1), lower)
    cola_ref[:packed, :] = jnp.where(odd_col, left, right)
    colb_ref[:packed, :] = jnp.where(odd_col, right, left)

    quarter = (height + 2 * HALF) // 4

    def strip(row, ref, rows, part, inner):
        for side, lanes in enumerate((head, tail)):
            shift = (HALF * (part + side)) % LANES
            piece = ref[rows, lanes]
            pack_ref[side, part, inner : inner + 16, :] = (
                pltpu.roll(piece, shift, 1) if shift else piece
            )

    target_strips(target_ref, ttop_ref, tbottom_ref, strip)
    part_of = lax.broadcasted_iota(jnp.int32, (quarter, LANES), 1) // HALF
    sides = []
    for side in range(2):
        piece = pack_ref[side, 0]
        for part in range(1, 4):
            piece = jnp.where(part_of == part, pack_ref[side, part], piece)
        sides.append(piece)
    cola_ref[packed:, :] = jnp.where(odd_col, sides[0], sides[1])
    colb_ref[packed:, :] = jnp.where(odd_col, sides[1], sides[0])


def image_kernel(
    index_ref,
    spot_ref,
    weight_ref,
    mask_ref,
    rowa_ref,
    rowb_ref,
    cola_ref,
    colb_ref,
    own_ref,
    ttop_ref,
    tbottom_ref,
    wave_ref,
    out_ref,
    fcol_ref,
    frow_ref,
    brow_ref,
    bcol_ref,
    target_ref,
    mhigh_ref,
    mlow_ref,
    nhigh_ref,
    nlow_ref,
    field_ref,
    ghigh_ref,
    gturn_ref,
    grad_ref,
):
    tile_rows, tile_cols = index_ref.shape
    rows_here = tile_rows * TILE
    high_rows = rows_here + 4 * HALF
    field_rows = rows_here + 2 * HALF
    groups = tile_cols // 4
    wide = 2 * HALF
    block = lax.broadcasted_iota(jnp.int32, (8, LANES), 1) // 32
    odd_row, odd_col = spot_ref[6] > 0, spot_ref[7] > 0
    build_bands(wave_ref, fcol_ref, frow_ref, brow_ref, bcol_ref)

    lane = lax.broadcasted_iota(jnp.int32, (wide, LANES), 1)
    for rows in range(0, high_rows, wide):
        outer = rows == 0 or rows == high_rows - wide
        from_a = odd_row if rows == 0 else jnp.logical_not(odd_row)
        half = high_rows // 2
        edge = slice(rows % half, rows % half + wide)
        one, other = cola_ref[edge, :], colb_ref[edge, :]
        turned, final = jnp.where(odd_col, one, other), jnp.where(odd_col, other, one)
        if rows < half:
            final = pltpu.roll(final, wide, 1)
        else:
            turned = pltpu.roll(turned, wide, 1)
        for g in range(groups + 1):
            fresh = final
            if g < groups:
                lanes = slice(LANES * g, LANES * (g + 1))
                if outer:
                    piece = jnp.where(from_a, rowa_ref[:, lanes], rowb_ref[:, lanes])
                else:
                    piece = mask_ref[rows - wide : rows, lanes]
                high, low = split(piece)
                nhigh_ref[rows : rows + wide, LANES * g : LANES * (g + 1)] = high
                nlow_ref[rows : rows + wide, LANES * g : LANES * (g + 1)] = low
                fresh = pltpu.roll(piece, wide, 1)
            high, low = split(jnp.where(lane < wide, turned, fresh))
            mhigh_ref[rows : rows + wide, LANES * g : LANES * (g + 1)] = high
            mlow_ref[rows : rows + wide, LANES * g : LANES * (g + 1)] = low
            turned = fresh
    packed = high_rows // 2
    near_lane = lax.broadcasted_iota(jnp.int32, (16, LANES), 1)

    def strip(row, ref, rows, part, inner):
        edge = slice(packed + inner, packed + inner + 16)
        back, ahead = (-HALF * part) % LANES, (HALF - HALF * part) % LANES
        one, other = cola_ref[edge, :], colb_ref[edge, :]
        turned, final = jnp.where(odd_col, one, other), jnp.where(odd_col, other, one)
        turned = pltpu.roll(turned, back, 1) if back else turned
        final = pltpu.roll(final, ahead, 1) if ahead else final
        for g in range(groups + 1):
            fresh = final
            if g < groups:
                fresh = pltpu.roll(ref[rows, LANES * g : LANES * (g + 1)], HALF, 1)
            target_ref[row : row + 16, LANES * g : LANES * (g + 1)] = jnp.where(
                near_lane < HALF, turned, fresh
            )
            turned = fresh

    target_strips(own_ref, ttop_ref, tbottom_ref, strip)

    def swapped(x):
        pieces = [
            pltpu.roll(x[:, c : c + LANES], LANES // 2, 1) for c in range(0, x.shape[1], LANES)
        ]
        return pieces[0] if len(pieces) == 1 else jnp.concatenate(pieces, axis=1)

    def columns(offset, width):
        blocks = width // LANES
        last = blocks == 1

        def windows(high_ref, low_ref):
            rows = []
            for j in range(blocks):
                place = pl.ds(pl.multiple_of(offset + j * LANES, LANES), LANES)
                high, low = high_ref[:, place], low_ref[:, place]
                rows.append(jnp.concatenate([high, low, high], axis=1))
            return rows[0] if last else jnp.concatenate(rows, axis=0)

        even_rows = windows(mhigh_ref, mlow_ref)
        odd_rows = None if last else windows(nhigh_ref, nlow_ref)
        left = lax.broadcasted_iota(jnp.int32, (high_rows, LANES), 1) < LANES // 2

        def band(quad, order):
            both = [
                jnp.concatenate(
                    [fcol_ref[2 * quad, order, v], fcol_ref[2 * quad + 1, order, v]], axis=1
                )
                for v in range(2)
            ]
            return jnp.concatenate([both[0], both[0], both[1]], axis=0)

        sums = [None, None]
        for quad in range(KERNELS // 4):
            even = mm(even_rows, band(quad, 0))
            odd = even if last else mm(odd_rows, band(quad, 1))
            four = range(4 * quad, 4 * quad + 4)
            if last:
                high, low = split(even)
                both = mm(jnp.concatenate([frow_ref[k, v] for k in four for v in range(2)], 0), high)
                more = mm(jnp.concatenate([frow_ref[k, 0] for k in four], axis=0), low)
            for h, k in enumerate(four):
                lanes = slice((h // 2) * LANES, (h // 2 + 1) * LANES)
                if last:
                    start = 2 * h * field_rows
                    field = both[start : start + field_rows, lanes]
                    field = field + both[start + field_rows : start + 2 * field_rows, lanes]
                    field = field + more[h * field_rows : (h + 1) * field_rows, lanes]
                else:
                    pieces = []
                    for j in range(blocks):
                        rows = slice(j * high_rows, (j + 1) * high_rows)
                        one, other = even[rows, lanes], odd[rows, lanes]
                        one, other = (other, one) if h % 2 else (one, other)
                        pieces.append(jnp.where(left, one, other))
                    high, low = split(jnp.concatenate(pieces, axis=1))
                    both = mm(jnp.concatenate([frow_ref[k, 0], frow_ref[k, 1]], axis=0), high)
                    field = both[:field_rows] + both[field_rows:] + mm(frow_ref[k, 0], low)
                field_ref[k, :, :width] = field
                term = weight_ref[k] * field * field
                sums[h % 2] = term if sums[h % 2] is None else sums[h % 2] + term
        intensity = sums[0] + swapped(sums[1])
        resist = 1.0 / (1.0 + jnp.exp(-STEEPNESS * (intensity - THRESHOLD)))
        place = pl.ds(pl.multiple_of(offset, LANES), width)
        target = target_ref[:, place]
        sensitivity = 2.0 * (resist - target) * STEEPNESS * resist * (1.0 - resist)
        row = spot_ref[2] + lax.broadcasted_iota(jnp.int32, (field_rows, width), 0)
        col = spot_ref[3] + offset + lax.broadcasted_iota(jnp.int32, (field_rows, width), 1)
        inside = (row >= 0) & (row < spot_ref[4]) & (col >= 0) & (col < spot_ref[5])
        sensitivity = jnp.where(inside, sensitivity, 0.0)
        ordered = (sensitivity, swapped(sensitivity))

        def product(k):
            return (2.0 * weight_ref[k]) * ordered[k % 2] * field_ref[k, :, :width]

        def keep(k, part):
            straight, turned = (part, swapped(part))[:: 1 - 2 * (k % 2)]
            ghigh_ref[k, :, place] = straight.astype(BF16)
            gturn_ref[k, :, place] = split(turned)[1]

        if last:
            half = left[:field_rows]
            for quad in range(KERNELS // 4):
                four = range(4 * quad, 4 * quad + 4)
                each = [product(k) for k in four]
                high, low = split(
                    jnp.concatenate(
                        [jnp.where(half, each[0], each[1]), jnp.where(half, each[2], each[3])],
                        axis=1,
                    )
                )
                near = [brow_ref[k, v, :, :field_rows] for k in four for v in range(2)]
                both = mm(jnp.concatenate(near, axis=0), high)
                more = mm(jnp.concatenate(near[::2], axis=0), low)
                for h, k in enumerate(four):
                    lanes = slice((h // 2) * LANES, (h // 2 + 1) * LANES)
                    start = 2 * h * rows_here
                    part = both[start : start + rows_here, lanes]
                    part = part + both[start + rows_here : start + 2 * rows_here, lanes]
                    keep(k, part + more[h * rows_here : (h + 1) * rows_here, lanes])
            return
        for k in range(KERNELS):
            high, low = split(product(k))
            near = brow_ref[k, 0, :, :field_rows]
            both = mm(jnp.concatenate([near, brow_ref[k, 1, :, :field_rows]], axis=0), high)
            keep(k, both[:rows_here] + both[rows_here:] + mm(near, low))

    supers = tile_cols * TILE // WIDE

    @pl.loop(0, supers)
    def _(jj):
        columns(jj * WIDE, WIDE)

    columns(supers * WIDE, LANES)

    lower = lax.broadcasted_iota(jnp.int32, (rows_here, LANES), 1) < LANES // 2

    def spread_back(k):
        stacked = []
        for jj in range(supers):
            c0 = WIDE * jj
            high = [ghigh_ref[k, :, c0 + LANES * n : c0 + LANES * (n + 1)] for n in range(3)]
            turn = [gturn_ref[k, :, c0 + LANES * n : c0 + LANES * (n + 1)] for n in range(3)]
            row = [
                high[0],
                high[1],
                jnp.where(lower, high[2], turn[0]),
                jnp.where(lower, turn[0], turn[1]),
                jnp.where(lower, turn[1], turn[2]),
                *high,
            ]
            stacked.append(jnp.concatenate(row, axis=1))
        return mm(jnp.concatenate(stacked, axis=0), bcol_ref[k])

    def add(part, fresh):
        for g in range(groups):
            rows = slice(g * rows_here, (g + 1) * rows_here)
            top = (g // 2) * rows_here
            piece = part[top : top + rows_here, LANES * (g % 2) : LANES * (g % 2 + 1)]
            grad_ref[rows, :] = piece if fresh else grad_ref[rows, :] + piece

    add(spread_back(0), True)

    @pl.loop(1, KERNELS)
    def _(k):
        add(spread_back(k), False)

    @pl.loop(0, tile_rows)
    def _(a):
        for g in range(groups):
            base = g * rows_here + a * TILE
            parts = [grad_ref[pl.ds(base + s, 8, stride=4), :] for s in range(4)]
            for b, tile in enumerate(transpose_blocks(parts, block)):
                place = pl.multiple_of(index_ref[a, 4 * g + b] * 8, 8)
                out_ref[pl.ds(place, 8), :] = tile


def to_rows(x):
    count = x.shape[0]
    return x.reshape(count // 8, 8, 8, LANES).transpose(0, 2, 1, 3).reshape(count * 8, LANES)


def from_rows(x):
    count = x.shape[0] // 8
    return x.reshape(count // 8, 8, 8, LANES).transpose(0, 2, 1, 3).reshape(count, 8 * LANES)


def kernel_call(body, name, shapes, scratch, scalars, inputs, unread=(), megabytes=8, out_space=pltpu.VMEM):
    single = not isinstance(shapes, list)
    spec = pl.BlockSpec(memory_space=pltpu.VMEM)
    outs = [shapes] if single else shapes
    result = pl.pallas_call(
        body,
        out_shape=outs,
        in_specs=[pl.BlockSpec(memory_space=pltpu.SMEM)] * len(scalars)
        + [spec] * len(inputs)
        + [pl.BlockSpec(memory_space=pl.ANY)] * len(unread),
        out_specs=[pl.BlockSpec(memory_space=out_space)] * len(outs),
        scratch_shapes=scratch,
        compiler_params=pltpu.CompilerParams(vmem_limit_bytes=megabytes * 2**20),
        name=name,
    )(*scalars, *inputs, *unread)
    return result[0] if single else result


def pairs(one, other, axis):
    count = lax.axis_size(axis)
    out = []
    for x, start in ((one, 0), (other, 1)):
        swap = [(i, i + 1) for i in range(start, count - 1, 2)]
        out.append(lax.ppermute(x, axis, swap + [(j, i) for i, j in swap]))
    return out


def doubled(table, axis):
    count = lax.axis_size(axis)
    bit = 1
    while bit < count:
        got = lax.ppermute(table, axis, [(i, i ^ bit) for i in range(count)])
        table = jnp.concatenate([table, got], axis=0)
        bit *= 2
    return table


def requests(match, value, capacity):
    rank = jnp.cumsum(match.astype(jnp.int32), axis=1) - 1
    hit = match[:, None, :] & (rank[:, None, :] == jnp.arange(capacity)[None, :, None])
    return jnp.max(jnp.where(hit, value[:, None, :], -1), axis=2)


def shards(cells, instance_cell, target, row_taps, col_taps, kernel_weight):
    deep, cores, cols = lax.axis_size("deep"), lax.axis_size("core"), lax.axis_size("col")
    everyone = ("deep", "core", "col")
    plane = ("core", "col")
    peers = cores * cols
    slots = cells.shape[0]
    tile_rows, tile_cols = instance_cell.shape
    tiles_here = tile_rows * tile_cols
    height, breadth = target.shape
    owners = deep * peers
    capacity = 2 * ((tiles_here + owners - 1) // owners)
    f32 = lambda *shape: jax.ShapeDtypeStruct(shape, F32)

    flat = to_rows(cells)
    ordered, named = kernel_call(
        spread_kernel,
        "spread",
        [f32(slots * 8, LANES), jax.ShapeDtypeStruct((1, tiles_here), jnp.int32)],
        [],
        [],
        [flat, instance_cell],
    )
    near = doubled(doubled(named, "col"), "core")
    levels = [ordered]
    for e in range(1, deep):
        levels.append(lax.ppermute(ordered, "deep", [(i, i ^ e) for i in range(deep)]))
    row_axes = ("deep", "core")
    my_row, my_col = lax.axis_index(row_axes), lax.axis_index("col")
    me = jnp.stack(
        [
            lax.axis_index(plane),
            lax.axis_index(everyone),
            my_row * height - HALF,
            my_col * breadth - HALF,
            jnp.int32(deep * cores * height),
            jnp.int32(cols * breadth),
            my_row % 2,
            my_col % 2,
        ]
    ).astype(jnp.int32)
    my_deep = lax.axis_index("deep")
    planes = deep // 2
    here = ((my_deep ^ jnp.arange(deep)) * peers + me[0])[None, :, None]
    match = (near // slots)[:, None, :] == here
    slot = jnp.broadcast_to((near % slots)[:, None, :], match.shape)
    asked = requests(
        match.reshape(peers * deep, tiles_here), slot.reshape(peers * deep, tiles_here), capacity
    ).reshape(peers, deep, capacity)
    waves = make_waves(row_taps, col_taps)
    size = peers * planes * capacity * 8
    packed = []
    for half in range(2):
        which = slice(half * planes, (half + 1) * planes)
        packed.append(
            kernel_call(
                pack_kernel,
                "pack",
                f32(size, LANES),
                [pltpu.VMEM((size, LANES), F32), pltpu.SemaphoreType.DMA((peers,))],
                [asked[:, which], me],
                levels[which],
                [waves] if half else [],
                out_space=pl.ANY,
            )
        )
    odd = me[6] > 0
    head, foot = target[:HALF], target[height - HALF :]
    packed[1], near, one, other = lax.optimization_barrier(
        (packed[1], near, jnp.where(odd, head, foot), jnp.where(odd, foot, head))
    )
    one, other = pairs(one, other, row_axes)
    above, below = jnp.where(odd, one, other), jnp.where(odd, other, one)
    arrived = [
        lax.all_to_all(x, plane, split_axis=0, concat_axis=0, tiled=True) for x in packed
    ]

    everything = doubled(near, "deep")
    wanted = requests(everything // slots == me[1], everything % slots, capacity)
    mine = named[0] // slots
    earlier = jnp.tri(tiles_here, k=-1, dtype=bool)

    def place(group, size):
        same = (group[:, None] == group[None, :]) & earlier
        where = group * size + jnp.sum(same.astype(jnp.int32), axis=1)
        return where.reshape(tile_rows, tile_cols)

    home = place(mine, capacity)
    theirs = home // capacity
    level = my_deep ^ (theirs // peers)
    index = (level // planes * peers + theirs % peers) * planes + level % planes
    index = index * capacity + home % capacity
    wide = 2 * HALF
    quarter = (height + wide) // 4
    edge = f32(height // 2 + wide + quarter, LANES)
    mask, rowa, rowb = kernel_call(
        assemble_kernel,
        "assemble",
        [f32(height, breadth), f32(wide, breadth), f32(wide, breadth)],
        [pltpu.VMEM((height * (breadth // LANES), LANES), F32)],
        [index, me],
        arrived,
    )
    rowa, rowb = pairs(rowa, rowb, row_axes)
    cola, colb = kernel_call(
        edges_kernel,
        "edges",
        [edge, edge],
        [pltpu.VMEM((2, 4, quarter, LANES), F32)],
        [me],
        [mask, rowa, rowb, target, above, below],
        [wanted],
    )
    cola, colb = pairs(cola, colb, "col")
    field_rows = height + 2 * HALF
    returned = kernel_call(
        image_kernel,
        "image",
        f32(owners * capacity * 8, LANES),
        [
            pltpu.VMEM((KERNELS // 2, 2, 2, LANES, LANES), BF16),
            pltpu.VMEM((KERNELS, 2, field_rows, 256), BF16),
            pltpu.VMEM((KERNELS, 2, LANES, 256), BF16),
            pltpu.VMEM((KERNELS, 1024, WIDE), BF16),
            pltpu.VMEM((field_rows, breadth + 128), F32),
            pltpu.VMEM((height + 4 * HALF, breadth + 128), BF16),
            pltpu.VMEM((height + 4 * HALF, breadth + 128), BF16),
            pltpu.VMEM((height + 4 * HALF, breadth), BF16),
            pltpu.VMEM((height + 4 * HALF, breadth), BF16),
            pltpu.VMEM((KERNELS, field_rows, WIDE), F32),
            pltpu.VMEM((KERNELS, height, breadth + 128), BF16),
            pltpu.VMEM((KERNELS, height, breadth + 128), BF16),
            pltpu.VMEM((height * (breadth // LANES), LANES), F32),
        ],
        [home, me, kernel_weight],
        [mask, rowa, rowb, cola, colb, target, above, below, waves],
        megabytes=36,
    )
    back = lax.all_to_all(returned, everyone, split_axis=0, concat_axis=0, tiled=True)
    stepped = kernel_call(
        step_kernel,
        "step",
        f32(slots * 8, LANES),
        [pltpu.VMEM((slots * 8, LANES), F32)] * 4,
        [wanted, me],
        [flat, back],
    )
    return from_rows(stepped)


def solution(mesh):
    rows, cols = mesh.devices.shape
    finer = Mesh(mesh.devices.reshape(rows // 2, 2, cols), ("deep", "core", "col"))
    row = ("deep", "core")
    placed = (P((*row, "col"), None), P(row, "col"), P(row, "col"), P(), P(), P())
    return jax.shard_map(
        shards, mesh=finer, in_specs=placed, out_specs=P((*row, "col"), None), check_vma=False
    )
```

```python
import jax
import jax.numpy as jnp
from jax import lax
from jax.experimental import pallas as pl
from jax.experimental.pallas import tpu as pltpu
from jax.sharding import Mesh
from jax.sharding import PartitionSpec as P

TILE = 32
TAPS = 65
HALF = 32
KERNELS = 8
LANES = 128
WIDE = 256

STEEPNESS = 4.0
THRESHOLD = 0.3
STEP_RATE = 0.5

F32 = jnp.float32
BF16 = jnp.bfloat16


def split(x):
    high = x.astype(BF16)
    return high, (x - high.astype(F32)).astype(BF16)


def mm(a, b):
    return jnp.dot(a, b, preferred_element_type=F32)


def build_bands(wave_ref, fcol_ref, frow_ref, brow_ref, bcol_ref):
    rows = lax.broadcasted_iota(jnp.int32, (LANES, LANES), 0)
    lanes = lax.broadcasted_iota(jnp.int32, (LANES, LANES), 1)
    zero = jnp.zeros((LANES, LANES), F32)

    def circular(index, start):
        base = jnp.broadcast_to(wave_ref[pl.ds(index, 1), :], (LANES, LANES))
        return pltpu.roll(base, start, 1, stride=1, stride_axis=0)

    def put(ref, kernel, r0, c0, block, height=LANES, breadth=LANES):
        high, low = split(block)
        ref[kernel, 0, r0 : r0 + height, c0 : c0 + breadth] = high[:height, :breadth]
        ref[kernel, 1, r0 : r0 + height, c0 : c0 + breadth] = low[:height, :breadth]

    half = lanes < LANES // 2

    @pl.loop(0, KERNELS)
    def _(k):
        near = circular(k, 0)
        put(frow_ref, k, 0, 0, jnp.where(lanes >= rows, near, zero))
        put(frow_ref, k, 0, LANES, jnp.where(lanes < rows, near, zero))
        put(frow_ref, k, LANES, 0, zero, 64)
        put(frow_ref, k, LANES, LANES, jnp.where(lanes >= rows, near, zero), 64)
        near = circular(2 * KERNELS + k, 0)
        put(brow_ref, k, 0, 0, jnp.where(lanes >= rows, near, zero))
        put(brow_ref, k, 0, LANES, jnp.where(lanes < rows, near, zero))
        near = circular(KERNELS + k, LANES // 2)
        diagonal = jnp.where(rows >= lanes, near, zero)
        beyond = jnp.where(rows < lanes, near, zero)
        for c0, blocks in ((0, (diagonal, beyond, zero)), (LANES, (zero, diagonal, beyond))):
            for n, block in enumerate(blocks):
                height = LANES if n < 2 else LANES // 2
                high, low = split(block)
                for start, piece in ((0, high), (320, high), (640, low)):
                    r0 = start + n * LANES
                    bcol_ref[k, r0 : r0 + height, c0 : c0 + LANES] = piece[:height]
        bcol_ref[k, 960:, :] = jnp.zeros((64, WIDE), BF16)

    @pl.loop(0, KERNELS // 2)
    def _(pair):
        first, second = 3 * KERNELS + 2 * pair, 3 * KERNELS + 2 * pair + 1
        for order, (one, other) in enumerate(((first, second), (second, first))):
            block = jnp.where(half, circular(one, LANES // 2), circular(other, 0))
            high, low = split(block)
            fcol_ref[pair, order, 0] = high
            fcol_ref[pair, order, 1] = low


def make_waves(row_taps, col_taps):
    taps = jnp.concatenate([row_taps, col_taps], axis=0)
    taps = jnp.concatenate([taps, taps[:, ::-1]], axis=0)
    return jnp.pad(taps, [(0, 0), (0, LANES - TAPS)])


def transpose_blocks(parts, block):
    turned = []
    for d in range(4):
        x = parts[d]
        for s in range(1, 4):
            x = jnp.where(block == s, parts[(s + d) % 4], x)
        turned.append(pltpu.roll(x, 32 * d, 1) if d else x)
    out = []
    for s in range(4):
        x = turned[(-s) % 4]
        for b in range(1, 4):
            x = jnp.where(block == b, turned[(b - s) % 4], x)
        out.append(x)
    return out


def spread_kernel(cells_ref, instance_ref, out_ref, named_ref):
    for c in range(out_ref.shape[0] // 8):
        out_ref[c * 8 : c * 8 + 8, :] = cells_ref[pl.ds((c // 8) * 64 + c % 8, 8, stride=8), :]
    rows = [instance_ref[a : a + 1, :] for a in range(instance_ref.shape[0])]
    named_ref[...] = jnp.concatenate(rows, axis=1)


def pack_kernel(asked_ref, me_ref, *rest):
    out_ref, stage_ref, sems = rest[-3:]
    peers, planes, capacity = asked_ref.shape
    chunk = planes * capacity * 8

    def send(i):
        rows = pl.ds(pl.multiple_of((me_ref[0] ^ i) * chunk, chunk), chunk)
        return pltpu.make_async_copy(stage_ref.at[rows, :], out_ref.at[rows, :], sems.at[i])

    @pl.loop(0, peers)
    def _(i):
        base = (me_ref[0] ^ i) * planes * capacity
        for e in range(planes):
            for j in range(capacity):
                asked = jnp.maximum(asked_ref[i, e, j], 0)
                tile = rest[e][pl.ds(pl.multiple_of(asked * 8, 8), 8), :]
                there = (base + e * capacity + j) * 8
                stage_ref[pl.ds(pl.multiple_of(there, 8), 8), :] = tile
        send(i).start()

    @pl.loop(0, peers)
    def _(i):
        send(i).wait()


def step_kernel(asked_ref, me_ref, cells_ref, tiles_ref, out_ref, *totals):
    owners, capacity = asked_ref.shape
    nothing = jnp.zeros((8, LANES), F32)
    for total in totals:
        total[...] = jnp.zeros_like(total)

    @pl.loop(0, owners)
    def _(i):
        base = (me_ref[1] ^ i) * capacity
        for j in range(capacity):
            asked = asked_ref[i, j]
            tile = tiles_ref[pl.ds(pl.multiple_of((base + j) * 8, 8), 8), :]
            there = pl.ds(pl.multiple_of(jnp.maximum(asked, 0) * 8, 8), 8)
            total = totals[j % len(totals)]
            total[there, :] += jnp.where(asked >= 0, tile, nothing)

    for c in range(out_ref.shape[0] // 8):
        rows = slice(c * 8, c * 8 + 8)
        total = totals[0][rows, :]
        for other in totals[1:]:
            total = total + other[rows, :]
        there = pl.ds((c // 8) * 64 + c % 8, 8, stride=8)
        out_ref[there, :] = cells_ref[there, :] - STEP_RATE * total


def target_strips(target_ref, top_ref, bottom_ref, strip):
    height = target_ref.shape[0]
    quarter = (height + 2 * HALF) // 4
    for row in range(0, height + 2 * HALF, 16):
        if row < HALF:
            ref, start = top_ref, row
        elif row < HALF + height:
            ref, start = target_ref, row - HALF
        else:
            ref, start = bottom_ref, row - HALF - height
        strip(row, ref, slice(start, start + 16), row // quarter, row % quarter)


def assemble_kernel(index_ref, spot_ref, tiles_ref, mask_ref, rowa_ref, rowb_ref, turned_ref):
    odd_row = spot_ref[6] > 0
    tile_rows, tile_cols = index_ref.shape
    height = tile_rows * TILE
    wide = 2 * HALF
    groups = tile_cols // 4
    block = lax.broadcasted_iota(jnp.int32, (8, LANES), 1) // 32

    @pl.loop(0, tile_rows)
    def _(a):
        for g in range(groups):
            parts = [
                tiles_ref[pl.ds(pl.multiple_of(index_ref[a, 4 * g + b] * 8, 8), 8), :]
                for b in range(4)
            ]
            for s, piece in enumerate(transpose_blocks(parts, block)):
                turned_ref[pl.ds(g * height + a * TILE + s, 8, stride=4), :] = piece

    for g in range(groups):
        lanes = slice(LANES * g, LANES * (g + 1))
        piece = turned_ref[g * height : (g + 1) * height, :]
        mask_ref[:, lanes] = piece
        rowa_ref[:, lanes] = jnp.where(odd_row, piece[:wide], piece[height - wide :])
        rowb_ref[:, lanes] = jnp.where(odd_row, piece[height - wide :], piece[:wide])


def edges_kernel(spot_ref, mask_ref, rowa_ref, rowb_ref, target_ref, ttop_ref, tbottom_ref, *rest):
    cola_ref, colb_ref, pack_ref = rest[-3:]
    odd_row, odd_col = spot_ref[6] > 0, spot_ref[7] > 0
    height, breadth = mask_ref.shape
    wide = 2 * HALF
    half = height // 2
    packed = half + wide
    lane = lax.broadcasted_iota(jnp.int32, (packed, LANES), 1)
    head, tail = slice(0, LANES), slice(breadth - LANES, breadth)

    def halves(lanes):
        one, other = rowa_ref[:, lanes], rowb_ref[:, lanes]
        top, bottom = jnp.where(odd_row, one, other), jnp.where(odd_row, other, one)
        upper = jnp.concatenate([top, mask_ref[:half, lanes]], axis=0)
        return upper, jnp.concatenate([mask_ref[half:, lanes], bottom], axis=0)

    upper, lower = halves(head)
    left = jnp.where(lane < wide, upper, pltpu.roll(lower, wide, 1))
    upper, lower = halves(tail)
    right = jnp.where(lane < wide, pltpu.roll(upper, wide, 1), lower)
    cola_ref[:packed, :] = jnp.where(odd_col, left, right)
    colb_ref[:packed, :] = jnp.where(odd_col, right, left)

    quarter = (height + 2 * HALF) // 4

    def strip(row, ref, rows, part, inner):
        for side, lanes in enumerate((head, tail)):
            shift = (HALF * (part + side)) % LANES
            piece = ref[rows, lanes]
            pack_ref[side, part, inner : inner + 16, :] = (
                pltpu.roll(piece, shift, 1) if shift else piece
            )

    target_strips(target_ref, ttop_ref, tbottom_ref, strip)
    part_of = lax.broadcasted_iota(jnp.int32, (quarter, LANES), 1) // HALF
    sides = []
    for side in range(2):
        piece = pack_ref[side, 0]
        for part in range(1, 4):
            piece = jnp.where(part_of == part, pack_ref[side, part], piece)
        sides.append(piece)
    cola_ref[packed:, :] = jnp.where(odd_col, sides[0], sides[1])
    colb_ref[packed:, :] = jnp.where(odd_col, sides[1], sides[0])


def image_kernel(
    index_ref,
    spot_ref,
    weight_ref,
    mask_ref,
    rowa_ref,
    rowb_ref,
    cola_ref,
    colb_ref,
    own_ref,
    ttop_ref,
    tbottom_ref,
    wave_ref,
    out_ref,
    fcol_ref,
    frow_ref,
    brow_ref,
    bcol_ref,
    target_ref,
    mhigh_ref,
    mlow_ref,
    nhigh_ref,
    nlow_ref,
    field_ref,
    ghigh_ref,
    gturn_ref,
    grad_ref,
):
    tile_rows, tile_cols = index_ref.shape
    rows_here = tile_rows * TILE
    high_rows = rows_here + 4 * HALF
    field_rows = rows_here + 2 * HALF
    groups = tile_cols // 4
    wide = 2 * HALF
    block = lax.broadcasted_iota(jnp.int32, (8, LANES), 1) // 32
    odd_row, odd_col = spot_ref[6] > 0, spot_ref[7] > 0
    build_bands(wave_ref, fcol_ref, frow_ref, brow_ref, bcol_ref)

    lane = lax.broadcasted_iota(jnp.int32, (wide, LANES), 1)
    for rows in range(0, high_rows, wide):
        outer = rows == 0 or rows == high_rows - wide
        from_a = odd_row if rows == 0 else jnp.logical_not(odd_row)
        half = high_rows // 2
        edge = slice(rows % half, rows % half + wide)
        one, other = cola_ref[edge, :], colb_ref[edge, :]
        turned, final = jnp.where(odd_col, one, other), jnp.where(odd_col, other, one)
        if rows < half:
            final = pltpu.roll(final, wide, 1)
        else:
            turned = pltpu.roll(turned, wide, 1)
        for g in range(groups + 1):
            fresh = final
            if g < groups:
                lanes = slice(LANES * g, LANES * (g + 1))
                if outer:
                    piece = jnp.where(from_a, rowa_ref[:, lanes], rowb_ref[:, lanes])
                else:
                    piece = mask_ref[rows - wide : rows, lanes]
                high, low = split(piece)
                nhigh_ref[rows : rows + wide, LANES * g : LANES * (g + 1)] = high
                nlow_ref[rows : rows + wide, LANES * g : LANES * (g + 1)] = low
                fresh = pltpu.roll(piece, wide, 1)
            high, low = split(jnp.where(lane < wide, turned, fresh))
            mhigh_ref[rows : rows + wide, LANES * g : LANES * (g + 1)] = high
            mlow_ref[rows : rows + wide, LANES * g : LANES * (g + 1)] = low
            turned = fresh
    packed = high_rows // 2
    near_lane = lax.broadcasted_iota(jnp.int32, (16, LANES), 1)

    def strip(row, ref, rows, part, inner):
        edge = slice(packed + inner, packed + inner + 16)
        back, ahead = (-HALF * part) % LANES, (HALF - HALF * part) % LANES
        one, other = cola_ref[edge, :], colb_ref[edge, :]
        turned, final = jnp.where(odd_col, one, other), jnp.where(odd_col, other, one)
        turned = pltpu.roll(turned, back, 1) if back else turned
        final = pltpu.roll(final, ahead, 1) if ahead else final
        for g in range(groups + 1):
            fresh = final
            if g < groups:
                fresh = pltpu.roll(ref[rows, LANES * g : LANES * (g + 1)], HALF, 1)
            target_ref[row : row + 16, LANES * g : LANES * (g + 1)] = jnp.where(
                near_lane < HALF, turned, fresh
            )
            turned = fresh

    target_strips(own_ref, ttop_ref, tbottom_ref, strip)

    def swapped(x):
        pieces = [
            pltpu.roll(x[:, c : c + LANES], LANES // 2, 1) for c in range(0, x.shape[1], LANES)
        ]
        return pieces[0] if len(pieces) == 1 else jnp.concatenate(pieces, axis=1)

    def columns(offset, width):
        blocks = width // LANES
        last = blocks == 1

        def windows(high_ref, low_ref):
            rows = []
            for j in range(blocks):
                place = pl.ds(pl.multiple_of(offset + j * LANES, LANES), LANES)
                high, low = high_ref[:, place], low_ref[:, place]
                rows.append(jnp.concatenate([high, low, high], axis=1))
            return rows[0] if last else jnp.concatenate(rows, axis=0)

        even_rows = windows(mhigh_ref, mlow_ref)
        odd_rows = None if last else windows(nhigh_ref, nlow_ref)
        left = lax.broadcasted_iota(jnp.int32, (high_rows, LANES), 1) < LANES // 2

        def band(quad, order):
            both = [
                jnp.concatenate(
                    [fcol_ref[2 * quad, order, v], fcol_ref[2 * quad + 1, order, v]], axis=1
                )
                for v in range(2)
            ]
            return jnp.concatenate([both[0], both[0], both[1]], axis=0)

        sums = [None, None]
        for quad in range(KERNELS // 4):
            even = mm(even_rows, band(quad, 0))
            odd = even if last else mm(odd_rows, band(quad, 1))
            four = range(4 * quad, 4 * quad + 4)
            if last:
                high, low = split(even)
                both = mm(jnp.concatenate([frow_ref[k, v] for k in four for v in range(2)], 0), high)
                more = mm(jnp.concatenate([frow_ref[k, 0] for k in four], axis=0), low)
            for h, k in enumerate(four):
                lanes = slice((h // 2) * LANES, (h // 2 + 1) * LANES)
                if last:
                    start = 2 * h * field_rows
                    field = both[start : start + field_rows, lanes]
                    field = field + both[start + field_rows : start + 2 * field_rows, lanes]
                    field = field + more[h * field_rows : (h + 1) * field_rows, lanes]
                else:
                    pieces = []
                    for j in range(blocks):
                        rows = slice(j * high_rows, (j + 1) * high_rows)
                        one, other = even[rows, lanes], odd[rows, lanes]
                        one, other = (other, one) if h % 2 else (one, other)
                        pieces.append(jnp.where(left, one, other))
                    high, low = split(jnp.concatenate(pieces, axis=1))
                    both = mm(jnp.concatenate([frow_ref[k, 0], frow_ref[k, 1]], axis=0), high)
                    field = both[:field_rows] + both[field_rows:] + mm(frow_ref[k, 0], low)
                field_ref[k, :, :width] = field
                term = weight_ref[k] * field * field
                sums[h % 2] = term if sums[h % 2] is None else sums[h % 2] + term
        intensity = sums[0] + swapped(sums[1])
        resist = 1.0 / (1.0 + jnp.exp(-STEEPNESS * (intensity - THRESHOLD)))
        place = pl.ds(pl.multiple_of(offset, LANES), width)
        target = target_ref[:, place]
        sensitivity = 2.0 * (resist - target) * STEEPNESS * resist * (1.0 - resist)
        row = spot_ref[2] + lax.broadcasted_iota(jnp.int32, (field_rows, width), 0)
        col = spot_ref[3] + offset + lax.broadcasted_iota(jnp.int32, (field_rows, width), 1)
        inside = (row >= 0) & (row < spot_ref[4]) & (col >= 0) & (col < spot_ref[5])
        sensitivity = jnp.where(inside, sensitivity, 0.0)
        ordered = (sensitivity, swapped(sensitivity))

        def product(k):
            return (2.0 * weight_ref[k]) * ordered[k % 2] * field_ref[k, :, :width]

        def keep(k, part):
            straight, turned = (part, swapped(part))[:: 1 - 2 * (k % 2)]
            ghigh_ref[k, :, place] = straight.astype(BF16)
            gturn_ref[k, :, place] = split(turned)[1]

        if last:
            half = left[:field_rows]
            for quad in range(KERNELS // 4):
                four = range(4 * quad, 4 * quad + 4)
                each = [product(k) for k in four]
                high, low = split(
                    jnp.concatenate(
                        [jnp.where(half, each[0], each[1]), jnp.where(half, each[2], each[3])],
                        axis=1,
                    )
                )
                near = [brow_ref[k, v, :, :field_rows] for k in four for v in range(2)]
                both = mm(jnp.concatenate(near, axis=0), high)
                more = mm(jnp.concatenate(near[::2], axis=0), low)
                for h, k in enumerate(four):
                    lanes = slice((h // 2) * LANES, (h // 2 + 1) * LANES)
                    start = 2 * h * rows_here
                    part = both[start : start + rows_here, lanes]
                    part = part + both[start + rows_here : start + 2 * rows_here, lanes]
                    keep(k, part + more[h * rows_here : (h + 1) * rows_here, lanes])
            return
        for k in range(KERNELS):
            high, low = split(product(k))
            near = brow_ref[k, 0, :, :field_rows]
            both = mm(jnp.concatenate([near, brow_ref[k, 1, :, :field_rows]], axis=0), high)
            keep(k, both[:rows_here] + both[rows_here:] + mm(near, low))

    supers = tile_cols * TILE // WIDE

    @pl.loop(0, supers)
    def _(jj):
        columns(jj * WIDE, WIDE)

    columns(supers * WIDE, LANES)

    lower = lax.broadcasted_iota(jnp.int32, (rows_here, LANES), 1) < LANES // 2

    def spread_back(k):
        stacked = []
        for jj in range(supers):
            c0 = WIDE * jj
            high = [ghigh_ref[k, :, c0 + LANES * n : c0 + LANES * (n + 1)] for n in range(3)]
            turn = [gturn_ref[k, :, c0 + LANES * n : c0 + LANES * (n + 1)] for n in range(3)]
            row = [
                high[0],
                high[1],
                jnp.where(lower, high[2], turn[0]),
                jnp.where(lower, turn[0], turn[1]),
                jnp.where(lower, turn[1], turn[2]),
                *high,
            ]
            stacked.append(jnp.concatenate(row, axis=1))
        return mm(jnp.concatenate(stacked, axis=0), bcol_ref[k])

    def add(part, fresh):
        for g in range(groups):
            rows = slice(g * rows_here, (g + 1) * rows_here)
            top = (g // 2) * rows_here
            piece = part[top : top + rows_here, LANES * (g % 2) : LANES * (g % 2 + 1)]
            grad_ref[rows, :] = piece if fresh else grad_ref[rows, :] + piece

    add(spread_back(0), True)

    @pl.loop(1, KERNELS)
    def _(k):
        add(spread_back(k), False)

    @pl.loop(0, tile_rows)
    def _(a):
        for g in range(groups):
            base = g * rows_here + a * TILE
            parts = [grad_ref[pl.ds(base + s, 8, stride=4), :] for s in range(4)]
            for b, tile in enumerate(transpose_blocks(parts, block)):
                place = pl.multiple_of(index_ref[a, 4 * g + b] * 8, 8)
                out_ref[pl.ds(place, 8), :] = tile


def to_rows(x):
    count = x.shape[0]
    return x.reshape(count // 8, 8, 8, LANES).transpose(0, 2, 1, 3).reshape(count * 8, LANES)


def from_rows(x):
    count = x.shape[0] // 8
    return x.reshape(count // 8, 8, 8, LANES).transpose(0, 2, 1, 3).reshape(count, 8 * LANES)


def kernel_call(body, name, shapes, scratch, scalars, inputs, unread=(), megabytes=8, out_space=pltpu.VMEM):
    single = not isinstance(shapes, list)
    spec = pl.BlockSpec(memory_space=pltpu.VMEM)
    outs = [shapes] if single else shapes
    result = pl.pallas_call(
        body,
        out_shape=outs,
        in_specs=[pl.BlockSpec(memory_space=pltpu.SMEM)] * len(scalars)
        + [spec] * len(inputs)
        + [pl.BlockSpec(memory_space=pl.ANY)] * len(unread),
        out_specs=[pl.BlockSpec(memory_space=out_space)] * len(outs),
        scratch_shapes=scratch,
        compiler_params=pltpu.CompilerParams(vmem_limit_bytes=megabytes * 2**20),
        name=name,
    )(*scalars, *inputs, *unread)
    return result[0] if single else result


def pairs(one, other, axis):
    count = lax.axis_size(axis)
    out = []
    for x, start in ((one, 0), (other, 1)):
        swap = [(i, i + 1) for i in range(start, count - 1, 2)]
        out.append(lax.ppermute(x, axis, swap + [(j, i) for i, j in swap]))
    return out


def doubled(table, axis):
    count = lax.axis_size(axis)
    bit = 1
    while bit < count:
        got = lax.ppermute(table, axis, [(i, i ^ bit) for i in range(count)])
        table = jnp.concatenate([table, got], axis=0)
        bit *= 2
    return table


def requests(match, value, capacity):
    rank = jnp.cumsum(match.astype(jnp.int32), axis=1) - 1
    hit = match[:, None, :] & (rank[:, None, :] == jnp.arange(capacity)[None, :, None])
    return jnp.max(jnp.where(hit, value[:, None, :], -1), axis=2)


def shards(cells, instance_cell, target, row_taps, col_taps, kernel_weight):
    deep, cores, cols = lax.axis_size("deep"), lax.axis_size("core"), lax.axis_size("col")
    everyone = ("deep", "core", "col")
    plane = ("core", "col")
    peers = cores * cols
    slots = cells.shape[0]
    tile_rows, tile_cols = instance_cell.shape
    tiles_here = tile_rows * tile_cols
    height, breadth = target.shape
    owners = deep * peers
    capacity = 2 * ((tiles_here + owners - 1) // owners)
    f32 = lambda *shape: jax.ShapeDtypeStruct(shape, F32)

    flat = to_rows(cells)
    ordered, named = kernel_call(
        spread_kernel,
        "spread",
        [f32(slots * 8, LANES), jax.ShapeDtypeStruct((1, tiles_here), jnp.int32)],
        [],
        [],
        [flat, instance_cell],
    )
    near = doubled(doubled(named, "col"), "core")
    levels = [ordered]
    for e in range(1, deep):
        levels.append(lax.ppermute(ordered, "deep", [(i, i ^ e) for i in range(deep)]))
    row_axes = ("deep", "core")
    my_row, my_col = lax.axis_index(row_axes), lax.axis_index("col")
    me = jnp.stack(
        [
            lax.axis_index(plane),
            lax.axis_index(everyone),
            my_row * height - HALF,
            my_col * breadth - HALF,
            jnp.int32(deep * cores * height),
            jnp.int32(cols * breadth),
            my_row % 2,
            my_col % 2,
        ]
    ).astype(jnp.int32)
    my_deep = lax.axis_index("deep")
    here = ((my_deep ^ jnp.arange(deep)) * peers + me[0])[None, :, None]
    match = (near // slots)[:, None, :] == here
    slot = jnp.broadcast_to((near % slots)[:, None, :], match.shape)
    asked = requests(
        match.reshape(peers * deep, tiles_here), slot.reshape(peers * deep, tiles_here), capacity
    ).reshape(peers, deep, capacity)
    waves = make_waves(row_taps, col_taps)
    size = peers * deep * capacity * 8
    packed = kernel_call(
        pack_kernel,
        "pack",
        f32(size, LANES),
        [pltpu.VMEM((size, LANES), F32), pltpu.SemaphoreType.DMA((peers,))],
        [asked, me],
        levels,
        [waves],
        out_space=pl.ANY,
    )
    odd = me[6] > 0
    head, foot = target[:HALF], target[height - HALF :]
    packed, near, one, other = lax.optimization_barrier(
        (packed, near, jnp.where(odd, head, foot), jnp.where(odd, foot, head))
    )
    one, other = pairs(one, other, row_axes)
    above, below = jnp.where(odd, one, other), jnp.where(odd, other, one)
    arrived = lax.all_to_all(packed, plane, split_axis=0, concat_axis=0, tiled=True)

    everything = doubled(near, "deep")
    wanted = requests(everything // slots == me[1], everything % slots, capacity)
    mine = named[0] // slots
    earlier = jnp.tri(tiles_here, k=-1, dtype=bool)

    def place(group, size):
        same = (group[:, None] == group[None, :]) & earlier
        where = group * size + jnp.sum(same.astype(jnp.int32), axis=1)
        return where.reshape(tile_rows, tile_cols)

    home = place(mine, capacity)
    theirs = home // capacity
    level = my_deep ^ (theirs // peers)
    index = (theirs % peers * deep + level) * capacity + home % capacity
    wide = 2 * HALF
    quarter = (height + wide) // 4
    edge = f32(height // 2 + wide + quarter, LANES)
    mask, rowa, rowb = kernel_call(
        assemble_kernel,
        "assemble",
        [f32(height, breadth), f32(wide, breadth), f32(wide, breadth)],
        [pltpu.VMEM((height * (breadth // LANES), LANES), F32)],
        [index, me],
        [arrived],
    )
    rowa, rowb = pairs(rowa, rowb, row_axes)
    cola, colb = kernel_call(
        edges_kernel,
        "edges",
        [edge, edge],
        [pltpu.VMEM((2, 4, quarter, LANES), F32)],
        [me],
        [mask, rowa, rowb, target, above, below],
        [wanted],
    )
    cola, colb = pairs(cola, colb, "col")
    field_rows = height + 2 * HALF
    returned = kernel_call(
        image_kernel,
        "image",
        f32(owners * capacity * 8, LANES),
        [
            pltpu.VMEM((KERNELS // 2, 2, 2, LANES, LANES), BF16),
            pltpu.VMEM((KERNELS, 2, field_rows, 256), BF16),
            pltpu.VMEM((KERNELS, 2, LANES, 256), BF16),
            pltpu.VMEM((KERNELS, 1024, WIDE), BF16),
            pltpu.VMEM((field_rows, breadth + 128), F32),
            pltpu.VMEM((height + 4 * HALF, breadth + 128), BF16),
            pltpu.VMEM((height + 4 * HALF, breadth + 128), BF16),
            pltpu.VMEM((height + 4 * HALF, breadth), BF16),
            pltpu.VMEM((height + 4 * HALF, breadth), BF16),
            pltpu.VMEM((KERNELS, field_rows, WIDE), F32),
            pltpu.VMEM((KERNELS, height, breadth + 128), BF16),
            pltpu.VMEM((KERNELS, height, breadth + 128), BF16),
            pltpu.VMEM((height * (breadth // LANES), LANES), F32),
        ],
        [home, me, kernel_weight],
        [mask, rowa, rowb, cola, colb, target, above, below, waves],
        megabytes=36,
    )
    back = lax.all_to_all(returned, everyone, split_axis=0, concat_axis=0, tiled=True)
    stepped = kernel_call(
        step_kernel,
        "step",
        f32(slots * 8, LANES),
        [pltpu.VMEM((slots * 8, LANES), F32)] * 4,
        [wanted, me],
        [flat, back],
    )
    return from_rows(stepped)


def solution(mesh):
    rows, cols = mesh.devices.shape
    finer = Mesh(mesh.devices.reshape(rows // 2, 2, cols), ("deep", "core", "col"))
    row = ("deep", "core")
    placed = (P((*row, "col"), None), P(row, "col"), P(row, "col"), P(), P(), P())
    return jax.shard_map(
        shards, mesh=finer, in_specs=placed, out_specs=P((*row, "col"), None), check_vma=False
    )
```

```python
import jax
import jax.numpy as jnp
from jax import lax
from jax.experimental import pallas as pl
from jax.experimental.pallas import tpu as pltpu
from jax.sharding import Mesh
from jax.sharding import PartitionSpec as P

TILE = 32
TAPS = 65
HALF = 32
KERNELS = 8
LANES = 128
WIDE = 256

STEEPNESS = 4.0
THRESHOLD = 0.3
STEP_RATE = 0.5

F32 = jnp.float32
BF16 = jnp.bfloat16


def split(x):
    high = x.astype(BF16)
    return high, (x - high.astype(F32)).astype(BF16)


def mm(a, b):
    return jnp.dot(a, b, preferred_element_type=F32)


def build_bands(wave_ref, fcol_ref, frow_ref, brow_ref, bcol_ref):
    rows = lax.broadcasted_iota(jnp.int32, (LANES, LANES), 0)
    lanes = lax.broadcasted_iota(jnp.int32, (LANES, LANES), 1)
    zero = jnp.zeros((LANES, LANES), F32)

    def circular(index, start):
        base = jnp.broadcast_to(wave_ref[pl.ds(index, 1), :], (LANES, LANES))
        return pltpu.roll(base, start, 1, stride=1, stride_axis=0)

    def put(ref, kernel, r0, c0, block, height=LANES, breadth=LANES):
        high, low = split(block)
        ref[kernel, 0, r0 : r0 + height, c0 : c0 + breadth] = high[:height, :breadth]
        ref[kernel, 1, r0 : r0 + height, c0 : c0 + breadth] = low[:height, :breadth]

    half = lanes < LANES // 2

    @pl.loop(0, KERNELS)
    def _(k):
        near = circular(k, 0)
        put(frow_ref, k, 0, 0, jnp.where(lanes >= rows, near, zero))
        put(frow_ref, k, 0, LANES, jnp.where(lanes < rows, near, zero))
        put(frow_ref, k, LANES, 0, zero, 64)
        put(frow_ref, k, LANES, LANES, jnp.where(lanes >= rows, near, zero), 64)
        near = circular(2 * KERNELS + k, 0)
        put(brow_ref, k, 0, 0, jnp.where(lanes >= rows, near, zero))
        put(brow_ref, k, 0, LANES, jnp.where(lanes < rows, near, zero))
        near = circular(KERNELS + k, LANES // 2)
        diagonal = jnp.where(rows >= lanes, near, zero)
        beyond = jnp.where(rows < lanes, near, zero)
        for c0, blocks in ((0, (diagonal, beyond, zero)), (LANES, (zero, diagonal, beyond))):
            for n, block in enumerate(blocks):
                height = LANES if n < 2 else LANES // 2
                high, low = split(block)
                for start, piece in ((0, high), (320, high), (640, low)):
                    r0 = start + n * LANES
                    bcol_ref[k, r0 : r0 + height, c0 : c0 + LANES] = piece[:height]
        bcol_ref[k, 960:, :] = jnp.zeros((64, WIDE), BF16)

    @pl.loop(0, KERNELS // 2)
    def _(pair):
        first, second = 3 * KERNELS + 2 * pair, 3 * KERNELS + 2 * pair + 1
        for order, (one, other) in enumerate(((first, second), (second, first))):
            block = jnp.where(half, circular(one, LANES // 2), circular(other, 0))
            high, low = split(block)
            fcol_ref[pair, order, 0] = high
            fcol_ref[pair, order, 1] = low


def make_waves(row_taps, col_taps):
    taps = jnp.concatenate([row_taps, col_taps], axis=0)
    taps = jnp.concatenate([taps, taps[:, ::-1]], axis=0)
    return jnp.pad(taps, [(0, 0), (0, LANES - TAPS)])


def transpose_blocks(parts, block):
    turned = []
    for d in range(4):
        x = parts[d]
        for s in range(1, 4):
            x = jnp.where(block == s, parts[(s + d) % 4], x)
        turned.append(pltpu.roll(x, 32 * d, 1) if d else x)
    out = []
    for s in range(4):
        x = turned[(-s) % 4]
        for b in range(1, 4):
            x = jnp.where(block == b, turned[(b - s) % 4], x)
        out.append(x)
    return out


def spread_kernel(cells_ref, instance_ref, out_ref, named_ref):
    for c in range(out_ref.shape[0] // 8):
        out_ref[c * 8 : c * 8 + 8, :] = cells_ref[pl.ds((c // 8) * 64 + c % 8, 8, stride=8), :]
    rows = [instance_ref[a : a + 1, :] for a in range(instance_ref.shape[0])]
    named_ref[...] = jnp.concatenate(rows, axis=1)


def pack_kernel(asked_ref, me_ref, *rest):
    out_ref, stage_ref, sems = rest[-3:]
    peers, planes, capacity = asked_ref.shape
    chunk = planes * capacity * 8

    def send(i):
        rows = pl.ds(pl.multiple_of((me_ref[0] ^ i) * chunk, chunk), chunk)
        return pltpu.make_async_copy(stage_ref.at[rows, :], out_ref.at[rows, :], sems.at[i])

    @pl.loop(0, peers)
    def _(i):
        base = (me_ref[0] ^ i) * planes * capacity
        for e in range(planes):
            for j in range(capacity):
                asked = jnp.maximum(asked_ref[i, e, j], 0)
                tile = rest[e][pl.ds(pl.multiple_of(asked * 8, 8), 8), :]
                there = (base + e * capacity + j) * 8
                stage_ref[pl.ds(pl.multiple_of(there, 8), 8), :] = tile
        send(i).start()

    @pl.loop(0, peers)
    def _(i):
        send(i).wait()


def step_kernel(asked_ref, me_ref, cells_ref, tiles_ref, out_ref, *totals):
    owners, capacity = asked_ref.shape
    nothing = jnp.zeros((8, LANES), F32)
    for total in totals:
        total[...] = jnp.zeros_like(total)

    @pl.loop(0, owners // 2)
    def _(pair):
        for n in range(2 * capacity):
            i, j = pair * 2 + n // capacity, n % capacity
            asked = asked_ref[i, j]
            place = ((me_ref[1] ^ i) * capacity + j) * 8
            tile = tiles_ref[pl.ds(pl.multiple_of(place, 8), 8), :]
            there = pl.ds(pl.multiple_of(jnp.maximum(asked, 0) * 8, 8), 8)
            total = totals[n % len(totals)]
            total[there, :] += jnp.where(asked >= 0, tile, nothing)

    for c in range(out_ref.shape[0] // 8):
        rows = slice(c * 8, c * 8 + 8)
        total = totals[0][rows, :]
        for other in totals[1:]:
            total = total + other[rows, :]
        there = pl.ds((c // 8) * 64 + c % 8, 8, stride=8)
        out_ref[there, :] = cells_ref[there, :] - STEP_RATE * total


def target_strips(target_ref, top_ref, bottom_ref, strip):
    height = target_ref.shape[0]
    quarter = (height + 2 * HALF) // 4
    for row in range(0, height + 2 * HALF, 16):
        if row < HALF:
            ref, start = top_ref, row
        elif row < HALF + height:
            ref, start = target_ref, row - HALF
        else:
            ref, start = bottom_ref, row - HALF - height
        strip(row, ref, slice(start, start + 16), row // quarter, row % quarter)


def assemble_kernel(index_ref, spot_ref, tiles_ref, mask_ref, rowa_ref, rowb_ref, turned_ref):
    odd_row = spot_ref[6] > 0
    tile_rows, tile_cols = index_ref.shape
    height = tile_rows * TILE
    wide = 2 * HALF
    groups = tile_cols // 4
    block = lax.broadcasted_iota(jnp.int32, (8, LANES), 1) // 32

    @pl.loop(0, tile_rows)
    def _(a):
        for g in range(groups):
            parts = [
                tiles_ref[pl.ds(pl.multiple_of(index_ref[a, 4 * g + b] * 8, 8), 8), :]
                for b in range(4)
            ]
            for s, piece in enumerate(transpose_blocks(parts, block)):
                turned_ref[pl.ds(g * height + a * TILE + s, 8, stride=4), :] = piece

    for g in range(groups):
        lanes = slice(LANES * g, LANES * (g + 1))
        piece = turned_ref[g * height : (g + 1) * height, :]
        mask_ref[:, lanes] = piece
        rowa_ref[:, lanes] = jnp.where(odd_row, piece[:wide], piece[height - wide :])
        rowb_ref[:, lanes] = jnp.where(odd_row, piece[height - wide :], piece[:wide])


def edges_kernel(spot_ref, mask_ref, rowa_ref, rowb_ref, target_ref, ttop_ref, tbottom_ref, *rest):
    cola_ref, colb_ref, pack_ref = rest[-3:]
    odd_row, odd_col = spot_ref[6] > 0, spot_ref[7] > 0
    height, breadth = mask_ref.shape
    wide = 2 * HALF
    half = height // 2
    packed = half + wide
    lane = lax.broadcasted_iota(jnp.int32, (packed, LANES), 1)
    head, tail = slice(0, LANES), slice(breadth - LANES, breadth)

    def halves(lanes):
        one, other = rowa_ref[:, lanes], rowb_ref[:, lanes]
        top, bottom = jnp.where(odd_row, one, other), jnp.where(odd_row, other, one)
        upper = jnp.concatenate([top, mask_ref[:half, lanes]], axis=0)
        return upper, jnp.concatenate([mask_ref[half:, lanes], bottom], axis=0)

    upper, lower = halves(head)
    left = jnp.where(lane < wide, upper, pltpu.roll(lower, wide, 1))
    upper, lower = halves(tail)
    right = jnp.where(lane < wide, pltpu.roll(upper, wide, 1), lower)
    cola_ref[:packed, :] = jnp.where(odd_col, left, right)
    colb_ref[:packed, :] = jnp.where(odd_col, right, left)

    quarter = (height + 2 * HALF) // 4

    def strip(row, ref, rows, part, inner):
        for side, lanes in enumerate((head, tail)):
            shift = (HALF * (part + side)) % LANES
            piece = ref[rows, lanes]
            pack_ref[side, part, inner : inner + 16, :] = (
                pltpu.roll(piece, shift, 1) if shift else piece
            )

    target_strips(target_ref, ttop_ref, tbottom_ref, strip)
    part_of = lax.broadcasted_iota(jnp.int32, (quarter, LANES), 1) // HALF
    sides = []
    for side in range(2):
        piece = pack_ref[side, 0]
        for part in range(1, 4):
            piece = jnp.where(part_of == part, pack_ref[side, part], piece)
        sides.append(piece)
    cola_ref[packed:, :] = jnp.where(odd_col, sides[0], sides[1])
    colb_ref[packed:, :] = jnp.where(odd_col, sides[1], sides[0])


def image_kernel(
    index_ref,
    spot_ref,
    weight_ref,
    mask_ref,
    rowa_ref,
    rowb_ref,
    cola_ref,
    colb_ref,
    own_ref,
    ttop_ref,
    tbottom_ref,
    wave_ref,
    out_ref,
    fcol_ref,
    frow_ref,
    brow_ref,
    bcol_ref,
    target_ref,
    mhigh_ref,
    mlow_ref,
    nhigh_ref,
    nlow_ref,
    field_ref,
    ghigh_ref,
    gturn_ref,
    grad_ref,
):
    tile_rows, tile_cols = index_ref.shape
    rows_here = tile_rows * TILE
    high_rows = rows_here + 4 * HALF
    field_rows = rows_here + 2 * HALF
    groups = tile_cols // 4
    wide = 2 * HALF
    block = lax.broadcasted_iota(jnp.int32, (8, LANES), 1) // 32
    odd_row, odd_col = spot_ref[6] > 0, spot_ref[7] > 0
    build_bands(wave_ref, fcol_ref, frow_ref, brow_ref, bcol_ref)

    lane = lax.broadcasted_iota(jnp.int32, (wide, LANES), 1)
    for rows in range(0, high_rows, wide):
        outer = rows == 0 or rows == high_rows - wide
        from_a = odd_row if rows == 0 else jnp.logical_not(odd_row)
        half = high_rows // 2
        edge = slice(rows % half, rows % half + wide)
        one, other = cola_ref[edge, :], colb_ref[edge, :]
        turned, final = jnp.where(odd_col, one, other), jnp.where(odd_col, other, one)
        if rows < half:
            final = pltpu.roll(final, wide, 1)
        else:
            turned = pltpu.roll(turned, wide, 1)
        for g in range(groups + 1):
            fresh = final
            if g < groups:
                lanes = slice(LANES * g, LANES * (g + 1))
                if outer:
                    piece = jnp.where(from_a, rowa_ref[:, lanes], rowb_ref[:, lanes])
                else:
                    piece = mask_ref[rows - wide : rows, lanes]
                high, low = split(piece)
                nhigh_ref[rows : rows + wide, LANES * g : LANES * (g + 1)] = high
                nlow_ref[rows : rows + wide, LANES * g : LANES * (g + 1)] = low
                fresh = pltpu.roll(piece, wide, 1)
            high, low = split(jnp.where(lane < wide, turned, fresh))
            mhigh_ref[rows : rows + wide, LANES * g : LANES * (g + 1)] = high
            mlow_ref[rows : rows + wide, LANES * g : LANES * (g + 1)] = low
            turned = fresh
    packed = high_rows // 2
    near_lane = lax.broadcasted_iota(jnp.int32, (16, LANES), 1)

    def strip(row, ref, rows, part, inner):
        edge = slice(packed + inner, packed + inner + 16)
        back, ahead = (-HALF * part) % LANES, (HALF - HALF * part) % LANES
        one, other = cola_ref[edge, :], colb_ref[edge, :]
        turned, final = jnp.where(odd_col, one, other), jnp.where(odd_col, other, one)
        turned = pltpu.roll(turned, back, 1) if back else turned
        final = pltpu.roll(final, ahead, 1) if ahead else final
        for g in range(groups + 1):
            fresh = final
            if g < groups:
                fresh = pltpu.roll(ref[rows, LANES * g : LANES * (g + 1)], HALF, 1)
            target_ref[row : row + 16, LANES * g : LANES * (g + 1)] = jnp.where(
                near_lane < HALF, turned, fresh
            )
            turned = fresh

    target_strips(own_ref, ttop_ref, tbottom_ref, strip)

    def swapped(x):
        pieces = [
            pltpu.roll(x[:, c : c + LANES], LANES // 2, 1) for c in range(0, x.shape[1], LANES)
        ]
        return pieces[0] if len(pieces) == 1 else jnp.concatenate(pieces, axis=1)

    def columns(offset, width):
        blocks = width // LANES
        last = blocks == 1

        def windows(high_ref, low_ref):
            rows = []
            for j in range(blocks):
                place = pl.ds(pl.multiple_of(offset + j * LANES, LANES), LANES)
                high, low = high_ref[:, place], low_ref[:, place]
                rows.append(jnp.concatenate([high, low, high], axis=1))
            return rows[0] if last else jnp.concatenate(rows, axis=0)

        even_rows = windows(mhigh_ref, mlow_ref)
        odd_rows = None if last else windows(nhigh_ref, nlow_ref)
        left = lax.broadcasted_iota(jnp.int32, (high_rows, LANES), 1) < LANES // 2

        def band(quad, order):
            both = [
                jnp.concatenate(
                    [fcol_ref[2 * quad, order, v], fcol_ref[2 * quad + 1, order, v]], axis=1
                )
                for v in range(2)
            ]
            return jnp.concatenate([both[0], both[0], both[1]], axis=0)

        sums = [None, None]
        for quad in range(KERNELS // 4):
            even = mm(even_rows, band(quad, 0))
            odd = even if last else mm(odd_rows, band(quad, 1))
            four = range(4 * quad, 4 * quad + 4)
            if last:
                high, low = split(even)
                both = mm(jnp.concatenate([frow_ref[k, v] for k in four for v in range(2)], 0), high)
                more = mm(jnp.concatenate([frow_ref[k, 0] for k in four], axis=0), low)
            for h, k in enumerate(four):
                lanes = slice((h // 2) * LANES, (h // 2 + 1) * LANES)
                if last:
                    start = 2 * h * field_rows
                    field = both[start : start + field_rows, lanes]
                    field = field + both[start + field_rows : start + 2 * field_rows, lanes]
                    field = field + more[h * field_rows : (h + 1) * field_rows, lanes]
                else:
                    pieces = []
                    for j in range(blocks):
                        rows = slice(j * high_rows, (j + 1) * high_rows)
                        one, other = even[rows, lanes], odd[rows, lanes]
                        one, other = (other, one) if h % 2 else (one, other)
                        pieces.append(jnp.where(left, one, other))
                    high, low = split(jnp.concatenate(pieces, axis=1))
                    both = mm(jnp.concatenate([frow_ref[k, 0], frow_ref[k, 1]], axis=0), high)
                    field = both[:field_rows] + both[field_rows:] + mm(frow_ref[k, 0], low)
                field_ref[k, :, :width] = field
                term = weight_ref[k] * field * field
                sums[h % 2] = term if sums[h % 2] is None else sums[h % 2] + term
        intensity = sums[0] + swapped(sums[1])
        resist = 1.0 / (1.0 + jnp.exp(-STEEPNESS * (intensity - THRESHOLD)))
        place = pl.ds(pl.multiple_of(offset, LANES), width)
        target = target_ref[:, place]
        sensitivity = 2.0 * (resist - target) * STEEPNESS * resist * (1.0 - resist)
        row = spot_ref[2] + lax.broadcasted_iota(jnp.int32, (field_rows, width), 0)
        col = spot_ref[3] + offset + lax.broadcasted_iota(jnp.int32, (field_rows, width), 1)
        inside = (row >= 0) & (row < spot_ref[4]) & (col >= 0) & (col < spot_ref[5])
        sensitivity = jnp.where(inside, sensitivity, 0.0)
        ordered = (sensitivity, swapped(sensitivity))

        def product(k):
            return (2.0 * weight_ref[k]) * ordered[k % 2] * field_ref[k, :, :width]

        def keep(k, part):
            straight, turned = (part, swapped(part))[:: 1 - 2 * (k % 2)]
            ghigh_ref[k, :, place] = straight.astype(BF16)
            gturn_ref[k, :, place] = split(turned)[1]

        if last:
            half = left[:field_rows]
            for quad in range(KERNELS // 4):
                four = range(4 * quad, 4 * quad + 4)
                each = [product(k) for k in four]
                high, low = split(
                    jnp.concatenate(
                        [jnp.where(half, each[0], each[1]), jnp.where(half, each[2], each[3])],
                        axis=1,
                    )
                )
                near = [brow_ref[k, v, :, :field_rows] for k in four for v in range(2)]
                both = mm(jnp.concatenate(near, axis=0), high)
                more = mm(jnp.concatenate(near[::2], axis=0), low)
                for h, k in enumerate(four):
                    lanes = slice((h // 2) * LANES, (h // 2 + 1) * LANES)
                    start = 2 * h * rows_here
                    part = both[start : start + rows_here, lanes]
                    part = part + both[start + rows_here : start + 2 * rows_here, lanes]
                    keep(k, part + more[h * rows_here : (h + 1) * rows_here, lanes])
            return
        for k in range(KERNELS):
            high, low = split(product(k))
            near = brow_ref[k, 0, :, :field_rows]
            both = mm(jnp.concatenate([near, brow_ref[k, 1, :, :field_rows]], axis=0), high)
            keep(k, both[:rows_here] + both[rows_here:] + mm(near, low))

    supers = tile_cols * TILE // WIDE

    @pl.loop(0, supers)
    def _(jj):
        columns(jj * WIDE, WIDE)

    columns(supers * WIDE, LANES)

    lower = lax.broadcasted_iota(jnp.int32, (rows_here, LANES), 1) < LANES // 2

    def windows_of(k, c0):
        high = [ghigh_ref[k, :, c0 + LANES * n : c0 + LANES * (n + 1)] for n in range(3)]
        turn = [gturn_ref[k, :, c0 + LANES * n : c0 + LANES * (n + 1)] for n in range(3)]
        return [
            high[0],
            high[1],
            jnp.where(lower, high[2], turn[0]),
            jnp.where(lower, turn[0], turn[1]),
            jnp.where(lower, turn[1], turn[2]),
            *high,
        ]

    together = 4
    grad_ref[...] = jnp.zeros_like(grad_ref)

    @pl.loop(0, KERNELS // together)
    def _(part_of):
        ks = [part_of * together + n for n in range(together)]
        stacked = [
            jnp.concatenate([x for k in ks for x in windows_of(k, WIDE * jj)], axis=1)
            for jj in range(supers)
        ]
        band = jnp.concatenate([bcol_ref[k] for k in ks], axis=0)
        part = mm(jnp.concatenate(stacked, axis=0), band)
        for g in range(groups):
            rows = slice(g * rows_here, (g + 1) * rows_here)
            top = (g // 2) * rows_here
            grad_ref[rows, :] += part[
                top : top + rows_here, LANES * (g % 2) : LANES * (g % 2 + 1)
            ]

    @pl.loop(0, tile_rows)
    def _(a):
        for g in range(groups):
            base = g * rows_here + a * TILE
            parts = [grad_ref[pl.ds(base + s, 8, stride=4), :] for s in range(4)]
            for b, tile in enumerate(transpose_blocks(parts, block)):
                place = pl.multiple_of(index_ref[a, 4 * g + b] * 8, 8)
                out_ref[pl.ds(place, 8), :] = tile


def to_rows(x):
    count = x.shape[0]
    return x.reshape(count // 8, 8, 8, LANES).transpose(0, 2, 1, 3).reshape(count * 8, LANES)


def from_rows(x):
    count = x.shape[0] // 8
    return x.reshape(count // 8, 8, 8, LANES).transpose(0, 2, 1, 3).reshape(count, 8 * LANES)


def kernel_call(body, name, shapes, scratch, scalars, inputs, unread=(), megabytes=8, out_space=pltpu.VMEM):
    single = not isinstance(shapes, list)
    spec = pl.BlockSpec(memory_space=pltpu.VMEM)
    outs = [shapes] if single else shapes
    result = pl.pallas_call(
        body,
        out_shape=outs,
        in_specs=[pl.BlockSpec(memory_space=pltpu.SMEM)] * len(scalars)
        + [spec] * len(inputs)
        + [pl.BlockSpec(memory_space=pl.ANY)] * len(unread),
        out_specs=[pl.BlockSpec(memory_space=out_space)] * len(outs),
        scratch_shapes=scratch,
        compiler_params=pltpu.CompilerParams(vmem_limit_bytes=megabytes * 2**20),
        name=name,
    )(*scalars, *inputs, *unread)
    return result[0] if single else result


def pairs(one, other, axis):
    count = lax.axis_size(axis)

    def exchange(x, start):
        swap = [(i, i + 1) for i in range(start, count - 1, 2)]
        return lax.ppermute(x, axis, swap + [(j, i) for i, j in swap])

    got = exchange(other, 1)
    return exchange(one, 0), got


def doubled(table, axis):
    count = lax.axis_size(axis)
    bit = 1
    while bit < count:
        got = lax.ppermute(table, axis, [(i, i ^ bit) for i in range(count)])
        table = jnp.concatenate([table, got], axis=0)
        bit *= 2
    return table


def requests(match, value, capacity):
    rank = jnp.cumsum(match.astype(jnp.int32), axis=1) - 1
    hit = match[:, None, :] & (rank[:, None, :] == jnp.arange(capacity)[None, :, None])
    return jnp.max(jnp.where(hit, value[:, None, :], -1), axis=2)


def shards(cells, instance_cell, target, row_taps, col_taps, kernel_weight):
    deep, cores, cols = lax.axis_size("deep"), lax.axis_size("core"), lax.axis_size("col")
    everyone = ("deep", "core", "col")
    plane = ("core", "col")
    peers = cores * cols
    slots = cells.shape[0]
    tile_rows, tile_cols = instance_cell.shape
    tiles_here = tile_rows * tile_cols
    height, breadth = target.shape
    owners = deep * peers
    capacity = 2 * ((tiles_here + owners - 1) // owners)
    f32 = lambda *shape: jax.ShapeDtypeStruct(shape, F32)

    flat = to_rows(cells)
    ordered, named = kernel_call(
        spread_kernel,
        "spread",
        [f32(slots * 8, LANES), jax.ShapeDtypeStruct((1, tiles_here), jnp.int32)],
        [],
        [],
        [flat, instance_cell],
    )
    near = doubled(doubled(named, "col"), "core")
    levels = [ordered]
    for e in range(1, deep):
        levels.append(lax.ppermute(ordered, "deep", [(i, i ^ e) for i in range(deep)]))
    row_axes = ("deep", "core")
    my_row, my_col = lax.axis_index(row_axes), lax.axis_index("col")
    me = jnp.stack(
        [
            lax.axis_index(plane),
            lax.axis_index(everyone),
            my_row * height - HALF,
            my_col * breadth - HALF,
            jnp.int32(deep * cores * height),
            jnp.int32(cols * breadth),
            my_row % 2,
            my_col % 2,
        ]
    ).astype(jnp.int32)
    my_deep = lax.axis_index("deep")
    here = ((my_deep ^ jnp.arange(deep)) * peers + me[0])[None, :, None]
    match = (near // slots)[:, None, :] == here
    slot = jnp.broadcast_to((near % slots)[:, None, :], match.shape)
    asked = requests(
        match.reshape(peers * deep, tiles_here), slot.reshape(peers * deep, tiles_here), capacity
    ).reshape(peers, deep, capacity)
    waves = make_waves(row_taps, col_taps)
    size = peers * deep * capacity * 8
    packed = kernel_call(
        pack_kernel,
        "pack",
        f32(size, LANES),
        [pltpu.VMEM((size, LANES), F32), pltpu.SemaphoreType.DMA((peers,))],
        [asked, me],
        levels,
        [waves],
        out_space=pl.ANY,
    )
    odd = me[6] > 0
    head, foot = target[:HALF], target[height - HALF :]
    packed, near, one, other = lax.optimization_barrier(
        (packed, near, jnp.where(odd, head, foot), jnp.where(odd, foot, head))
    )
    one, other = pairs(one, other, row_axes)
    above, below = jnp.where(odd, one, other), jnp.where(odd, other, one)
    arrived = lax.all_to_all(packed, plane, split_axis=0, concat_axis=0, tiled=True)

    everything = doubled(near, "deep")
    wanted = requests(everything // slots == me[1], everything % slots, capacity)
    mine = named[0] // slots
    earlier = jnp.tri(tiles_here, k=-1, dtype=bool)

    def place(group, size):
        same = (group[:, None] == group[None, :]) & earlier
        where = group * size + jnp.sum(same.astype(jnp.int32), axis=1)
        return where.reshape(tile_rows, tile_cols)

    home = place(mine, capacity)
    theirs = home // capacity
    level = my_deep ^ (theirs // peers)
    index = (theirs % peers * deep + level) * capacity + home % capacity
    wide = 2 * HALF
    quarter = (height + wide) // 4
    edge = f32(height // 2 + wide + quarter, LANES)
    mask, rowa, rowb = kernel_call(
        assemble_kernel,
        "assemble",
        [f32(height, breadth), f32(wide, breadth), f32(wide, breadth)],
        [pltpu.VMEM((height * (breadth // LANES), LANES), F32)],
        [index, me],
        [arrived],
    )
    rowa, rowb = pairs(rowa, rowb, row_axes)
    cola, colb = kernel_call(
        edges_kernel,
        "edges",
        [edge, edge],
        [pltpu.VMEM((2, 4, quarter, LANES), F32)],
        [me],
        [mask, rowa, rowb, target, above, below],
        [wanted],
    )
    cola, colb = pairs(cola, colb, "col")
    field_rows = height + 2 * HALF
    returned = kernel_call(
        image_kernel,
        "image",
        f32(owners * capacity * 8, LANES),
        [
            pltpu.VMEM((KERNELS // 2, 2, 2, LANES, LANES), BF16),
            pltpu.VMEM((KERNELS, 2, field_rows, 256), BF16),
            pltpu.VMEM((KERNELS, 2, LANES, 256), BF16),
            pltpu.VMEM((KERNELS, 1024, WIDE), BF16),
            pltpu.VMEM((field_rows, breadth + 128), F32),
            pltpu.VMEM((height + 4 * HALF, breadth + 128), BF16),
            pltpu.VMEM((height + 4 * HALF, breadth + 128), BF16),
            pltpu.VMEM((height + 4 * HALF, breadth), BF16),
            pltpu.VMEM((height + 4 * HALF, breadth), BF16),
            pltpu.VMEM((KERNELS, field_rows, WIDE), F32),
            pltpu.VMEM((KERNELS, height, breadth + 128), BF16),
            pltpu.VMEM((KERNELS, height, breadth + 128), BF16),
            pltpu.VMEM((height * (breadth // LANES), LANES), F32),
        ],
        [home, me, kernel_weight],
        [mask, rowa, rowb, cola, colb, target, above, below, waves],
        megabytes=36,
    )
    back = lax.all_to_all(returned, everyone, split_axis=0, concat_axis=0, tiled=True)
    stepped = kernel_call(
        step_kernel,
        "step",
        f32(slots * 8, LANES),
        [pltpu.VMEM((slots * 8, LANES), F32)] * 8,
        [wanted, me],
        [flat, back],
    )
    return from_rows(stepped)


def solution(mesh):
    rows, cols = mesh.devices.shape
    finer = Mesh(mesh.devices.reshape(rows // 2, 2, cols), ("deep", "core", "col"))
    row = ("deep", "core")
    placed = (P((*row, "col"), None), P(row, "col"), P(row, "col"), P(), P(), P())
    return jax.shard_map(
        shards, mesh=finer, in_specs=placed, out_specs=P((*row, "col"), None), check_vma=False
    )
```

```python
import jax
import jax.numpy as jnp
from jax import lax
from jax.experimental import pallas as pl
from jax.experimental.pallas import tpu as pltpu
from jax.sharding import Mesh
from jax.sharding import PartitionSpec as P

TILE = 32
TAPS = 65
HALF = 32
KERNELS = 8
LANES = 128
WIDE = 256

STEEPNESS = 4.0
THRESHOLD = 0.3
STEP_RATE = 0.5

F32 = jnp.float32
BF16 = jnp.bfloat16


def split(x):
    high = x.astype(BF16)
    return high, (x - high.astype(F32)).astype(BF16)


def mm(a, b):
    return jnp.dot(a, b, preferred_element_type=F32)


def build_bands(wave_ref, fcol_ref, frow_ref, brow_ref, bcol_ref):
    rows = lax.broadcasted_iota(jnp.int32, (LANES, LANES), 0)
    lanes = lax.broadcasted_iota(jnp.int32, (LANES, LANES), 1)
    zero = jnp.zeros((LANES, LANES), F32)

    def circular(index, start):
        base = jnp.broadcast_to(wave_ref[pl.ds(index, 1), :], (LANES, LANES))
        return pltpu.roll(base, start, 1, stride=1, stride_axis=0)

    def put(ref, kernel, r0, c0, block, height=LANES, breadth=LANES):
        high, low = split(block)
        ref[kernel, 0, r0 : r0 + height, c0 : c0 + breadth] = high[:height, :breadth]
        ref[kernel, 1, r0 : r0 + height, c0 : c0 + breadth] = low[:height, :breadth]

    half = lanes < LANES // 2

    @pl.loop(0, KERNELS)
    def _(k):
        near = circular(k, 0)
        put(frow_ref, k, 0, 0, jnp.where(lanes >= rows, near, zero))
        put(frow_ref, k, 0, LANES, jnp.where(lanes < rows, near, zero))
        put(frow_ref, k, LANES, 0, zero, 64)
        put(frow_ref, k, LANES, LANES, jnp.where(lanes >= rows, near, zero), 64)
        near = circular(2 * KERNELS + k, 0)
        put(brow_ref, k, 0, 0, jnp.where(lanes >= rows, near, zero))
        put(brow_ref, k, 0, LANES, jnp.where(lanes < rows, near, zero))
        near = circular(KERNELS + k, LANES // 2)
        diagonal = jnp.where(rows >= lanes, near, zero)
        beyond = jnp.where(rows < lanes, near, zero)
        for c0, blocks in ((0, (diagonal, beyond, zero)), (LANES, (zero, diagonal, beyond))):
            for n, block in enumerate(blocks):
                height = LANES if n < 2 else LANES // 2
                high, low = split(block)
                for start, piece in ((0, high), (320, high), (640, low)):
                    r0 = start + n * LANES
                    bcol_ref[k, r0 : r0 + height, c0 : c0 + LANES] = piece[:height]
        bcol_ref[k, 960:, :] = jnp.zeros((64, WIDE), BF16)

    @pl.loop(0, KERNELS // 2)
    def _(pair):
        first, second = 3 * KERNELS + 2 * pair, 3 * KERNELS + 2 * pair + 1
        for order, (one, other) in enumerate(((first, second), (second, first))):
            block = jnp.where(half, circular(one, LANES // 2), circular(other, 0))
            high, low = split(block)
            fcol_ref[pair, order, 0] = high
            fcol_ref[pair, order, 1] = low


def make_waves(row_taps, col_taps):
    taps = jnp.concatenate([row_taps, col_taps], axis=0)
    taps = jnp.concatenate([taps, taps[:, ::-1]], axis=0)
    return jnp.pad(taps, [(0, 0), (0, LANES - TAPS)])


def transpose_blocks(parts, block):
    turned = []
    for d in range(4):
        x = parts[d]
        for s in range(1, 4):
            x = jnp.where(block == s, parts[(s + d) % 4], x)
        turned.append(pltpu.roll(x, 32 * d, 1) if d else x)
    out = []
    for s in range(4):
        x = turned[(-s) % 4]
        for b in range(1, 4):
            x = jnp.where(block == b, turned[(b - s) % 4], x)
        out.append(x)
    return out


def spread_kernel(cells_ref, instance_ref, out_ref, named_ref):
    for c in range(out_ref.shape[0] // 8):
        out_ref[c * 8 : c * 8 + 8, :] = cells_ref[pl.ds((c // 8) * 64 + c % 8, 8, stride=8), :]
    rows = [instance_ref[a : a + 1, :] for a in range(instance_ref.shape[0])]
    named_ref[...] = jnp.concatenate(rows, axis=1)


def pack_kernel(asked_ref, me_ref, *rest):
    out_ref, stage_ref, sems = rest[-3:]
    peers, planes, capacity = asked_ref.shape
    chunk = planes * capacity * 8

    def send(i):
        rows = pl.ds(pl.multiple_of((me_ref[0] ^ i) * chunk, chunk), chunk)
        return pltpu.make_async_copy(stage_ref.at[rows, :], out_ref.at[rows, :], sems.at[i])

    @pl.loop(0, peers)
    def _(i):
        base = (me_ref[0] ^ i) * planes * capacity
        for e in range(planes):
            for j in range(capacity):
                asked = jnp.maximum(asked_ref[i, e, j], 0)
                tile = rest[e][pl.ds(pl.multiple_of(asked * 8, 8), 8), :]
                there = (base + e * capacity + j) * 8
                stage_ref[pl.ds(pl.multiple_of(there, 8), 8), :] = tile
        send(i).start()

    @pl.loop(0, peers)
    def _(i):
        send(i).wait()


def step_kernel(asked_ref, me_ref, cells_ref, tiles_ref, out_ref, *totals):
    owners, capacity = asked_ref.shape
    nothing = jnp.zeros((8, LANES), F32)
    for total in totals:
        total[...] = jnp.zeros_like(total)

    @pl.loop(0, owners // 2)
    def _(pair):
        for n in range(2 * capacity):
            i, j = pair * 2 + n // capacity, n % capacity
            asked = asked_ref[i, j]
            place = ((me_ref[1] ^ i) * capacity + j) * 8
            tile = tiles_ref[pl.ds(pl.multiple_of(place, 8), 8), :]
            there = pl.ds(pl.multiple_of(jnp.maximum(asked, 0) * 8, 8), 8)
            total = totals[n % len(totals)]
            total[there, :] += jnp.where(asked >= 0, tile, nothing)

    for c in range(out_ref.shape[0] // 8):
        rows = slice(c * 8, c * 8 + 8)
        total = totals[0][rows, :]
        for other in totals[1:]:
            total = total + other[rows, :]
        there = pl.ds((c // 8) * 64 + c % 8, 8, stride=8)
        out_ref[there, :] = cells_ref[there, :] - STEP_RATE * total


def target_strips(target_ref, top_ref, bottom_ref, strip):
    height = target_ref.shape[0]
    quarter = (height + 2 * HALF) // 4
    for row in range(0, height + 2 * HALF, 16):
        if row < HALF:
            ref, start = top_ref, row
        elif row < HALF + height:
            ref, start = target_ref, row - HALF
        else:
            ref, start = bottom_ref, row - HALF - height
        strip(row, ref, slice(start, start + 16), row // quarter, row % quarter)


def assemble_kernel(index_ref, spot_ref, tiles_ref, mask_ref, rowa_ref, rowb_ref, turned_ref):
    odd_row = spot_ref[6] > 0
    tile_rows, tile_cols = index_ref.shape
    height = tile_rows * TILE
    wide = 2 * HALF
    groups = tile_cols // 4
    block = lax.broadcasted_iota(jnp.int32, (8, LANES), 1) // 32

    @pl.loop(0, tile_rows)
    def _(a):
        for g in range(groups):
            parts = [
                tiles_ref[pl.ds(pl.multiple_of(index_ref[a, 4 * g + b] * 8, 8), 8), :]
                for b in range(4)
            ]
            for s, piece in enumerate(transpose_blocks(parts, block)):
                turned_ref[pl.ds(g * height + a * TILE + s, 8, stride=4), :] = piece

    for g in range(groups):
        lanes = slice(LANES * g, LANES * (g + 1))
        piece = turned_ref[g * height : (g + 1) * height, :]
        mask_ref[:, lanes] = piece
        rowa_ref[:, lanes] = jnp.where(odd_row, piece[:wide], piece[height - wide :])
        rowb_ref[:, lanes] = jnp.where(odd_row, piece[height - wide :], piece[:wide])


def edges_kernel(spot_ref, mask_ref, rowa_ref, rowb_ref, target_ref, ttop_ref, tbottom_ref, *rest):
    cola_ref, colb_ref, pack_ref = rest[-3:]
    odd_row, odd_col = spot_ref[6] > 0, spot_ref[7] > 0
    height, breadth = mask_ref.shape
    wide = 2 * HALF
    half = height // 2
    packed = half + wide
    lane = lax.broadcasted_iota(jnp.int32, (packed, LANES), 1)
    head, tail = slice(0, LANES), slice(breadth - LANES, breadth)

    def halves(lanes):
        one, other = rowa_ref[:, lanes], rowb_ref[:, lanes]
        top, bottom = jnp.where(odd_row, one, other), jnp.where(odd_row, other, one)
        upper = jnp.concatenate([top, mask_ref[:half, lanes]], axis=0)
        return upper, jnp.concatenate([mask_ref[half:, lanes], bottom], axis=0)

    upper, lower = halves(head)
    left = jnp.where(lane < wide, upper, pltpu.roll(lower, wide, 1))
    upper, lower = halves(tail)
    right = jnp.where(lane < wide, pltpu.roll(upper, wide, 1), lower)
    cola_ref[:packed, :] = jnp.where(odd_col, left, right)
    colb_ref[:packed, :] = jnp.where(odd_col, right, left)

    quarter = (height + 2 * HALF) // 4

    def strip(row, ref, rows, part, inner):
        for side, lanes in enumerate((head, tail)):
            shift = (HALF * (part + side)) % LANES
            piece = ref[rows, lanes]
            pack_ref[side, part, inner : inner + 16, :] = (
                pltpu.roll(piece, shift, 1) if shift else piece
            )

    target_strips(target_ref, ttop_ref, tbottom_ref, strip)
    part_of = lax.broadcasted_iota(jnp.int32, (quarter, LANES), 1) // HALF
    sides = []
    for side in range(2):
        piece = pack_ref[side, 0]
        for part in range(1, 4):
            piece = jnp.where(part_of == part, pack_ref[side, part], piece)
        sides.append(piece)
    cola_ref[packed:, :] = jnp.where(odd_col, sides[0], sides[1])
    colb_ref[packed:, :] = jnp.where(odd_col, sides[1], sides[0])


def image_kernel(
    index_ref,
    spot_ref,
    weight_ref,
    mask_ref,
    rowa_ref,
    rowb_ref,
    cola_ref,
    colb_ref,
    own_ref,
    ttop_ref,
    tbottom_ref,
    wave_ref,
    out_ref,
    fcol_ref,
    frow_ref,
    brow_ref,
    bcol_ref,
    target_ref,
    mhigh_ref,
    mlow_ref,
    nhigh_ref,
    nlow_ref,
    field_ref,
    ghigh_ref,
    gturn_ref,
    grad_ref,
    tiles_ref,
    sent,
):
    tile_rows, tile_cols = index_ref.shape
    rows_here = tile_rows * TILE
    high_rows = rows_here + 4 * HALF
    field_rows = rows_here + 2 * HALF
    groups = tile_cols // 4
    wide = 2 * HALF
    block = lax.broadcasted_iota(jnp.int32, (8, LANES), 1) // 32
    odd_row, odd_col = spot_ref[6] > 0, spot_ref[7] > 0
    build_bands(wave_ref, fcol_ref, frow_ref, brow_ref, bcol_ref)

    lane = lax.broadcasted_iota(jnp.int32, (wide, LANES), 1)
    for rows in range(0, high_rows, wide):
        outer = rows == 0 or rows == high_rows - wide
        from_a = odd_row if rows == 0 else jnp.logical_not(odd_row)
        half = high_rows // 2
        edge = slice(rows % half, rows % half + wide)
        one, other = cola_ref[edge, :], colb_ref[edge, :]
        turned, final = jnp.where(odd_col, one, other), jnp.where(odd_col, other, one)
        if rows < half:
            final = pltpu.roll(final, wide, 1)
        else:
            turned = pltpu.roll(turned, wide, 1)
        for g in range(groups + 1):
            fresh = final
            if g < groups:
                lanes = slice(LANES * g, LANES * (g + 1))
                if outer:
                    piece = jnp.where(from_a, rowa_ref[:, lanes], rowb_ref[:, lanes])
                else:
                    piece = mask_ref[rows - wide : rows, lanes]
                high, low = split(piece)
                nhigh_ref[rows : rows + wide, LANES * g : LANES * (g + 1)] = high
                nlow_ref[rows : rows + wide, LANES * g : LANES * (g + 1)] = low
                fresh = pltpu.roll(piece, wide, 1)
            high, low = split(jnp.where(lane < wide, turned, fresh))
            mhigh_ref[rows : rows + wide, LANES * g : LANES * (g + 1)] = high
            mlow_ref[rows : rows + wide, LANES * g : LANES * (g + 1)] = low
            turned = fresh
    packed = high_rows // 2
    near_lane = lax.broadcasted_iota(jnp.int32, (16, LANES), 1)

    def strip(row, ref, rows, part, inner):
        edge = slice(packed + inner, packed + inner + 16)
        back, ahead = (-HALF * part) % LANES, (HALF - HALF * part) % LANES
        one, other = cola_ref[edge, :], colb_ref[edge, :]
        turned, final = jnp.where(odd_col, one, other), jnp.where(odd_col, other, one)
        turned = pltpu.roll(turned, back, 1) if back else turned
        final = pltpu.roll(final, ahead, 1) if ahead else final
        for g in range(groups + 1):
            fresh = final
            if g < groups:
                fresh = pltpu.roll(ref[rows, LANES * g : LANES * (g + 1)], HALF, 1)
            target_ref[row : row + 16, LANES * g : LANES * (g + 1)] = jnp.where(
                near_lane < HALF, turned, fresh
            )
            turned = fresh

    target_strips(own_ref, ttop_ref, tbottom_ref, strip)

    def swapped(x):
        pieces = [
            pltpu.roll(x[:, c : c + LANES], LANES // 2, 1) for c in range(0, x.shape[1], LANES)
        ]
        return pieces[0] if len(pieces) == 1 else jnp.concatenate(pieces, axis=1)

    def columns(offset, width):
        blocks = width // LANES
        last = blocks == 1

        def windows(high_ref, low_ref):
            rows = []
            for j in range(blocks):
                place = pl.ds(pl.multiple_of(offset + j * LANES, LANES), LANES)
                high, low = high_ref[:, place], low_ref[:, place]
                rows.append(jnp.concatenate([high, low, high], axis=1))
            return rows[0] if last else jnp.concatenate(rows, axis=0)

        even_rows = windows(mhigh_ref, mlow_ref)
        odd_rows = None if last else windows(nhigh_ref, nlow_ref)
        left = lax.broadcasted_iota(jnp.int32, (high_rows, LANES), 1) < LANES // 2

        def band(quad, order):
            both = [
                jnp.concatenate(
                    [fcol_ref[2 * quad, order, v], fcol_ref[2 * quad + 1, order, v]], axis=1
                )
                for v in range(2)
            ]
            return jnp.concatenate([both[0], both[0], both[1]], axis=0)

        sums = [None, None]
        for quad in range(KERNELS // 4):
            even = mm(even_rows, band(quad, 0))
            odd = even if last else mm(odd_rows, band(quad, 1))
            four = range(4 * quad, 4 * quad + 4)
            if last:
                high, low = split(even)
                both = mm(jnp.concatenate([frow_ref[k, v] for k in four for v in range(2)], 0), high)
                more = mm(jnp.concatenate([frow_ref[k, 0] for k in four], axis=0), low)
            for h, k in enumerate(four):
                lanes = slice((h // 2) * LANES, (h // 2 + 1) * LANES)
                if last:
                    start = 2 * h * field_rows
                    field = both[start : start + field_rows, lanes]
                    field = field + both[start + field_rows : start + 2 * field_rows, lanes]
                    field = field + more[h * field_rows : (h + 1) * field_rows, lanes]
                else:
                    pieces = []
                    for j in range(blocks):
                        rows = slice(j * high_rows, (j + 1) * high_rows)
                        one, other = even[rows, lanes], odd[rows, lanes]
                        one, other = (other, one) if h % 2 else (one, other)
                        pieces.append(jnp.where(left, one, other))
                    high, low = split(jnp.concatenate(pieces, axis=1))
                    both = mm(jnp.concatenate([frow_ref[k, 0], frow_ref[k, 1]], axis=0), high)
                    field = both[:field_rows] + both[field_rows:] + mm(frow_ref[k, 0], low)
                field_ref[k, :, :width] = field
                term = weight_ref[k] * field * field
                sums[h % 2] = term if sums[h % 2] is None else sums[h % 2] + term
        intensity = sums[0] + swapped(sums[1])
        resist = 1.0 / (1.0 + jnp.exp(-STEEPNESS * (intensity - THRESHOLD)))
        place = pl.ds(pl.multiple_of(offset, LANES), width)
        target = target_ref[:, place]
        sensitivity = 2.0 * (resist - target) * STEEPNESS * resist * (1.0 - resist)
        row = spot_ref[2] + lax.broadcasted_iota(jnp.int32, (field_rows, width), 0)
        col = spot_ref[3] + offset + lax.broadcasted_iota(jnp.int32, (field_rows, width), 1)
        inside = (row >= 0) & (row < spot_ref[4]) & (col >= 0) & (col < spot_ref[5])
        sensitivity = jnp.where(inside, sensitivity, 0.0)
        ordered = (sensitivity, swapped(sensitivity))

        def product(k):
            return (2.0 * weight_ref[k]) * ordered[k % 2] * field_ref[k, :, :width]

        def keep(k, part):
            straight, turned = (part, swapped(part))[:: 1 - 2 * (k % 2)]
            ghigh_ref[k, :, place] = straight.astype(BF16)
            gturn_ref[k, :, place] = split(turned)[1]

        if last:
            half = left[:field_rows]
            for quad in range(KERNELS // 4):
                four = range(4 * quad, 4 * quad + 4)
                each = [product(k) for k in four]
                high, low = split(
                    jnp.concatenate(
                        [jnp.where(half, each[0], each[1]), jnp.where(half, each[2], each[3])],
                        axis=1,
                    )
                )
                near = [brow_ref[k, v, :, :field_rows] for k in four for v in range(2)]
                both = mm(jnp.concatenate(near, axis=0), high)
                more = mm(jnp.concatenate(near[::2], axis=0), low)
                for h, k in enumerate(four):
                    lanes = slice((h // 2) * LANES, (h // 2 + 1) * LANES)
                    start = 2 * h * rows_here
                    part = both[start : start + rows_here, lanes]
                    part = part + both[start + rows_here : start + 2 * rows_here, lanes]
                    keep(k, part + more[h * rows_here : (h + 1) * rows_here, lanes])
            return
        for k in range(KERNELS):
            high, low = split(product(k))
            near = brow_ref[k, 0, :, :field_rows]
            both = mm(jnp.concatenate([near, brow_ref[k, 1, :, :field_rows]], axis=0), high)
            keep(k, both[:rows_here] + both[rows_here:] + mm(near, low))

    supers = tile_cols * TILE // WIDE

    @pl.loop(0, supers)
    def _(jj):
        columns(jj * WIDE, WIDE)

    columns(supers * WIDE, LANES)

    lower = lax.broadcasted_iota(jnp.int32, (rows_here, LANES), 1) < LANES // 2

    def windows_of(k, c0):
        high = [ghigh_ref[k, :, c0 + LANES * n : c0 + LANES * (n + 1)] for n in range(3)]
        turn = [gturn_ref[k, :, c0 + LANES * n : c0 + LANES * (n + 1)] for n in range(3)]
        return [
            high[0],
            high[1],
            jnp.where(lower, high[2], turn[0]),
            jnp.where(lower, turn[0], turn[1]),
            jnp.where(lower, turn[1], turn[2]),
            *high,
        ]

    stacked = [
        jnp.concatenate([x for k in range(KERNELS) for x in windows_of(k, WIDE * jj)], axis=1)
        for jj in range(supers)
    ]
    band = jnp.concatenate([bcol_ref[k] for k in range(KERNELS)], axis=0)
    part = mm(jnp.concatenate(stacked, axis=0), band)
    for g in range(groups):
        rows = slice(g * rows_here, (g + 1) * rows_here)
        top = (g // 2) * rows_here
        grad_ref[rows, :] = part[top : top + rows_here, LANES * (g % 2) : LANES * (g % 2 + 1)]

    @pl.loop(0, tile_rows)
    def _(a):
        for g in range(groups):
            base = g * rows_here + a * TILE
            parts = [grad_ref[pl.ds(base + s, 8, stride=4), :] for s in range(4)]
            for b, tile in enumerate(transpose_blocks(parts, block)):
                home = pl.multiple_of(index_ref[a, 4 * g + b] * 8, 8)
                here = pl.ds(pl.multiple_of((a * tile_cols + 4 * g + b) * 8, 8), 8)
                tiles_ref[here, :] = tile
                pltpu.make_async_copy(
                    tiles_ref.at[here, :], out_ref.at[pl.ds(home, 8), :], sent
                ).start()

    every = tiles_ref.shape[0]
    pltpu.make_async_copy(tiles_ref, out_ref.at[pl.ds(0, every), :], sent).wait()


def to_rows(x):
    count = x.shape[0]
    return x.reshape(count // 8, 8, 8, LANES).transpose(0, 2, 1, 3).reshape(count * 8, LANES)


def from_rows(x):
    count = x.shape[0] // 8
    return x.reshape(count // 8, 8, 8, LANES).transpose(0, 2, 1, 3).reshape(count, 8 * LANES)


def kernel_call(body, name, shapes, scratch, scalars, inputs, unread=(), megabytes=8, out_space=pltpu.VMEM):
    single = not isinstance(shapes, list)
    spec = pl.BlockSpec(memory_space=pltpu.VMEM)
    outs = [shapes] if single else shapes
    result = pl.pallas_call(
        body,
        out_shape=outs,
        in_specs=[pl.BlockSpec(memory_space=pltpu.SMEM)] * len(scalars)
        + [spec] * len(inputs)
        + [pl.BlockSpec(memory_space=pl.ANY)] * len(unread),
        out_specs=[pl.BlockSpec(memory_space=out_space)] * len(outs),
        scratch_shapes=scratch,
        compiler_params=pltpu.CompilerParams(vmem_limit_bytes=megabytes * 2**20),
        name=name,
    )(*scalars, *inputs, *unread)
    return result[0] if single else result


def pairs(one, other, axis):
    count = lax.axis_size(axis)

    def exchange(x, start):
        swap = [(i, i + 1) for i in range(start, count - 1, 2)]
        return lax.ppermute(x, axis, swap + [(j, i) for i, j in swap])

    got = exchange(other, 1)
    return exchange(one, 0), got


def doubled(table, axis):
    count = lax.axis_size(axis)
    bit = 1
    while bit < count:
        got = lax.ppermute(table, axis, [(i, i ^ bit) for i in range(count)])
        table = jnp.concatenate([table, got], axis=0)
        bit *= 2
    return table


def requests(match, value, capacity):
    rank = jnp.cumsum(match.astype(jnp.int32), axis=1) - 1
    hit = match[:, None, :] & (rank[:, None, :] == jnp.arange(capacity)[None, :, None])
    return jnp.max(jnp.where(hit, value[:, None, :], -1), axis=2)


def shards(cells, instance_cell, target, row_taps, col_taps, kernel_weight):
    deep, cores, cols = lax.axis_size("deep"), lax.axis_size("core"), lax.axis_size("col")
    everyone = ("deep", "core", "col")
    plane = ("core", "col")
    peers = cores * cols
    slots = cells.shape[0]
    tile_rows, tile_cols = instance_cell.shape
    tiles_here = tile_rows * tile_cols
    height, breadth = target.shape
    owners = deep * peers
    capacity = 2 * ((tiles_here + owners - 1) // owners)
    f32 = lambda *shape: jax.ShapeDtypeStruct(shape, F32)

    flat = to_rows(cells)
    ordered, named = kernel_call(
        spread_kernel,
        "spread",
        [f32(slots * 8, LANES), jax.ShapeDtypeStruct((1, tiles_here), jnp.int32)],
        [],
        [],
        [flat, instance_cell],
    )
    near = doubled(doubled(named, "col"), "core")
    levels = [ordered]
    for e in range(1, deep):
        levels.append(lax.ppermute(ordered, "deep", [(i, i ^ e) for i in range(deep)]))
    row_axes = ("deep", "core")
    my_row, my_col = lax.axis_index(row_axes), lax.axis_index("col")
    me = jnp.stack(
        [
            lax.axis_index(plane),
            lax.axis_index(everyone),
            my_row * height - HALF,
            my_col * breadth - HALF,
            jnp.int32(deep * cores * height),
            jnp.int32(cols * breadth),
            my_row % 2,
            my_col % 2,
        ]
    ).astype(jnp.int32)
    my_deep = lax.axis_index("deep")
    here = ((my_deep ^ jnp.arange(deep)) * peers + me[0])[None, :, None]
    match = (near // slots)[:, None, :] == here
    slot = jnp.broadcast_to((near % slots)[:, None, :], match.shape)
    asked = requests(
        match.reshape(peers * deep, tiles_here), slot.reshape(peers * deep, tiles_here), capacity
    ).reshape(peers, deep, capacity)
    waves = make_waves(row_taps, col_taps)
    size = peers * deep * capacity * 8
    packed = kernel_call(
        pack_kernel,
        "pack",
        f32(size, LANES),
        [pltpu.VMEM((size, LANES), F32), pltpu.SemaphoreType.DMA((peers,))],
        [asked, me],
        levels,
        [waves],
        out_space=pl.ANY,
    )
    odd = me[6] > 0
    head, foot = target[:HALF], target[height - HALF :]
    packed, near, one, other = lax.optimization_barrier(
        (packed, near, jnp.where(odd, head, foot), jnp.where(odd, foot, head))
    )
    one, other = pairs(one, other, row_axes)
    above, below = jnp.where(odd, one, other), jnp.where(odd, other, one)
    arrived = lax.all_to_all(packed, plane, split_axis=0, concat_axis=0, tiled=True)

    everything = doubled(near, "deep")
    wanted = requests(everything // slots == me[1], everything % slots, capacity)
    mine = named[0] // slots
    earlier = jnp.tri(tiles_here, k=-1, dtype=bool)

    def place(group, size):
        same = (group[:, None] == group[None, :]) & earlier
        where = group * size + jnp.sum(same.astype(jnp.int32), axis=1)
        return where.reshape(tile_rows, tile_cols)

    home = place(mine, capacity)
    theirs = home // capacity
    level = my_deep ^ (theirs // peers)
    index = (theirs % peers * deep + level) * capacity + home % capacity
    wide = 2 * HALF
    quarter = (height + wide) // 4
    edge = f32(height // 2 + wide + quarter, LANES)
    mask, rowa, rowb = kernel_call(
        assemble_kernel,
        "assemble",
        [f32(height, breadth), f32(wide, breadth), f32(wide, breadth)],
        [pltpu.VMEM((height * (breadth // LANES), LANES), F32)],
        [index, me],
        [arrived],
    )
    rowa, rowb = pairs(rowa, rowb, row_axes)
    cola, colb = kernel_call(
        edges_kernel,
        "edges",
        [edge, edge],
        [pltpu.VMEM((2, 4, quarter, LANES), F32)],
        [me],
        [mask, rowa, rowb, target, above, below],
        [wanted],
    )
    cola, colb = pairs(cola, colb, "col")
    field_rows = height + 2 * HALF
    returned = kernel_call(
        image_kernel,
        "image",
        f32(owners * capacity * 8, LANES),
        [
            pltpu.VMEM((KERNELS // 2, 2, 2, LANES, LANES), BF16),
            pltpu.VMEM((KERNELS, 2, field_rows, 256), BF16),
            pltpu.VMEM((KERNELS, 2, LANES, 256), BF16),
            pltpu.VMEM((KERNELS, 1024, WIDE), BF16),
            pltpu.VMEM((field_rows, breadth + 128), F32),
            pltpu.VMEM((height + 4 * HALF, breadth + 128), BF16),
            pltpu.VMEM((height + 4 * HALF, breadth + 128), BF16),
            pltpu.VMEM((height + 4 * HALF, breadth), BF16),
            pltpu.VMEM((height + 4 * HALF, breadth), BF16),
            pltpu.VMEM((KERNELS, field_rows, WIDE), F32),
            pltpu.VMEM((KERNELS, height, breadth + 128), BF16),
            pltpu.VMEM((KERNELS, height, breadth + 128), BF16),
            pltpu.VMEM((height * (breadth // LANES), LANES), F32),
            pltpu.VMEM((tiles_here * 8, LANES), F32),
            pltpu.SemaphoreType.DMA,
        ],
        [home, me, kernel_weight],
        [mask, rowa, rowb, cola, colb, target, above, below, waves],
        megabytes=36,
        out_space=pl.ANY,
    )
    back = lax.all_to_all(returned, everyone, split_axis=0, concat_axis=0, tiled=True)
    stepped = kernel_call(
        step_kernel,
        "step",
        f32(slots * 8, LANES),
        [pltpu.VMEM((slots * 8, LANES), F32)] * 8,
        [wanted, me],
        [flat, back],
    )
    return from_rows(stepped)


def solution(mesh):
    rows, cols = mesh.devices.shape
    finer = Mesh(mesh.devices.reshape(rows // 2, 2, cols), ("deep", "core", "col"))
    row = ("deep", "core")
    placed = (P((*row, "col"), None), P(row, "col"), P(row, "col"), P(), P(), P())
    return jax.shard_map(
        shards, mesh=finer, in_specs=placed, out_specs=P((*row, "col"), None), check_vma=False
    )
```

```python
import jax
import jax.numpy as jnp
from jax import lax
from jax.experimental import pallas as pl
from jax.experimental.pallas import tpu as pltpu
from jax.sharding import Mesh
from jax.sharding import PartitionSpec as P

TILE = 32
TAPS = 65
HALF = 32
KERNELS = 8
LANES = 128
WIDE = 256

STEEPNESS = 4.0
THRESHOLD = 0.3
STEP_RATE = 0.5

F32 = jnp.float32
BF16 = jnp.bfloat16


def split(x):
    high = x.astype(BF16)
    return high, (x - high.astype(F32)).astype(BF16)


def mm(a, b):
    return jnp.dot(a, b, preferred_element_type=F32)


def build_bands(wave_ref, fcol_ref, frow_ref, brow_ref, bcol_ref):
    rows = lax.broadcasted_iota(jnp.int32, (LANES, LANES), 0)
    lanes = lax.broadcasted_iota(jnp.int32, (LANES, LANES), 1)
    zero = jnp.zeros((LANES, LANES), F32)

    def circular(index, start):
        base = jnp.broadcast_to(wave_ref[pl.ds(index, 1), :], (LANES, LANES))
        return pltpu.roll(base, start, 1, stride=1, stride_axis=0)

    def put(ref, kernel, r0, c0, block, height=LANES, breadth=LANES):
        high, low = split(block)
        ref[kernel, 0, r0 : r0 + height, c0 : c0 + breadth] = high[:height, :breadth]
        ref[kernel, 1, r0 : r0 + height, c0 : c0 + breadth] = low[:height, :breadth]

    half = lanes < LANES // 2

    @pl.loop(0, KERNELS)
    def _(k):
        near = circular(k, 0)
        put(frow_ref, k, 0, 0, jnp.where(lanes >= rows, near, zero))
        put(frow_ref, k, 0, LANES, jnp.where(lanes < rows, near, zero))
        put(frow_ref, k, LANES, 0, zero, 64)
        put(frow_ref, k, LANES, LANES, jnp.where(lanes >= rows, near, zero), 64)
        near = circular(2 * KERNELS + k, 0)
        put(brow_ref, k, 0, 0, jnp.where(lanes >= rows, near, zero))
        put(brow_ref, k, 0, LANES, jnp.where(lanes < rows, near, zero))
        near = circular(KERNELS + k, LANES // 2)
        diagonal = jnp.where(rows >= lanes, near, zero)
        beyond = jnp.where(rows < lanes, near, zero)
        for c0, blocks in ((0, (diagonal, beyond, zero)), (LANES, (zero, diagonal, beyond))):
            for n, block in enumerate(blocks):
                height = LANES if n < 2 else LANES // 2
                high, low = split(block)
                for start, piece in ((0, high), (320, high), (640, low)):
                    r0 = start + n * LANES
                    bcol_ref[k, r0 : r0 + height, c0 : c0 + LANES] = piece[:height]
        bcol_ref[k, 960:, :] = jnp.zeros((64, WIDE), BF16)

    @pl.loop(0, KERNELS // 2)
    def _(pair):
        first, second = 3 * KERNELS + 2 * pair, 3 * KERNELS + 2 * pair + 1
        for order, (one, other) in enumerate(((first, second), (second, first))):
            block = jnp.where(half, circular(one, LANES // 2), circular(other, 0))
            high, low = split(block)
            fcol_ref[pair, order, 0] = high
            fcol_ref[pair, order, 1] = low


def make_waves(row_taps, col_taps):
    taps = jnp.concatenate([row_taps, col_taps], axis=0)
    taps = jnp.concatenate([taps, taps[:, ::-1]], axis=0)
    return jnp.pad(taps, [(0, 0), (0, LANES - TAPS)])


def transpose_blocks(parts, block):
    turned = []
    for d in range(4):
        x = parts[d]
        for s in range(1, 4):
            x = jnp.where(block == s, parts[(s + d) % 4], x)
        turned.append(pltpu.roll(x, 32 * d, 1) if d else x)
    out = []
    for s in range(4):
        x = turned[(-s) % 4]
        for b in range(1, 4):
            x = jnp.where(block == b, turned[(b - s) % 4], x)
        out.append(x)
    return out


def spread_kernel(cells_ref, out_ref):
    for c in range(out_ref.shape[0] // 8):
        out_ref[c * 8 : c * 8 + 8, :] = cells_ref[pl.ds((c // 8) * 64 + c % 8, 8, stride=8), :]


def pack_kernel(asked_ref, me_ref, *rest):
    out_ref, stage_ref, sems = rest[-3:]
    peers, planes, capacity = asked_ref.shape
    chunk = planes * capacity * 8

    def send(i):
        rows = pl.ds(pl.multiple_of((me_ref[0] ^ i) * chunk, chunk), chunk)
        return pltpu.make_async_copy(stage_ref.at[rows, :], out_ref.at[rows, :], sems.at[i])

    @pl.loop(0, peers)
    def _(i):
        base = (me_ref[0] ^ i) * planes * capacity
        for e in range(planes):
            for j in range(capacity):
                asked = jnp.maximum(asked_ref[i, e, j], 0)
                tile = rest[e][pl.ds(pl.multiple_of(asked * 8, 8), 8), :]
                there = (base + e * capacity + j) * 8
                stage_ref[pl.ds(pl.multiple_of(there, 8), 8), :] = tile
        send(i).start()

    @pl.loop(0, peers)
    def _(i):
        send(i).wait()


def step_kernel(asked_ref, me_ref, cells_ref, tiles_ref, out_ref, *totals):
    owners, capacity = asked_ref.shape
    nothing = jnp.zeros((8, LANES), F32)
    for total in totals:
        total[...] = jnp.zeros_like(total)

    @pl.loop(0, owners // 2)
    def _(pair):
        for n in range(2 * capacity):
            i, j = pair * 2 + n // capacity, n % capacity
            asked = asked_ref[i, j]
            place = ((me_ref[1] ^ i) * capacity + j) * 8
            tile = tiles_ref[pl.ds(pl.multiple_of(place, 8), 8), :]
            there = pl.ds(pl.multiple_of(jnp.maximum(asked, 0) * 8, 8), 8)
            total = totals[n % len(totals)]
            total[there, :] += jnp.where(asked >= 0, tile, nothing)

    for c in range(out_ref.shape[0] // 8):
        rows = slice(c * 8, c * 8 + 8)
        total = totals[0][rows, :]
        for other in totals[1:]:
            total = total + other[rows, :]
        there = pl.ds((c // 8) * 64 + c % 8, 8, stride=8)
        out_ref[there, :] = cells_ref[there, :] - STEP_RATE * total


def target_strips(target_ref, top_ref, bottom_ref, strip):
    height = target_ref.shape[0]
    quarter = (height + 2 * HALF) // 4
    for row in range(0, height + 2 * HALF, 16):
        if row < HALF:
            ref, start = top_ref, row
        elif row < HALF + height:
            ref, start = target_ref, row - HALF
        else:
            ref, start = bottom_ref, row - HALF - height
        strip(row, ref, slice(start, start + 16), row // quarter, row % quarter)


def assemble_kernel(index_ref, spot_ref, tiles_ref, mask_ref, rowa_ref, rowb_ref, turned_ref):
    odd_row = spot_ref[6] > 0
    tile_rows, tile_cols = index_ref.shape
    height = tile_rows * TILE
    wide = 2 * HALF
    groups = tile_cols // 4
    block = lax.broadcasted_iota(jnp.int32, (8, LANES), 1) // 32

    @pl.loop(0, tile_rows)
    def _(a):
        for g in range(groups):
            parts = [
                tiles_ref[pl.ds(pl.multiple_of(index_ref[a, 4 * g + b] * 8, 8), 8), :]
                for b in range(4)
            ]
            for s, piece in enumerate(transpose_blocks(parts, block)):
                turned_ref[pl.ds(g * height + a * TILE + s, 8, stride=4), :] = piece

    for g in range(groups):
        lanes = slice(LANES * g, LANES * (g + 1))
        piece = turned_ref[g * height : (g + 1) * height, :]
        mask_ref[:, lanes] = piece
        rowa_ref[:, lanes] = jnp.where(odd_row, piece[:wide], piece[height - wide :])
        rowb_ref[:, lanes] = jnp.where(odd_row, piece[height - wide :], piece[:wide])


def edges_kernel(spot_ref, mask_ref, rowa_ref, rowb_ref, target_ref, ttop_ref, tbottom_ref, *rest):
    cola_ref, colb_ref, pack_ref = rest[-3:]
    odd_row, odd_col = spot_ref[6] > 0, spot_ref[7] > 0
    height, breadth = mask_ref.shape
    wide = 2 * HALF
    half = height // 2
    packed = half + wide
    lane = lax.broadcasted_iota(jnp.int32, (packed, LANES), 1)
    head, tail = slice(0, LANES), slice(breadth - LANES, breadth)

    def halves(lanes):
        one, other = rowa_ref[:, lanes], rowb_ref[:, lanes]
        top, bottom = jnp.where(odd_row, one, other), jnp.where(odd_row, other, one)
        upper = jnp.concatenate([top, mask_ref[:half, lanes]], axis=0)
        return upper, jnp.concatenate([mask_ref[half:, lanes], bottom], axis=0)

    upper, lower = halves(head)
    left = jnp.where(lane < wide, upper, pltpu.roll(lower, wide, 1))
    upper, lower = halves(tail)
    right = jnp.where(lane < wide, pltpu.roll(upper, wide, 1), lower)
    cola_ref[:packed, :] = jnp.where(odd_col, left, right)
    colb_ref[:packed, :] = jnp.where(odd_col, right, left)

    quarter = (height + 2 * HALF) // 4

    def strip(row, ref, rows, part, inner):
        for side, lanes in enumerate((head, tail)):
            shift = (HALF * (part + side)) % LANES
            piece = ref[rows, lanes]
            pack_ref[side, part, inner : inner + 16, :] = (
                pltpu.roll(piece, shift, 1) if shift else piece
            )

    target_strips(target_ref, ttop_ref, tbottom_ref, strip)
    part_of = lax.broadcasted_iota(jnp.int32, (quarter, LANES), 1) // HALF
    sides = []
    for side in range(2):
        piece = pack_ref[side, 0]
        for part in range(1, 4):
            piece = jnp.where(part_of == part, pack_ref[side, part], piece)
        sides.append(piece)
    cola_ref[packed:, :] = jnp.where(odd_col, sides[0], sides[1])
    colb_ref[packed:, :] = jnp.where(odd_col, sides[1], sides[0])


def image_kernel(
    index_ref,
    spot_ref,
    weight_ref,
    mask_ref,
    rowa_ref,
    rowb_ref,
    cola_ref,
    colb_ref,
    own_ref,
    ttop_ref,
    tbottom_ref,
    wave_ref,
    out_ref,
    fcol_ref,
    frow_ref,
    brow_ref,
    bcol_ref,
    target_ref,
    mhigh_ref,
    mlow_ref,
    nhigh_ref,
    nlow_ref,
    field_ref,
    ghigh_ref,
    gturn_ref,
    grad_ref,
):
    tile_rows, tile_cols = index_ref.shape
    rows_here = tile_rows * TILE
    high_rows = rows_here + 4 * HALF
    field_rows = rows_here + 2 * HALF
    groups = tile_cols // 4
    wide = 2 * HALF
    block = lax.broadcasted_iota(jnp.int32, (8, LANES), 1) // 32
    odd_row, odd_col = spot_ref[6] > 0, spot_ref[7] > 0
    build_bands(wave_ref, fcol_ref, frow_ref, brow_ref, bcol_ref)

    lane = lax.broadcasted_iota(jnp.int32, (wide, LANES), 1)
    for rows in range(0, high_rows, wide):
        outer = rows == 0 or rows == high_rows - wide
        from_a = odd_row if rows == 0 else jnp.logical_not(odd_row)
        half = high_rows // 2
        edge = slice(rows % half, rows % half + wide)
        one, other = cola_ref[edge, :], colb_ref[edge, :]
        turned, final = jnp.where(odd_col, one, other), jnp.where(odd_col, other, one)
        if rows < half:
            final = pltpu.roll(final, wide, 1)
        else:
            turned = pltpu.roll(turned, wide, 1)
        for g in range(groups + 1):
            fresh = final
            if g < groups:
                lanes = slice(LANES * g, LANES * (g + 1))
                if outer:
                    piece = jnp.where(from_a, rowa_ref[:, lanes], rowb_ref[:, lanes])
                else:
                    piece = mask_ref[rows - wide : rows, lanes]
                high, low = split(piece)
                nhigh_ref[rows : rows + wide, LANES * g : LANES * (g + 1)] = high
                nlow_ref[rows : rows + wide, LANES * g : LANES * (g + 1)] = low
                fresh = pltpu.roll(piece, wide, 1)
            high, low = split(jnp.where(lane < wide, turned, fresh))
            mhigh_ref[rows : rows + wide, LANES * g : LANES * (g + 1)] = high
            mlow_ref[rows : rows + wide, LANES * g : LANES * (g + 1)] = low
            turned = fresh
    packed = high_rows // 2
    near_lane = lax.broadcasted_iota(jnp.int32, (16, LANES), 1)

    def strip(row, ref, rows, part, inner):
        edge = slice(packed + inner, packed + inner + 16)
        back, ahead = (-HALF * part) % LANES, (HALF - HALF * part) % LANES
        one, other = cola_ref[edge, :], colb_ref[edge, :]
        turned, final = jnp.where(odd_col, one, other), jnp.where(odd_col, other, one)
        turned = pltpu.roll(turned, back, 1) if back else turned
        final = pltpu.roll(final, ahead, 1) if ahead else final
        for g in range(groups + 1):
            fresh = final
            if g < groups:
                fresh = pltpu.roll(ref[rows, LANES * g : LANES * (g + 1)], HALF, 1)
            target_ref[row : row + 16, LANES * g : LANES * (g + 1)] = jnp.where(
                near_lane < HALF, turned, fresh
            )
            turned = fresh

    target_strips(own_ref, ttop_ref, tbottom_ref, strip)

    def swapped(x):
        pieces = [
            pltpu.roll(x[:, c : c + LANES], LANES // 2, 1) for c in range(0, x.shape[1], LANES)
        ]
        return pieces[0] if len(pieces) == 1 else jnp.concatenate(pieces, axis=1)

    def columns(offset, width):
        blocks = width // LANES
        last = blocks == 1

        def windows(high_ref, low_ref):
            rows = []
            for j in range(blocks):
                place = pl.ds(pl.multiple_of(offset + j * LANES, LANES), LANES)
                high, low = high_ref[:, place], low_ref[:, place]
                rows.append(jnp.concatenate([high, low, high], axis=1))
            return rows[0] if last else jnp.concatenate(rows, axis=0)

        even_rows = windows(mhigh_ref, mlow_ref)
        odd_rows = None if last else windows(nhigh_ref, nlow_ref)
        left = lax.broadcasted_iota(jnp.int32, (high_rows, LANES), 1) < LANES // 2

        def band(quad, order):
            both = [
                jnp.concatenate(
                    [fcol_ref[2 * quad, order, v], fcol_ref[2 * quad + 1, order, v]], axis=1
                )
                for v in range(2)
            ]
            return jnp.concatenate([both[0], both[0], both[1]], axis=0)

        sums = [None, None]
        for quad in range(KERNELS // 4):
            even = mm(even_rows, band(quad, 0))
            odd = even if last else mm(odd_rows, band(quad, 1))
            four = range(4 * quad, 4 * quad + 4)
            if last:
                high, low = split(even)
                both = mm(jnp.concatenate([frow_ref[k, v] for k in four for v in range(2)], 0), high)
                more = mm(jnp.concatenate([frow_ref[k, 0] for k in four], axis=0), low)
            for h, k in enumerate(four):
                lanes = slice((h // 2) * LANES, (h // 2 + 1) * LANES)
                if last:
                    start = 2 * h * field_rows
                    field = both[start : start + field_rows, lanes]
                    field = field + both[start + field_rows : start + 2 * field_rows, lanes]
                    field = field + more[h * field_rows : (h + 1) * field_rows, lanes]
                else:
                    pieces = []
                    for j in range(blocks):
                        rows = slice(j * high_rows, (j + 1) * high_rows)
                        one, other = even[rows, lanes], odd[rows, lanes]
                        one, other = (other, one) if h % 2 else (one, other)
                        pieces.append(jnp.where(left, one, other))
                    high, low = split(jnp.concatenate(pieces, axis=1))
                    both = mm(jnp.concatenate([frow_ref[k, 0], frow_ref[k, 1]], axis=0), high)
                    field = both[:field_rows] + both[field_rows:] + mm(frow_ref[k, 0], low)
                field_ref[k, :, :width] = field
                term = weight_ref[k] * field * field
                sums[h % 2] = term if sums[h % 2] is None else sums[h % 2] + term
        intensity = sums[0] + swapped(sums[1])
        resist = 1.0 / (1.0 + jnp.exp(-STEEPNESS * (intensity - THRESHOLD)))
        place = pl.ds(pl.multiple_of(offset, LANES), width)
        target = target_ref[:, place]
        sensitivity = 2.0 * (resist - target) * STEEPNESS * resist * (1.0 - resist)
        row = spot_ref[2] + lax.broadcasted_iota(jnp.int32, (field_rows, width), 0)
        col = spot_ref[3] + offset + lax.broadcasted_iota(jnp.int32, (field_rows, width), 1)
        inside = (row >= 0) & (row < spot_ref[4]) & (col >= 0) & (col < spot_ref[5])
        sensitivity = jnp.where(inside, sensitivity, 0.0)
        ordered = (sensitivity, swapped(sensitivity))

        def product(k):
            return (2.0 * weight_ref[k]) * ordered[k % 2] * field_ref[k, :, :width]

        def keep(k, part):
            straight, turned = (part, swapped(part))[:: 1 - 2 * (k % 2)]
            ghigh_ref[k, :, place] = straight.astype(BF16)
            gturn_ref[k, :, place] = split(turned)[1]

        if last:
            half = left[:field_rows]
            for quad in range(KERNELS // 4):
                four = range(4 * quad, 4 * quad + 4)
                each = [product(k) for k in four]
                high, low = split(
                    jnp.concatenate(
                        [jnp.where(half, each[0], each[1]), jnp.where(half, each[2], each[3])],
                        axis=1,
                    )
                )
                near = [brow_ref[k, v, :, :field_rows] for k in four for v in range(2)]
                both = mm(jnp.concatenate(near, axis=0), high)
                more = mm(jnp.concatenate(near[::2], axis=0), low)
                for h, k in enumerate(four):
                    lanes = slice((h // 2) * LANES, (h // 2 + 1) * LANES)
                    start = 2 * h * rows_here
                    part = both[start : start + rows_here, lanes]
                    part = part + both[start + rows_here : start + 2 * rows_here, lanes]
                    keep(k, part + more[h * rows_here : (h + 1) * rows_here, lanes])
            return
        for k in range(KERNELS):
            high, low = split(product(k))
            near = brow_ref[k, 0, :, :field_rows]
            both = mm(jnp.concatenate([near, brow_ref[k, 1, :, :field_rows]], axis=0), high)
            keep(k, both[:rows_here] + both[rows_here:] + mm(near, low))

    supers = tile_cols * TILE // WIDE

    @pl.loop(0, supers)
    def _(jj):
        columns(jj * WIDE, WIDE)

    columns(supers * WIDE, LANES)

    lower = lax.broadcasted_iota(jnp.int32, (rows_here, LANES), 1) < LANES // 2

    def windows_of(k, c0):
        high = [ghigh_ref[k, :, c0 + LANES * n : c0 + LANES * (n + 1)] for n in range(3)]
        turn = [gturn_ref[k, :, c0 + LANES * n : c0 + LANES * (n + 1)] for n in range(3)]
        return [
            high[0],
            high[1],
            jnp.where(lower, high[2], turn[0]),
            jnp.where(lower, turn[0], turn[1]),
            jnp.where(lower, turn[1], turn[2]),
            *high,
        ]

    together = 4
    grad_ref[...] = jnp.zeros_like(grad_ref)

    @pl.loop(0, KERNELS // together)
    def _(part_of):
        ks = [part_of * together + n for n in range(together)]
        stacked = [
            jnp.concatenate([x for k in ks for x in windows_of(k, WIDE * jj)], axis=1)
            for jj in range(supers)
        ]
        band = jnp.concatenate([bcol_ref[k] for k in ks], axis=0)
        part = mm(jnp.concatenate(stacked, axis=0), band)
        for g in range(groups):
            rows = slice(g * rows_here, (g + 1) * rows_here)
            top = (g // 2) * rows_here
            grad_ref[rows, :] += part[
                top : top + rows_here, LANES * (g % 2) : LANES * (g % 2 + 1)
            ]

    @pl.loop(0, tile_rows)
    def _(a):
        for g in range(groups):
            base = g * rows_here + a * TILE
            parts = [grad_ref[pl.ds(base + s, 8, stride=4), :] for s in range(4)]
            for b, tile in enumerate(transpose_blocks(parts, block)):
                place = pl.multiple_of(index_ref[a, 4 * g + b] * 8, 8)
                out_ref[pl.ds(place, 8), :] = tile


def to_rows(x):
    count = x.shape[0]
    return x.reshape(count // 8, 8, 8, LANES).transpose(0, 2, 1, 3).reshape(count * 8, LANES)


def from_rows(x):
    count = x.shape[0] // 8
    return x.reshape(count // 8, 8, 8, LANES).transpose(0, 2, 1, 3).reshape(count, 8 * LANES)


def kernel_call(body, name, shapes, scratch, scalars, inputs, unread=(), megabytes=8, out_space=pltpu.VMEM):
    single = not isinstance(shapes, list)
    spec = pl.BlockSpec(memory_space=pltpu.VMEM)
    outs = [shapes] if single else shapes
    result = pl.pallas_call(
        body,
        out_shape=outs,
        in_specs=[pl.BlockSpec(memory_space=pltpu.SMEM)] * len(scalars)
        + [spec] * len(inputs)
        + [pl.BlockSpec(memory_space=pl.ANY)] * len(unread),
        out_specs=[pl.BlockSpec(memory_space=out_space)] * len(outs),
        scratch_shapes=scratch,
        compiler_params=pltpu.CompilerParams(vmem_limit_bytes=megabytes * 2**20),
        name=name,
    )(*scalars, *inputs, *unread)
    return result[0] if single else result


def pairs(one, other, axis):
    count = lax.axis_size(axis)

    def exchange(x, start):
        swap = [(i, i + 1) for i in range(start, count - 1, 2)]
        return lax.ppermute(x, axis, swap + [(j, i) for i, j in swap])

    got = exchange(other, 1)
    return exchange(one, 0), got


def doubled(table, axis):
    count = lax.axis_size(axis)
    bit = 1
    while bit < count:
        got = lax.ppermute(table, axis, [(i, i ^ bit) for i in range(count)])
        table = jnp.concatenate([table, got], axis=0)
        bit *= 2
    return table


def requests(match, value, capacity):
    rank = jnp.cumsum(match.astype(jnp.int32), axis=1) - 1
    hit = match[:, None, :] & (rank[:, None, :] == jnp.arange(capacity)[None, :, None])
    return jnp.max(jnp.where(hit, value[:, None, :], -1), axis=2)


def shards(cells, instance_cell, target, row_taps, col_taps, kernel_weight):
    deep, cores, cols = lax.axis_size("deep"), lax.axis_size("core"), lax.axis_size("col")
    everyone = ("deep", "core", "col")
    plane = ("core", "col")
    peers = cores * cols
    slots = cells.shape[0]
    tile_rows, tile_cols = instance_cell.shape
    tiles_here = tile_rows * tile_cols
    height, breadth = target.shape
    owners = deep * peers
    capacity = 2 * ((tiles_here + owners - 1) // owners)
    f32 = lambda *shape: jax.ShapeDtypeStruct(shape, F32)

    flat = to_rows(cells)
    ordered = kernel_call(spread_kernel, "spread", f32(slots * 8, LANES), [], [], [flat])
    named = instance_cell.reshape(1, -1)
    near = doubled(doubled(named, "col"), "core")
    levels = [ordered]
    for e in range(1, deep):
        levels.append(lax.ppermute(ordered, "deep", [(i, i ^ e) for i in range(deep)]))
    row_axes = ("deep", "core")
    my_row, my_col = lax.axis_index(row_axes), lax.axis_index("col")
    me = jnp.stack(
        [
            lax.axis_index(plane),
            lax.axis_index(everyone),
            my_row * height - HALF,
            my_col * breadth - HALF,
            jnp.int32(deep * cores * height),
            jnp.int32(cols * breadth),
            my_row % 2,
            my_col % 2,
        ]
    ).astype(jnp.int32)
    my_deep = lax.axis_index("deep")
    here = ((my_deep ^ jnp.arange(deep)) * peers + me[0])[None, :, None]
    match = (near // slots)[:, None, :] == here
    slot = jnp.broadcast_to((near % slots)[:, None, :], match.shape)
    asked = requests(
        match.reshape(peers * deep, tiles_here), slot.reshape(peers * deep, tiles_here), capacity
    ).reshape(peers, deep, capacity)
    waves = make_waves(row_taps, col_taps)
    size = peers * deep * capacity * 8
    packed = kernel_call(
        pack_kernel,
        "pack",
        f32(size, LANES),
        [pltpu.VMEM((size, LANES), F32), pltpu.SemaphoreType.DMA((peers,))],
        [asked, me],
        levels,
        [waves],
        out_space=pl.ANY,
    )
    odd = me[6] > 0
    head, foot = target[:HALF], target[height - HALF :]
    packed, near, one, other = lax.optimization_barrier(
        (packed, near, jnp.where(odd, head, foot), jnp.where(odd, foot, head))
    )
    one, other = pairs(one, other, row_axes)
    above, below = jnp.where(odd, one, other), jnp.where(odd, other, one)
    arrived = lax.all_to_all(packed, plane, split_axis=0, concat_axis=0, tiled=True)

    everything = doubled(near, "deep")
    wanted = requests(everything // slots == me[1], everything % slots, capacity)
    mine = named[0] // slots
    earlier = jnp.tri(tiles_here, k=-1, dtype=bool)

    def place(group, size):
        same = (group[:, None] == group[None, :]) & earlier
        where = group * size + jnp.sum(same.astype(jnp.int32), axis=1)
        return where.reshape(tile_rows, tile_cols)

    home = place(mine, capacity)
    theirs = home // capacity
    level = my_deep ^ (theirs // peers)
    index = (theirs % peers * deep + level) * capacity + home % capacity
    wide = 2 * HALF
    quarter = (height + wide) // 4
    edge = f32(height // 2 + wide + quarter, LANES)
    mask, rowa, rowb = kernel_call(
        assemble_kernel,
        "assemble",
        [f32(height, breadth), f32(wide, breadth), f32(wide, breadth)],
        [pltpu.VMEM((height * (breadth // LANES), LANES), F32)],
        [index, me],
        [arrived],
    )
    rowa, rowb = pairs(rowa, rowb, row_axes)
    cola, colb = kernel_call(
        edges_kernel,
        "edges",
        [edge, edge],
        [pltpu.VMEM((2, 4, quarter, LANES), F32)],
        [me],
        [mask, rowa, rowb, target, above, below],
        [wanted],
    )
    cola, colb = pairs(cola, colb, "col")
    field_rows = height + 2 * HALF
    returned = kernel_call(
        image_kernel,
        "image",
        f32(owners * capacity * 8, LANES),
        [
            pltpu.VMEM((KERNELS // 2, 2, 2, LANES, LANES), BF16),
            pltpu.VMEM((KERNELS, 2, field_rows, 256), BF16),
            pltpu.VMEM((KERNELS, 2, LANES, 256), BF16),
            pltpu.VMEM((KERNELS, 1024, WIDE), BF16),
            pltpu.VMEM((field_rows, breadth + 128), F32),
            pltpu.VMEM((height + 4 * HALF, breadth + 128), BF16),
            pltpu.VMEM((height + 4 * HALF, breadth + 128), BF16),
            pltpu.VMEM((height + 4 * HALF, breadth), BF16),
            pltpu.VMEM((height + 4 * HALF, breadth), BF16),
            pltpu.VMEM((KERNELS, field_rows, WIDE), F32),
            pltpu.VMEM((KERNELS, height, breadth + 128), BF16),
            pltpu.VMEM((KERNELS, height, breadth + 128), BF16),
            pltpu.VMEM((height * (breadth // LANES), LANES), F32),
        ],
        [home, me, kernel_weight],
        [mask, rowa, rowb, cola, colb, target, above, below, waves],
        megabytes=36,
    )
    back = lax.all_to_all(returned, everyone, split_axis=0, concat_axis=0, tiled=True)
    stepped = kernel_call(
        step_kernel,
        "step",
        f32(slots * 8, LANES),
        [pltpu.VMEM((slots * 8, LANES), F32)] * 8,
        [wanted, me],
        [flat, back],
    )
    return from_rows(stepped)


def solution(mesh):
    rows, cols = mesh.devices.shape
    finer = Mesh(mesh.devices.reshape(rows // 2, 2, cols), ("deep", "core", "col"))
    row = ("deep", "core")
    placed = (P((*row, "col"), None), P(row, "col"), P(row, "col"), P(), P(), P())
    return jax.shard_map(
        shards, mesh=finer, in_specs=placed, out_specs=P((*row, "col"), None), check_vma=False
    )
```

```python
import jax
import jax.numpy as jnp
from jax import lax
from jax.experimental import pallas as pl
from jax.experimental.pallas import tpu as pltpu
from jax.sharding import Mesh
from jax.sharding import PartitionSpec as P

TILE = 32
TAPS = 65
HALF = 32
KERNELS = 8
LANES = 128
WIDE = 256

STEEPNESS = 4.0
THRESHOLD = 0.3
STEP_RATE = 0.5

F32 = jnp.float32
BF16 = jnp.bfloat16


def split(x):
    high = x.astype(BF16)
    return high, (x - high.astype(F32)).astype(BF16)


def mm(a, b):
    return jnp.dot(a, b, preferred_element_type=F32)


def build_bands(wave_ref, fcol_ref, frow_ref, brow_ref, bcol_ref):
    rows = lax.broadcasted_iota(jnp.int32, (LANES, LANES), 0)
    lanes = lax.broadcasted_iota(jnp.int32, (LANES, LANES), 1)
    zero = jnp.zeros((LANES, LANES), F32)

    def circular(index, start):
        base = jnp.broadcast_to(wave_ref[pl.ds(index, 1), :], (LANES, LANES))
        return pltpu.roll(base, start, 1, stride=1, stride_axis=0)

    def put(ref, kernel, r0, c0, block, height=LANES, breadth=LANES):
        high, low = split(block)
        ref[kernel, 0, r0 : r0 + height, c0 : c0 + breadth] = high[:height, :breadth]
        ref[kernel, 1, r0 : r0 + height, c0 : c0 + breadth] = low[:height, :breadth]

    half = lanes < LANES // 2

    @pl.loop(0, KERNELS)
    def _(k):
        near = circular(k, 0)
        put(frow_ref, k, 0, 0, jnp.where(lanes >= rows, near, zero))
        put(frow_ref, k, 0, LANES, jnp.where(lanes < rows, near, zero))
        put(frow_ref, k, LANES, 0, zero, 64)
        put(frow_ref, k, LANES, LANES, jnp.where(lanes >= rows, near, zero), 64)
        near = circular(2 * KERNELS + k, 0)
        put(brow_ref, k, 0, 0, jnp.where(lanes >= rows, near, zero))
        put(brow_ref, k, 0, LANES, jnp.where(lanes < rows, near, zero))
        near = circular(KERNELS + k, LANES // 2)
        diagonal = jnp.where(rows >= lanes, near, zero)
        beyond = jnp.where(rows < lanes, near, zero)
        for c0, blocks in ((0, (diagonal, beyond, zero)), (LANES, (zero, diagonal, beyond))):
            for n, block in enumerate(blocks):
                height = LANES if n < 2 else LANES // 2
                high, low = split(block)
                for start, piece in ((0, high), (320, high), (640, low)):
                    r0 = start + n * LANES
                    bcol_ref[k, r0 : r0 + height, c0 : c0 + LANES] = piece[:height]
        bcol_ref[k, 960:, :] = jnp.zeros((64, WIDE), BF16)

    @pl.loop(0, KERNELS // 2)
    def _(pair):
        first, second = 3 * KERNELS + 2 * pair, 3 * KERNELS + 2 * pair + 1
        for order, (one, other) in enumerate(((first, second), (second, first))):
            block = jnp.where(half, circular(one, LANES // 2), circular(other, 0))
            high, low = split(block)
            fcol_ref[pair, order, 0] = high
            fcol_ref[pair, order, 1] = low


def make_waves(row_taps, col_taps):
    taps = jnp.concatenate([row_taps, col_taps], axis=0)
    taps = jnp.concatenate([taps, taps[:, ::-1]], axis=0)
    return jnp.pad(taps, [(0, 0), (0, LANES - TAPS)])


def transpose_blocks(parts, block):
    turned = []
    for d in range(4):
        x = parts[d]
        for s in range(1, 4):
            x = jnp.where(block == s, parts[(s + d) % 4], x)
        turned.append(pltpu.roll(x, 32 * d, 1) if d else x)
    out = []
    for s in range(4):
        x = turned[(-s) % 4]
        for b in range(1, 4):
            x = jnp.where(block == b, turned[(b - s) % 4], x)
        out.append(x)
    return out


def spread_kernel(cells_ref, out_ref):
    for c in range(out_ref.shape[0] // 8):
        out_ref[c * 8 : c * 8 + 8, :] = cells_ref[pl.ds((c // 8) * 64 + c % 8, 8, stride=8), :]


def pack_kernel(asked_ref, me_ref, *rest):
    out_ref, stage_ref, sems = rest[-3:]
    peers, planes, capacity = asked_ref.shape
    chunk = planes * capacity * 8

    def send(i):
        rows = pl.ds(pl.multiple_of((me_ref[0] ^ i) * chunk, chunk), chunk)
        return pltpu.make_async_copy(stage_ref.at[rows, :], out_ref.at[rows, :], sems.at[i])

    @pl.loop(0, peers)
    def _(i):
        base = (me_ref[0] ^ i) * planes * capacity
        for e in range(planes):
            for j in range(capacity):
                asked = jnp.maximum(asked_ref[i, e, j], 0)
                tile = rest[e][pl.ds(pl.multiple_of(asked * 8, 8), 8), :]
                there = (base + e * capacity + j) * 8
                stage_ref[pl.ds(pl.multiple_of(there, 8), 8), :] = tile
        send(i).start()

    @pl.loop(0, peers)
    def _(i):
        send(i).wait()


def step_kernel(asked_ref, me_ref, cells_ref, tiles_ref, out_ref, *totals):
    owners, capacity = asked_ref.shape
    nothing = jnp.zeros((8, LANES), F32)
    for total in totals:
        total[...] = jnp.zeros_like(total)

    @pl.loop(0, owners // 2)
    def _(pair):
        for n in range(2 * capacity):
            i, j = pair * 2 + n // capacity, n % capacity
            asked = asked_ref[i, j]
            place = ((me_ref[1] ^ i) * capacity + j) * 8
            tile = tiles_ref[pl.ds(pl.multiple_of(place, 8), 8), :]
            there = pl.ds(pl.multiple_of(jnp.maximum(asked, 0) * 8, 8), 8)
            total = totals[n % len(totals)]
            total[there, :] += jnp.where(asked >= 0, tile, nothing)

    for c in range(out_ref.shape[0] // 8):
        rows = slice(c * 8, c * 8 + 8)
        total = totals[0][rows, :]
        for other in totals[1:]:
            total = total + other[rows, :]
        there = pl.ds((c // 8) * 64 + c % 8, 8, stride=8)
        out_ref[there, :] = cells_ref[there, :] - STEP_RATE * total


def target_strips(target_ref, top_ref, bottom_ref, strip):
    height = target_ref.shape[0]
    quarter = (height + 2 * HALF) // 4
    for row in range(0, height + 2 * HALF, 16):
        if row < HALF:
            ref, start = top_ref, row
        elif row < HALF + height:
            ref, start = target_ref, row - HALF
        else:
            ref, start = bottom_ref, row - HALF - height
        strip(row, ref, slice(start, start + 16), row // quarter, row % quarter)


def assemble_kernel(index_ref, spot_ref, tiles_ref, mask_ref, rowa_ref, rowb_ref, turned_ref):
    odd_row = spot_ref[6] > 0
    tile_rows, tile_cols = index_ref.shape
    height = tile_rows * TILE
    wide = 2 * HALF
    groups = tile_cols // 4
    block = lax.broadcasted_iota(jnp.int32, (8, LANES), 1) // 32

    @pl.loop(0, tile_rows)
    def _(a):
        for g in range(groups):
            parts = [
                tiles_ref[pl.ds(pl.multiple_of(index_ref[a, 4 * g + b] * 8, 8), 8), :]
                for b in range(4)
            ]
            for s, piece in enumerate(transpose_blocks(parts, block)):
                turned_ref[pl.ds(g * height + a * TILE + s, 8, stride=4), :] = piece

    for g in range(groups):
        lanes = slice(LANES * g, LANES * (g + 1))
        piece = turned_ref[g * height : (g + 1) * height, :]
        mask_ref[:, lanes] = piece
        rowa_ref[:, lanes] = jnp.where(odd_row, piece[:wide], piece[height - wide :])
        rowb_ref[:, lanes] = jnp.where(odd_row, piece[height - wide :], piece[:wide])


def edges_kernel(spot_ref, mask_ref, rowa_ref, rowb_ref, target_ref, ttop_ref, tbottom_ref, *rest):
    cola_ref, colb_ref, pack_ref = rest[-3:]

    def odd(n, x, y):
        return jnp.where(jnp.broadcast_to(spot_ref[n : n + 1, :], x.shape) > 0, x, y)

    height, breadth = mask_ref.shape
    wide = 2 * HALF
    half = height // 2
    packed = half + wide
    lane = lax.broadcasted_iota(jnp.int32, (packed, LANES), 1)
    head, tail = slice(0, LANES), slice(breadth - LANES, breadth)

    def halves(lanes):
        one, other = rowa_ref[:, lanes], rowb_ref[:, lanes]
        top, bottom = odd(6, one, other), odd(6, other, one)
        upper = jnp.concatenate([top, mask_ref[:half, lanes]], axis=0)
        return upper, jnp.concatenate([mask_ref[half:, lanes], bottom], axis=0)

    upper, lower = halves(head)
    left = jnp.where(lane < wide, upper, pltpu.roll(lower, wide, 1))
    upper, lower = halves(tail)
    right = jnp.where(lane < wide, pltpu.roll(upper, wide, 1), lower)
    cola_ref[:packed, :] = odd(7, left, right)
    colb_ref[:packed, :] = odd(7, right, left)

    quarter = (height + 2 * HALF) // 4

    def strip(row, ref, rows, part, inner):
        for side, lanes in enumerate((head, tail)):
            shift = (HALF * (part + side)) % LANES
            piece = ref[rows, lanes]
            pack_ref[side, part, inner : inner + 16, :] = (
                pltpu.roll(piece, shift, 1) if shift else piece
            )

    target_strips(target_ref, ttop_ref, tbottom_ref, strip)
    part_of = lax.broadcasted_iota(jnp.int32, (quarter, LANES), 1) // HALF
    sides = []
    for side in range(2):
        piece = pack_ref[side, 0]
        for part in range(1, 4):
            piece = jnp.where(part_of == part, pack_ref[side, part], piece)
        sides.append(piece)
    cola_ref[packed:, :] = odd(7, sides[0], sides[1])
    colb_ref[packed:, :] = odd(7, sides[1], sides[0])


def image_kernel(
    index_ref,
    spot_ref,
    weight_ref,
    mask_ref,
    rowa_ref,
    rowb_ref,
    cola_ref,
    colb_ref,
    own_ref,
    ttop_ref,
    tbottom_ref,
    wave_ref,
    out_ref,
    fcol_ref,
    frow_ref,
    brow_ref,
    bcol_ref,
    target_ref,
    mhigh_ref,
    mlow_ref,
    nhigh_ref,
    nlow_ref,
    field_ref,
    ghigh_ref,
    gturn_ref,
    grad_ref,
):
    tile_rows, tile_cols = index_ref.shape
    rows_here = tile_rows * TILE
    high_rows = rows_here + 4 * HALF
    field_rows = rows_here + 2 * HALF
    groups = tile_cols // 4
    wide = 2 * HALF
    block = lax.broadcasted_iota(jnp.int32, (8, LANES), 1) // 32
    odd_row, odd_col = spot_ref[6] > 0, spot_ref[7] > 0
    build_bands(wave_ref, fcol_ref, frow_ref, brow_ref, bcol_ref)

    lane = lax.broadcasted_iota(jnp.int32, (wide, LANES), 1)
    for rows in range(0, high_rows, wide):
        outer = rows == 0 or rows == high_rows - wide
        from_a = odd_row if rows == 0 else jnp.logical_not(odd_row)
        half = high_rows // 2
        edge = slice(rows % half, rows % half + wide)
        one, other = cola_ref[edge, :], colb_ref[edge, :]
        turned, final = jnp.where(odd_col, one, other), jnp.where(odd_col, other, one)
        if rows < half:
            final = pltpu.roll(final, wide, 1)
        else:
            turned = pltpu.roll(turned, wide, 1)
        for g in range(groups + 1):
            fresh = final
            if g < groups:
                lanes = slice(LANES * g, LANES * (g + 1))
                if outer:
                    piece = jnp.where(from_a, rowa_ref[:, lanes], rowb_ref[:, lanes])
                else:
                    piece = mask_ref[rows - wide : rows, lanes]
                high, low = split(piece)
                nhigh_ref[rows : rows + wide, LANES * g : LANES * (g + 1)] = high
                nlow_ref[rows : rows + wide, LANES * g : LANES * (g + 1)] = low
                fresh = pltpu.roll(piece, wide, 1)
            high, low = split(jnp.where(lane < wide, turned, fresh))
            mhigh_ref[rows : rows + wide, LANES * g : LANES * (g + 1)] = high
            mlow_ref[rows : rows + wide, LANES * g : LANES * (g + 1)] = low
            turned = fresh
    packed = high_rows // 2
    near_lane = lax.broadcasted_iota(jnp.int32, (16, LANES), 1)

    def strip(row, ref, rows, part, inner):
        edge = slice(packed + inner, packed + inner + 16)
        back, ahead = (-HALF * part) % LANES, (HALF - HALF * part) % LANES
        one, other = cola_ref[edge, :], colb_ref[edge, :]
        turned, final = jnp.where(odd_col, one, other), jnp.where(odd_col, other, one)
        turned = pltpu.roll(turned, back, 1) if back else turned
        final = pltpu.roll(final, ahead, 1) if ahead else final
        for g in range(groups + 1):
            fresh = final
            if g < groups:
                fresh = pltpu.roll(ref[rows, LANES * g : LANES * (g + 1)], HALF, 1)
            target_ref[row : row + 16, LANES * g : LANES * (g + 1)] = jnp.where(
                near_lane < HALF, turned, fresh
            )
            turned = fresh

    target_strips(own_ref, ttop_ref, tbottom_ref, strip)

    def swapped(x):
        pieces = [
            pltpu.roll(x[:, c : c + LANES], LANES // 2, 1) for c in range(0, x.shape[1], LANES)
        ]
        return pieces[0] if len(pieces) == 1 else jnp.concatenate(pieces, axis=1)

    def columns(offset, width):
        blocks = width // LANES
        last = blocks == 1

        def windows(high_ref, low_ref):
            rows = []
            for j in range(blocks):
                place = pl.ds(pl.multiple_of(offset + j * LANES, LANES), LANES)
                high, low = high_ref[:, place], low_ref[:, place]
                rows.append(jnp.concatenate([high, low, high], axis=1))
            return rows[0] if last else jnp.concatenate(rows, axis=0)

        even_rows = windows(mhigh_ref, mlow_ref)
        odd_rows = None if last else windows(nhigh_ref, nlow_ref)
        left = lax.broadcasted_iota(jnp.int32, (high_rows, LANES), 1) < LANES // 2

        def band(quad, order):
            both = [
                jnp.concatenate(
                    [fcol_ref[2 * quad, order, v], fcol_ref[2 * quad + 1, order, v]], axis=1
                )
                for v in range(2)
            ]
            return jnp.concatenate([both[0], both[0], both[1]], axis=0)

        sums = [None, None]
        for quad in range(KERNELS // 4):
            even = mm(even_rows, band(quad, 0))
            odd = even if last else mm(odd_rows, band(quad, 1))
            four = range(4 * quad, 4 * quad + 4)
            if last:
                high, low = split(even)
                both = mm(jnp.concatenate([frow_ref[k, v] for k in four for v in range(2)], 0), high)
                more = mm(jnp.concatenate([frow_ref[k, 0] for k in four], axis=0), low)
            for h, k in enumerate(four):
                lanes = slice((h // 2) * LANES, (h // 2 + 1) * LANES)
                if last:
                    start = 2 * h * field_rows
                    field = both[start : start + field_rows, lanes]
                    field = field + both[start + field_rows : start + 2 * field_rows, lanes]
                    field = field + more[h * field_rows : (h + 1) * field_rows, lanes]
                else:
                    pieces = []
                    for j in range(blocks):
                        rows = slice(j * high_rows, (j + 1) * high_rows)
                        one, other = even[rows, lanes], odd[rows, lanes]
                        one, other = (other, one) if h % 2 else (one, other)
                        pieces.append(jnp.where(left, one, other))
                    high, low = split(jnp.concatenate(pieces, axis=1))
                    both = mm(jnp.concatenate([frow_ref[k, 0], frow_ref[k, 1]], axis=0), high)
                    field = both[:field_rows] + both[field_rows:] + mm(frow_ref[k, 0], low)
                field_ref[k, :, :width] = field
                term = weight_ref[k] * field * field
                sums[h % 2] = term if sums[h % 2] is None else sums[h % 2] + term
        intensity = sums[0] + swapped(sums[1])
        resist = 1.0 / (1.0 + jnp.exp(-STEEPNESS * (intensity - THRESHOLD)))
        place = pl.ds(pl.multiple_of(offset, LANES), width)
        target = target_ref[:, place]
        sensitivity = 2.0 * (resist - target) * STEEPNESS * resist * (1.0 - resist)
        row = spot_ref[2] + lax.broadcasted_iota(jnp.int32, (field_rows, width), 0)
        col = spot_ref[3] + offset + lax.broadcasted_iota(jnp.int32, (field_rows, width), 1)
        inside = (row >= 0) & (row < spot_ref[4]) & (col >= 0) & (col < spot_ref[5])
        sensitivity = jnp.where(inside, sensitivity, 0.0)
        ordered = (sensitivity, swapped(sensitivity))

        def product(k):
            return (2.0 * weight_ref[k]) * ordered[k % 2] * field_ref[k, :, :width]

        def keep(k, part):
            straight, turned = (part, swapped(part))[:: 1 - 2 * (k % 2)]
            ghigh_ref[k, :, place] = straight.astype(BF16)
            gturn_ref[k, :, place] = split(turned)[1]

        if last:
            half = left[:field_rows]
            for quad in range(KERNELS // 4):
                four = range(4 * quad, 4 * quad + 4)
                each = [product(k) for k in four]
                high, low = split(
                    jnp.concatenate(
                        [jnp.where(half, each[0], each[1]), jnp.where(half, each[2], each[3])],
                        axis=1,
                    )
                )
                near = [brow_ref[k, v, :, :field_rows] for k in four for v in range(2)]
                both = mm(jnp.concatenate(near, axis=0), high)
                more = mm(jnp.concatenate(near[::2], axis=0), low)
                for h, k in enumerate(four):
                    lanes = slice((h // 2) * LANES, (h // 2 + 1) * LANES)
                    start = 2 * h * rows_here
                    part = both[start : start + rows_here, lanes]
                    part = part + both[start + rows_here : start + 2 * rows_here, lanes]
                    keep(k, part + more[h * rows_here : (h + 1) * rows_here, lanes])
            return
        for k in range(KERNELS):
            high, low = split(product(k))
            near = brow_ref[k, 0, :, :field_rows]
            both = mm(jnp.concatenate([near, brow_ref[k, 1, :, :field_rows]], axis=0), high)
            keep(k, both[:rows_here] + both[rows_here:] + mm(near, low))

    supers = tile_cols * TILE // WIDE

    @pl.loop(0, supers)
    def _(jj):
        columns(jj * WIDE, WIDE)

    columns(supers * WIDE, LANES)

    lower = lax.broadcasted_iota(jnp.int32, (rows_here, LANES), 1) < LANES // 2

    def windows_of(k, c0):
        high = [ghigh_ref[k, :, c0 + LANES * n : c0 + LANES * (n + 1)] for n in range(3)]
        turn = [gturn_ref[k, :, c0 + LANES * n : c0 + LANES * (n + 1)] for n in range(3)]
        return [
            high[0],
            high[1],
            jnp.where(lower, high[2], turn[0]),
            jnp.where(lower, turn[0], turn[1]),
            jnp.where(lower, turn[1], turn[2]),
            *high,
        ]

    together = 4
    grad_ref[...] = jnp.zeros_like(grad_ref)

    @pl.loop(0, KERNELS // together)
    def _(part_of):
        ks = [part_of * together + n for n in range(together)]
        stacked = [
            jnp.concatenate([x for k in ks for x in windows_of(k, WIDE * jj)], axis=1)
            for jj in range(supers)
        ]
        band = jnp.concatenate([bcol_ref[k] for k in ks], axis=0)
        part = mm(jnp.concatenate(stacked, axis=0), band)
        for g in range(groups):
            rows = slice(g * rows_here, (g + 1) * rows_here)
            top = (g // 2) * rows_here
            grad_ref[rows, :] += part[
                top : top + rows_here, LANES * (g % 2) : LANES * (g % 2 + 1)
            ]

    @pl.loop(0, tile_rows)
    def _(a):
        for g in range(groups):
            base = g * rows_here + a * TILE
            parts = [grad_ref[pl.ds(base + s, 8, stride=4), :] for s in range(4)]
            for b, tile in enumerate(transpose_blocks(parts, block)):
                place = pl.multiple_of(index_ref[a, 4 * g + b] * 8, 8)
                out_ref[pl.ds(place, 8), :] = tile


def to_rows(x):
    count = x.shape[0]
    return x.reshape(count // 8, 8, 8, LANES).transpose(0, 2, 1, 3).reshape(count * 8, LANES)


def from_rows(x):
    count = x.shape[0] // 8
    return x.reshape(count // 8, 8, 8, LANES).transpose(0, 2, 1, 3).reshape(count, 8 * LANES)


def kernel_call(body, name, shapes, scratch, scalars, inputs, unread=(), megabytes=8, out_space=pltpu.VMEM):
    single = not isinstance(shapes, list)
    spec = pl.BlockSpec(memory_space=pltpu.VMEM)
    outs = [shapes] if single else shapes
    result = pl.pallas_call(
        body,
        out_shape=outs,
        in_specs=[pl.BlockSpec(memory_space=pltpu.SMEM)] * len(scalars)
        + [spec] * len(inputs)
        + [pl.BlockSpec(memory_space=pl.ANY)] * len(unread),
        out_specs=[pl.BlockSpec(memory_space=out_space)] * len(outs),
        scratch_shapes=scratch,
        compiler_params=pltpu.CompilerParams(vmem_limit_bytes=megabytes * 2**20),
        name=name,
    )(*scalars, *inputs, *unread)
    return result[0] if single else result


def pairs(one, other, axis):
    count = lax.axis_size(axis)

    def exchange(x, start):
        swap = [(i, i + 1) for i in range(start, count - 1, 2)]
        return lax.ppermute(x, axis, swap + [(j, i) for i, j in swap])

    got = exchange(other, 1)
    return exchange(one, 0), got


def doubled(table, axis):
    count = lax.axis_size(axis)
    bit = 1
    while bit < count:
        got = lax.ppermute(table, axis, [(i, i ^ bit) for i in range(count)])
        table = jnp.concatenate([table, got], axis=0)
        bit *= 2
    return table


def requests(match, value, capacity):
    rank = jnp.cumsum(match.astype(jnp.int32), axis=1) - 1
    hit = match[:, None, :] & (rank[:, None, :] == jnp.arange(capacity)[None, :, None])
    return jnp.max(jnp.where(hit, value[:, None, :], -1), axis=2)


def shards(cells, instance_cell, target, row_taps, col_taps, kernel_weight):
    deep, cores, cols = lax.axis_size("deep"), lax.axis_size("core"), lax.axis_size("col")
    everyone = ("deep", "core", "col")
    plane = ("core", "col")
    peers = cores * cols
    slots = cells.shape[0]
    tile_rows, tile_cols = instance_cell.shape
    tiles_here = tile_rows * tile_cols
    height, breadth = target.shape
    owners = deep * peers
    capacity = 2 * ((tiles_here + owners - 1) // owners)
    f32 = lambda *shape: jax.ShapeDtypeStruct(shape, F32)

    flat = to_rows(cells)
    ordered = kernel_call(spread_kernel, "spread", f32(slots * 8, LANES), [], [], [flat])
    named = instance_cell.reshape(1, -1)
    near = doubled(doubled(named, "col"), "core")
    levels = [ordered]
    for e in range(1, deep):
        levels.append(lax.ppermute(ordered, "deep", [(i, i ^ e) for i in range(deep)]))
    row_axes = ("deep", "core")
    my_row, my_col = lax.axis_index(row_axes), lax.axis_index("col")
    me = jnp.stack(
        [
            lax.axis_index(plane),
            lax.axis_index(everyone),
            my_row * height - HALF,
            my_col * breadth - HALF,
            jnp.int32(deep * cores * height),
            jnp.int32(cols * breadth),
            my_row % 2,
            my_col % 2,
        ]
    ).astype(jnp.int32)
    my_deep = lax.axis_index("deep")
    here = ((my_deep ^ jnp.arange(deep)) * peers + me[0])[None, :, None]
    match = (near // slots)[:, None, :] == here
    slot = jnp.broadcast_to((near % slots)[:, None, :], match.shape)
    asked = requests(
        match.reshape(peers * deep, tiles_here), slot.reshape(peers * deep, tiles_here), capacity
    ).reshape(peers, deep, capacity)
    waves = make_waves(row_taps, col_taps)
    size = peers * deep * capacity * 8
    packed = kernel_call(
        pack_kernel,
        "pack",
        f32(size, LANES),
        [pltpu.VMEM((size, LANES), F32), pltpu.SemaphoreType.DMA((peers,))],
        [asked, me],
        levels,
        [waves],
        out_space=pl.ANY,
    )
    odd = me[6] > 0
    head, foot = target[:HALF], target[height - HALF :]
    packed, near, one, other = lax.optimization_barrier(
        (packed, near, jnp.where(odd, head, foot), jnp.where(odd, foot, head))
    )
    one, other = pairs(one, other, row_axes)
    above, below = jnp.where(odd, one, other), jnp.where(odd, other, one)
    arrived = lax.all_to_all(packed, plane, split_axis=0, concat_axis=0, tiled=True)

    everything = doubled(near, "deep")
    wanted = requests(everything // slots == me[1], everything % slots, capacity)
    mine = named[0] // slots
    earlier = jnp.tri(tiles_here, k=-1, dtype=bool)

    def place(group, size):
        same = (group[:, None] == group[None, :]) & earlier
        where = group * size + jnp.sum(same.astype(jnp.int32), axis=1)
        return where.reshape(tile_rows, tile_cols)

    home = place(mine, capacity)
    theirs = home // capacity
    level = my_deep ^ (theirs // peers)
    index = (theirs % peers * deep + level) * capacity + home % capacity
    wide = 2 * HALF
    quarter = (height + wide) // 4
    edge = f32(height // 2 + wide + quarter, LANES)
    mask, rowa, rowb = kernel_call(
        assemble_kernel,
        "assemble",
        [f32(height, breadth), f32(wide, breadth), f32(wide, breadth)],
        [pltpu.VMEM((height * (breadth // LANES), LANES), F32)],
        [index, me],
        [arrived],
    )
    rowa, rowb = pairs(rowa, rowb, row_axes)
    cola, colb = kernel_call(
        edges_kernel,
        "edges",
        [edge, edge],
        [pltpu.VMEM((2, 4, quarter, LANES), F32)],
        [],
        [jnp.broadcast_to(me[:, None], (8, LANES)), mask, rowa, rowb, target, above, below],
        [wanted],
    )
    cola, colb = pairs(cola, colb, "col")
    field_rows = height + 2 * HALF
    returned = kernel_call(
        image_kernel,
        "image",
        f32(owners * capacity * 8, LANES),
        [
            pltpu.VMEM((KERNELS // 2, 2, 2, LANES, LANES), BF16),
            pltpu.VMEM((KERNELS, 2, field_rows, 256), BF16),
            pltpu.VMEM((KERNELS, 2, LANES, 256), BF16),
            pltpu.VMEM((KERNELS, 1024, WIDE), BF16),
            pltpu.VMEM((field_rows, breadth + 128), F32),
            pltpu.VMEM((height + 4 * HALF, breadth + 128), BF16),
            pltpu.VMEM((height + 4 * HALF, breadth + 128), BF16),
            pltpu.VMEM((height + 4 * HALF, breadth), BF16),
            pltpu.VMEM((height + 4 * HALF, breadth), BF16),
            pltpu.VMEM((KERNELS, field_rows, WIDE), F32),
            pltpu.VMEM((KERNELS, height, breadth + 128), BF16),
            pltpu.VMEM((KERNELS, height, breadth + 128), BF16),
            pltpu.VMEM((height * (breadth // LANES), LANES), F32),
        ],
        [home, me, kernel_weight],
        [mask, rowa, rowb, cola, colb, target, above, below, waves],
        megabytes=36,
    )
    back = lax.all_to_all(returned, everyone, split_axis=0, concat_axis=0, tiled=True)
    stepped = kernel_call(
        step_kernel,
        "step",
        f32(slots * 8, LANES),
        [pltpu.VMEM((slots * 8, LANES), F32)] * 8,
        [wanted, me],
        [flat, back],
    )
    return from_rows(stepped)


def solution(mesh):
    rows, cols = mesh.devices.shape
    finer = Mesh(mesh.devices.reshape(rows // 2, 2, cols), ("deep", "core", "col"))
    row = ("deep", "core")
    placed = (P((*row, "col"), None), P(row, "col"), P(row, "col"), P(), P(), P())
    return jax.shard_map(
        shards, mesh=finer, in_specs=placed, out_specs=P((*row, "col"), None), check_vma=False
    )
```

```python
import jax
import jax.numpy as jnp
from jax import lax
from jax.experimental import pallas as pl
from jax.experimental.pallas import tpu as pltpu
from jax.sharding import Mesh
from jax.sharding import PartitionSpec as P

TILE = 32
TAPS = 65
HALF = 32
KERNELS = 8
LANES = 128
WIDE = 256

STEEPNESS = 4.0
THRESHOLD = 0.3
STEP_RATE = 0.5

F32 = jnp.float32
BF16 = jnp.bfloat16


def split(x):
    high = x.astype(BF16)
    return high, (x - high.astype(F32)).astype(BF16)


def mm(a, b):
    return jnp.dot(a, b, preferred_element_type=F32)


def build_bands(wave_ref, fcol_ref, frow_ref, brow_ref, bcol_ref):
    rows = lax.broadcasted_iota(jnp.int32, (LANES, LANES), 0)
    lanes = lax.broadcasted_iota(jnp.int32, (LANES, LANES), 1)
    zero = jnp.zeros((LANES, LANES), F32)

    def circular(index, start):
        base = jnp.broadcast_to(wave_ref[pl.ds(index, 1), :], (LANES, LANES))
        return pltpu.roll(base, start, 1, stride=1, stride_axis=0)

    def put(ref, kernel, r0, c0, block, height=LANES, breadth=LANES):
        high, low = split(block)
        ref[kernel, 0, r0 : r0 + height, c0 : c0 + breadth] = high[:height, :breadth]
        ref[kernel, 1, r0 : r0 + height, c0 : c0 + breadth] = low[:height, :breadth]

    half = lanes < LANES // 2

    @pl.loop(0, KERNELS)
    def _(k):
        near = circular(k, 0)
        put(frow_ref, k, 0, 0, jnp.where(lanes >= rows, near, zero))
        put(frow_ref, k, 0, LANES, jnp.where(lanes < rows, near, zero))
        put(frow_ref, k, LANES, 0, zero, 64)
        put(frow_ref, k, LANES, LANES, jnp.where(lanes >= rows, near, zero), 64)
        near = circular(2 * KERNELS + k, 0)
        put(brow_ref, k, 0, 0, jnp.where(lanes >= rows, near, zero))
        put(brow_ref, k, 0, LANES, jnp.where(lanes < rows, near, zero))
        near = circular(KERNELS + k, LANES // 2)
        diagonal = jnp.where(rows >= lanes, near, zero)
        beyond = jnp.where(rows < lanes, near, zero)
        for c0, blocks in ((0, (diagonal, beyond, zero)), (LANES, (zero, diagonal, beyond))):
            for n, block in enumerate(blocks):
                height = LANES if n < 2 else LANES // 2
                high, low = split(block)
                for start, piece in ((0, high), (320, high), (640, low)):
                    r0 = start + n * LANES
                    bcol_ref[k, r0 : r0 + height, c0 : c0 + LANES] = piece[:height]
        bcol_ref[k, 960:, :] = jnp.zeros((64, WIDE), BF16)

    @pl.loop(0, KERNELS // 2)
    def _(pair):
        first, second = 3 * KERNELS + 2 * pair, 3 * KERNELS + 2 * pair + 1
        for order, (one, other) in enumerate(((first, second), (second, first))):
            block = jnp.where(half, circular(one, LANES // 2), circular(other, 0))
            high, low = split(block)
            fcol_ref[pair, order, 0] = high
            fcol_ref[pair, order, 1] = low


def make_waves(row_taps, col_taps):
    taps = jnp.concatenate([row_taps, col_taps], axis=0)
    taps = jnp.concatenate([taps, taps[:, ::-1]], axis=0)
    return jnp.pad(taps, [(0, 0), (0, LANES - TAPS)])


def transpose_blocks(parts, block):
    turned = []
    for d in range(4):
        x = parts[d]
        for s in range(1, 4):
            x = jnp.where(block == s, parts[(s + d) % 4], x)
        turned.append(pltpu.roll(x, 32 * d, 1) if d else x)
    out = []
    for s in range(4):
        x = turned[(-s) % 4]
        for b in range(1, 4):
            x = jnp.where(block == b, turned[(b - s) % 4], x)
        out.append(x)
    return out


def spread_kernel(cells_ref, out_ref):
    for c in range(out_ref.shape[0] // 8):
        out_ref[c * 8 : c * 8 + 8, :] = cells_ref[pl.ds((c // 8) * 64 + c % 8, 8, stride=8), :]


def pack_kernel(asked_ref, me_ref, *rest):
    out_ref, stage_ref, sems = rest[-3:]
    peers, planes, capacity = asked_ref.shape
    chunk = planes * capacity * 8

    def send(i):
        rows = pl.ds(pl.multiple_of((me_ref[0] ^ i) * chunk, chunk), chunk)
        return pltpu.make_async_copy(stage_ref.at[rows, :], out_ref.at[rows, :], sems.at[i])

    @pl.loop(0, peers)
    def _(i):
        base = (me_ref[0] ^ i) * planes * capacity
        for e in range(planes):
            for j in range(capacity):
                asked = jnp.maximum(asked_ref[i, e, j], 0)
                tile = rest[e][pl.ds(pl.multiple_of(asked * 8, 8), 8), :]
                there = (base + e * capacity + j) * 8
                stage_ref[pl.ds(pl.multiple_of(there, 8), 8), :] = tile
        send(i).start()

    @pl.loop(0, peers)
    def _(i):
        send(i).wait()


def step_kernel(asked_ref, me_ref, cells_ref, tiles_ref, out_ref, *totals):
    owners, capacity = asked_ref.shape
    nothing = jnp.zeros((8, LANES), F32)
    for total in totals:
        total[...] = jnp.zeros_like(total)

    @pl.loop(0, owners // 2)
    def _(pair):
        for n in range(2 * capacity):
            i, j = pair * 2 + n // capacity, n % capacity
            asked = asked_ref[i, j]
            place = ((me_ref[1] ^ i) * capacity + j) * 8
            tile = tiles_ref[pl.ds(pl.multiple_of(place, 8), 8), :]
            there = pl.ds(pl.multiple_of(jnp.maximum(asked, 0) * 8, 8), 8)
            total = totals[n % len(totals)]
            total[there, :] += jnp.where(asked >= 0, tile, nothing)

    for c in range(out_ref.shape[0] // 8):
        rows = slice(c * 8, c * 8 + 8)
        total = totals[0][rows, :]
        for other in totals[1:]:
            total = total + other[rows, :]
        there = pl.ds((c // 8) * 64 + c % 8, 8, stride=8)
        out_ref[there, :] = cells_ref[there, :] - STEP_RATE * total


def target_strips(target_ref, top_ref, bottom_ref, strip):
    height = target_ref.shape[0]
    quarter = (height + 2 * HALF) // 4
    for row in range(0, height + 2 * HALF, 16):
        if row < HALF:
            ref, start = top_ref, row
        elif row < HALF + height:
            ref, start = target_ref, row - HALF
        else:
            ref, start = bottom_ref, row - HALF - height
        strip(row, ref, slice(start, start + 16), row // quarter, row % quarter)


def assemble_kernel(index_ref, spot_ref, tiles_ref, mask_ref, rowa_ref, rowb_ref, turned_ref):
    odd_row = spot_ref[6] > 0
    tile_rows, tile_cols = index_ref.shape
    height = tile_rows * TILE
    wide = 2 * HALF
    groups = tile_cols // 4
    block = lax.broadcasted_iota(jnp.int32, (8, LANES), 1) // 32

    @pl.loop(0, tile_rows)
    def _(a):
        for g in range(groups):
            parts = [
                tiles_ref[pl.ds(pl.multiple_of(index_ref[a, 4 * g + b] * 8, 8), 8), :]
                for b in range(4)
            ]
            for s, piece in enumerate(transpose_blocks(parts, block)):
                turned_ref[pl.ds(g * height + a * TILE + s, 8, stride=4), :] = piece

    for g in range(groups):
        lanes = slice(LANES * g, LANES * (g + 1))
        piece = turned_ref[g * height : (g + 1) * height, :]
        mask_ref[:, lanes] = piece
        rowa_ref[:, lanes] = jnp.where(odd_row, piece[:wide], piece[height - wide :])
        rowb_ref[:, lanes] = jnp.where(odd_row, piece[height - wide :], piece[:wide])


def edges_kernel(spot_ref, mask_ref, rowa_ref, rowb_ref, target_ref, ttop_ref, tbottom_ref, *rest):
    cola_ref, colb_ref, pack_ref = rest[-3:]

    def odd(n, x, y):
        return jnp.where(jnp.broadcast_to(spot_ref[n : n + 1, :], x.shape) > 0, x, y)

    height, breadth = mask_ref.shape
    wide = 2 * HALF
    half = height // 2
    packed = half + wide
    lane = lax.broadcasted_iota(jnp.int32, (packed, LANES), 1)
    head, tail = slice(0, LANES), slice(breadth - LANES, breadth)

    def halves(lanes):
        one, other = rowa_ref[:, lanes], rowb_ref[:, lanes]
        top, bottom = odd(6, one, other), odd(6, other, one)
        upper = jnp.concatenate([top, mask_ref[:half, lanes]], axis=0)
        return upper, jnp.concatenate([mask_ref[half:, lanes], bottom], axis=0)

    upper, lower = halves(head)
    left = jnp.where(lane < wide, upper, pltpu.roll(lower, wide, 1))
    upper, lower = halves(tail)
    right = jnp.where(lane < wide, pltpu.roll(upper, wide, 1), lower)
    cola_ref[:packed, :] = odd(7, left, right)
    colb_ref[:packed, :] = odd(7, right, left)

    quarter = (height + 2 * HALF) // 4

    def strip(row, ref, rows, part, inner):
        for side, lanes in enumerate((head, tail)):
            shift = (HALF * (part + side)) % LANES
            piece = ref[rows, lanes]
            pack_ref[side, part, inner : inner + 16, :] = (
                pltpu.roll(piece, shift, 1) if shift else piece
            )

    target_strips(target_ref, ttop_ref, tbottom_ref, strip)
    part_of = lax.broadcasted_iota(jnp.int32, (quarter, LANES), 1) // HALF
    sides = []
    for side in range(2):
        piece = pack_ref[side, 0]
        for part in range(1, 4):
            piece = jnp.where(part_of == part, pack_ref[side, part], piece)
        sides.append(piece)
    cola_ref[packed:, :] = odd(7, sides[0], sides[1])
    colb_ref[packed:, :] = odd(7, sides[1], sides[0])


def image_kernel(
    index_ref,
    spot_ref,
    weight_ref,
    mask_ref,
    rowa_ref,
    rowb_ref,
    cola_ref,
    colb_ref,
    own_ref,
    ttop_ref,
    tbottom_ref,
    wave_ref,
    out_ref,
    fcol_ref,
    frow_ref,
    brow_ref,
    bcol_ref,
    target_ref,
    mhigh_ref,
    mlow_ref,
    nhigh_ref,
    nlow_ref,
    field_ref,
    ghigh_ref,
    gturn_ref,
    grad_ref,
):
    tile_rows, tile_cols = index_ref.shape
    rows_here = tile_rows * TILE
    high_rows = rows_here + 4 * HALF
    field_rows = rows_here + 2 * HALF
    groups = tile_cols // 4
    wide = 2 * HALF
    block = lax.broadcasted_iota(jnp.int32, (8, LANES), 1) // 32
    odd_row, odd_col = spot_ref[6] > 0, spot_ref[7] > 0
    build_bands(wave_ref, fcol_ref, frow_ref, brow_ref, bcol_ref)

    lane = lax.broadcasted_iota(jnp.int32, (wide, LANES), 1)
    for rows in range(0, high_rows, wide):
        outer = rows == 0 or rows == high_rows - wide
        from_a = odd_row if rows == 0 else jnp.logical_not(odd_row)
        half = high_rows // 2
        edge = slice(rows % half, rows % half + wide)
        one, other = cola_ref[edge, :], colb_ref[edge, :]
        turned, final = jnp.where(odd_col, one, other), jnp.where(odd_col, other, one)
        if rows < half:
            final = pltpu.roll(final, wide, 1)
        else:
            turned = pltpu.roll(turned, wide, 1)
        for g in range(groups + 1):
            fresh = final
            if g < groups:
                lanes = slice(LANES * g, LANES * (g + 1))
                if outer:
                    piece = jnp.where(from_a, rowa_ref[:, lanes], rowb_ref[:, lanes])
                else:
                    piece = mask_ref[rows - wide : rows, lanes]
                high, low = split(piece)
                nhigh_ref[rows : rows + wide, LANES * g : LANES * (g + 1)] = high
                nlow_ref[rows : rows + wide, LANES * g : LANES * (g + 1)] = low
                fresh = pltpu.roll(piece, wide, 1)
            high, low = split(jnp.where(lane < wide, turned, fresh))
            mhigh_ref[rows : rows + wide, LANES * g : LANES * (g + 1)] = high
            mlow_ref[rows : rows + wide, LANES * g : LANES * (g + 1)] = low
            turned = fresh
    packed = high_rows // 2
    near_lane = lax.broadcasted_iota(jnp.int32, (16, LANES), 1)

    def strip(row, ref, rows, part, inner):
        edge = slice(packed + inner, packed + inner + 16)
        back, ahead = (-HALF * part) % LANES, (HALF - HALF * part) % LANES
        one, other = cola_ref[edge, :], colb_ref[edge, :]
        turned, final = jnp.where(odd_col, one, other), jnp.where(odd_col, other, one)
        turned = pltpu.roll(turned, back, 1) if back else turned
        final = pltpu.roll(final, ahead, 1) if ahead else final
        for g in range(groups + 1):
            fresh = final
            if g < groups:
                fresh = pltpu.roll(ref[rows, LANES * g : LANES * (g + 1)], HALF, 1)
            target_ref[row : row + 16, LANES * g : LANES * (g + 1)] = jnp.where(
                near_lane < HALF, turned, fresh
            )
            turned = fresh

    target_strips(own_ref, ttop_ref, tbottom_ref, strip)

    def swapped(x):
        pieces = [
            pltpu.roll(x[:, c : c + LANES], LANES // 2, 1) for c in range(0, x.shape[1], LANES)
        ]
        return pieces[0] if len(pieces) == 1 else jnp.concatenate(pieces, axis=1)

    def columns(offset, width):
        blocks = width // LANES
        last = blocks == 1

        def windows(high_ref, low_ref):
            rows = []
            for j in range(blocks):
                place = pl.ds(pl.multiple_of(offset + j * LANES, LANES), LANES)
                high, low = high_ref[:, place], low_ref[:, place]
                rows.append(jnp.concatenate([high, low, high], axis=1))
            return rows[0] if last else jnp.concatenate(rows, axis=0)

        even_rows = windows(mhigh_ref, mlow_ref)
        odd_rows = None if last else windows(nhigh_ref, nlow_ref)
        left = lax.broadcasted_iota(jnp.int32, (high_rows, LANES), 1) < LANES // 2

        def band(quad, order):
            both = [
                jnp.concatenate(
                    [fcol_ref[2 * quad, order, v], fcol_ref[2 * quad + 1, order, v]], axis=1
                )
                for v in range(2)
            ]
            return jnp.concatenate([both[0], both[0], both[1]], axis=0)

        sums = [None, None]
        for quad in range(KERNELS // 4):
            even = mm(even_rows, band(quad, 0))
            odd = even if last else mm(odd_rows, band(quad, 1))
            four = range(4 * quad, 4 * quad + 4)
            if last:
                high, low = split(even)
                both = mm(jnp.concatenate([frow_ref[k, v] for k in four for v in range(2)], 0), high)
                more = mm(jnp.concatenate([frow_ref[k, 0] for k in four], axis=0), low)
            for h, k in enumerate(four):
                lanes = slice((h // 2) * LANES, (h // 2 + 1) * LANES)
                if last:
                    start = 2 * h * field_rows
                    field = both[start : start + field_rows, lanes]
                    field = field + both[start + field_rows : start + 2 * field_rows, lanes]
                    field = field + more[h * field_rows : (h + 1) * field_rows, lanes]
                else:
                    pieces = []
                    for j in range(blocks):
                        rows = slice(j * high_rows, (j + 1) * high_rows)
                        one, other = even[rows, lanes], odd[rows, lanes]
                        one, other = (other, one) if h % 2 else (one, other)
                        pieces.append(jnp.where(left, one, other))
                    high, low = split(jnp.concatenate(pieces, axis=1))
                    both = mm(jnp.concatenate([frow_ref[k, 0], frow_ref[k, 1]], axis=0), high)
                    field = both[:field_rows] + both[field_rows:] + mm(frow_ref[k, 0], low)
                field_ref[k, :, :width] = field
                term = weight_ref[k] * field * field
                sums[h % 2] = term if sums[h % 2] is None else sums[h % 2] + term
        intensity = sums[0] + swapped(sums[1])
        resist = 1.0 / (1.0 + jnp.exp(-STEEPNESS * (intensity - THRESHOLD)))
        place = pl.ds(pl.multiple_of(offset, LANES), width)
        target = target_ref[:, place]
        sensitivity = 2.0 * (resist - target) * STEEPNESS * resist * (1.0 - resist)
        row = spot_ref[2] + lax.broadcasted_iota(jnp.int32, (field_rows, width), 0)
        col = spot_ref[3] + offset + lax.broadcasted_iota(jnp.int32, (field_rows, width), 1)
        inside = (row >= 0) & (row < spot_ref[4]) & (col >= 0) & (col < spot_ref[5])
        sensitivity = jnp.where(inside, sensitivity, 0.0)
        ordered = (sensitivity, swapped(sensitivity))

        def product(k):
            return (2.0 * weight_ref[k]) * ordered[k % 2] * field_ref[k, :, :width]

        def keep(k, part):
            straight, turned = (part, swapped(part))[:: 1 - 2 * (k % 2)]
            ghigh_ref[k, :, place] = straight.astype(BF16)
            gturn_ref[k, :, place] = split(turned)[1]

        if last:
            half = left[:field_rows]
            for quad in range(KERNELS // 4):
                four = range(4 * quad, 4 * quad + 4)
                each = [product(k) for k in four]
                high, low = split(
                    jnp.concatenate(
                        [jnp.where(half, each[0], each[1]), jnp.where(half, each[2], each[3])],
                        axis=1,
                    )
                )
                near = [brow_ref[k, v, :, :field_rows] for k in four for v in range(2)]
                both = mm(jnp.concatenate(near, axis=0), high)
                more = mm(jnp.concatenate(near[::2], axis=0), low)
                for h, k in enumerate(four):
                    lanes = slice((h // 2) * LANES, (h // 2 + 1) * LANES)
                    start = 2 * h * rows_here
                    part = both[start : start + rows_here, lanes]
                    part = part + both[start + rows_here : start + 2 * rows_here, lanes]
                    keep(k, part + more[h * rows_here : (h + 1) * rows_here, lanes])
            return
        for k in range(KERNELS):
            high, low = split(product(k))
            near = brow_ref[k, 0, :, :field_rows]
            both = mm(jnp.concatenate([near, brow_ref[k, 1, :, :field_rows]], axis=0), high)
            keep(k, both[:rows_here] + both[rows_here:] + mm(near, low))

    supers = tile_cols * TILE // WIDE

    @pl.loop(0, supers)
    def _(jj):
        columns(jj * WIDE, WIDE)

    columns(supers * WIDE, LANES)

    lower = lax.broadcasted_iota(jnp.int32, (rows_here, LANES), 1) < LANES // 2

    def windows_of(k, c0):
        high = [ghigh_ref[k, :, c0 + LANES * n : c0 + LANES * (n + 1)] for n in range(3)]
        turn = [gturn_ref[k, :, c0 + LANES * n : c0 + LANES * (n + 1)] for n in range(3)]
        return [
            high[0],
            high[1],
            jnp.where(lower, high[2], turn[0]),
            jnp.where(lower, turn[0], turn[1]),
            jnp.where(lower, turn[1], turn[2]),
            *high,
        ]

    together = 4
    grad_ref[...] = jnp.zeros_like(grad_ref)

    @pl.loop(0, KERNELS // together)
    def _(part_of):
        ks = [part_of * together + n for n in range(together)]
        stacked = [
            jnp.concatenate([x for k in ks for x in windows_of(k, WIDE * jj)], axis=1)
            for jj in range(supers)
        ]
        band = jnp.concatenate([bcol_ref[k] for k in ks], axis=0)
        part = mm(jnp.concatenate(stacked, axis=0), band)
        for g in range(groups):
            rows = slice(g * rows_here, (g + 1) * rows_here)
            top = (g // 2) * rows_here
            grad_ref[rows, :] += part[
                top : top + rows_here, LANES * (g % 2) : LANES * (g % 2 + 1)
            ]

    @pl.loop(0, tile_rows)
    def _(a):
        for g in range(groups):
            base = g * rows_here + a * TILE
            parts = [grad_ref[pl.ds(base + s, 8, stride=4), :] for s in range(4)]
            for b, tile in enumerate(transpose_blocks(parts, block)):
                place = pl.multiple_of(index_ref[a, 4 * g + b] * 8, 8)
                out_ref[pl.ds(place, 8), :] = tile


def to_rows(x):
    count = x.shape[0]
    return x.reshape(count // 8, 8, 8, LANES).transpose(0, 2, 1, 3).reshape(count * 8, LANES)


def from_rows(x):
    count = x.shape[0] // 8
    return x.reshape(count // 8, 8, 8, LANES).transpose(0, 2, 1, 3).reshape(count, 8 * LANES)


def kernel_call(body, name, shapes, scratch, scalars, inputs, unread=(), megabytes=8, out_space=pltpu.VMEM):
    single = not isinstance(shapes, list)
    spec = pl.BlockSpec(memory_space=pltpu.VMEM)
    outs = [shapes] if single else shapes
    result = pl.pallas_call(
        body,
        out_shape=outs,
        in_specs=[pl.BlockSpec(memory_space=pltpu.SMEM)] * len(scalars)
        + [spec] * len(inputs)
        + [pl.BlockSpec(memory_space=pl.ANY)] * len(unread),
        out_specs=[pl.BlockSpec(memory_space=out_space)] * len(outs),
        scratch_shapes=scratch,
        compiler_params=pltpu.CompilerParams(vmem_limit_bytes=megabytes * 2**20),
        name=name,
    )(*scalars, *inputs, *unread)
    return result[0] if single else result


def pairs(one, other, axis):
    count = lax.axis_size(axis)

    def exchange(x, start):
        swap = [(i, i + 1) for i in range(start, count - 1, 2)]
        return lax.ppermute(x, axis, swap + [(j, i) for i, j in swap])

    got = exchange(other, 1)
    return exchange(one, 0), got


def doubled(table, axis):
    count = lax.axis_size(axis)
    bit = 1
    while bit < count:
        got = lax.ppermute(table, axis, [(i, i ^ bit) for i in range(count)])
        table = jnp.concatenate([table, got], axis=0)
        bit *= 2
    return table


def requests(match, value, capacity):
    rank = jnp.cumsum(match.astype(jnp.int32), axis=1) - 1
    hit = match[:, None, :] & (rank[:, None, :] == jnp.arange(capacity)[None, :, None])
    return jnp.max(jnp.where(hit, value[:, None, :], -1), axis=2)


def shards(cells, instance_cell, target, row_taps, col_taps, kernel_weight):
    deep, cores, cols = lax.axis_size("deep"), lax.axis_size("core"), lax.axis_size("col")
    everyone = ("deep", "core", "col")
    plane = ("core", "col")
    peers = cores * cols
    slots = cells.shape[0]
    tile_rows, tile_cols = instance_cell.shape
    tiles_here = tile_rows * tile_cols
    height, breadth = target.shape
    owners = deep * peers
    capacity = 2 * ((tiles_here + owners - 1) // owners)
    f32 = lambda *shape: jax.ShapeDtypeStruct(shape, F32)

    flat = to_rows(cells)
    ordered = kernel_call(spread_kernel, "spread", f32(slots * 8, LANES), [], [], [flat])
    named = instance_cell.reshape(1, -1)
    near = doubled(doubled(named, "col"), "core")
    levels = [ordered]
    for e in range(1, deep):
        levels.append(lax.ppermute(ordered, "deep", [(i, i ^ e) for i in range(deep)]))
    row_axes = ("deep", "core")
    my_row, my_col = lax.axis_index(row_axes), lax.axis_index("col")
    me = jnp.stack(
        [
            lax.axis_index(plane),
            lax.axis_index(everyone),
            my_row * height - HALF,
            my_col * breadth - HALF,
            jnp.int32(deep * cores * height),
            jnp.int32(cols * breadth),
            my_row % 2,
            my_col % 2,
        ]
    ).astype(jnp.int32)
    my_deep = lax.axis_index("deep")
    here = ((my_deep ^ jnp.arange(deep)) * peers + me[0])[None, :, None]
    match = (near // slots)[:, None, :] == here
    slot = jnp.broadcast_to((near % slots)[:, None, :], match.shape)
    asked = requests(
        match.reshape(peers * deep, tiles_here), slot.reshape(peers * deep, tiles_here), capacity
    ).reshape(peers, deep, capacity)
    waves = make_waves(row_taps, col_taps)
    size = peers * deep * capacity * 8
    packed = kernel_call(
        pack_kernel,
        "pack",
        f32(size, LANES),
        [pltpu.VMEM((size, LANES), F32), pltpu.SemaphoreType.DMA((peers,))],
        [asked, me],
        levels,
        out_space=pl.ANY,
    )
    odd = me[6] > 0
    head, foot = target[:HALF], target[height - HALF :]
    packed, near, one, other = lax.optimization_barrier(
        (packed, near, jnp.where(odd, head, foot), jnp.where(odd, foot, head))
    )
    one, other = pairs(one, other, row_axes)
    above, below = jnp.where(odd, one, other), jnp.where(odd, other, one)
    arrived = lax.all_to_all(packed, plane, split_axis=0, concat_axis=0, tiled=True)

    everything = doubled(near, "deep")
    wanted = requests(everything // slots == me[1], everything % slots, capacity)
    mine = named[0] // slots
    earlier = jnp.tri(tiles_here, k=-1, dtype=bool)

    def place(group, size):
        same = (group[:, None] == group[None, :]) & earlier
        where = group * size + jnp.sum(same.astype(jnp.int32), axis=1)
        return where.reshape(tile_rows, tile_cols)

    home = place(mine, capacity)
    theirs = home // capacity
    level = my_deep ^ (theirs // peers)
    index = (theirs % peers * deep + level) * capacity + home % capacity
    wide = 2 * HALF
    quarter = (height + wide) // 4
    edge = f32(height // 2 + wide + quarter, LANES)
    mask, rowa, rowb = kernel_call(
        assemble_kernel,
        "assemble",
        [f32(height, breadth), f32(wide, breadth), f32(wide, breadth)],
        [pltpu.VMEM((height * (breadth // LANES), LANES), F32)],
        [index, me],
        [arrived],
    )
    rowa, rowb = pairs(rowa, rowb, row_axes)
    cola, colb = kernel_call(
        edges_kernel,
        "edges",
        [edge, edge],
        [pltpu.VMEM((2, 4, quarter, LANES), F32)],
        [],
        [jnp.broadcast_to(me[:, None], (8, LANES)), mask, rowa, rowb, target, above, below],
        [wanted],
    )
    cola, colb = pairs(cola, colb, "col")
    field_rows = height + 2 * HALF
    returned = kernel_call(
        image_kernel,
        "image",
        f32(owners * capacity * 8, LANES),
        [
            pltpu.VMEM((KERNELS // 2, 2, 2, LANES, LANES), BF16),
            pltpu.VMEM((KERNELS, 2, field_rows, 256), BF16),
            pltpu.VMEM((KERNELS, 2, LANES, 256), BF16),
            pltpu.VMEM((KERNELS, 1024, WIDE), BF16),
            pltpu.VMEM((field_rows, breadth + 128), F32),
            pltpu.VMEM((height + 4 * HALF, breadth + 128), BF16),
            pltpu.VMEM((height + 4 * HALF, breadth + 128), BF16),
            pltpu.VMEM((height + 4 * HALF, breadth), BF16),
            pltpu.VMEM((height + 4 * HALF, breadth), BF16),
            pltpu.VMEM((KERNELS, field_rows, WIDE), F32),
            pltpu.VMEM((KERNELS, height, breadth + 128), BF16),
            pltpu.VMEM((KERNELS, height, breadth + 128), BF16),
            pltpu.VMEM((height * (breadth // LANES), LANES), F32),
        ],
        [home, me, kernel_weight],
        [mask, rowa, rowb, cola, colb, target, above, below, waves],
        megabytes=36,
    )
    back = lax.all_to_all(returned, everyone, split_axis=0, concat_axis=0, tiled=True)
    stepped = kernel_call(
        step_kernel,
        "step",
        f32(slots * 8, LANES),
        [pltpu.VMEM((slots * 8, LANES), F32)] * 8,
        [wanted, me],
        [flat, back],
    )
    return from_rows(stepped)


def solution(mesh):
    rows, cols = mesh.devices.shape
    finer = Mesh(mesh.devices.reshape(rows // 2, 2, cols), ("deep", "core", "col"))
    row = ("deep", "core")
    placed = (P((*row, "col"), None), P(row, "col"), P(row, "col"), P(), P(), P())
    return jax.shard_map(
        shards, mesh=finer, in_specs=placed, out_specs=P((*row, "col"), None), check_vma=False
    )
```
